32 devices in a mesh: dp: 4 (over z), ctx: 8 (over y, x, core).
Axes of the slice: x: 2, y: 2, z: 4, core: 2. Of those that a mesh axis runs over, the one named last changes fastest.
Arguments:
- inputs: bfloat16 [512, 8, 2048], P('ctx', 'dp'), may hold values from -8 to 8
- lengths: int32 [4, 2], P('dp'), may hold values from 1 to 512, as said below
- w_qkv: bfloat16 [2048, 6144], P(('dp', 'ctx')), may hold values from -0.125 to 0.125
- b_qkv: bfloat16 [6144], P(('dp', 'ctx')), may hold values from -0.5 to 0.5
- w_out: bfloat16 [2048, 2048], P(('dp', 'ctx')), may hold values from -1 to 1
- w_gate: bfloat16 [2048, 5632], P(('dp', 'ctx')), may hold values from -0.125 to 0.125
- w_up: bfloat16 [2048, 5632], P(('dp', 'ctx')), may hold values from -0.125 to 0.125
- w_down: bfloat16 [5632, 2048], P(('dp', 'ctx')), may hold values from -0.078125 to 0.078125
- gain_one: bfloat16 [2048], P(('dp', 'ctx')), may hold values from 0.25 to 1.75
- shift_one: bfloat16 [2048], P(('dp', 'ctx')), may hold values from -0.5 to 0.5
- gain_two: bfloat16 [2048], P(('dp', 'ctx')), may hold values from 0.25 to 1.75
- shift_two: bfloat16 [2048], P(('dp', 'ctx')), may hold values from -0.5 to 0.5
- cotangent: bfloat16 [512, 8, 2048], P('ctx', 'dp'), may hold values from -6 to 6
Outputs:
- output: bfloat16 [512, 8, 2048], P('ctx', 'dp')
- input_grad: float32 [512, 8, 2048], P('ctx', 'dp')
- grad_qkv: float32 [2048, 6144], P(('dp', 'ctx'))
- grad_bias: float32 [6144], P(('dp', 'ctx'))
- grad_out: float32 [2048, 2048], P(('dp', 'ctx'))
- grad_gate: float32 [2048, 5632], P(('dp', 'ctx'))
- grad_up: float32 [2048, 5632], P(('dp', 'ctx'))
- grad_down: float32 [5632, 2048], P(('dp', 'ctx'))
- grad_gain_one: float32 [2048], P(('dp', 'ctx'))
- grad_shift_one: float32 [2048], P(('dp', 'ctx'))
- grad_gain_two: float32 [2048], P(('dp', 'ctx'))
- grad_shift_two: float32 [2048], P(('dp', 'ctx'))
The draws below stay inside these ranges and needn't reach their ends.
Inputs may be any that keep to these rules, and one draw needn't show every extreme that they name: In every row one slot, drawn from the seed, has length exactly 512; the other slots' lengths are drawn evenly from 1 to 512.
All inputs are finite; a program needn't handle non-finite values.
Results may differ from the reference program's by a relative error of at most 0.018.
Values may be sent and summed in bfloat16 or wider, within the bound.
A program may use at most 448 MiB of HBM per device.

```python
import jax
import jax.numpy as jnp
from jax import lax

D = 2048
FF = 5632
HEADS = 32
HEAD_DIM = 64
ROTARY = 16
SEQS = 2
SLOT_LEN = 512
GROUPS = 4
SLOTS = 8


def draw_lengths(key, part):
    key = jax.random.fold_in(key, 7)
    pick_key, length_key = jax.random.split(key)
    chosen = jax.random.randint(pick_key, (GROUPS, 1), 0, SEQS)
    random_len = jax.random.randint(length_key, (GROUPS, SEQS), 1, SLOT_LEN + 1)
    slot_ids = jnp.arange(SEQS, dtype=jnp.int32)[None, :]
    return jnp.where(slot_ids == chosen, SLOT_LEN, random_len).astype(jnp.int32)


def spiked(entries, stream_key, source, target, parts, factor):
    owner, partner = [(jnp.arange(entries.shape[position]) // (entries.shape[position] // parts)).reshape([-1 if axis == position else 1 for axis in range(entries.ndim)]) for position in (source, target)]
    chosen = jax.random.permutation(stream_key, parts)[partner]
    strong = (owner == chosen) | (owner == (partner + parts // 2) % parts)
    return jnp.where(strong, factor * entries, entries)


def shard_levels(key, shape, shards, smallest, high):
    gain = 1.0
    for position, shards_of in shards:
        draws = jax.random.uniform(jax.random.fold_in(jax.random.fold_in(key, 6), position), (shards_of,), jnp.float32, smallest / len(shards), high / len(shards))
        gain = gain * jnp.repeat(jnp.exp(draws), shape[position] // shards_of).reshape((-1,) + (1,) * (len(shape) - 1 - position))
    return gain


def normal_values(rng, dims, spread, limit, cuts=(), kind=jnp.bfloat16):
    values = jax.random.normal(rng, dims, jnp.float32) * spread
    if len(cuts) > 0:
        values = shard_levels(rng, dims, cuts, -0.22, 0.18) * values
    return jnp.clip(values, min=-limit, max=limit).astype(kind)


def noise_with(own_key, extent, scale, most, cuts, heavy, kind=jnp.bfloat16):
    values = scale * jax.random.normal(own_key, extent, jnp.float32)
    if cuts:
        values = values * shard_levels(own_key, extent, cuts, -0.22, 0.18)
    return jnp.clip(spiked(values, jax.random.fold_in(own_key, 3), *heavy), -most, most).astype(kind)


def setup_inputs(seed: int = 0) -> dict:
    splits = jax.random.split(jax.random.key(seed), 14)
    return {
        "inputs": noise_with(splits[0], (SLOT_LEN, SLOTS, D), 1.0, 8.0, ((0, 8), (1, 4)), (0, 2, 8, 2.0)),
        "lengths": draw_lengths(jax.random.fold_in(splits[13], 71), 0),
        "w_qkv": normal_values(splits[2], (D, 3 * D), D ** -0.5, 0.125, ((0, 32),)),
        "b_qkv": jnp.clip(jax.random.uniform(splits[3], (3 * D,), jnp.float32, -0.5, 0.5) * shard_levels(splits[3], (3 * D,), ((0, 32),), -0.4, 0.0), -0.5, 0.5).astype(jnp.bfloat16),
        "w_out": normal_values(splits[4], (D, D), (D // 64) ** -0.5, 1.0, ((0, 32),)),
        "w_gate": normal_values(splits[5], (D, FF), D ** -0.5, 0.125, ((0, 32),)),
        "w_up": normal_values(splits[6], (D, FF), D ** -0.5, 0.125, ((0, 32),)),
        "w_down": normal_values(splits[7], (FF, D), FF ** -0.5, 0.078125, ((0, 32),)),
        "gain_one": jnp.clip(0.25 + 1.5 * jax.random.uniform(splits[8], (D,), jnp.float32) ** shard_levels(splits[8], (D,), ((0, 32),), -0.2, 0.2), 0.25, 1.75).astype(jnp.bfloat16),
        "shift_one": jnp.clip(jax.random.uniform(splits[9], (D,), jnp.float32, -0.5, 0.5) * shard_levels(splits[9], (D,), ((0, 32),), -0.4, 0.0), -0.5, 0.5).astype(jnp.bfloat16),
        "gain_two": jnp.clip(0.25 + 1.5 * jax.random.uniform(splits[10], (D,), jnp.float32) ** shard_levels(splits[10], (D,), ((0, 32),), -0.2, 0.2), 0.25, 1.75).astype(jnp.bfloat16),
        "shift_two": jnp.clip(jax.random.uniform(splits[11], (D,), jnp.float32, -0.5, 0.5) * shard_levels(splits[11], (D,), ((0, 32),), -0.4, 0.0), -0.5, 0.5).astype(jnp.bfloat16),
        "cotangent": normal_values(splits[12], (SLOT_LEN, SLOTS, D), 1.0, 6.0, ((0, 8), (1, 4))),
    }


@jax.custom_vjp
def low(v):
    return lax.optimization_barrier(v.astype(jnp.bfloat16)).astype(jnp.float32)

@jax.custom_vjp
def low_back(v):
    return v

def low_keep(v):
    return (low(v), None)

def low_pass(kept, grad):
    return (grad,)

def back_keep(v):
    return (v, None)

def back_low(kept, grad):
    return (low(grad),)
low.defvjp(low_keep, low_pass)
low_back.defvjp(back_keep, back_low)
epsilon = 1e-05
masked_value = -1e+30

def matmul(left, right):
    return jnp.dot(left, right, precision=lax.Precision.HIGHEST)

def layer_norm(values, gain_vec, shift_vec):
    row_mean = lax.optimization_barrier(jnp.mean(values, -1, keepdims=True))
    centred = values - row_mean
    variance = lax.optimization_barrier(jnp.mean(centred * centred, -1, keepdims=True))
    return centred * lax.rsqrt(variance + epsilon) * gain_vec + shift_vec

def rotary_tables(positions):
    counter = jnp.arange(ROTARY // 2, dtype=jnp.float32)
    frequency = 10000.0 ** (-2.0 * counter / ROTARY)
    angles = positions.astype(jnp.float32)[:, None] * frequency[None, :]
    return (jnp.cos(angles), jnp.sin(angles))

def rotate(values, cos_table, sin_table):
    half_dims = ROTARY // 2
    first_half = values[..., :half_dims]
    second_half = values[..., half_dims:ROTARY]
    return jnp.concatenate([first_half * cos_table - second_half * sin_table, second_half * cos_table + first_half * sin_table, values[..., ROTARY:]], -1)

def slot_layer(params, slot_input, slot_length):
    w_qkv, b_qkv, w_out, w_gate, w_up, w_down, gain_one, shift_one, gain_two, shift_two = params
    positions = jnp.arange(SLOT_LEN)
    normed_one = low(layer_norm(slot_input, gain_one, shift_one))
    joined = low_back(matmul(normed_one, w_qkv) + b_qkv).reshape(SLOT_LEN, 3, HEADS, HEAD_DIM)
    cos_table, sin_table = rotary_tables(positions)
    cos_table = cos_table[:, None, :]
    sin_table = sin_table[:, None, :]
    queries = low(rotate(joined[:, 0], cos_table, sin_table))
    keys_rot = low(rotate(joined[:, 1], cos_table, sin_table))
    values_low = low(joined[:, 2])
    scores = low_back(jnp.einsum('qhd,khd->hqk', queries, keys_rot, precision=lax.Precision.HIGHEST) * 0.125)
    allowed = ((positions[None, :] <= positions[:, None]) & (positions[:, None] < slot_length))[None]
    masked = jnp.where(allowed, scores, masked_value)
    row_peak = lax.optimization_barrier(jnp.max(masked, -1, keepdims=True))
    weights = jnp.where(allowed, jnp.exp(masked - row_peak), 0.0)
    probs = low(weights / jnp.maximum(lax.optimization_barrier(jnp.sum(weights, -1, keepdims=True)), 1.0))
    attended = jnp.einsum('hqk,khd->qhd', probs, values_low, precision=lax.Precision.HIGHEST).reshape(SLOT_LEN, D)
    hidden_in = slot_input + low_back(matmul(low(low_back(attended)), w_out))
    normed_two = low(layer_norm(hidden_in, gain_two, shift_two))
    gate = low_back(matmul(normed_two, w_gate))
    upward = low_back(matmul(normed_two, w_up))
    product = low(jax.nn.silu(gate) * upward)
    return hidden_in + matmul(product, w_down)

def reference(inputs, lengths, w_qkv, b_qkv, w_out, w_gate, w_up, w_down, gain_one, shift_one, gain_two, shift_two, cotangent):
    params = tuple((tensor.astype(jnp.float32) for tensor in (w_qkv, b_qkv, w_out, w_gate, w_up, w_down, gain_one, shift_one, gain_two, shift_two)))
    slot_lengths = lengths.reshape(SLOTS).astype(jnp.int32)
    slot_inputs = jnp.transpose(inputs.astype(jnp.float32), (1, 0, 2))
    layer = jax.checkpoint(slot_layer)

    def forward(weight_set, slot_data):
        return lax.map(lambda slot_pair: layer(weight_set, slot_pair[0], slot_pair[1]), (slot_data, slot_lengths))
    result, pullback = jax.vjp(forward, params, slot_inputs)
    grad_params, grad_inputs = pullback(jnp.transpose(cotangent.astype(jnp.float32), (1, 0, 2)))
    return (jnp.transpose(result, (1, 0, 2)).astype(jnp.bfloat16), jnp.transpose(grad_inputs, (1, 0, 2)), grad_params[0], grad_params[1], grad_params[2], grad_params[3], grad_params[4], grad_params[5], grad_params[6], grad_params[7], grad_params[8], grad_params[9])
```

```python
import math

import jax
import jax.numpy as jnp
from jax import lax
from jax.sharding import PartitionSpec as P

HEADS = 32
HEAD_DIM = 64
ROTARY = 16


epsilon = 1e-05
masked_value = -1e30


def layer_stats(values):
    row_mean = jnp.mean(values, -1, keepdims=True)
    centred = values - row_mean
    inverse = lax.rsqrt(jnp.mean(centred * centred, -1, keepdims=True) + epsilon)
    return (centred * inverse, inverse)


def norm_back(grad_normed, scaled, inverse, gain_vec):
    grad_hat = grad_normed * gain_vec
    return inverse * (
        grad_hat
        - jnp.mean(grad_hat, -1, keepdims=True)
        - scaled * jnp.mean(grad_hat * scaled, -1, keepdims=True)
    )


def rotary_tables(positions):
    counter = jnp.arange(ROTARY // 2, dtype=jnp.float32)
    frequency = 10000.0 ** (-2.0 * counter / ROTARY)
    angles = positions.astype(jnp.float32)[:, None] * frequency[None, :]
    return (jnp.cos(angles)[:, None, None, :], jnp.sin(angles)[:, None, None, :])


def rotate(values, cos_table, sin_table):
    half_dims = ROTARY // 2
    first_half = values[..., :half_dims]
    second_half = values[..., half_dims:ROTARY]
    return jnp.concatenate(
        [
            first_half * cos_table - second_half * sin_table,
            second_half * cos_table + first_half * sin_table,
            values[..., ROTARY:],
        ],
        -1,
    )


def over_blocks(step_fn, running, gathered):
    total_rows = gathered.shape[0]
    tile_rows = math.gcd(total_rows, 512)

    def visit_block(number, current):
        block_start = number * tile_rows
        block_part = lax.dynamic_slice_in_dim(gathered, block_start, tile_rows, 0)
        return step_fn(current, block_part, block_start)

    return lax.fori_loop(0, total_rows // tile_rows, visit_block, running)


def gathered_shards(
    inputs,
    lengths,
    w_qkv,
    b_qkv,
    w_out,
    w_gate,
    w_up,
    w_down,
    gain_one,
    shift_one,
    gain_two,
    shift_two,
    cotangent,
):
    local_rows, slot_count, width = inputs.shape
    positions = lax.axis_index("ctx") * local_rows + jnp.arange(local_rows, dtype=jnp.int32)
    live_rows = positions[:, None] < lengths[0][None, :]
    live_heads = jnp.transpose(live_rows)[:, None, :, None]
    cos_table, sin_table = rotary_tables(positions)

    def allowed_mask(offset, count):
        key_pos = offset + jnp.arange(count, dtype=jnp.int32)
        causal = key_pos[None, :] <= positions[:, None]
        return causal[None, None, :, :] & live_heads

    def split_heads(block_part):
        count = block_part.shape[0]
        key_part = block_part[:, :, 0].reshape(count, slot_count, HEADS, HEAD_DIM)
        value_part = block_part[:, :, 1].reshape(count, slot_count, HEADS, HEAD_DIM)
        return (key_part, value_part)

    attn_full = (
        lax.all_gather(w_qkv, ("dp", "ctx"), axis=0, tiled=True),
        lax.all_gather(b_qkv, ("dp", "ctx"), axis=0, tiled=True),
        lax.all_gather(w_out, ("dp", "ctx"), axis=0, tiled=True),
        lax.all_gather(gain_one, ("dp", "ctx"), axis=0, tiled=True),
        lax.all_gather(shift_one, ("dp", "ctx"), axis=0, tiled=True),
    )
    qkv_full, bias_full, out_full, gain_one_full, shift_one_full = attn_full
    source = inputs.astype(jnp.float32)
    scaled_one, inverse_one = layer_stats(source)
    normed_one = (
        scaled_one * gain_one_full.astype(jnp.float32) + shift_one_full.astype(jnp.float32)
    ).astype(jnp.bfloat16)
    joined = jnp.einsum(
        "rsd,de->rse", normed_one, qkv_full, preferred_element_type=jnp.float32
    ) + bias_full.astype(jnp.float32)
    query_pre = joined[..., :width].reshape(local_rows, slot_count, HEADS, HEAD_DIM)
    key_pre = joined[..., width : 2 * width].reshape(local_rows, slot_count, HEADS, HEAD_DIM)
    queries = rotate(query_pre, cos_table, sin_table).astype(jnp.bfloat16)
    keys_rot = rotate(key_pre, cos_table, sin_table).reshape(local_rows, slot_count, width)
    key_value = jnp.stack([keys_rot, joined[..., 2 * width :]], 2).astype(jnp.bfloat16)
    block_part = lax.all_gather(key_value, "ctx", axis=0, tiled=True)
    run_peak = jnp.full((slot_count, HEADS, local_rows), masked_value, jnp.float32)
    key_part, value_part = split_heads(block_part)
    scores = (
        jnp.einsum("qshd,kshd->shqk", queries, key_part, preferred_element_type=jnp.float32) * 0.125
    )
    allowed = allowed_mask(jnp.int32(0), block_part.shape[0])
    masked = jnp.where(allowed, scores, masked_value)
    new_peak = jnp.maximum(run_peak, jnp.max(masked, -1))
    weights = jnp.where(allowed, jnp.exp(masked - new_peak[..., None]), 0.0)
    new_sum = jnp.sum(weights, -1)
    new_acc = jnp.einsum(
        "shqk,kshd->shqd",
        weights.astype(jnp.bfloat16),
        value_part,
        preferred_element_type=jnp.float32,
    )
    final_sum = jnp.maximum(new_sum, 1.0)
    log_sum = new_peak + jnp.log(final_sum)
    attended = jnp.transpose(new_acc / final_sum[..., None], (2, 0, 1, 3))
    attended_low = attended.reshape(local_rows, slot_count, width).astype(jnp.bfloat16)
    hidden_in = source + jnp.einsum(
        "rsd,de->rse", attended_low, out_full, preferred_element_type=jnp.float32
    )
    mlp_full = (
        lax.all_gather(w_gate, ("dp", "ctx"), axis=0, tiled=True),
        lax.all_gather(w_up, ("dp", "ctx"), axis=0, tiled=True),
        lax.all_gather(w_down, ("dp", "ctx"), axis=0, tiled=True),
        lax.all_gather(gain_two, ("dp", "ctx"), axis=0, tiled=True),
        lax.all_gather(shift_two, ("dp", "ctx"), axis=0, tiled=True),
    )
    gate_full, up_full, down_full, gain_two_full, shift_two_full = mlp_full
    scaled_two, inverse_two = layer_stats(hidden_in)
    normed_two = (
        scaled_two * gain_two_full.astype(jnp.float32) + shift_two_full.astype(jnp.float32)
    ).astype(jnp.bfloat16)
    gate = jnp.einsum("rsd,df->rsf", normed_two, gate_full, preferred_element_type=jnp.float32)
    upward = jnp.einsum("rsd,df->rsf", normed_two, up_full, preferred_element_type=jnp.float32)
    sigmoid = jax.nn.sigmoid(gate)
    product = (gate * sigmoid * upward).astype(jnp.bfloat16)
    result = hidden_in + jnp.einsum(
        "rsf,fd->rsd", product, down_full, preferred_element_type=jnp.float32
    )
    gate_back, up_back, down_back, gain_two_back = (
        lax.all_gather(w_gate, ("dp", "ctx"), axis=0, tiled=True),
        lax.all_gather(w_up, ("dp", "ctx"), axis=0, tiled=True),
        lax.all_gather(w_down, ("dp", "ctx"), axis=0, tiled=True),
        lax.all_gather(gain_two, ("dp", "ctx"), axis=0, tiled=True),
    )
    grad_down = jnp.einsum("rsf,rsd->fd", product, cotangent, preferred_element_type=jnp.float32)
    grad_product = jnp.einsum(
        "rsd,fd->rsf", cotangent, down_back, preferred_element_type=jnp.float32
    )
    grad_gate_act = (grad_product * upward * sigmoid * (1.0 + gate * (1.0 - sigmoid))).astype(
        jnp.bfloat16
    )
    grad_up_act = (grad_product * gate * sigmoid).astype(jnp.bfloat16)
    grad_gate = jnp.einsum(
        "rsd,rsf->df", normed_two, grad_gate_act, preferred_element_type=jnp.float32
    )
    grad_up = jnp.einsum("rsd,rsf->df", normed_two, grad_up_act, preferred_element_type=jnp.float32)
    grad_normed_two = jnp.einsum(
        "rsf,df->rsd", grad_gate_act, gate_back, preferred_element_type=jnp.float32
    ) + jnp.einsum("rsf,df->rsd", grad_up_act, up_back, preferred_element_type=jnp.float32)
    grad_gain_two = jnp.sum(grad_normed_two * scaled_two, (0, 1))
    grad_shift_two = jnp.sum(grad_normed_two, (0, 1))
    grad_hidden = cotangent.astype(jnp.float32) + norm_back(
        grad_normed_two, scaled_two, inverse_two, gain_two_back.astype(jnp.float32)
    )
    mlp_sums = (
        lax.psum_scatter(grad_gate, ("dp", "ctx"), scatter_dimension=0, tiled=True),
        lax.psum_scatter(grad_up, ("dp", "ctx"), scatter_dimension=0, tiled=True),
        lax.psum_scatter(grad_down, ("dp", "ctx"), scatter_dimension=0, tiled=True),
        lax.psum_scatter(grad_gain_two, ("dp", "ctx"), scatter_dimension=0, tiled=True),
        lax.psum_scatter(grad_shift_two, ("dp", "ctx"), scatter_dimension=0, tiled=True),
    )
    qkv_back, out_back, gain_one_back = (
        lax.all_gather(w_qkv, ("dp", "ctx"), axis=0, tiled=True),
        lax.all_gather(w_out, ("dp", "ctx"), axis=0, tiled=True),
        lax.all_gather(gain_one, ("dp", "ctx"), axis=0, tiled=True),
    )
    hidden_low = grad_hidden.astype(jnp.bfloat16)
    grad_out = jnp.einsum(
        "rsd,rse->de", attended_low, hidden_low, preferred_element_type=jnp.float32
    )
    grad_attended = jnp.einsum(
        "rse,de->rsd", hidden_low, out_back, preferred_element_type=jnp.float32
    )
    grad_heads = grad_attended.reshape(local_rows, slot_count, HEADS, HEAD_DIM).astype(jnp.bfloat16)
    delta = jnp.transpose(jnp.sum(grad_heads.astype(jnp.float32) * attended, -1), (1, 2, 0))
    key_value_all = lax.all_gather(key_value, "ctx", axis=0, tiled=True)

    def grad_parts(block_part, offset):
        key_part, value_part = split_heads(block_part)
        scores = (
            jnp.einsum("qshd,kshd->shqk", queries, key_part, preferred_element_type=jnp.float32)
            * 0.125
        )
        allowed = allowed_mask(offset, block_part.shape[0])
        probs = jnp.where(allowed, jnp.exp(scores - log_sum[..., None]), 0.0)
        grad_prob = jnp.einsum(
            "qshd,kshd->shqk", grad_heads, value_part, preferred_element_type=jnp.float32
        )
        grad_score = (probs * (grad_prob - delta[..., None])).astype(jnp.bfloat16)
        return (key_part, probs, grad_score)

    def query_step(running, block_part, offset):
        key_part, probs, grad_score = grad_parts(block_part, offset)
        return running + jnp.einsum(
            "shqk,kshd->shqd", grad_score, key_part, preferred_element_type=jnp.float32
        )

    grad_query = (
        over_blocks(
            query_step,
            jnp.zeros((slot_count, HEADS, local_rows, HEAD_DIM), jnp.float32),
            key_value_all,
        )
        * 0.125
    )
    count = local_rows * lax.axis_size("ctx")
    tile_rows = math.gcd(count, 512)

    def one_block(number):
        block_start = number * tile_rows
        block_part = lax.dynamic_slice_in_dim(key_value_all, block_start, tile_rows, 0)
        key_part, probs, grad_score = grad_parts(block_part, block_start)
        grad_key = (
            jnp.einsum("shqk,qshd->kshd", grad_score, queries, preferred_element_type=jnp.float32)
            * 0.125
        )
        grad_value = jnp.einsum(
            "shqk,qshd->kshd",
            probs.astype(jnp.bfloat16),
            grad_heads,
            preferred_element_type=jnp.float32,
        )
        return jnp.stack(
            [
                grad_key.reshape(tile_rows, slot_count, width),
                grad_value.reshape(tile_rows, slot_count, width),
            ],
            2,
        )

    blocks = lax.map(one_block, jnp.arange(count // tile_rows, dtype=jnp.int32))
    grad_key_value = lax.psum_scatter(
        blocks.reshape(count, slot_count, 2, width).astype(jnp.bfloat16),
        "ctx",
        scatter_dimension=0,
        tiled=True,
    ).astype(jnp.float32)
    grad_query_pre = rotate(jnp.transpose(grad_query, (2, 0, 1, 3)), cos_table, -sin_table)
    grad_key_pre = rotate(
        grad_key_value[:, :, 0].reshape(local_rows, slot_count, HEADS, HEAD_DIM),
        cos_table,
        -sin_table,
    )
    grad_joined = jnp.concatenate(
        [
            grad_query_pre.reshape(local_rows, slot_count, width),
            grad_key_pre.reshape(local_rows, slot_count, width),
            grad_key_value[:, :, 1],
        ],
        -1,
    ).astype(jnp.bfloat16)
    grad_qkv = jnp.einsum(
        "rsd,rse->de", normed_one, grad_joined, preferred_element_type=jnp.float32
    )
    grad_bias = jnp.sum(grad_joined.astype(jnp.float32), (0, 1))
    grad_normed_one = jnp.einsum(
        "rse,de->rsd", grad_joined, qkv_back, preferred_element_type=jnp.float32
    )
    grad_gain_one = jnp.sum(grad_normed_one * scaled_one, (0, 1))
    grad_shift_one = jnp.sum(grad_normed_one, (0, 1))
    input_grad = grad_hidden + norm_back(
        grad_normed_one, scaled_one, inverse_one, gain_one_back.astype(jnp.float32)
    )
    attn_sums = (
        lax.psum_scatter(grad_qkv, ("dp", "ctx"), scatter_dimension=0, tiled=True),
        lax.psum_scatter(grad_bias, ("dp", "ctx"), scatter_dimension=0, tiled=True),
        lax.psum_scatter(grad_out, ("dp", "ctx"), scatter_dimension=0, tiled=True),
        lax.psum_scatter(grad_gain_one, ("dp", "ctx"), scatter_dimension=0, tiled=True),
        lax.psum_scatter(grad_shift_one, ("dp", "ctx"), scatter_dimension=0, tiled=True),
    )
    return (
        result.astype(jnp.bfloat16),
        input_grad,
        attn_sums[0],
        attn_sums[1],
        attn_sums[2],
        mlp_sums[0],
        mlp_sums[1],
        mlp_sums[2],
        attn_sums[3],
        attn_sums[4],
        mlp_sums[3],
        mlp_sums[4],
    )


def tensor_shards(
    inputs,
    lengths,
    w_qkv,
    b_qkv,
    w_out,
    w_gate,
    w_up,
    w_down,
    gain_one,
    shift_one,
    gain_two,
    shift_two,
    cotangent,
):
    rows, slots, width = inputs.shape
    f32, b16 = jnp.float32, jnp.bfloat16
    zs, n = lax.axis_size("dp"), lax.axis_size("ctx")
    me = lax.axis_index("ctx")
    local = rows * slots
    tokens = local * n
    seq = rows * n
    wrows = w_qkv.shape[0]
    ff_block = w_down.shape[0]
    heads = HEADS // n
    hc = heads * HEAD_DIM
    ffc = ff_block * zs

    def dot(a, b, dims):
        return lax.dot_general(a, b, (dims, ((), ())), preferred_element_type=f32)

    def local_tokens(v):
        return jnp.transpose(v, (1, 0, 2)).reshape(local, width)

    def back_tokens(v):
        return jnp.transpose(v.reshape(slots, rows, width), (1, 0, 2))

    def exchange(v):
        return lax.all_to_all(v, "ctx", 0, 0, tiled=True)

    def gather_ctx(v):
        return lax.all_gather(v, "ctx", axis=0, tiled=True)

    def scatter_ctx(v):
        return lax.psum_scatter(v.astype(b16), "ctx", scatter_dimension=0, tiled=True).astype(f32)

    def gather_dp(v):
        return lax.all_gather(v, "dp", axis=0, tiled=True)

    def scatter_dp(v):
        return lax.psum_scatter(v.astype(b16), "dp", scatter_dimension=0, tiled=True)

    xs = local_tokens(inputs)
    dy = local_tokens(cotangent)
    qkv_send = jnp.transpose(w_qkv.reshape(wrows, 3, zs, n, HEAD_DIM), (3, 0, 1, 2, 4)).reshape(
        n, wrows, 3 * hc
    )

    def ff_send(w):
        return jnp.transpose(w.reshape(wrows, zs, n, ff_block), (2, 0, 1, 3)).reshape(
            n, wrows, ffc
        )

    gu_send = jnp.concatenate([ff_send(w_gate), ff_send(w_up)], -1)
    small = lax.all_gather(
        jnp.concatenate([b_qkv, gain_one, shift_one, gain_two, shift_two]), ("dp", "ctx"), axis=0
    ).astype(f32)
    nb = b_qkv.shape[0]
    bias_full = small[:, :nb].reshape(3, zs, n, HEAD_DIM)
    bias_own = lax.dynamic_index_in_dim(bias_full, me, 2, keepdims=False).reshape(1, 3 * hc)
    g1, s1, g2, s2 = [
        small[:, nb + i * wrows : nb + (i + 1) * wrows].reshape(1, width) for i in range(4)
    ]

    w_qkv_c = gather_dp(exchange(qkv_send).reshape(n * wrows, 3 * hc))
    w_gu_c = gather_dp(exchange(gu_send).reshape(n * wrows, 2 * ffc))
    w_out_c = gather_dp(w_out)
    w_down_c = gather_dp(w_down)

    counter = jnp.arange(ROTARY // 2, dtype=f32)
    angles = jnp.arange(seq, dtype=f32)[:, None] * (10000.0 ** (-2.0 * counter / ROTARY))[None, :]
    cos_t, sin_t = jnp.cos(angles), jnp.sin(angles)
    zero = jnp.zeros_like(sin_t)
    rest = jnp.ones((seq, HEAD_DIM - ROTARY), f32)
    table_c = jnp.tile(jnp.concatenate([cos_t, cos_t, rest], -1), (1, heads))
    table_l = jnp.tile(jnp.concatenate([-sin_t, zero, 0 * rest], -1), (1, heads))
    table_r = jnp.tile(jnp.concatenate([zero, sin_t, 0 * rest], -1), (1, heads))

    def by_slot(v):
        return v.reshape(n, slots, rows, v.shape[-1]).transpose(1, 0, 2, 3).reshape(
            slots, seq, v.shape[-1]
        )

    def by_device(v):
        return v.reshape(slots, n, rows, v.shape[-1]).transpose(1, 0, 2, 3).reshape(
            tokens, v.shape[-1]
        )

    def turn(v, sign):
        half = ROTARY // 2
        return (
            v * table_c
            + sign * jnp.roll(v, -half, -1) * table_l
            + sign * jnp.roll(v, half, -1) * table_r
        )

    x32 = xs.astype(f32)
    n1, r1 = layer_stats(x32)
    a1 = (n1 * g1 + s1).astype(b16)
    a1_all = gather_ctx(a1)
    joined = by_slot(dot(a1_all, w_qkv_c, ((1,), (0,))) + bias_own)
    q = turn(joined[..., :hc], 1.0).astype(b16)
    k = turn(joined[..., hc : 2 * hc], 1.0).astype(b16)
    v = joined[..., 2 * hc :].astype(b16)

    def heads_of(t):
        return t.reshape(slots, seq, heads, HEAD_DIM)

    at = jnp.arange(seq, dtype=jnp.int32)
    allowed = (at[None, :] <= at[:, None])[None] & (at[None, :, None] < lengths[0][:, None, None])
    scores = jnp.einsum("sqhd,skhd->shqk", heads_of(q), heads_of(k), preferred_element_type=f32)
    scores = jnp.where(allowed[:, None], scores * 0.125, masked_value)
    peak = jnp.max(scores, -1, keepdims=True)
    weights = jnp.where(allowed[:, None], jnp.exp(scores - peak), 0.0)
    probs = (weights / jnp.maximum(jnp.sum(weights, -1, keepdims=True), 1.0)).astype(b16)
    attended = jnp.einsum("shqk,skhd->sqhd", probs, heads_of(v), preferred_element_type=f32)
    ob = by_device(attended.reshape(slots, seq, hc).astype(b16))
    hidden = x32 + scatter_ctx(dot(ob, w_out_c, ((1,), (0,))))
    n2, r2 = layer_stats(hidden)
    a2_all = gather_ctx((n2 * g2 + s2).astype(b16))

    gu = dot(a2_all, w_gu_c, ((1,), (0,)))
    gate, up = gu[:, :ffc], gu[:, ffc:]
    sig = jax.nn.sigmoid(gate)
    z = (gate * sig * up).astype(b16)
    result = hidden + scatter_ctx(dot(z, w_down_c, ((1,), (0,))))
    dy_all = gather_ctx(dy)
    grad_down = scatter_dp(dot(z, dy_all, ((0,), (0,)))).astype(f32)
    dz = dot(dy_all, w_down_c, ((1,), (1,)))
    dg = (dz * up * sig * (1.0 + gate * (1.0 - sig))).astype(b16)
    du = (dz * gate * sig).astype(b16)
    dgu = jnp.concatenate([dg, du], -1)
    grad_gu = exchange(scatter_dp(dot(a2_all, dgu, ((0,), (0,)))).reshape(n, wrows, 2 * ffc))
    da2 = scatter_ctx(dot(dgu, w_gu_c, ((1,), (1,))))
    gain_two_part = jnp.sum(da2 * n2, 0)
    shift_two_part = jnp.sum(da2, 0)
    dh = dy.astype(f32) + norm_back(da2, n2, r2, g2)
    dh_all = gather_ctx(dh.astype(b16))

    grad_out = scatter_dp(dot(ob, dh_all, ((0,), (0,)))).astype(f32)
    do = heads_of(by_slot(dot(dh_all, w_out_c, ((1,), (1,))).astype(b16)))
    dp = jnp.einsum("sqhd,skhd->shqk", do, heads_of(v), preferred_element_type=f32)
    p32 = probs.astype(f32)
    ds = (p32 * (dp - jnp.sum(p32 * dp, -1, keepdims=True))).astype(b16)
    dq = jnp.einsum("shqk,skhd->sqhd", ds, heads_of(k), preferred_element_type=f32) * 0.125
    dk = jnp.einsum("shqk,sqhd->skhd", ds, heads_of(q), preferred_element_type=f32) * 0.125
    dv = jnp.einsum("shqk,sqhd->skhd", probs, do, preferred_element_type=f32)
    dj = by_device(
        jnp.concatenate(
            [
                turn(dq.reshape(slots, seq, hc), -1.0),
                turn(dk.reshape(slots, seq, hc), -1.0),
                dv.reshape(slots, seq, hc),
            ],
            -1,
        ).astype(b16)
    )
    grad_qkv = exchange(scatter_dp(dot(a1_all, dj, ((0,), (0,)))).reshape(n, wrows, 3 * hc))
    bias_part = jnp.sum(dj.astype(f32), 0).reshape(3, zs, 1, HEAD_DIM)
    da1 = scatter_ctx(dot(dj, w_qkv_c, ((1,), (1,))))
    gain_one_part = jnp.sum(da1 * n1, 0)
    shift_one_part = jnp.sum(da1, 0)
    input_grad = dh + norm_back(da1, n1, r1, g1)

    own = (jnp.arange(n) == me)[None, None, :, None]
    devices = zs * n
    pieces = jnp.concatenate(
        [
            jnp.where(own, bias_part, 0.0).reshape(devices, nb),
            gain_one_part.reshape(devices, wrows),
            shift_one_part.reshape(devices, wrows),
            gain_two_part.reshape(devices, wrows),
            shift_two_part.reshape(devices, wrows),
        ],
        -1,
    )
    summed = lax.psum_scatter(pieces, ("dp", "ctx"), scatter_dimension=0, tiled=True)[0]

    def ff_back(part):
        return jnp.transpose(part.reshape(n, wrows, zs, ff_block), (1, 2, 0, 3)).reshape(
            wrows, zs * n * ff_block
        ).astype(f32)

    grad_qkv = jnp.transpose(grad_qkv.reshape(n, wrows, 3, zs, HEAD_DIM), (1, 2, 3, 0, 4)).reshape(
        wrows, 3 * width
    ).astype(f32)
    return (
        back_tokens(result.astype(b16)),
        back_tokens(input_grad),
        grad_qkv,
        summed[:nb],
        grad_out,
        ff_back(grad_gu[..., :ffc]),
        ff_back(grad_gu[..., ffc:]),
        grad_down,
        summed[nb : nb + wrows],
        summed[nb + wrows : nb + 2 * wrows],
        summed[nb + 2 * wrows : nb + 3 * wrows],
        summed[nb + 3 * wrows :],
    )


def solution(mesh):
    zs, n = mesh.shape["dp"], mesh.shape["ctx"]
    shards = tensor_shards if HEADS == zs * n else gathered_shards

    placed = (
        P("ctx", "dp", None),
        P("dp", None),
        P(("dp", "ctx"), None),
        P(("dp", "ctx")),
        P(("dp", "ctx"), None),
        P(("dp", "ctx"), None),
        P(("dp", "ctx"), None),
        P(("dp", "ctx"), None),
        P(("dp", "ctx")),
        P(("dp", "ctx")),
        P(("dp", "ctx")),
        P(("dp", "ctx")),
        P("ctx", "dp", None),
    )
    return jax.shard_map(
        shards,
        mesh=mesh,
        in_specs=placed,
        out_specs=(
            P("ctx", "dp", None),
            P("ctx", "dp", None),
            P(("dp", "ctx"), None),
            P(("dp", "ctx")),
            P(("dp", "ctx"), None),
            P(("dp", "ctx"), None),
            P(("dp", "ctx"), None),
            P(("dp", "ctx"), None),
            P(("dp", "ctx")),
            P(("dp", "ctx")),
            P(("dp", "ctx")),
            P(("dp", "ctx")),
        ),
        check_vma=False,
    )
```

```python
import functools
import itertools
import math

import jax
import jax.numpy as jnp
from jax import lax
from jax.experimental import pallas as pl
from jax.experimental.pallas import tpu as pltpu
from jax.sharding import PartitionSpec as P

HEADS = 32
HEAD_DIM = 64
ROTARY = 16


epsilon = 1e-05
masked_value = -1e30


def layer_stats(values):
    row_mean = jnp.mean(values, -1, keepdims=True)
    centred = values - row_mean
    inverse = lax.rsqrt(jnp.mean(centred * centred, -1, keepdims=True) + epsilon)
    return (centred * inverse, inverse)


def norm_back(grad_normed, scaled, inverse, gain_vec):
    grad_hat = grad_normed * gain_vec
    return inverse * (
        grad_hat
        - jnp.mean(grad_hat, -1, keepdims=True)
        - scaled * jnp.mean(grad_hat * scaled, -1, keepdims=True)
    )


def rotary_tables(positions):
    counter = jnp.arange(ROTARY // 2, dtype=jnp.float32)
    frequency = 10000.0 ** (-2.0 * counter / ROTARY)
    angles = positions.astype(jnp.float32)[:, None] * frequency[None, :]
    return (jnp.cos(angles)[:, None, None, :], jnp.sin(angles)[:, None, None, :])


def rotate(values, cos_table, sin_table):
    half_dims = ROTARY // 2
    first_half = values[..., :half_dims]
    second_half = values[..., half_dims:ROTARY]
    return jnp.concatenate(
        [
            first_half * cos_table - second_half * sin_table,
            second_half * cos_table + first_half * sin_table,
            values[..., ROTARY:],
        ],
        -1,
    )


def over_blocks(step_fn, running, gathered):
    total_rows = gathered.shape[0]
    tile_rows = math.gcd(total_rows, 512)

    def visit_block(number, current):
        block_start = number * tile_rows
        block_part = lax.dynamic_slice_in_dim(gathered, block_start, tile_rows, 0)
        return step_fn(current, block_part, block_start)

    return lax.fori_loop(0, total_rows // tile_rows, visit_block, running)


def gathered_shards(
    inputs,
    lengths,
    w_qkv,
    b_qkv,
    w_out,
    w_gate,
    w_up,
    w_down,
    gain_one,
    shift_one,
    gain_two,
    shift_two,
    cotangent,
):
    local_rows, slot_count, width = inputs.shape
    positions = lax.axis_index("ctx") * local_rows + jnp.arange(local_rows, dtype=jnp.int32)
    live_rows = positions[:, None] < lengths[0][None, :]
    live_heads = jnp.transpose(live_rows)[:, None, :, None]
    cos_table, sin_table = rotary_tables(positions)

    def allowed_mask(offset, count):
        key_pos = offset + jnp.arange(count, dtype=jnp.int32)
        causal = key_pos[None, :] <= positions[:, None]
        return causal[None, None, :, :] & live_heads

    def split_heads(block_part):
        count = block_part.shape[0]
        key_part = block_part[:, :, 0].reshape(count, slot_count, HEADS, HEAD_DIM)
        value_part = block_part[:, :, 1].reshape(count, slot_count, HEADS, HEAD_DIM)
        return (key_part, value_part)

    attn_full = (
        lax.all_gather(w_qkv, ("dp", "ctx"), axis=0, tiled=True),
        lax.all_gather(b_qkv, ("dp", "ctx"), axis=0, tiled=True),
        lax.all_gather(w_out, ("dp", "ctx"), axis=0, tiled=True),
        lax.all_gather(gain_one, ("dp", "ctx"), axis=0, tiled=True),
        lax.all_gather(shift_one, ("dp", "ctx"), axis=0, tiled=True),
    )
    qkv_full, bias_full, out_full, gain_one_full, shift_one_full = attn_full
    source = inputs.astype(jnp.float32)
    scaled_one, inverse_one = layer_stats(source)
    normed_one = (
        scaled_one * gain_one_full.astype(jnp.float32) + shift_one_full.astype(jnp.float32)
    ).astype(jnp.bfloat16)
    joined = jnp.einsum(
        "rsd,de->rse", normed_one, qkv_full, preferred_element_type=jnp.float32
    ) + bias_full.astype(jnp.float32)
    query_pre = joined[..., :width].reshape(local_rows, slot_count, HEADS, HEAD_DIM)
    key_pre = joined[..., width : 2 * width].reshape(local_rows, slot_count, HEADS, HEAD_DIM)
    queries = rotate(query_pre, cos_table, sin_table).astype(jnp.bfloat16)
    keys_rot = rotate(key_pre, cos_table, sin_table).reshape(local_rows, slot_count, width)
    key_value = jnp.stack([keys_rot, joined[..., 2 * width :]], 2).astype(jnp.bfloat16)
    block_part = lax.all_gather(key_value, "ctx", axis=0, tiled=True)
    run_peak = jnp.full((slot_count, HEADS, local_rows), masked_value, jnp.float32)
    key_part, value_part = split_heads(block_part)
    scores = (
        jnp.einsum("qshd,kshd->shqk", queries, key_part, preferred_element_type=jnp.float32) * 0.125
    )
    allowed = allowed_mask(jnp.int32(0), block_part.shape[0])
    masked = jnp.where(allowed, scores, masked_value)
    new_peak = jnp.maximum(run_peak, jnp.max(masked, -1))
    weights = jnp.where(allowed, jnp.exp(masked - new_peak[..., None]), 0.0)
    new_sum = jnp.sum(weights, -1)
    new_acc = jnp.einsum(
        "shqk,kshd->shqd",
        weights.astype(jnp.bfloat16),
        value_part,
        preferred_element_type=jnp.float32,
    )
    final_sum = jnp.maximum(new_sum, 1.0)
    log_sum = new_peak + jnp.log(final_sum)
    attended = jnp.transpose(new_acc / final_sum[..., None], (2, 0, 1, 3))
    attended_low = attended.reshape(local_rows, slot_count, width).astype(jnp.bfloat16)
    hidden_in = source + jnp.einsum(
        "rsd,de->rse", attended_low, out_full, preferred_element_type=jnp.float32
    )
    mlp_full = (
        lax.all_gather(w_gate, ("dp", "ctx"), axis=0, tiled=True),
        lax.all_gather(w_up, ("dp", "ctx"), axis=0, tiled=True),
        lax.all_gather(w_down, ("dp", "ctx"), axis=0, tiled=True),
        lax.all_gather(gain_two, ("dp", "ctx"), axis=0, tiled=True),
        lax.all_gather(shift_two, ("dp", "ctx"), axis=0, tiled=True),
    )
    gate_full, up_full, down_full, gain_two_full, shift_two_full = mlp_full
    scaled_two, inverse_two = layer_stats(hidden_in)
    normed_two = (
        scaled_two * gain_two_full.astype(jnp.float32) + shift_two_full.astype(jnp.float32)
    ).astype(jnp.bfloat16)
    gate = jnp.einsum("rsd,df->rsf", normed_two, gate_full, preferred_element_type=jnp.float32)
    upward = jnp.einsum("rsd,df->rsf", normed_two, up_full, preferred_element_type=jnp.float32)
    sigmoid = jax.nn.sigmoid(gate)
    product = (gate * sigmoid * upward).astype(jnp.bfloat16)
    result = hidden_in + jnp.einsum(
        "rsf,fd->rsd", product, down_full, preferred_element_type=jnp.float32
    )
    gate_back, up_back, down_back, gain_two_back = (
        lax.all_gather(w_gate, ("dp", "ctx"), axis=0, tiled=True),
        lax.all_gather(w_up, ("dp", "ctx"), axis=0, tiled=True),
        lax.all_gather(w_down, ("dp", "ctx"), axis=0, tiled=True),
        lax.all_gather(gain_two, ("dp", "ctx"), axis=0, tiled=True),
    )
    grad_down = jnp.einsum("rsf,rsd->fd", product, cotangent, preferred_element_type=jnp.float32)
    grad_product = jnp.einsum(
        "rsd,fd->rsf", cotangent, down_back, preferred_element_type=jnp.float32
    )
    grad_gate_act = (grad_product * upward * sigmoid * (1.0 + gate * (1.0 - sigmoid))).astype(
        jnp.bfloat16
    )
    grad_up_act = (grad_product * gate * sigmoid).astype(jnp.bfloat16)
    grad_gate = jnp.einsum(
        "rsd,rsf->df", normed_two, grad_gate_act, preferred_element_type=jnp.float32
    )
    grad_up = jnp.einsum("rsd,rsf->df", normed_two, grad_up_act, preferred_element_type=jnp.float32)
    grad_normed_two = jnp.einsum(
        "rsf,df->rsd", grad_gate_act, gate_back, preferred_element_type=jnp.float32
    ) + jnp.einsum("rsf,df->rsd", grad_up_act, up_back, preferred_element_type=jnp.float32)
    grad_gain_two = jnp.sum(grad_normed_two * scaled_two, (0, 1))
    grad_shift_two = jnp.sum(grad_normed_two, (0, 1))
    grad_hidden = cotangent.astype(jnp.float32) + norm_back(
        grad_normed_two, scaled_two, inverse_two, gain_two_back.astype(jnp.float32)
    )
    mlp_sums = (
        lax.psum_scatter(grad_gate, ("dp", "ctx"), scatter_dimension=0, tiled=True),
        lax.psum_scatter(grad_up, ("dp", "ctx"), scatter_dimension=0, tiled=True),
        lax.psum_scatter(grad_down, ("dp", "ctx"), scatter_dimension=0, tiled=True),
        lax.psum_scatter(grad_gain_two, ("dp", "ctx"), scatter_dimension=0, tiled=True),
        lax.psum_scatter(grad_shift_two, ("dp", "ctx"), scatter_dimension=0, tiled=True),
    )
    qkv_back, out_back, gain_one_back = (
        lax.all_gather(w_qkv, ("dp", "ctx"), axis=0, tiled=True),
        lax.all_gather(w_out, ("dp", "ctx"), axis=0, tiled=True),
        lax.all_gather(gain_one, ("dp", "ctx"), axis=0, tiled=True),
    )
    hidden_low = grad_hidden.astype(jnp.bfloat16)
    grad_out = jnp.einsum(
        "rsd,rse->de", attended_low, hidden_low, preferred_element_type=jnp.float32
    )
    grad_attended = jnp.einsum(
        "rse,de->rsd", hidden_low, out_back, preferred_element_type=jnp.float32
    )
    grad_heads = grad_attended.reshape(local_rows, slot_count, HEADS, HEAD_DIM).astype(jnp.bfloat16)
    delta = jnp.transpose(jnp.sum(grad_heads.astype(jnp.float32) * attended, -1), (1, 2, 0))
    key_value_all = lax.all_gather(key_value, "ctx", axis=0, tiled=True)

    def grad_parts(block_part, offset):
        key_part, value_part = split_heads(block_part)
        scores = (
            jnp.einsum("qshd,kshd->shqk", queries, key_part, preferred_element_type=jnp.float32)
            * 0.125
        )
        allowed = allowed_mask(offset, block_part.shape[0])
        probs = jnp.where(allowed, jnp.exp(scores - log_sum[..., None]), 0.0)
        grad_prob = jnp.einsum(
            "qshd,kshd->shqk", grad_heads, value_part, preferred_element_type=jnp.float32
        )
        grad_score = (probs * (grad_prob - delta[..., None])).astype(jnp.bfloat16)
        return (key_part, probs, grad_score)

    def query_step(running, block_part, offset):
        key_part, probs, grad_score = grad_parts(block_part, offset)
        return running + jnp.einsum(
            "shqk,kshd->shqd", grad_score, key_part, preferred_element_type=jnp.float32
        )

    grad_query = (
        over_blocks(
            query_step,
            jnp.zeros((slot_count, HEADS, local_rows, HEAD_DIM), jnp.float32),
            key_value_all,
        )
        * 0.125
    )
    count = local_rows * lax.axis_size("ctx")
    tile_rows = math.gcd(count, 512)

    def one_block(number):
        block_start = number * tile_rows
        block_part = lax.dynamic_slice_in_dim(key_value_all, block_start, tile_rows, 0)
        key_part, probs, grad_score = grad_parts(block_part, block_start)
        grad_key = (
            jnp.einsum("shqk,qshd->kshd", grad_score, queries, preferred_element_type=jnp.float32)
            * 0.125
        )
        grad_value = jnp.einsum(
            "shqk,qshd->kshd",
            probs.astype(jnp.bfloat16),
            grad_heads,
            preferred_element_type=jnp.float32,
        )
        return jnp.stack(
            [
                grad_key.reshape(tile_rows, slot_count, width),
                grad_value.reshape(tile_rows, slot_count, width),
            ],
            2,
        )

    blocks = lax.map(one_block, jnp.arange(count // tile_rows, dtype=jnp.int32))
    grad_key_value = lax.psum_scatter(
        blocks.reshape(count, slot_count, 2, width).astype(jnp.bfloat16),
        "ctx",
        scatter_dimension=0,
        tiled=True,
    ).astype(jnp.float32)
    grad_query_pre = rotate(jnp.transpose(grad_query, (2, 0, 1, 3)), cos_table, -sin_table)
    grad_key_pre = rotate(
        grad_key_value[:, :, 0].reshape(local_rows, slot_count, HEADS, HEAD_DIM),
        cos_table,
        -sin_table,
    )
    grad_joined = jnp.concatenate(
        [
            grad_query_pre.reshape(local_rows, slot_count, width),
            grad_key_pre.reshape(local_rows, slot_count, width),
            grad_key_value[:, :, 1],
        ],
        -1,
    ).astype(jnp.bfloat16)
    grad_qkv = jnp.einsum(
        "rsd,rse->de", normed_one, grad_joined, preferred_element_type=jnp.float32
    )
    grad_bias = jnp.sum(grad_joined.astype(jnp.float32), (0, 1))
    grad_normed_one = jnp.einsum(
        "rse,de->rsd", grad_joined, qkv_back, preferred_element_type=jnp.float32
    )
    grad_gain_one = jnp.sum(grad_normed_one * scaled_one, (0, 1))
    grad_shift_one = jnp.sum(grad_normed_one, (0, 1))
    input_grad = grad_hidden + norm_back(
        grad_normed_one, scaled_one, inverse_one, gain_one_back.astype(jnp.float32)
    )
    attn_sums = (
        lax.psum_scatter(grad_qkv, ("dp", "ctx"), scatter_dimension=0, tiled=True),
        lax.psum_scatter(grad_bias, ("dp", "ctx"), scatter_dimension=0, tiled=True),
        lax.psum_scatter(grad_out, ("dp", "ctx"), scatter_dimension=0, tiled=True),
        lax.psum_scatter(grad_gain_one, ("dp", "ctx"), scatter_dimension=0, tiled=True),
        lax.psum_scatter(grad_shift_one, ("dp", "ctx"), scatter_dimension=0, tiled=True),
    )
    return (
        result.astype(jnp.bfloat16),
        input_grad,
        attn_sums[0],
        attn_sums[1],
        attn_sums[2],
        mlp_sums[0],
        mlp_sums[1],
        mlp_sums[2],
        attn_sums[3],
        attn_sums[4],
        mlp_sums[3],
        mlp_sums[4],
    )


MESH = pl.DeviceIdType.MESH
HBM = pl.BlockSpec(memory_space=pltpu.HBM)
VMEM = pl.BlockSpec(memory_space=pltpu.VMEM)


def flip(index, mask):
    for bit in (1, 2, 4):
        if mask & bit:
            index = index + bit - 2 * bit * ((index // bit) % 2)
    return index


class Wires:
    def __init__(self, send, recv):
        self.send, self.recv = send, recv
        self.z, self.c = lax.axis_index("dp"), lax.axis_index("ctx")
        self.inner = (self.z == 1) | (self.z == 2)
        self.outer = (self.z == 0) | (self.z == 3)
        self.number = itertools.count()

    def put(self, src, dst, z_mask, c_mask):
        i = next(self.number)
        return pltpu.make_async_remote_copy(
            src_ref=src,
            dst_ref=dst,
            send_sem=self.send.at[i],
            recv_sem=self.recv.at[i],
            device_id=(flip(self.z, z_mask), flip(self.c, c_mask)),
            device_id_type=MESH,
        )

    def greet(self, zs, n):
        barrier = pltpu.get_barrier_semaphore()
        for m in range(1, zs):
            pl.semaphore_signal(
                barrier, inc=1, device_id=(flip(self.z, m), self.c), device_id_type=MESH
            )
        for m in range(1, n):
            pl.semaphore_signal(
                barrier, inc=1, device_id=(self.z, flip(self.c, m)), device_id_type=MESH
            )
        pl.semaphore_wait(barrier, zs + n - 2)


class DepthGather:
    def __init__(self, wires, part):
        z = wires.z
        self.wires = wires
        self.near = wires.put(part(z), part(z), 1, 0)
        self.skip = wires.put(part(z), part(z), 2, 0)
        self.mid = wires.put(part(z), part(z), 3, 0)
        far = flip(z, 2)
        self.on = wires.put(part(far), part(far), 1, 0)

    def start(self):
        self.skip.start()
        pl.when(self.wires.inner)(self.mid.start)
        self.near.start()

    def forward(self):
        @pl.when(self.wires.inner)
        def _():
            self.skip.wait_recv()
            self.on.start()

    def finish(self):
        self.near.wait_recv()
        self.near.wait_send()
        self.skip.wait_send()

        @pl.when(self.wires.inner)
        def _():
            self.mid.wait_recv()
            self.mid.wait_send()
            self.on.wait_send()

        @pl.when(self.wires.outer)
        def _():
            self.skip.wait_recv()
            self.on.wait_recv()


class LayerGather:
    def __init__(self, wires, buf, source=None):
        c = wires.c
        mine = buf.at[c] if source is None else source
        self.direct = {m: wires.put(mine, buf.at[c], 0, m) for m in (2, 4, 6, 1)}
        self.on = {
            m: wires.put(buf.at[flip(c, m)], buf.at[flip(c, m)], 0, 1) for m in (2, 4, 6)
        }

    def start(self):
        for m in (2, 4, 6, 1):
            self.direct[m].start()

    def forward(self, m):
        self.direct[m].wait_recv()
        self.on[m].start()

    def arrived(self, m):
        (self.direct[1] if m == 1 else self.on[m - 1]).wait_recv()

    def sent(self):
        for copy in (*self.direct.values(), *self.on.values()):
            copy.wait_send()


def pack_columns(dst, refs, n, zs):
    for i in range(n):
        pieces = []
        for ref, block in refs:
            pieces += [ref[:, block * (j * n + i) : block * (j * n + i + 1)] for j in range(zs)]
        dst[i] = jnp.concatenate(pieces, -1)


def spread_kernel(
    zs,
    n,
    w_qkv,
    w_gate,
    w_up,
    w_out,
    xs,
    dy,
    small,
    qkv_all,
    out_all,
    gu_own,
    xs_all,
    dy_all,
    small_all,
    qkv_send,
    gu_send,
    send,
    recv,
    local,
):
    wires = Wires(send, recv)
    z, c = wires.z, wires.c
    hc = HEAD_DIM * HEADS // n
    width = HEADS * HEAD_DIM
    ff_block = w_gate.shape[1] // (zs * n)

    own = [
        pltpu.make_async_copy(w_out, out_all.at[z], local.at[0]),
        pltpu.make_async_copy(qkv_send.at[c], qkv_all.at[z, c], local.at[1]),
        pltpu.make_async_copy(gu_send.at[c], gu_own.at[c], local.at[2]),
        pltpu.make_async_copy(xs, xs_all.at[c], local.at[3]),
        pltpu.make_async_copy(dy, dy_all.at[c], local.at[4]),
        pltpu.make_async_copy(small, small_all.at[z, c], local.at[5]),
    ]
    for i in (0, 3, 4, 5):
        own[i].start()
    pack_columns(
        qkv_send, [(w_qkv.at[:, i * width : (i + 1) * width], HEAD_DIM) for i in range(3)], n, zs
    )
    own[1].start()
    wires.greet(zs, n)
    for i in (0, 5):
        own[i].wait()

    out_z = DepthGather(wires, lambda i: out_all.at[i])
    out_z.start()
    qkv_x = [
        wires.put(qkv_send.at[flip(c, m)], qkv_all.at[z, c], 0, m) for m in range(1, n)
    ]
    for copy in qkv_x:
        copy.start()
    small_z = [wires.put(small_all.at[z, c], small_all.at[z, c], m, 0) for m in range(1, zs)]
    for copy in small_z:
        copy.start()
    xs_g = LayerGather(wires, xs_all, xs)
    xs_g.start()
    pack_columns(gu_send, [(w_gate, ff_block), (w_up, ff_block)], n, zs)
    own[2].start()
    for copy in small_z:
        copy.wait_recv()
    small_x = [
        wires.put(small_all.at[:, c], small_all.at[:, c], 0, m) for m in range(1, n)
    ]
    for copy in small_x:
        copy.start()
    own[1].wait()
    for copy in qkv_x:
        copy.wait_recv()
    half = n // 2
    qkv_z = [
        DepthGather(wires, lambda i, p=p: qkv_all.at[i, p * half : (p + 1) * half])
        for p in range(2)
    ]
    for part in qkv_z:
        part.start()
    out_z.forward()
    gu_x = [wires.put(gu_send.at[flip(c, m)], gu_own.at[c], 0, m) for m in range(1, n)]
    for copy in gu_x:
        copy.start()
    for m in (2, 4, 6):
        xs_g.forward(m)
    dy_g = LayerGather(wires, dy_all, dy)
    dy_g.start()
    qkv_z[0].forward()
    for m in (2, 4, 6):
        dy_g.forward(m)
    qkv_z[1].forward()

    for i in (2, 3, 4):
        own[i].wait()
    for group in (xs_g, dy_g):
        for m in (1, 3, 5, 7):
            group.arrived(m)
        group.sent()
    for copy in small_z:
        copy.wait_send()
    for copy in qkv_x:
        copy.wait_send()
    for copy in (*small_x, *gu_x):
        copy.wait()
    for part in (out_z, *qkv_z):
        part.finish()


def spread(zs, n, w_qkv, w_gate, w_up, w_out, xs, dy, small):
    wrows, width = w_out.shape
    qc, gc = w_qkv.shape[1] // n, 2 * w_gate.shape[1] // n
    b16 = jnp.bfloat16
    return pl.pallas_call(
        functools.partial(spread_kernel, zs, n),
        out_shape=[
            jax.ShapeDtypeStruct((zs, n, wrows, qc), b16),
            jax.ShapeDtypeStruct((zs, wrows, width), b16),
            jax.ShapeDtypeStruct((n, wrows, gc), b16),
            jax.ShapeDtypeStruct((n, *xs.shape), b16),
            jax.ShapeDtypeStruct((n, *dy.shape), b16),
            jax.ShapeDtypeStruct((zs, n, *small.shape), small.dtype),
        ],
        in_specs=[VMEM, VMEM, VMEM, HBM, HBM, HBM, HBM],
        out_specs=[HBM] * 6,
        scratch_shapes=[
            pltpu.VMEM((n, wrows, qc), b16),
            pltpu.VMEM((n, wrows, gc), b16),
            pltpu.SemaphoreType.DMA((64,)),
            pltpu.SemaphoreType.DMA((64,)),
            pltpu.SemaphoreType.DMA((6,)),
        ],
        compiler_params=pltpu.CompilerParams(
            collective_id=1, has_side_effects=True, vmem_limit_bytes=32 << 20
        ),
        name="spread",
    )(w_qkv, w_gate, w_up, w_out, xs, dy, small)


def tensor_shards(
    inputs,
    lengths,
    w_qkv,
    b_qkv,
    w_out,
    w_gate,
    w_up,
    w_down,
    gain_one,
    shift_one,
    gain_two,
    shift_two,
    cotangent,
):
    rows, slots, width = inputs.shape
    f32, b16 = jnp.float32, jnp.bfloat16
    zs, n = lax.axis_size("dp"), lax.axis_size("ctx")
    me = lax.axis_index("ctx")
    local = rows * slots
    tokens = local * n
    seq = rows * n
    wrows = w_qkv.shape[0]
    ff_block = w_down.shape[0]
    heads = HEADS // n
    hc = heads * HEAD_DIM
    ffc = ff_block * zs

    def dot(a, b, dims):
        return lax.dot_general(a, b, (dims, ((), ())), preferred_element_type=f32)

    def local_tokens(v):
        return jnp.transpose(v, (1, 0, 2)).reshape(local, width)

    def back_tokens(v):
        return jnp.transpose(v.reshape(slots, rows, width), (1, 0, 2))

    def exchange(v):
        return lax.all_to_all(v, "ctx", 0, 0, tiled=True)

    def gather_ctx(v):
        return lax.all_gather(v, "ctx", axis=0, tiled=True)

    def scatter_ctx(v):
        return lax.psum_scatter(v.astype(b16), "ctx", scatter_dimension=0, tiled=True).astype(f32)

    def gather_dp(v):
        return lax.all_gather(v, "dp", axis=0, tiled=True)

    def scatter_dp(v):
        return lax.psum_scatter(v.astype(b16), "dp", scatter_dimension=0, tiled=True)

    xs = local_tokens(inputs)
    dy = local_tokens(cotangent)
    small = jnp.concatenate([b_qkv, gain_one, shift_one, gain_two, shift_two]).astype(f32)
    small = jnp.pad(small, (0, 1024 - small.shape[0])).reshape(8, 128)
    w_qkv_c, w_out_c, gu_own, a_all, dy_all, small = spread(
        zs, n, w_qkv, w_gate, w_up, w_out, xs, dy, small
    )
    small = small.reshape(zs * n, 1024)
    dy_all = dy_all.reshape(tokens, width)
    w_qkv_c = w_qkv_c.reshape(width, 3 * hc)
    w_out_c = w_out_c.reshape(hc, width)
    nb = b_qkv.shape[0]
    bias_full = small[:, :nb].reshape(3, zs, n, HEAD_DIM)
    bias_own = lax.dynamic_index_in_dim(bias_full, me, 2, keepdims=False).reshape(1, 3 * hc)
    g1, s1, g2, s2 = [
        small[:, nb + i * wrows : nb + (i + 1) * wrows].reshape(1, width) for i in range(4)
    ]

    w_gu_c = gather_dp(gu_own.reshape(n * wrows, 2 * ffc))
    w_down_c = gather_dp(w_down)

    counter = jnp.arange(ROTARY // 2, dtype=f32)
    angles = jnp.arange(seq, dtype=f32)[:, None] * (10000.0 ** (-2.0 * counter / ROTARY))[None, :]
    cos_t, sin_t = jnp.cos(angles), jnp.sin(angles)
    zero = jnp.zeros_like(sin_t)
    rest = jnp.ones((seq, HEAD_DIM - ROTARY), f32)
    table_c = jnp.tile(jnp.concatenate([cos_t, cos_t, rest], -1), (1, heads))
    table_l = jnp.tile(jnp.concatenate([-sin_t, zero, 0 * rest], -1), (1, heads))
    table_r = jnp.tile(jnp.concatenate([zero, sin_t, 0 * rest], -1), (1, heads))

    def by_slot(v):
        return v.reshape(n, slots, rows, v.shape[-1]).transpose(1, 0, 2, 3).reshape(
            slots, seq, v.shape[-1]
        )

    def by_device(v):
        return v.reshape(slots, n, rows, v.shape[-1]).transpose(1, 0, 2, 3).reshape(
            tokens, v.shape[-1]
        )

    def turn(v, sign):
        half = ROTARY // 2
        return (
            v * table_c
            + sign * jnp.roll(v, -half, -1) * table_l
            + sign * jnp.roll(v, half, -1) * table_r
        )

    x32 = xs.astype(f32)
    n1, r1 = layer_stats(x32)
    a1_all = (layer_stats(a_all.reshape(tokens, width).astype(f32))[0] * g1 + s1).astype(b16)
    joined = by_slot(dot(a1_all, w_qkv_c, ((1,), (0,))) + bias_own)
    q = turn(joined[..., :hc], 1.0).astype(b16)
    k = turn(joined[..., hc : 2 * hc], 1.0).astype(b16)
    v = joined[..., 2 * hc :].astype(b16)

    def heads_of(t):
        return t.reshape(slots, seq, heads, HEAD_DIM)

    at = jnp.arange(seq, dtype=jnp.int32)
    allowed = (at[None, :] <= at[:, None])[None] & (at[None, :, None] < lengths[0][:, None, None])
    scores = jnp.einsum("sqhd,skhd->shqk", heads_of(q), heads_of(k), preferred_element_type=f32)
    scores = jnp.where(allowed[:, None], scores * 0.125, masked_value)
    peak = jnp.max(scores, -1, keepdims=True)
    weights = jnp.where(allowed[:, None], jnp.exp(scores - peak), 0.0)
    probs = (weights / jnp.maximum(jnp.sum(weights, -1, keepdims=True), 1.0)).astype(b16)
    attended = jnp.einsum("shqk,skhd->sqhd", probs, heads_of(v), preferred_element_type=f32)
    ob = by_device(attended.reshape(slots, seq, hc).astype(b16))
    hidden = x32 + scatter_ctx(dot(ob, w_out_c, ((1,), (0,))))
    n2, r2 = layer_stats(hidden)
    a2_all = gather_ctx((n2 * g2 + s2).astype(b16))

    gu = dot(a2_all, w_gu_c, ((1,), (0,)))
    gate, up = gu[:, :ffc], gu[:, ffc:]
    sig = jax.nn.sigmoid(gate)
    z = (gate * sig * up).astype(b16)
    result = hidden + scatter_ctx(dot(z, w_down_c, ((1,), (0,))))
    grad_down = scatter_dp(dot(z, dy_all, ((0,), (0,)))).astype(f32)
    dz = dot(dy_all, w_down_c, ((1,), (1,)))
    dg = (dz * up * sig * (1.0 + gate * (1.0 - sig))).astype(b16)
    du = (dz * gate * sig).astype(b16)
    dgu = jnp.concatenate([dg, du], -1)
    grad_gu = exchange(scatter_dp(dot(a2_all, dgu, ((0,), (0,)))).reshape(n, wrows, 2 * ffc))
    da2 = scatter_ctx(dot(dgu, w_gu_c, ((1,), (1,))))
    gain_two_part = jnp.sum(da2 * n2, 0)
    shift_two_part = jnp.sum(da2, 0)
    dh = dy.astype(f32) + norm_back(da2, n2, r2, g2)
    dh_all = gather_ctx(dh.astype(b16))

    grad_out = scatter_dp(dot(ob, dh_all, ((0,), (0,)))).astype(f32)
    do = heads_of(by_slot(dot(dh_all, w_out_c, ((1,), (1,))).astype(b16)))
    dp = jnp.einsum("sqhd,skhd->shqk", do, heads_of(v), preferred_element_type=f32)
    p32 = probs.astype(f32)
    ds = (p32 * (dp - jnp.sum(p32 * dp, -1, keepdims=True))).astype(b16)
    dq = jnp.einsum("shqk,skhd->sqhd", ds, heads_of(k), preferred_element_type=f32) * 0.125
    dk = jnp.einsum("shqk,sqhd->skhd", ds, heads_of(q), preferred_element_type=f32) * 0.125
    dv = jnp.einsum("shqk,sqhd->skhd", probs, do, preferred_element_type=f32)
    dj = by_device(
        jnp.concatenate(
            [
                turn(dq.reshape(slots, seq, hc), -1.0),
                turn(dk.reshape(slots, seq, hc), -1.0),
                dv.reshape(slots, seq, hc),
            ],
            -1,
        ).astype(b16)
    )
    grad_qkv = exchange(scatter_dp(dot(a1_all, dj, ((0,), (0,)))).reshape(n, wrows, 3 * hc))
    bias_part = jnp.sum(dj.astype(f32), 0).reshape(3, zs, 1, HEAD_DIM)
    da1 = scatter_ctx(dot(dj, w_qkv_c, ((1,), (1,))))
    gain_one_part = jnp.sum(da1 * n1, 0)
    shift_one_part = jnp.sum(da1, 0)
    input_grad = dh + norm_back(da1, n1, r1, g1)

    own = (jnp.arange(n) == me)[None, None, :, None]
    devices = zs * n
    pieces = jnp.concatenate(
        [
            jnp.where(own, bias_part, 0.0).reshape(devices, nb),
            gain_one_part.reshape(devices, wrows),
            shift_one_part.reshape(devices, wrows),
            gain_two_part.reshape(devices, wrows),
            shift_two_part.reshape(devices, wrows),
        ],
        -1,
    )
    summed = lax.psum_scatter(pieces, ("dp", "ctx"), scatter_dimension=0, tiled=True)[0]

    def ff_back(part):
        return jnp.transpose(part.reshape(n, wrows, zs, ff_block), (1, 2, 0, 3)).reshape(
            wrows, zs * n * ff_block
        ).astype(f32)

    grad_qkv = jnp.transpose(grad_qkv.reshape(n, wrows, 3, zs, HEAD_DIM), (1, 2, 3, 0, 4)).reshape(
        wrows, 3 * width
    ).astype(f32)
    return (
        back_tokens(result.astype(b16)),
        back_tokens(input_grad),
        grad_qkv,
        summed[:nb],
        grad_out,
        ff_back(grad_gu[..., :ffc]),
        ff_back(grad_gu[..., ffc:]),
        grad_down,
        summed[nb : nb + wrows],
        summed[nb + wrows : nb + 2 * wrows],
        summed[nb + 2 * wrows : nb + 3 * wrows],
        summed[nb + 3 * wrows :],
    )


def solution(mesh):
    zs, n = mesh.shape["dp"], mesh.shape["ctx"]
    shards = tensor_shards if (zs, n) == (4, 8) and HEADS == 32 else gathered_shards

    placed = (
        P("ctx", "dp", None),
        P("dp", None),
        P(("dp", "ctx"), None),
        P(("dp", "ctx")),
        P(("dp", "ctx"), None),
        P(("dp", "ctx"), None),
        P(("dp", "ctx"), None),
        P(("dp", "ctx"), None),
        P(("dp", "ctx")),
        P(("dp", "ctx")),
        P(("dp", "ctx")),
        P(("dp", "ctx")),
        P("ctx", "dp", None),
    )
    return jax.shard_map(
        shards,
        mesh=mesh,
        in_specs=placed,
        out_specs=(
            P("ctx", "dp", None),
            P("ctx", "dp", None),
            P(("dp", "ctx"), None),
            P(("dp", "ctx")),
            P(("dp", "ctx"), None),
            P(("dp", "ctx"), None),
            P(("dp", "ctx"), None),
            P(("dp", "ctx"), None),
            P(("dp", "ctx")),
            P(("dp", "ctx")),
            P(("dp", "ctx")),
            P(("dp", "ctx")),
        ),
        check_vma=False,
    )
```

```python
import functools
import itertools
import math

import jax
import jax.numpy as jnp
from jax import lax
from jax.experimental import pallas as pl
from jax.experimental.pallas import tpu as pltpu
from jax.sharding import PartitionSpec as P

HEADS = 32
HEAD_DIM = 64
ROTARY = 16


epsilon = 1e-05
masked_value = -1e30


def layer_stats(values):
    row_mean = jnp.mean(values, -1, keepdims=True)
    centred = values - row_mean
    inverse = lax.rsqrt(jnp.mean(centred * centred, -1, keepdims=True) + epsilon)
    return (centred * inverse, inverse)


def norm_back(grad_normed, scaled, inverse, gain_vec):
    grad_hat = grad_normed * gain_vec
    return inverse * (
        grad_hat
        - jnp.mean(grad_hat, -1, keepdims=True)
        - scaled * jnp.mean(grad_hat * scaled, -1, keepdims=True)
    )


def rotary_tables(positions):
    counter = jnp.arange(ROTARY // 2, dtype=jnp.float32)
    frequency = 10000.0 ** (-2.0 * counter / ROTARY)
    angles = positions.astype(jnp.float32)[:, None] * frequency[None, :]
    return (jnp.cos(angles)[:, None, None, :], jnp.sin(angles)[:, None, None, :])


def rotate(values, cos_table, sin_table):
    half_dims = ROTARY // 2
    first_half = values[..., :half_dims]
    second_half = values[..., half_dims:ROTARY]
    return jnp.concatenate(
        [
            first_half * cos_table - second_half * sin_table,
            second_half * cos_table + first_half * sin_table,
            values[..., ROTARY:],
        ],
        -1,
    )


def over_blocks(step_fn, running, gathered):
    total_rows = gathered.shape[0]
    tile_rows = math.gcd(total_rows, 512)

    def visit_block(number, current):
        block_start = number * tile_rows
        block_part = lax.dynamic_slice_in_dim(gathered, block_start, tile_rows, 0)
        return step_fn(current, block_part, block_start)

    return lax.fori_loop(0, total_rows // tile_rows, visit_block, running)


def gathered_shards(
    inputs,
    lengths,
    w_qkv,
    b_qkv,
    w_out,
    w_gate,
    w_up,
    w_down,
    gain_one,
    shift_one,
    gain_two,
    shift_two,
    cotangent,
):
    local_rows, slot_count, width = inputs.shape
    positions = lax.axis_index("ctx") * local_rows + jnp.arange(local_rows, dtype=jnp.int32)
    live_rows = positions[:, None] < lengths[0][None, :]
    live_heads = jnp.transpose(live_rows)[:, None, :, None]
    cos_table, sin_table = rotary_tables(positions)

    def allowed_mask(offset, count):
        key_pos = offset + jnp.arange(count, dtype=jnp.int32)
        causal = key_pos[None, :] <= positions[:, None]
        return causal[None, None, :, :] & live_heads

    def split_heads(block_part):
        count = block_part.shape[0]
        key_part = block_part[:, :, 0].reshape(count, slot_count, HEADS, HEAD_DIM)
        value_part = block_part[:, :, 1].reshape(count, slot_count, HEADS, HEAD_DIM)
        return (key_part, value_part)

    attn_full = (
        lax.all_gather(w_qkv, ("dp", "ctx"), axis=0, tiled=True),
        lax.all_gather(b_qkv, ("dp", "ctx"), axis=0, tiled=True),
        lax.all_gather(w_out, ("dp", "ctx"), axis=0, tiled=True),
        lax.all_gather(gain_one, ("dp", "ctx"), axis=0, tiled=True),
        lax.all_gather(shift_one, ("dp", "ctx"), axis=0, tiled=True),
    )
    qkv_full, bias_full, out_full, gain_one_full, shift_one_full = attn_full
    source = inputs.astype(jnp.float32)
    scaled_one, inverse_one = layer_stats(source)
    normed_one = (
        scaled_one * gain_one_full.astype(jnp.float32) + shift_one_full.astype(jnp.float32)
    ).astype(jnp.bfloat16)
    joined = jnp.einsum(
        "rsd,de->rse", normed_one, qkv_full, preferred_element_type=jnp.float32
    ) + bias_full.astype(jnp.float32)
    query_pre = joined[..., :width].reshape(local_rows, slot_count, HEADS, HEAD_DIM)
    key_pre = joined[..., width : 2 * width].reshape(local_rows, slot_count, HEADS, HEAD_DIM)
    queries = rotate(query_pre, cos_table, sin_table).astype(jnp.bfloat16)
    keys_rot = rotate(key_pre, cos_table, sin_table).reshape(local_rows, slot_count, width)
    key_value = jnp.stack([keys_rot, joined[..., 2 * width :]], 2).astype(jnp.bfloat16)
    block_part = lax.all_gather(key_value, "ctx", axis=0, tiled=True)
    run_peak = jnp.full((slot_count, HEADS, local_rows), masked_value, jnp.float32)
    key_part, value_part = split_heads(block_part)
    scores = (
        jnp.einsum("qshd,kshd->shqk", queries, key_part, preferred_element_type=jnp.float32) * 0.125
    )
    allowed = allowed_mask(jnp.int32(0), block_part.shape[0])
    masked = jnp.where(allowed, scores, masked_value)
    new_peak = jnp.maximum(run_peak, jnp.max(masked, -1))
    weights = jnp.where(allowed, jnp.exp(masked - new_peak[..., None]), 0.0)
    new_sum = jnp.sum(weights, -1)
    new_acc = jnp.einsum(
        "shqk,kshd->shqd",
        weights.astype(jnp.bfloat16),
        value_part,
        preferred_element_type=jnp.float32,
    )
    final_sum = jnp.maximum(new_sum, 1.0)
    log_sum = new_peak + jnp.log(final_sum)
    attended = jnp.transpose(new_acc / final_sum[..., None], (2, 0, 1, 3))
    attended_low = attended.reshape(local_rows, slot_count, width).astype(jnp.bfloat16)
    hidden_in = source + jnp.einsum(
        "rsd,de->rse", attended_low, out_full, preferred_element_type=jnp.float32
    )
    mlp_full = (
        lax.all_gather(w_gate, ("dp", "ctx"), axis=0, tiled=True),
        lax.all_gather(w_up, ("dp", "ctx"), axis=0, tiled=True),
        lax.all_gather(w_down, ("dp", "ctx"), axis=0, tiled=True),
        lax.all_gather(gain_two, ("dp", "ctx"), axis=0, tiled=True),
        lax.all_gather(shift_two, ("dp", "ctx"), axis=0, tiled=True),
    )
    gate_full, up_full, down_full, gain_two_full, shift_two_full = mlp_full
    scaled_two, inverse_two = layer_stats(hidden_in)
    normed_two = (
        scaled_two * gain_two_full.astype(jnp.float32) + shift_two_full.astype(jnp.float32)
    ).astype(jnp.bfloat16)
    gate = jnp.einsum("rsd,df->rsf", normed_two, gate_full, preferred_element_type=jnp.float32)
    upward = jnp.einsum("rsd,df->rsf", normed_two, up_full, preferred_element_type=jnp.float32)
    sigmoid = jax.nn.sigmoid(gate)
    product = (gate * sigmoid * upward).astype(jnp.bfloat16)
    result = hidden_in + jnp.einsum(
        "rsf,fd->rsd", product, down_full, preferred_element_type=jnp.float32
    )
    gate_back, up_back, down_back, gain_two_back = (
        lax.all_gather(w_gate, ("dp", "ctx"), axis=0, tiled=True),
        lax.all_gather(w_up, ("dp", "ctx"), axis=0, tiled=True),
        lax.all_gather(w_down, ("dp", "ctx"), axis=0, tiled=True),
        lax.all_gather(gain_two, ("dp", "ctx"), axis=0, tiled=True),
    )
    grad_down = jnp.einsum("rsf,rsd->fd", product, cotangent, preferred_element_type=jnp.float32)
    grad_product = jnp.einsum(
        "rsd,fd->rsf", cotangent, down_back, preferred_element_type=jnp.float32
    )
    grad_gate_act = (grad_product * upward * sigmoid * (1.0 + gate * (1.0 - sigmoid))).astype(
        jnp.bfloat16
    )
    grad_up_act = (grad_product * gate * sigmoid).astype(jnp.bfloat16)
    grad_gate = jnp.einsum(
        "rsd,rsf->df", normed_two, grad_gate_act, preferred_element_type=jnp.float32
    )
    grad_up = jnp.einsum("rsd,rsf->df", normed_two, grad_up_act, preferred_element_type=jnp.float32)
    grad_normed_two = jnp.einsum(
        "rsf,df->rsd", grad_gate_act, gate_back, preferred_element_type=jnp.float32
    ) + jnp.einsum("rsf,df->rsd", grad_up_act, up_back, preferred_element_type=jnp.float32)
    grad_gain_two = jnp.sum(grad_normed_two * scaled_two, (0, 1))
    grad_shift_two = jnp.sum(grad_normed_two, (0, 1))
    grad_hidden = cotangent.astype(jnp.float32) + norm_back(
        grad_normed_two, scaled_two, inverse_two, gain_two_back.astype(jnp.float32)
    )
    mlp_sums = (
        lax.psum_scatter(grad_gate, ("dp", "ctx"), scatter_dimension=0, tiled=True),
        lax.psum_scatter(grad_up, ("dp", "ctx"), scatter_dimension=0, tiled=True),
        lax.psum_scatter(grad_down, ("dp", "ctx"), scatter_dimension=0, tiled=True),
        lax.psum_scatter(grad_gain_two, ("dp", "ctx"), scatter_dimension=0, tiled=True),
        lax.psum_scatter(grad_shift_two, ("dp", "ctx"), scatter_dimension=0, tiled=True),
    )
    qkv_back, out_back, gain_one_back = (
        lax.all_gather(w_qkv, ("dp", "ctx"), axis=0, tiled=True),
        lax.all_gather(w_out, ("dp", "ctx"), axis=0, tiled=True),
        lax.all_gather(gain_one, ("dp", "ctx"), axis=0, tiled=True),
    )
    hidden_low = grad_hidden.astype(jnp.bfloat16)
    grad_out = jnp.einsum(
        "rsd,rse->de", attended_low, hidden_low, preferred_element_type=jnp.float32
    )
    grad_attended = jnp.einsum(
        "rse,de->rsd", hidden_low, out_back, preferred_element_type=jnp.float32
    )
    grad_heads = grad_attended.reshape(local_rows, slot_count, HEADS, HEAD_DIM).astype(jnp.bfloat16)
    delta = jnp.transpose(jnp.sum(grad_heads.astype(jnp.float32) * attended, -1), (1, 2, 0))
    key_value_all = lax.all_gather(key_value, "ctx", axis=0, tiled=True)

    def grad_parts(block_part, offset):
        key_part, value_part = split_heads(block_part)
        scores = (
            jnp.einsum("qshd,kshd->shqk", queries, key_part, preferred_element_type=jnp.float32)
            * 0.125
        )
        allowed = allowed_mask(offset, block_part.shape[0])
        probs = jnp.where(allowed, jnp.exp(scores - log_sum[..., None]), 0.0)
        grad_prob = jnp.einsum(
            "qshd,kshd->shqk", grad_heads, value_part, preferred_element_type=jnp.float32
        )
        grad_score = (probs * (grad_prob - delta[..., None])).astype(jnp.bfloat16)
        return (key_part, probs, grad_score)

    def query_step(running, block_part, offset):
        key_part, probs, grad_score = grad_parts(block_part, offset)
        return running + jnp.einsum(
            "shqk,kshd->shqd", grad_score, key_part, preferred_element_type=jnp.float32
        )

    grad_query = (
        over_blocks(
            query_step,
            jnp.zeros((slot_count, HEADS, local_rows, HEAD_DIM), jnp.float32),
            key_value_all,
        )
        * 0.125
    )
    count = local_rows * lax.axis_size("ctx")
    tile_rows = math.gcd(count, 512)

    def one_block(number):
        block_start = number * tile_rows
        block_part = lax.dynamic_slice_in_dim(key_value_all, block_start, tile_rows, 0)
        key_part, probs, grad_score = grad_parts(block_part, block_start)
        grad_key = (
            jnp.einsum("shqk,qshd->kshd", grad_score, queries, preferred_element_type=jnp.float32)
            * 0.125
        )
        grad_value = jnp.einsum(
            "shqk,qshd->kshd",
            probs.astype(jnp.bfloat16),
            grad_heads,
            preferred_element_type=jnp.float32,
        )
        return jnp.stack(
            [
                grad_key.reshape(tile_rows, slot_count, width),
                grad_value.reshape(tile_rows, slot_count, width),
            ],
            2,
        )

    blocks = lax.map(one_block, jnp.arange(count // tile_rows, dtype=jnp.int32))
    grad_key_value = lax.psum_scatter(
        blocks.reshape(count, slot_count, 2, width).astype(jnp.bfloat16),
        "ctx",
        scatter_dimension=0,
        tiled=True,
    ).astype(jnp.float32)
    grad_query_pre = rotate(jnp.transpose(grad_query, (2, 0, 1, 3)), cos_table, -sin_table)
    grad_key_pre = rotate(
        grad_key_value[:, :, 0].reshape(local_rows, slot_count, HEADS, HEAD_DIM),
        cos_table,
        -sin_table,
    )
    grad_joined = jnp.concatenate(
        [
            grad_query_pre.reshape(local_rows, slot_count, width),
            grad_key_pre.reshape(local_rows, slot_count, width),
            grad_key_value[:, :, 1],
        ],
        -1,
    ).astype(jnp.bfloat16)
    grad_qkv = jnp.einsum(
        "rsd,rse->de", normed_one, grad_joined, preferred_element_type=jnp.float32
    )
    grad_bias = jnp.sum(grad_joined.astype(jnp.float32), (0, 1))
    grad_normed_one = jnp.einsum(
        "rse,de->rsd", grad_joined, qkv_back, preferred_element_type=jnp.float32
    )
    grad_gain_one = jnp.sum(grad_normed_one * scaled_one, (0, 1))
    grad_shift_one = jnp.sum(grad_normed_one, (0, 1))
    input_grad = grad_hidden + norm_back(
        grad_normed_one, scaled_one, inverse_one, gain_one_back.astype(jnp.float32)
    )
    attn_sums = (
        lax.psum_scatter(grad_qkv, ("dp", "ctx"), scatter_dimension=0, tiled=True),
        lax.psum_scatter(grad_bias, ("dp", "ctx"), scatter_dimension=0, tiled=True),
        lax.psum_scatter(grad_out, ("dp", "ctx"), scatter_dimension=0, tiled=True),
        lax.psum_scatter(grad_gain_one, ("dp", "ctx"), scatter_dimension=0, tiled=True),
        lax.psum_scatter(grad_shift_one, ("dp", "ctx"), scatter_dimension=0, tiled=True),
    )
    return (
        result.astype(jnp.bfloat16),
        input_grad,
        attn_sums[0],
        attn_sums[1],
        attn_sums[2],
        mlp_sums[0],
        mlp_sums[1],
        mlp_sums[2],
        attn_sums[3],
        attn_sums[4],
        mlp_sums[3],
        mlp_sums[4],
    )


MESH = pl.DeviceIdType.MESH
HBM = pl.BlockSpec(memory_space=pltpu.HBM)
VMEM = pl.BlockSpec(memory_space=pltpu.VMEM)


def flip(index, mask):
    for bit in (1, 2, 4):
        if mask & bit:
            index = index + bit - 2 * bit * ((index // bit) % 2)
    return index


class Wires:
    def __init__(self, send, recv):
        self.send, self.recv = send, recv
        self.z, self.c = lax.axis_index("dp"), lax.axis_index("ctx")
        self.inner = (self.z == 1) | (self.z == 2)
        self.outer = (self.z == 0) | (self.z == 3)
        self.number = itertools.count()

    def put(self, src, dst, z_mask, c_mask):
        i = next(self.number)
        return pltpu.make_async_remote_copy(
            src_ref=src,
            dst_ref=dst,
            send_sem=self.send.at[i],
            recv_sem=self.recv.at[i],
            device_id=(flip(self.z, z_mask), flip(self.c, c_mask)),
            device_id_type=MESH,
        )

    def greet(self, zs, n):
        barrier = pltpu.get_barrier_semaphore()
        for m in range(1, zs):
            pl.semaphore_signal(
                barrier, inc=1, device_id=(flip(self.z, m), self.c), device_id_type=MESH
            )
        for m in range(1, n):
            pl.semaphore_signal(
                barrier, inc=1, device_id=(self.z, flip(self.c, m)), device_id_type=MESH
            )
        pl.semaphore_wait(barrier, zs + n - 2)


class DepthGather:
    def __init__(self, wires, part):
        z = wires.z
        self.wires = wires
        self.near = wires.put(part(z), part(z), 1, 0)
        self.skip = wires.put(part(z), part(z), 2, 0)
        self.mid = wires.put(part(z), part(z), 3, 0)
        far = flip(z, 2)
        self.on = wires.put(part(far), part(far), 1, 0)

    def start(self):
        self.skip.start()
        pl.when(self.wires.inner)(self.mid.start)
        self.near.start()

    def forward(self):
        @pl.when(self.wires.inner)
        def _():
            self.skip.wait_recv()
            self.on.start()

    def finish(self):
        self.near.wait_recv()
        self.near.wait_send()
        self.skip.wait_send()

        @pl.when(self.wires.inner)
        def _():
            self.mid.wait_recv()
            self.mid.wait_send()
            self.on.wait_send()

        @pl.when(self.wires.outer)
        def _():
            self.skip.wait_recv()
            self.on.wait_recv()


class LayerGather:
    def __init__(self, wires, buf, source=None):
        c = wires.c
        mine = buf.at[c] if source is None else source
        self.direct = {m: wires.put(mine, buf.at[c], 0, m) for m in (2, 4, 6, 1)}
        self.on = {
            m: wires.put(buf.at[flip(c, m)], buf.at[flip(c, m)], 0, 1) for m in (2, 4, 6)
        }

    def start(self):
        for m in (2, 4, 6, 1):
            self.direct[m].start()

    def forward(self, m):
        self.direct[m].wait_recv()
        self.on[m].start()

    def arrived(self, m):
        (self.direct[1] if m == 1 else self.on[m - 1]).wait_recv()

    def sent(self):
        for copy in (*self.direct.values(), *self.on.values()):
            copy.wait_send()


def pack_columns(dst, refs, n, zs):
    for i in range(n):
        pieces = []
        for ref, block in refs:
            pieces += [ref[:, block * (j * n + i) : block * (j * n + i + 1)] for j in range(zs)]
        dst[i] = jnp.concatenate(pieces, -1)


def spread_kernel(
    zs,
    n,
    w_qkv,
    w_gate,
    w_up,
    w_out,
    xs,
    dy,
    small,
    qkv_all,
    out_all,
    gu_own,
    xs_all,
    dy_all,
    small_all,
    qkv_send,
    gu_send,
    send,
    recv,
    local,
):
    wires = Wires(send, recv)
    z, c = wires.z, wires.c
    hc = HEAD_DIM * HEADS // n
    width = HEADS * HEAD_DIM
    ff_block = w_gate.shape[1] // (zs * n)

    own = [
        pltpu.make_async_copy(w_out, out_all.at[z], local.at[0]),
        pltpu.make_async_copy(qkv_send.at[c], qkv_all.at[z, c], local.at[1]),
        pltpu.make_async_copy(gu_send.at[c], gu_own.at[c], local.at[2]),
        pltpu.make_async_copy(xs, xs_all.at[c], local.at[3]),
        pltpu.make_async_copy(dy, dy_all.at[c], local.at[4]),
        pltpu.make_async_copy(small, small_all.at[z, c], local.at[5]),
    ]
    for i in (0, 3, 4, 5):
        own[i].start()
    pack_columns(
        qkv_send, [(w_qkv.at[:, i * width : (i + 1) * width], HEAD_DIM) for i in range(3)], n, zs
    )
    own[1].start()
    wires.greet(zs, n)
    for i in (0, 5):
        own[i].wait()

    out_z = DepthGather(wires, lambda i: out_all.at[i])
    out_z.start()
    qkv_x = [
        wires.put(qkv_send.at[flip(c, m)], qkv_all.at[z, c], 0, m) for m in range(1, n)
    ]
    for copy in qkv_x:
        copy.start()
    small_z = [wires.put(small_all.at[z, c], small_all.at[z, c], m, 0) for m in range(1, zs)]
    for copy in small_z:
        copy.start()
    xs_g = LayerGather(wires, xs_all, xs)
    xs_g.start()
    pack_columns(gu_send, [(w_gate, ff_block), (w_up, ff_block)], n, zs)
    own[2].start()
    for copy in small_z:
        copy.wait_recv()
    small_x = [
        wires.put(small_all.at[:, c], small_all.at[:, c], 0, m) for m in range(1, n)
    ]
    for copy in small_x:
        copy.start()
    own[1].wait()
    for copy in qkv_x:
        copy.wait_recv()
    half = n // 2
    qkv_z = [
        DepthGather(wires, lambda i, p=p: qkv_all.at[i, p * half : (p + 1) * half])
        for p in range(2)
    ]
    for part in qkv_z:
        part.start()
    out_z.forward()
    gu_x = [wires.put(gu_send.at[flip(c, m)], gu_own.at[c], 0, m) for m in range(1, n)]
    for copy in gu_x:
        copy.start()
    for m in (2, 4, 6):
        xs_g.forward(m)
    dy_g = LayerGather(wires, dy_all, dy)
    dy_g.start()
    qkv_z[0].forward()
    for m in (2, 4, 6):
        dy_g.forward(m)
    qkv_z[1].forward()

    for i in (2, 3, 4):
        own[i].wait()
    for group in (xs_g, dy_g):
        for m in (1, 3, 5, 7):
            group.arrived(m)
        group.sent()
    for copy in small_z:
        copy.wait_send()
    for copy in qkv_x:
        copy.wait_send()
    for copy in (*small_x, *gu_x):
        copy.wait()
    for part in (out_z, *qkv_z):
        part.finish()


def spread(zs, n, w_qkv, w_gate, w_up, w_out, xs, dy, small):
    wrows, width = w_out.shape
    qc, gc = w_qkv.shape[1] // n, 2 * w_gate.shape[1] // n
    b16 = jnp.bfloat16
    return pl.pallas_call(
        functools.partial(spread_kernel, zs, n),
        out_shape=[
            jax.ShapeDtypeStruct((zs, n, wrows, qc), b16),
            jax.ShapeDtypeStruct((zs, wrows, width), b16),
            jax.ShapeDtypeStruct((n, wrows, gc), b16),
            jax.ShapeDtypeStruct((n, *xs.shape), b16),
            jax.ShapeDtypeStruct((n, *dy.shape), b16),
            jax.ShapeDtypeStruct((zs, n, *small.shape), small.dtype),
        ],
        in_specs=[VMEM, VMEM, VMEM, HBM, HBM, HBM, HBM],
        out_specs=[HBM] * 6,
        scratch_shapes=[
            pltpu.VMEM((n, wrows, qc), b16),
            pltpu.VMEM((n, wrows, gc), b16),
            pltpu.SemaphoreType.DMA((64,)),
            pltpu.SemaphoreType.DMA((64,)),
            pltpu.SemaphoreType.DMA((6,)),
        ],
        compiler_params=pltpu.CompilerParams(
            collective_id=1, has_side_effects=True, vmem_limit_bytes=32 << 20
        ),
        name="spread",
    )(w_qkv, w_gate, w_up, w_out, xs, dy, small)


class LayerScatter:
    def __init__(self, wires, part, near, far):
        c = wires.c
        self.c, self.part, self.near, self.far = c, part, near, far
        self.pair = {
            m: wires.put(part.at[flip(c, m + 1)], near.at[m // 2], 0, 1) for m in (6, 4, 2, 0)
        }
        self.chips = {
            m: wires.put(part.at[flip(c, m)], far.at[m // 2 - 1], 0, m) for m in (6, 4, 2)
        }

    def start(self):
        for copy in self.pair.values():
            copy.start()

    def step(self, m):
        self.pair[m].wait_recv()
        to = flip(self.c, m)
        self.part[to] = (
            self.part[to].astype(jnp.float32) + self.near[m // 2].astype(jnp.float32)
        ).astype(self.part.dtype)
        self.chips[m].start()

    def total(self):
        self.pair[0].wait_recv()
        result = self.part[self.c].astype(jnp.float32) + self.near[0].astype(jnp.float32)
        for m in (2, 4, 6):
            self.chips[m].wait_recv()
            result = result + self.far[m // 2 - 1].astype(jnp.float32)
        return result

    def sent(self):
        for copy in (*self.pair.values(), *self.chips.values()):
            copy.wait_send()


def dot(a, b, dims=((1,), (0,))):
    return lax.dot_general(a, b, (dims, ((), ())), preferred_element_type=jnp.float32)


def turn_pair(values, table, sign):
    half = ROTARY // 2
    columns = values.shape[-1]
    return (
        values * table[0]
        + sign * (pltpu.roll(values, columns - half, 1) * table[1])
        + sign * (pltpu.roll(values, half, 1) * table[2])
    )


def head_mask(rows, columns, head):
    return lax.broadcasted_iota(jnp.int32, (rows, columns), 1) // HEAD_DIM == head


def forward_kernel(
    zs,
    n,
    lengths,
    norms,
    bias,
    tables,
    xs_all,
    w_qkv,
    w_out,
    gu_own,
    a1_out,
    qkv_out,
    probs_out,
    ob_out,
    hidden_out,
    a2_out,
    w_gu_out,
    gu_out,
    zz_out,
    xs_v,
    a1_v,
    w_qkv_v,
    w_out_v,
    qkv_v,
    probs_v,
    ob_v,
    part,
    near,
    far,
    hidden_v,
    a2_v,
    w_gu_v,
    gu_v,
    zz_v,
    send,
    recv,
    local,
    drain,
):
    f32, b16 = jnp.float32, jnp.bfloat16
    wires = Wires(send, recv)
    z, c = wires.z, wires.c
    _, slots, rows, hc = ob_v.shape
    tokens, width = n * slots * rows, a1_v.shape[-1]
    seq = n * rows
    heads = hc // HEAD_DIM
    ffc = zz_v.shape[-1]
    chunks = 4
    chunk = w_gu_v.shape[1] // chunks

    loads = [
        pltpu.make_async_copy(gu_own, w_gu_v.at[z], local.at[0]),
        pltpu.make_async_copy(xs_all, xs_v, local.at[1]),
        pltpu.make_async_copy(w_qkv, w_qkv_v, local.at[2]),
        pltpu.make_async_copy(w_out, w_out_v, local.at[3]),
    ]
    for copy in loads:
        copy.start()
    wires.greet(zs, n)
    loads[0].wait()
    gu_z = [
        DepthGather(wires, lambda i, p=p: w_gu_v.at[i, p * chunk : (p + 1) * chunk])
        for p in range(chunks)
    ]
    for part_z in gu_z:
        part_z.start()
    stores = []

    def store(src, dst):
        copy = pltpu.make_async_copy(src, dst, drain.at[len(stores)])
        copy.start()
        stores.append(copy)

    for copy in loads[1:]:
        copy.wait()

    def project(i, carry):
        x = xs_v[pl.ds(2 * i, 2)].reshape(2 * slots * rows, width).astype(f32)
        a1 = (layer_stats(x)[0] * norms[0:1] + norms[1:2]).astype(b16)
        a1_v[pl.ds(2 * i, 2)] = a1.reshape(2, slots * rows, width)
        joined = dot(a1, w_qkv_v[...].reshape(width, 3 * hc)) + bias[...]
        for j in range(2):
            table = tables[:, 2 * i + j]
            for s in range(slots):
                at = (j * slots + s) * rows
                piece = joined[at : at + rows]
                qkv_v[0, s, 2 * i + j] = turn_pair(piece[:, :hc], table, 1.0).astype(b16)
                qkv_v[1, s, 2 * i + j] = turn_pair(piece[:, hc : 2 * hc], table, 1.0).astype(b16)
                qkv_v[2, s, 2 * i + j] = piece[:, 2 * hc :].astype(b16)
        return carry

    lax.fori_loop(0, n // 2, project, 0)
    store(a1_v, a1_out)
    store(qkv_v, qkv_out)

    half = seq // 2

    def attend(s, carry):
        q, k, v = [qkv_v[i, s].reshape(seq, hc) for i in range(3)]
        length = lengths[0, s]
        for part_q in range(2):
            keys = (part_q + 1) * half
            at = part_q * half
            query = q[at : at + half]
            row = lax.broadcasted_iota(jnp.int32, (half, keys), 0) + at
            key = lax.broadcasted_iota(jnp.int32, (half, keys), 1)
            allowed = (key <= row) & (row < length)
            out = jnp.zeros((half, hc), f32)
            for h in range(heads):
                mask = head_mask(half, hc, h)
                scores = dot(jnp.where(mask, query, 0).astype(b16), k[:keys], ((1,), (1,)))
                scores = jnp.where(allowed, scores * 0.125, masked_value)
                peak = jnp.max(scores, -1, keepdims=True)
                weights = jnp.where(allowed, jnp.exp(scores - peak), 0.0)
                total = jnp.maximum(jnp.sum(weights, -1, keepdims=True), 1.0)
                probs = (weights * (1.0 / total)).astype(b16)
                probs_v[s, h, at : at + half, 0:keys] = probs
                out = jnp.where(mask, dot(probs, v[:keys]), out)
            ob_v[part_q * n // 2 : (part_q + 1) * n // 2, s] = out.astype(b16).reshape(
                n // 2, rows, hc
            )
        return carry

    lax.fori_loop(0, slots, attend, 0)
    store(probs_v, probs_out)
    store(ob_v, ob_out)

    def to_hidden(i, carry):
        part[i] = dot(
            ob_v[i].reshape(slots * rows, hc), w_out_v[...].reshape(hc, width)
        ).astype(b16)
        return carry

    lax.fori_loop(0, n, to_hidden, 0)
    sums = LayerScatter(wires, part, near, far)
    sums.start()
    for m in (6, 4, 2):
        sums.step(m)
    gu_z[0].forward()
    hidden = xs_v[c].astype(f32) + sums.total()
    hidden_v[...] = hidden
    store(hidden_v, hidden_out)
    a2_v[c] = (layer_stats(hidden)[0] * norms[2:3] + norms[3:4]).astype(b16)
    a2_g = LayerGather(wires, a2_v)
    a2_g.start()
    gu_z[1].forward()
    for m in (2, 4, 6):
        a2_g.forward(m)
    gu_z[2].forward()
    for m in (1, 3, 5, 7):
        a2_g.arrived(m)
    gu_z[3].forward()
    store(a2_v, a2_out)
    for part_z in gu_z:
        part_z.finish()
    store(w_gu_v, w_gu_out)

    def feed(i, carry):
        a2 = a2_v[pl.ds(2 * i, 2)].reshape(2 * slots * rows, width)
        gu = dot(a2, w_gu_v[...].reshape(width, 2 * ffc))
        gu_v[i] = gu
        gate = gu[:, :ffc]
        zz_v[i] = (gate * jax.nn.sigmoid(gate) * gu[:, ffc:]).astype(b16)
        return carry

    lax.fori_loop(0, n // 2, feed, 0)
    store(gu_v, gu_out)
    store(zz_v, zz_out)
    sums.sent()
    a2_g.sent()
    for copy in stores:
        copy.wait()


def forward(zs, n, slots, lengths, norms, bias, tables, xs_all, w_qkv, w_out, gu_own):
    _, local, width = xs_all.shape
    rows = local // slots
    seq = rows * n
    heads = HEADS // n
    hc = heads * HEAD_DIM
    gc = gu_own.shape[-1]
    f32, b16 = jnp.float32, jnp.bfloat16
    kept = [
        ((n, local, width), b16),
        ((3, slots, n, rows, hc), b16),
        ((slots, heads, seq, seq), b16),
        ((n, slots, rows, hc), b16),
        ((local, width), f32),
        ((n, local, width), b16),
        ((zs, *gu_own.shape), b16),
        ((n // 2, 2 * local, gc), f32),
        ((n // 2, 2 * local, gc // 2), b16),
    ]
    a1, qkv, probs, ob, hidden, a2, w_gu, gu, zz = [pltpu.VMEM(*k) for k in kept]
    return pl.pallas_call(
        functools.partial(forward_kernel, zs, n),
        out_shape=[jax.ShapeDtypeStruct(*k) for k in kept],
        in_specs=[pl.BlockSpec(memory_space=pltpu.SMEM)] + [VMEM] * 3 + [HBM] * 4,
        out_specs=[HBM] * len(kept),
        scratch_shapes=[
            pltpu.VMEM(xs_all.shape, b16),
            a1,
            pltpu.VMEM(w_qkv.shape, b16),
            pltpu.VMEM(w_out.shape, b16),
            qkv,
            probs,
            ob,
            pltpu.VMEM((n, local, width), b16),
            pltpu.VMEM((n // 2, local, width), b16),
            pltpu.VMEM((n // 2 - 1, local, width), b16),
            hidden,
            a2,
            w_gu,
            gu,
            zz,
            pltpu.SemaphoreType.DMA((40,)),
            pltpu.SemaphoreType.DMA((40,)),
            pltpu.SemaphoreType.DMA((4,)),
            pltpu.SemaphoreType.DMA((len(kept),)),
        ],
        compiler_params=pltpu.CompilerParams(
            collective_id=2, has_side_effects=True, vmem_limit_bytes=60 << 20
        ),
        name="forward",
    )(lengths, norms, bias, tables, xs_all, w_qkv, w_out, gu_own)


class DepthScatter:
    def __init__(self, wires, part, relay, boxes):
        z = wires.z
        self.wires, self.part, self.relay_box, self.boxes = wires, part, relay, boxes
        self.far = wires.put(part(flip(z, 3)), relay, 1, 0)
        self.skip = wires.put(part(flip(z, 2)), boxes[1], 2, 0)
        self.near = wires.put(part(flip(z, 1)), boxes[0], 1, 0)
        self.mid = wires.put(part(flip(z, 3)), boxes[2], 3, 0)

    def start(self):
        @pl.when(self.wires.outer)
        def _():
            self.far.start()
            self.skip.start()
            self.boxes[2][...] = jnp.zeros_like(self.boxes[2])

        pl.when(self.wires.inner)(self.mid.start)
        self.near.start()

    def relay(self):
        @pl.when(self.wires.inner)
        def _():
            self.far.wait_recv()
            to = self.part(flip(self.wires.z, 2))
            to[...] = (
                to[...].astype(jnp.float32) + self.relay_box[...].astype(jnp.float32)
            ).astype(to.dtype)
            self.skip.start()

    def total(self):
        self.near.wait_recv()
        self.skip.wait_recv()
        pl.when(self.wires.inner)(self.mid.wait_recv)
        result = self.part(self.wires.z)[...].astype(jnp.float32)
        for box in self.boxes:
            result = result + box[...].astype(jnp.float32)
        return result

    def sent(self):
        self.near.wait_send()
        self.skip.wait_send()
        pl.when(self.wires.outer)(self.far.wait_send)
        pl.when(self.wires.inner)(self.mid.wait_send)


class Moves:
    def __init__(self, sems):
        self.sems, self.number, self.stores = sems, itertools.count(), []

    def load(self, src, dst):
        copy = pltpu.make_async_copy(src, dst, self.sems.at[next(self.number)])
        copy.start()
        return copy

    def store(self, src, dst):
        self.stores.append(self.load(src, dst))

    def finish(self):
        for copy in self.stores:
            copy.wait()


def pieces_of(total, number, unit):
    units = total // unit
    cuts = [units * i // number * unit for i in range(number + 1)]
    return [(a, b - a) for a, b in zip(cuts[:-1], cuts[1:])]


def middle_kernel(
    zs,
    n,
    zz,
    gu,
    dy_all,
    w_down,
    dgu_out,
    w_down_out,
    grad_down_out,
    zz_v,
    gu_v,
    dy_v,
    w_down_v,
    dgu_v,
    gd_v,
    relay_v,
    box_v,
    total_v,
    send,
    recv,
    local,
):
    f32, b16 = jnp.float32, jnp.bfloat16
    wires = Wires(send, recv)
    moves = Moves(local)
    z = wires.z
    _, block, width = w_down_v.shape
    ffc = zs * block
    tokens = n * dy_v.shape[1]
    wait_down = moves.load(w_down, w_down_v.at[z])
    wait_zz = moves.load(zz, zz_v)
    wait_dy = moves.load(dy_all, dy_v)
    wait_gu = moves.load(gu, gu_v)
    wires.greet(zs, n)
    wait_down.wait()
    down_z = [
        DepthGather(wires, lambda i, a=a, s=s: w_down_v.at[i, a : a + s])
        for a, s in pieces_of(block, 4, 16)
    ]
    for part in down_z:
        part.start()
    wait_zz.wait()
    wait_dy.wait()
    number = 4
    tile = width // number
    sums = [
        DepthScatter(
            wires,
            lambda i, a=p * tile: gd_v.at[i, :, a : a + tile],
            relay_v.at[:, p * tile : (p + 1) * tile],
            [box_v.at[j, :, p * tile : (p + 1) * tile] for j in range(3)],
        )
        for p in range(number)
    ]
    for p in range(number):
        gd = dot(
            zz_v[...].reshape(tokens, ffc),
            dy_v[:, :, p * tile : (p + 1) * tile].reshape(tokens, tile),
            ((0,), (0,)),
        )
        gd_v[:, :, p * tile : (p + 1) * tile] = gd.astype(b16).reshape(zs, block, tile)
        sums[p].start()
    for p in range(number):
        down_z[p].forward()
        sums[p].relay()
    for part in down_z:
        part.finish()
    moves.store(w_down_v, w_down_out)
    wait_gu.wait()

    def back(i, carry):
        dz = dot(
            dy_v[pl.ds(2 * i, 2)].reshape(tokens // (n // 2), width),
            w_down_v[...].reshape(ffc, width),
            ((1,), (1,)),
        )
        gu_block = gu_v[i]
        gate, up = gu_block[:, :ffc], gu_block[:, ffc:]
        sig = jax.nn.sigmoid(gate)
        dg = dz * up * sig * (1.0 + gate * (1.0 - sig))
        du = dz * gate * sig
        dgu_v[i] = jnp.concatenate([dg, du], -1).astype(b16)
        return carry

    lax.fori_loop(0, n // 2, back, 0)
    moves.store(dgu_v, dgu_out)
    for p in range(number):
        total_v[:, p * tile : (p + 1) * tile] = sums[p].total()
    moves.store(total_v, grad_down_out)
    for part in sums:
        part.sent()
    moves.finish()


def middle(zs, n, zz, gu, dy_all, w_down):
    f32, b16 = jnp.float32, jnp.bfloat16
    block, width = w_down.shape
    return pl.pallas_call(
        functools.partial(middle_kernel, zs, n),
        out_shape=[
            jax.ShapeDtypeStruct(gu.shape, b16),
            jax.ShapeDtypeStruct((zs, block, width), b16),
            jax.ShapeDtypeStruct((block, width), f32),
        ],
        in_specs=[HBM] * 4,
        out_specs=[HBM] * 3,
        scratch_shapes=[
            pltpu.VMEM(zz.shape, b16),
            pltpu.VMEM(gu.shape, f32),
            pltpu.VMEM(dy_all.shape, b16),
            pltpu.VMEM((zs, block, width), b16),
            pltpu.VMEM(gu.shape, b16),
            pltpu.VMEM((zs, block, width), b16),
            pltpu.VMEM((block, width), b16),
            pltpu.VMEM((3, block, width), b16),
            pltpu.VMEM((block, width), f32),
            pltpu.SemaphoreType.DMA((40,)),
            pltpu.SemaphoreType.DMA((40,)),
            pltpu.SemaphoreType.DMA((8,)),
        ],
        compiler_params=pltpu.CompilerParams(
            collective_id=3, has_side_effects=True, vmem_limit_bytes=60 << 20
        ),
        name="middle",
    )(zz, gu, dy_all, w_down)


def backward_kernel(
    zs,
    n,
    norms,
    tables,
    a2_all,
    dgu,
    w_gu,
    w_out,
    qkv,
    probs,
    ob,
    hidden,
    dy_all,
    ggu_out,
    grad_out_out,
    dh_out,
    dj_out,
    gains_out,
    bias_out,
    a2_v,
    dgu_v,
    w_gu_v,
    w_out_v,
    qkv_v,
    probs_v,
    ob_v,
    hidden_v,
    dy_v,
    ggu_v,
    relay_v,
    box_v,
    part,
    near,
    far,
    dh_v,
    dh_all,
    go_v,
    go_relay,
    go_box,
    go_total,
    do_v,
    dqkv_v,
    dj_v,
    send,
    recv,
    local,
):
    f32, b16 = jnp.float32, jnp.bfloat16
    wires = Wires(send, recv)
    moves = Moves(local)
    z, c = wires.z, wires.c
    _, slots, rows, hc = ob_v.shape
    width = dh_v.shape[-1]
    tokens, seq, local_rows = n * slots * rows, n * rows, slots * rows
    heads = hc // HEAD_DIM
    depth, gc = ggu_v.shape[1:]

    wait_a2 = moves.load(a2_all, a2_v)
    wait_dgu = moves.load(dgu, dgu_v)
    wait_w = moves.load(w_gu, w_gu_v)
    waits = [
        moves.load(hidden, hidden_v),
        moves.load(dy_all.at[c], dy_v),
        moves.load(w_out, w_out_v),
        moves.load(qkv, qkv_v),
        moves.load(probs, probs_v),
        moves.load(ob, ob_v),
    ]
    wires.greet(zs, n)
    wait_a2.wait()
    wait_dgu.wait()

    number = 4
    size = depth // number
    sums = [
        DepthScatter(
            wires,
            lambda i, a=p * size: ggu_v.at[i, a : a + size],
            relay_v.at[p * size : (p + 1) * size],
            [box_v.at[j, p * size : (p + 1) * size] for j in range(3)],
        )
        for p in range(number)
    ]
    step = 2 * size
    for p in range(number // 2):

        def weigh(i, carry, p=p):
            at = pl.multiple_of(i * depth + p * step, step)
            left = a2_v[:, :, pl.ds(at, step)].reshape(tokens, step)
            ggu_v[i, p * step : (p + 1) * step] = dot(
                left, dgu_v[...].reshape(tokens, gc), ((0,), (0,))
            ).astype(b16)
            return carry

        lax.fori_loop(0, zs, weigh, 0)
        sums[2 * p].start()
        sums[2 * p + 1].start()

    wait_w.wait()

    def normed(i, carry):
        part[pl.ds(2 * i, 2)] = (
            dot(dgu_v[i], w_gu_v[...].reshape(width, gc), ((1,), (1,)))
            .astype(b16)
            .reshape(2, local_rows, width)
        )
        return carry

    lax.fori_loop(0, n // 2, normed, 0)
    sums[0].relay()
    da2_sums = LayerScatter(wires, part, near, far)
    da2_sums.start()
    for m in (6, 4, 2):
        da2_sums.step(m)
    for copy in waits:
        copy.wait()
    n2, r2 = layer_stats(hidden_v[...])
    sums[1].relay()
    da2 = da2_sums.total()
    gains_out[0:1] = jnp.sum(da2 * n2, 0, keepdims=True)
    gains_out[1:2] = jnp.sum(da2, 0, keepdims=True)
    dh = dy_v[...].astype(f32) + norm_back(da2, n2, r2, norms[2:3])
    dh_v[...] = dh
    moves.store(dh_v, dh_out)
    dh_all[c] = dh.astype(b16)
    dh_g = LayerGather(wires, dh_all)
    dh_g.start()
    for m in (2, 4, 6):
        dh_g.forward(m)
    sums[2].relay()
    for m in (1, 3, 5, 7):
        dh_g.arrived(m)

    def heads_back(i, carry):
        do_v[i] = (
            dot(dh_all[i], w_out_v[...].reshape(hc, width), ((1,), (1,)))
            .astype(b16)
            .reshape(slots, rows, hc)
        )
        return carry

    lax.fori_loop(0, n, heads_back, 0)

    half = seq // 2

    def attend(s, carry):
        q, k, v = [qkv_v[i, s].reshape(seq, hc) for i in range(3)]
        do_s = do_v[:, s].reshape(seq, hc)
        dqkv_v[...] = jnp.zeros_like(dqkv_v)
        for part_q in range(2):
            keys = (part_q + 1) * half
            at = part_q * half
            query, do_q = q[at : at + half], do_s[at : at + half]
            dq = jnp.zeros((half, hc), f32)
            for h in range(heads):
                mask, mask_k = head_mask(half, hc, h), head_mask(keys, hc, h)
                do_h = jnp.where(mask, do_q, 0).astype(b16)
                low = probs_v[s, h, at : at + half, 0:keys]
                p32 = low.astype(f32)
                t = p32 * dot(do_h, v[:keys], ((1,), (1,)))
                ds = (t - p32 * jnp.sum(t, -1, keepdims=True)).astype(b16)
                dq = jnp.where(mask, dot(ds, k[:keys]), dq)
                dk = dot(ds, query, ((0,), (0,)))
                dv = dot(low, do_h, ((0,), (0,)))
                dqkv_v[1, 0:keys] += jnp.where(mask_k, dk, 0.0)
                dqkv_v[2, 0:keys] += dv
            dqkv_v[0, at : at + half] = dq
        dq, dk = dqkv_v[0] * 0.125, dqkv_v[1] * 0.125
        table = [tables[i].reshape(seq, hc) for i in range(3)]
        dj = [turn_pair(dq, table, -1.0), turn_pair(dk, table, -1.0), dqkv_v[2]]
        for i in range(3):
            dj_v[:, s, :, i * hc : (i + 1) * hc] = dj[i].astype(b16).reshape(n, rows, hc)
        return carry

    lax.fori_loop(0, slots, attend, 0)
    moves.store(dj_v, dj_out)
    sums[3].relay()
    dj_all = dj_v[...].reshape(tokens, 3 * hc).astype(f32)
    bias_out[...] = jnp.sum(dj_all, 0, keepdims=True)

    go_sums = DepthScatter(
        wires, lambda i: go_v.at[i], go_relay, [go_box.at[j] for j in range(3)]
    )
    tile = width // 4
    for p in range(4):
        go = dot(
            ob_v[...].reshape(tokens, hc),
            dh_all[:, :, p * tile : (p + 1) * tile].reshape(tokens, tile),
            ((0,), (0,)),
        )
        go_v[:, :, p * tile : (p + 1) * tile] = go.astype(b16).reshape(zs, hc // zs, tile)
    go_sums.start()
    for p in range(number):
        a = p * size
        ggu_v[z, a : a + size] = sums[p].total().astype(b16)
        moves.store(ggu_v.at[z, a : a + size], ggu_out.at[a : a + size])
    go_sums.relay()
    go_total[...] = go_sums.total()
    moves.store(go_total, grad_out_out)
    for group in (*sums, go_sums, da2_sums, dh_g):
        group.sent()
    moves.finish()


def backward(zs, n, norms, tables, a2_all, dgu, w_gu, w_out, qkv, probs, ob, hidden, dy_all):
    f32, b16 = jnp.float32, jnp.bfloat16
    _, slots, rows, hc = ob.shape
    local, width = hidden.shape
    _, depth, gc = w_gu.shape
    seq = n * rows
    wide = (n, local, width)

    def buf(like):
        return pltpu.VMEM(like.shape, like.dtype)

    return pl.pallas_call(
        functools.partial(backward_kernel, zs, n),
        out_shape=[
            jax.ShapeDtypeStruct((depth, gc), b16),
            jax.ShapeDtypeStruct((hc // zs, width), f32),
            jax.ShapeDtypeStruct((local, width), f32),
            jax.ShapeDtypeStruct((n, slots, rows, 3 * hc), b16),
            jax.ShapeDtypeStruct((2, width), f32),
            jax.ShapeDtypeStruct((1, 3 * hc), f32),
        ],
        in_specs=[VMEM] * 2 + [HBM] * 9,
        out_specs=[HBM] * 4 + [VMEM] * 2,
        scratch_shapes=[
            *[buf(v) for v in (a2_all, dgu, w_gu, w_out, qkv, probs, ob, hidden)],
            pltpu.VMEM((local, width), b16),
            pltpu.VMEM((zs, depth, gc), b16),
            pltpu.VMEM((depth, gc), b16),
            pltpu.VMEM((3, depth, gc), b16),
            pltpu.VMEM(wide, b16),
            pltpu.VMEM((n // 2, local, width), b16),
            pltpu.VMEM((n // 2 - 1, local, width), b16),
            pltpu.VMEM((local, width), f32),
            pltpu.VMEM(wide, b16),
            pltpu.VMEM((zs, hc // zs, width), b16),
            pltpu.VMEM((hc // zs, width), b16),
            pltpu.VMEM((3, hc // zs, width), b16),
            pltpu.VMEM((hc // zs, width), f32),
            pltpu.VMEM(ob.shape, b16),
            pltpu.VMEM((3, seq, hc), f32),
            pltpu.VMEM((n, slots, rows, 3 * hc), b16),
            pltpu.SemaphoreType.DMA((48,)),
            pltpu.SemaphoreType.DMA((48,)),
            pltpu.SemaphoreType.DMA((24,)),
        ],
        compiler_params=pltpu.CompilerParams(
            collective_id=4, has_side_effects=True, vmem_limit_bytes=62 << 20
        ),
        name="backward",
    )(norms, tables, a2_all, dgu, w_gu, w_out, qkv, probs, ob, hidden, dy_all)


def tensor_shards(
    inputs,
    lengths,
    w_qkv,
    b_qkv,
    w_out,
    w_gate,
    w_up,
    w_down,
    gain_one,
    shift_one,
    gain_two,
    shift_two,
    cotangent,
):
    rows, slots, width = inputs.shape
    f32, b16 = jnp.float32, jnp.bfloat16
    zs, n = lax.axis_size("dp"), lax.axis_size("ctx")
    me = lax.axis_index("ctx")
    local = rows * slots
    tokens = local * n
    seq = rows * n
    wrows = w_qkv.shape[0]
    ff_block = w_down.shape[0]
    heads = HEADS // n
    hc = heads * HEAD_DIM
    ffc = ff_block * zs

    def dot(a, b, dims):
        return lax.dot_general(a, b, (dims, ((), ())), preferred_element_type=f32)

    def local_tokens(v):
        return jnp.transpose(v, (1, 0, 2)).reshape(local, width)

    def back_tokens(v):
        return jnp.transpose(v.reshape(slots, rows, width), (1, 0, 2))

    def exchange(v):
        return lax.all_to_all(v, "ctx", 0, 0, tiled=True)

    def gather_ctx(v):
        return lax.all_gather(v, "ctx", axis=0, tiled=True)

    def scatter_ctx(v):
        return lax.psum_scatter(v.astype(b16), "ctx", scatter_dimension=0, tiled=True).astype(f32)

    def gather_dp(v):
        return lax.all_gather(v, "dp", axis=0, tiled=True)

    def scatter_dp(v):
        return lax.psum_scatter(v.astype(b16), "dp", scatter_dimension=0, tiled=True)

    xs = local_tokens(inputs)
    dy = local_tokens(cotangent)
    small = jnp.concatenate([b_qkv, gain_one, shift_one, gain_two, shift_two]).astype(f32)
    small = jnp.pad(small, (0, 1024 - small.shape[0])).reshape(8, 128)
    w_qkv_c, w_out_c, gu_own, a_all, dy_all, small = spread(
        zs, n, w_qkv, w_gate, w_up, w_out, xs, dy, small
    )
    small = small.reshape(zs * n, 1024)
    dy_all = dy_all.reshape(tokens, width)
    nb = b_qkv.shape[0]
    bias_full = small[:, :nb].reshape(3, zs, n, HEAD_DIM)
    bias_own = lax.dynamic_index_in_dim(bias_full, me, 2, keepdims=False).reshape(1, 3 * hc)
    g1, s1, g2, s2 = [
        small[:, nb + i * wrows : nb + (i + 1) * wrows].reshape(1, width) for i in range(4)
    ]


    counter = jnp.arange(ROTARY // 2, dtype=f32)
    angles = jnp.arange(seq, dtype=f32)[:, None] * (10000.0 ** (-2.0 * counter / ROTARY))[None, :]
    cos_t, sin_t = jnp.cos(angles), jnp.sin(angles)
    zero = jnp.zeros_like(sin_t)
    rest = jnp.ones((seq, HEAD_DIM - ROTARY), f32)
    table_c = jnp.tile(jnp.concatenate([cos_t, cos_t, rest], -1), (1, heads))
    table_l = jnp.tile(jnp.concatenate([-sin_t, zero, 0 * rest], -1), (1, heads))
    table_r = jnp.tile(jnp.concatenate([zero, sin_t, 0 * rest], -1), (1, heads))

    def by_slot(v):
        return v.reshape(n, slots, rows, v.shape[-1]).transpose(1, 0, 2, 3).reshape(
            slots, seq, v.shape[-1]
        )

    def by_device(v):
        return v.reshape(slots, n, rows, v.shape[-1]).transpose(1, 0, 2, 3).reshape(
            tokens, v.shape[-1]
        )

    def turn(v, sign):
        half = ROTARY // 2
        return (
            v * table_c
            + sign * jnp.roll(v, -half, -1) * table_l
            + sign * jnp.roll(v, half, -1) * table_r
        )

    tables = jnp.stack([table_c, table_l, table_r]).reshape(3, n, rows, hc)
    norms = jnp.concatenate([g1, s1, g2, s2])
    a1_all, qkv, probs, ob, hidden, a2_all, w_gu_c, gu, z = forward(
        zs, n, slots, lengths, norms, bias_own, tables, a_all, w_qkv_c, w_out_c,
        gu_own.reshape(n * wrows, 2 * ffc),
    )
    dgu, w_down_c, grad_down = middle(zs, n, z, gu, dy_all.reshape(n, local, width), w_down)
    ggu, grad_out, dh, dj, gains_two, bias_part = backward(
        zs, n, norms, tables, a2_all, dgu, w_gu_c, w_out_c, qkv, probs, ob, hidden,
        dy_all.reshape(n, local, width),
    )
    grad_gu = exchange(ggu.reshape(n, wrows, 2 * ffc))
    gain_two_part, shift_two_part = gains_two[0], gains_two[1]
    bias_part = bias_part.reshape(3, zs, 1, HEAD_DIM)
    w_qkv_c = w_qkv_c.reshape(width, 3 * hc)
    a1_all = a1_all.reshape(tokens, width)
    dj = dj.reshape(tokens, 3 * hc)
    n1, r1 = layer_stats(xs.astype(f32))
    z = z.reshape(tokens, ffc)
    w_down_c = w_down_c.reshape(ffc, width)
    result = hidden + scatter_ctx(dot(z, w_down_c, ((1,), (0,))))
    grad_qkv = exchange(scatter_dp(dot(a1_all, dj, ((0,), (0,)))).reshape(n, wrows, 3 * hc))
    da1 = scatter_ctx(dot(dj, w_qkv_c, ((1,), (1,))))
    gain_one_part = jnp.sum(da1 * n1, 0)
    shift_one_part = jnp.sum(da1, 0)
    input_grad = dh + norm_back(da1, n1, r1, g1)

    own = (jnp.arange(n) == me)[None, None, :, None]
    devices = zs * n
    pieces = jnp.concatenate(
        [
            jnp.where(own, bias_part, 0.0).reshape(devices, nb),
            gain_one_part.reshape(devices, wrows),
            shift_one_part.reshape(devices, wrows),
            gain_two_part.reshape(devices, wrows),
            shift_two_part.reshape(devices, wrows),
        ],
        -1,
    )
    summed = lax.psum_scatter(pieces, ("dp", "ctx"), scatter_dimension=0, tiled=True)[0]

    def ff_back(part):
        return jnp.transpose(part.reshape(n, wrows, zs, ff_block), (1, 2, 0, 3)).reshape(
            wrows, zs * n * ff_block
        ).astype(f32)

    grad_qkv = jnp.transpose(grad_qkv.reshape(n, wrows, 3, zs, HEAD_DIM), (1, 2, 3, 0, 4)).reshape(
        wrows, 3 * width
    ).astype(f32)
    return (
        back_tokens(result.astype(b16)),
        back_tokens(input_grad),
        grad_qkv,
        summed[:nb],
        grad_out,
        ff_back(grad_gu[..., :ffc]),
        ff_back(grad_gu[..., ffc:]),
        grad_down,
        summed[nb : nb + wrows],
        summed[nb + wrows : nb + 2 * wrows],
        summed[nb + 2 * wrows : nb + 3 * wrows],
        summed[nb + 3 * wrows :],
    )


def solution(mesh):
    zs, n = mesh.shape["dp"], mesh.shape["ctx"]
    shards = tensor_shards if (zs, n) == (4, 8) and HEADS == 32 else gathered_shards

    placed = (
        P("ctx", "dp", None),
        P("dp", None),
        P(("dp", "ctx"), None),
        P(("dp", "ctx")),
        P(("dp", "ctx"), None),
        P(("dp", "ctx"), None),
        P(("dp", "ctx"), None),
        P(("dp", "ctx"), None),
        P(("dp", "ctx")),
        P(("dp", "ctx")),
        P(("dp", "ctx")),
        P(("dp", "ctx")),
        P("ctx", "dp", None),
    )
    return jax.shard_map(
        shards,
        mesh=mesh,
        in_specs=placed,
        out_specs=(
            P("ctx", "dp", None),
            P("ctx", "dp", None),
            P(("dp", "ctx"), None),
            P(("dp", "ctx")),
            P(("dp", "ctx"), None),
            P(("dp", "ctx"), None),
            P(("dp", "ctx"), None),
            P(("dp", "ctx"), None),
            P(("dp", "ctx")),
            P(("dp", "ctx")),
            P(("dp", "ctx")),
            P(("dp", "ctx")),
        ),
        check_vma=False,
    )
```

```python
import functools
import itertools
import math

import jax
import jax.numpy as jnp
from jax import lax
from jax.experimental import pallas as pl
from jax.experimental.pallas import tpu as pltpu
from jax.sharding import PartitionSpec as P

HEADS = 32
HEAD_DIM = 64
ROTARY = 16


epsilon = 1e-05
masked_value = -1e30


def layer_stats(values):
    row_mean = jnp.mean(values, -1, keepdims=True)
    centred = values - row_mean
    inverse = lax.rsqrt(jnp.mean(centred * centred, -1, keepdims=True) + epsilon)
    return (centred * inverse, inverse)


def norm_back(grad_normed, scaled, inverse, gain_vec):
    grad_hat = grad_normed * gain_vec
    return inverse * (
        grad_hat
        - jnp.mean(grad_hat, -1, keepdims=True)
        - scaled * jnp.mean(grad_hat * scaled, -1, keepdims=True)
    )


def rotary_tables(positions):
    counter = jnp.arange(ROTARY // 2, dtype=jnp.float32)
    frequency = 10000.0 ** (-2.0 * counter / ROTARY)
    angles = positions.astype(jnp.float32)[:, None] * frequency[None, :]
    return (jnp.cos(angles)[:, None, None, :], jnp.sin(angles)[:, None, None, :])


def rotate(values, cos_table, sin_table):
    half_dims = ROTARY // 2
    first_half = values[..., :half_dims]
    second_half = values[..., half_dims:ROTARY]
    return jnp.concatenate(
        [
            first_half * cos_table - second_half * sin_table,
            second_half * cos_table + first_half * sin_table,
            values[..., ROTARY:],
        ],
        -1,
    )


def over_blocks(step_fn, running, gathered):
    total_rows = gathered.shape[0]
    tile_rows = math.gcd(total_rows, 512)

    def visit_block(number, current):
        block_start = number * tile_rows
        block_part = lax.dynamic_slice_in_dim(gathered, block_start, tile_rows, 0)
        return step_fn(current, block_part, block_start)

    return lax.fori_loop(0, total_rows // tile_rows, visit_block, running)


def gathered_shards(
    inputs,
    lengths,
    w_qkv,
    b_qkv,
    w_out,
    w_gate,
    w_up,
    w_down,
    gain_one,
    shift_one,
    gain_two,
    shift_two,
    cotangent,
):
    local_rows, slot_count, width = inputs.shape
    positions = lax.axis_index("ctx") * local_rows + jnp.arange(local_rows, dtype=jnp.int32)
    live_rows = positions[:, None] < lengths[0][None, :]
    live_heads = jnp.transpose(live_rows)[:, None, :, None]
    cos_table, sin_table = rotary_tables(positions)

    def allowed_mask(offset, count):
        key_pos = offset + jnp.arange(count, dtype=jnp.int32)
        causal = key_pos[None, :] <= positions[:, None]
        return causal[None, None, :, :] & live_heads

    def split_heads(block_part):
        count = block_part.shape[0]
        key_part = block_part[:, :, 0].reshape(count, slot_count, HEADS, HEAD_DIM)
        value_part = block_part[:, :, 1].reshape(count, slot_count, HEADS, HEAD_DIM)
        return (key_part, value_part)

    attn_full = (
        lax.all_gather(w_qkv, ("dp", "ctx"), axis=0, tiled=True),
        lax.all_gather(b_qkv, ("dp", "ctx"), axis=0, tiled=True),
        lax.all_gather(w_out, ("dp", "ctx"), axis=0, tiled=True),
        lax.all_gather(gain_one, ("dp", "ctx"), axis=0, tiled=True),
        lax.all_gather(shift_one, ("dp", "ctx"), axis=0, tiled=True),
    )
    qkv_full, bias_full, out_full, gain_one_full, shift_one_full = attn_full
    source = inputs.astype(jnp.float32)
    scaled_one, inverse_one = layer_stats(source)
    normed_one = (
        scaled_one * gain_one_full.astype(jnp.float32) + shift_one_full.astype(jnp.float32)
    ).astype(jnp.bfloat16)
    joined = jnp.einsum(
        "rsd,de->rse", normed_one, qkv_full, preferred_element_type=jnp.float32
    ) + bias_full.astype(jnp.float32)
    query_pre = joined[..., :width].reshape(local_rows, slot_count, HEADS, HEAD_DIM)
    key_pre = joined[..., width : 2 * width].reshape(local_rows, slot_count, HEADS, HEAD_DIM)
    queries = rotate(query_pre, cos_table, sin_table).astype(jnp.bfloat16)
    keys_rot = rotate(key_pre, cos_table, sin_table).reshape(local_rows, slot_count, width)
    key_value = jnp.stack([keys_rot, joined[..., 2 * width :]], 2).astype(jnp.bfloat16)
    block_part = lax.all_gather(key_value, "ctx", axis=0, tiled=True)
    run_peak = jnp.full((slot_count, HEADS, local_rows), masked_value, jnp.float32)
    key_part, value_part = split_heads(block_part)
    scores = (
        jnp.einsum("qshd,kshd->shqk", queries, key_part, preferred_element_type=jnp.float32) * 0.125
    )
    allowed = allowed_mask(jnp.int32(0), block_part.shape[0])
    masked = jnp.where(allowed, scores, masked_value)
    new_peak = jnp.maximum(run_peak, jnp.max(masked, -1))
    weights = jnp.where(allowed, jnp.exp(masked - new_peak[..., None]), 0.0)
    new_sum = jnp.sum(weights, -1)
    new_acc = jnp.einsum(
        "shqk,kshd->shqd",
        weights.astype(jnp.bfloat16),
        value_part,
        preferred_element_type=jnp.float32,
    )
    final_sum = jnp.maximum(new_sum, 1.0)
    log_sum = new_peak + jnp.log(final_sum)
    attended = jnp.transpose(new_acc / final_sum[..., None], (2, 0, 1, 3))
    attended_low = attended.reshape(local_rows, slot_count, width).astype(jnp.bfloat16)
    hidden_in = source + jnp.einsum(
        "rsd,de->rse", attended_low, out_full, preferred_element_type=jnp.float32
    )
    mlp_full = (
        lax.all_gather(w_gate, ("dp", "ctx"), axis=0, tiled=True),
        lax.all_gather(w_up, ("dp", "ctx"), axis=0, tiled=True),
        lax.all_gather(w_down, ("dp", "ctx"), axis=0, tiled=True),
        lax.all_gather(gain_two, ("dp", "ctx"), axis=0, tiled=True),
        lax.all_gather(shift_two, ("dp", "ctx"), axis=0, tiled=True),
    )
    gate_full, up_full, down_full, gain_two_full, shift_two_full = mlp_full
    scaled_two, inverse_two = layer_stats(hidden_in)
    normed_two = (
        scaled_two * gain_two_full.astype(jnp.float32) + shift_two_full.astype(jnp.float32)
    ).astype(jnp.bfloat16)
    gate = jnp.einsum("rsd,df->rsf", normed_two, gate_full, preferred_element_type=jnp.float32)
    upward = jnp.einsum("rsd,df->rsf", normed_two, up_full, preferred_element_type=jnp.float32)
    sigmoid = jax.nn.sigmoid(gate)
    product = (gate * sigmoid * upward).astype(jnp.bfloat16)
    result = hidden_in + jnp.einsum(
        "rsf,fd->rsd", product, down_full, preferred_element_type=jnp.float32
    )
    gate_back, up_back, down_back, gain_two_back = (
        lax.all_gather(w_gate, ("dp", "ctx"), axis=0, tiled=True),
        lax.all_gather(w_up, ("dp", "ctx"), axis=0, tiled=True),
        lax.all_gather(w_down, ("dp", "ctx"), axis=0, tiled=True),
        lax.all_gather(gain_two, ("dp", "ctx"), axis=0, tiled=True),
    )
    grad_down = jnp.einsum("rsf,rsd->fd", product, cotangent, preferred_element_type=jnp.float32)
    grad_product = jnp.einsum(
        "rsd,fd->rsf", cotangent, down_back, preferred_element_type=jnp.float32
    )
    grad_gate_act = (grad_product * upward * sigmoid * (1.0 + gate * (1.0 - sigmoid))).astype(
        jnp.bfloat16
    )
    grad_up_act = (grad_product * gate * sigmoid).astype(jnp.bfloat16)
    grad_gate = jnp.einsum(
        "rsd,rsf->df", normed_two, grad_gate_act, preferred_element_type=jnp.float32
    )
    grad_up = jnp.einsum("rsd,rsf->df", normed_two, grad_up_act, preferred_element_type=jnp.float32)
    grad_normed_two = jnp.einsum(
        "rsf,df->rsd", grad_gate_act, gate_back, preferred_element_type=jnp.float32
    ) + jnp.einsum("rsf,df->rsd", grad_up_act, up_back, preferred_element_type=jnp.float32)
    grad_gain_two = jnp.sum(grad_normed_two * scaled_two, (0, 1))
    grad_shift_two = jnp.sum(grad_normed_two, (0, 1))
    grad_hidden = cotangent.astype(jnp.float32) + norm_back(
        grad_normed_two, scaled_two, inverse_two, gain_two_back.astype(jnp.float32)
    )
    mlp_sums = (
        lax.psum_scatter(grad_gate, ("dp", "ctx"), scatter_dimension=0, tiled=True),
        lax.psum_scatter(grad_up, ("dp", "ctx"), scatter_dimension=0, tiled=True),
        lax.psum_scatter(grad_down, ("dp", "ctx"), scatter_dimension=0, tiled=True),
        lax.psum_scatter(grad_gain_two, ("dp", "ctx"), scatter_dimension=0, tiled=True),
        lax.psum_scatter(grad_shift_two, ("dp", "ctx"), scatter_dimension=0, tiled=True),
    )
    qkv_back, out_back, gain_one_back = (
        lax.all_gather(w_qkv, ("dp", "ctx"), axis=0, tiled=True),
        lax.all_gather(w_out, ("dp", "ctx"), axis=0, tiled=True),
        lax.all_gather(gain_one, ("dp", "ctx"), axis=0, tiled=True),
    )
    hidden_low = grad_hidden.astype(jnp.bfloat16)
    grad_out = jnp.einsum(
        "rsd,rse->de", attended_low, hidden_low, preferred_element_type=jnp.float32
    )
    grad_attended = jnp.einsum(
        "rse,de->rsd", hidden_low, out_back, preferred_element_type=jnp.float32
    )
    grad_heads = grad_attended.reshape(local_rows, slot_count, HEADS, HEAD_DIM).astype(jnp.bfloat16)
    delta = jnp.transpose(jnp.sum(grad_heads.astype(jnp.float32) * attended, -1), (1, 2, 0))
    key_value_all = lax.all_gather(key_value, "ctx", axis=0, tiled=True)

    def grad_parts(block_part, offset):
        key_part, value_part = split_heads(block_part)
        scores = (
            jnp.einsum("qshd,kshd->shqk", queries, key_part, preferred_element_type=jnp.float32)
            * 0.125
        )
        allowed = allowed_mask(offset, block_part.shape[0])
        probs = jnp.where(allowed, jnp.exp(scores - log_sum[..., None]), 0.0)
        grad_prob = jnp.einsum(
            "qshd,kshd->shqk", grad_heads, value_part, preferred_element_type=jnp.float32
        )
        grad_score = (probs * (grad_prob - delta[..., None])).astype(jnp.bfloat16)
        return (key_part, probs, grad_score)

    def query_step(running, block_part, offset):
        key_part, probs, grad_score = grad_parts(block_part, offset)
        return running + jnp.einsum(
            "shqk,kshd->shqd", grad_score, key_part, preferred_element_type=jnp.float32
        )

    grad_query = (
        over_blocks(
            query_step,
            jnp.zeros((slot_count, HEADS, local_rows, HEAD_DIM), jnp.float32),
            key_value_all,
        )
        * 0.125
    )
    count = local_rows * lax.axis_size("ctx")
    tile_rows = math.gcd(count, 512)

    def one_block(number):
        block_start = number * tile_rows
        block_part = lax.dynamic_slice_in_dim(key_value_all, block_start, tile_rows, 0)
        key_part, probs, grad_score = grad_parts(block_part, block_start)
        grad_key = (
            jnp.einsum("shqk,qshd->kshd", grad_score, queries, preferred_element_type=jnp.float32)
            * 0.125
        )
        grad_value = jnp.einsum(
            "shqk,qshd->kshd",
            probs.astype(jnp.bfloat16),
            grad_heads,
            preferred_element_type=jnp.float32,
        )
        return jnp.stack(
            [
                grad_key.reshape(tile_rows, slot_count, width),
                grad_value.reshape(tile_rows, slot_count, width),
            ],
            2,
        )

    blocks = lax.map(one_block, jnp.arange(count // tile_rows, dtype=jnp.int32))
    grad_key_value = lax.psum_scatter(
        blocks.reshape(count, slot_count, 2, width).astype(jnp.bfloat16),
        "ctx",
        scatter_dimension=0,
        tiled=True,
    ).astype(jnp.float32)
    grad_query_pre = rotate(jnp.transpose(grad_query, (2, 0, 1, 3)), cos_table, -sin_table)
    grad_key_pre = rotate(
        grad_key_value[:, :, 0].reshape(local_rows, slot_count, HEADS, HEAD_DIM),
        cos_table,
        -sin_table,
    )
    grad_joined = jnp.concatenate(
        [
            grad_query_pre.reshape(local_rows, slot_count, width),
            grad_key_pre.reshape(local_rows, slot_count, width),
            grad_key_value[:, :, 1],
        ],
        -1,
    ).astype(jnp.bfloat16)
    grad_qkv = jnp.einsum(
        "rsd,rse->de", normed_one, grad_joined, preferred_element_type=jnp.float32
    )
    grad_bias = jnp.sum(grad_joined.astype(jnp.float32), (0, 1))
    grad_normed_one = jnp.einsum(
        "rse,de->rsd", grad_joined, qkv_back, preferred_element_type=jnp.float32
    )
    grad_gain_one = jnp.sum(grad_normed_one * scaled_one, (0, 1))
    grad_shift_one = jnp.sum(grad_normed_one, (0, 1))
    input_grad = grad_hidden + norm_back(
        grad_normed_one, scaled_one, inverse_one, gain_one_back.astype(jnp.float32)
    )
    attn_sums = (
        lax.psum_scatter(grad_qkv, ("dp", "ctx"), scatter_dimension=0, tiled=True),
        lax.psum_scatter(grad_bias, ("dp", "ctx"), scatter_dimension=0, tiled=True),
        lax.psum_scatter(grad_out, ("dp", "ctx"), scatter_dimension=0, tiled=True),
        lax.psum_scatter(grad_gain_one, ("dp", "ctx"), scatter_dimension=0, tiled=True),
        lax.psum_scatter(grad_shift_one, ("dp", "ctx"), scatter_dimension=0, tiled=True),
    )
    return (
        result.astype(jnp.bfloat16),
        input_grad,
        attn_sums[0],
        attn_sums[1],
        attn_sums[2],
        mlp_sums[0],
        mlp_sums[1],
        mlp_sums[2],
        attn_sums[3],
        attn_sums[4],
        mlp_sums[3],
        mlp_sums[4],
    )


MESH = pl.DeviceIdType.MESH
HBM = pl.BlockSpec(memory_space=pltpu.HBM)
VMEM = pl.BlockSpec(memory_space=pltpu.VMEM)


def flip(index, mask):
    for bit in (1, 2, 4):
        if mask & bit:
            index = index + bit - 2 * bit * ((index // bit) % 2)
    return index


class Wires:
    def __init__(self, send, recv):
        self.send, self.recv = send, recv
        self.z, self.c = lax.axis_index("dp"), lax.axis_index("ctx")
        self.inner = (self.z == 1) | (self.z == 2)
        self.outer = (self.z == 0) | (self.z == 3)
        self.number = itertools.count()

    def put(self, src, dst, z_mask, c_mask):
        i = next(self.number)
        return pltpu.make_async_remote_copy(
            src_ref=src,
            dst_ref=dst,
            send_sem=self.send.at[i],
            recv_sem=self.recv.at[i],
            device_id=(flip(self.z, z_mask), flip(self.c, c_mask)),
            device_id_type=MESH,
        )

    def greet(self, zs, n):
        barrier = pltpu.get_barrier_semaphore()
        for m in range(1, zs):
            pl.semaphore_signal(
                barrier, inc=1, device_id=(flip(self.z, m), self.c), device_id_type=MESH
            )
        for m in range(1, n):
            pl.semaphore_signal(
                barrier, inc=1, device_id=(self.z, flip(self.c, m)), device_id_type=MESH
            )
        pl.semaphore_wait(barrier, zs + n - 2)


class DepthGather:
    def __init__(self, wires, part):
        z = wires.z
        self.wires = wires
        self.near = wires.put(part(z), part(z), 1, 0)
        self.skip = wires.put(part(z), part(z), 2, 0)
        self.mid = wires.put(part(z), part(z), 3, 0)
        far = flip(z, 2)
        self.on = wires.put(part(far), part(far), 1, 0)

    def start(self):
        self.skip.start()
        pl.when(self.wires.inner)(self.mid.start)
        self.near.start()

    def forward(self):
        @pl.when(self.wires.inner)
        def _():
            self.skip.wait_recv()
            self.on.start()

    def finish(self):
        self.near.wait_recv()
        self.near.wait_send()
        self.skip.wait_send()

        @pl.when(self.wires.inner)
        def _():
            self.mid.wait_recv()
            self.mid.wait_send()
            self.on.wait_send()

        @pl.when(self.wires.outer)
        def _():
            self.skip.wait_recv()
            self.on.wait_recv()


class LayerGather:
    def __init__(self, wires, buf, source=None):
        c = wires.c
        mine = buf.at[c] if source is None else source
        self.direct = {m: wires.put(mine, buf.at[c], 0, m) for m in (2, 4, 6, 1)}
        self.on = {
            m: wires.put(buf.at[flip(c, m)], buf.at[flip(c, m)], 0, 1) for m in (2, 4, 6)
        }

    def start(self):
        for m in (2, 4, 6, 1):
            self.direct[m].start()

    def forward(self, m):
        self.direct[m].wait_recv()
        self.on[m].start()

    def arrived(self, m):
        (self.direct[1] if m == 1 else self.on[m - 1]).wait_recv()

    def sent(self):
        for copy in (*self.direct.values(), *self.on.values()):
            copy.wait_send()


def pack_columns(dst, refs, n, zs):
    for i in range(n):
        pieces = []
        for ref, block in refs:
            pieces += [ref[:, block * (j * n + i) : block * (j * n + i + 1)] for j in range(zs)]
        dst[i] = jnp.concatenate(pieces, -1)


def spread_kernel(
    zs,
    n,
    w_qkv,
    w_gate,
    w_up,
    w_out,
    xs,
    dy,
    small,
    qkv_all,
    out_all,
    gu_own,
    xs_all,
    dy_all,
    small_all,
    qkv_send,
    gu_send,
    send,
    recv,
    local,
):
    wires = Wires(send, recv)
    z, c = wires.z, wires.c
    hc = HEAD_DIM * HEADS // n
    width = HEADS * HEAD_DIM
    ff_block = w_gate.shape[1] // (zs * n)

    own = [
        pltpu.make_async_copy(w_out, out_all.at[z], local.at[0]),
        pltpu.make_async_copy(qkv_send.at[c], qkv_all.at[z, c], local.at[1]),
        pltpu.make_async_copy(gu_send.at[c], gu_own.at[c], local.at[2]),
        pltpu.make_async_copy(xs, xs_all.at[c], local.at[3]),
        pltpu.make_async_copy(dy, dy_all.at[c], local.at[4]),
        pltpu.make_async_copy(small, small_all.at[z, c], local.at[5]),
    ]
    for i in (0, 3, 4, 5):
        own[i].start()
    pack_columns(
        qkv_send, [(w_qkv.at[:, i * width : (i + 1) * width], HEAD_DIM) for i in range(3)], n, zs
    )
    own[1].start()
    wires.greet(zs, n)
    for i in (0, 5):
        own[i].wait()

    out_z = DepthGather(wires, lambda i: out_all.at[i])
    out_z.start()
    qkv_x = [
        wires.put(qkv_send.at[flip(c, m)], qkv_all.at[z, c], 0, m) for m in range(1, n)
    ]
    for copy in qkv_x:
        copy.start()
    small_z = [wires.put(small_all.at[z, c], small_all.at[z, c], m, 0) for m in range(1, zs)]
    for copy in small_z:
        copy.start()
    xs_g = LayerGather(wires, xs_all, xs)
    xs_g.start()
    pack_columns(gu_send, [(w_gate, ff_block), (w_up, ff_block)], n, zs)
    own[2].start()
    for copy in small_z:
        copy.wait_recv()
    small_x = [
        wires.put(small_all.at[:, c], small_all.at[:, c], 0, m) for m in range(1, n)
    ]
    for copy in small_x:
        copy.start()
    own[1].wait()
    for copy in qkv_x:
        copy.wait_recv()
    half = n // 2
    qkv_z = [
        DepthGather(wires, lambda i, p=p: qkv_all.at[i, p * half : (p + 1) * half])
        for p in range(2)
    ]
    for part in qkv_z:
        part.start()
    out_z.forward()
    gu_x = [wires.put(gu_send.at[flip(c, m)], gu_own.at[c], 0, m) for m in range(1, n)]
    for copy in gu_x:
        copy.start()
    for m in (2, 4, 6):
        xs_g.forward(m)
    dy_g = LayerGather(wires, dy_all, dy)
    dy_g.start()
    qkv_z[0].forward()
    for m in (2, 4, 6):
        dy_g.forward(m)
    qkv_z[1].forward()

    for i in (2, 3, 4):
        own[i].wait()
    for group in (xs_g, dy_g):
        for m in (1, 3, 5, 7):
            group.arrived(m)
        group.sent()
    for copy in small_z:
        copy.wait_send()
    for copy in qkv_x:
        copy.wait_send()
    for copy in (*small_x, *gu_x):
        copy.wait()
    for part in (out_z, *qkv_z):
        part.finish()


def spread(zs, n, w_qkv, w_gate, w_up, w_out, xs, dy, small):
    wrows, width = w_out.shape
    qc, gc = w_qkv.shape[1] // n, 2 * w_gate.shape[1] // n
    b16 = jnp.bfloat16
    return pl.pallas_call(
        functools.partial(spread_kernel, zs, n),
        out_shape=[
            jax.ShapeDtypeStruct((zs, n, wrows, qc), b16),
            jax.ShapeDtypeStruct((zs, wrows, width), b16),
            jax.ShapeDtypeStruct((n, wrows, gc), b16),
            jax.ShapeDtypeStruct((n, *xs.shape), b16),
            jax.ShapeDtypeStruct((n, *dy.shape), b16),
            jax.ShapeDtypeStruct((zs, n, *small.shape), small.dtype),
        ],
        in_specs=[VMEM, VMEM, VMEM, HBM, HBM, HBM, HBM],
        out_specs=[HBM] * 6,
        scratch_shapes=[
            pltpu.VMEM((n, wrows, qc), b16),
            pltpu.VMEM((n, wrows, gc), b16),
            pltpu.SemaphoreType.DMA((64,)),
            pltpu.SemaphoreType.DMA((64,)),
            pltpu.SemaphoreType.DMA((6,)),
        ],
        compiler_params=pltpu.CompilerParams(
            collective_id=1, has_side_effects=True, vmem_limit_bytes=32 << 20
        ),
        name="spread",
    )(w_qkv, w_gate, w_up, w_out, xs, dy, small)


class LayerScatter:
    def __init__(self, wires, part, near, far):
        c = wires.c
        self.c, self.part, self.near, self.far = c, part, near, far
        self.pair = {
            m: wires.put(part.at[flip(c, m + 1)], near.at[m // 2], 0, 1) for m in (6, 4, 2, 0)
        }
        self.chips = {
            m: wires.put(part.at[flip(c, m)], far.at[m // 2 - 1], 0, m) for m in (6, 4, 2)
        }

    def start(self):
        for copy in self.pair.values():
            copy.start()

    def step(self, m):
        self.pair[m].wait_recv()
        to = flip(self.c, m)
        self.part[to] = (
            self.part[to].astype(jnp.float32) + self.near[m // 2].astype(jnp.float32)
        ).astype(self.part.dtype)
        self.chips[m].start()

    def total(self):
        self.pair[0].wait_recv()
        result = self.part[self.c].astype(jnp.float32) + self.near[0].astype(jnp.float32)
        for m in (2, 4, 6):
            self.chips[m].wait_recv()
            result = result + self.far[m // 2 - 1].astype(jnp.float32)
        return result

    def sent(self):
        for copy in (*self.pair.values(), *self.chips.values()):
            copy.wait_send()


def dot(a, b, dims=((1,), (0,))):
    return lax.dot_general(a, b, (dims, ((), ())), preferred_element_type=jnp.float32)


def turn_pair(values, table, sign):
    half = ROTARY // 2
    columns = values.shape[-1]
    return (
        values * table[0]
        + sign * (pltpu.roll(values, columns - half, 1) * table[1])
        + sign * (pltpu.roll(values, half, 1) * table[2])
    )


def head_mask(rows, columns, head):
    return lax.broadcasted_iota(jnp.int32, (rows, columns), 1) // HEAD_DIM == head


def forward_kernel(
    zs,
    n,
    lengths,
    norms,
    bias,
    tables,
    xs_all,
    w_qkv,
    w_out,
    gu_own,
    a1_out,
    qkv_out,
    probs_out,
    ob_out,
    hidden_out,
    a2_out,
    w_gu_out,
    gu_out,
    zz_out,
    xs_v,
    a1_v,
    w_qkv_v,
    w_out_v,
    qkv_v,
    probs_v,
    ob_v,
    part,
    near,
    far,
    hidden_v,
    a2_v,
    w_gu_v,
    gu_v,
    zz_v,
    send,
    recv,
    local,
    drain,
):
    f32, b16 = jnp.float32, jnp.bfloat16
    wires = Wires(send, recv)
    z, c = wires.z, wires.c
    _, slots, rows, hc = ob_v.shape
    tokens, width = n * slots * rows, a1_v.shape[-1]
    seq = n * rows
    heads = hc // HEAD_DIM
    ffc = zz_v.shape[-1]
    chunks = 4
    chunk = w_gu_v.shape[1] // chunks

    loads = [
        pltpu.make_async_copy(gu_own, w_gu_v.at[z], local.at[0]),
        pltpu.make_async_copy(xs_all, xs_v, local.at[1]),
        pltpu.make_async_copy(w_qkv, w_qkv_v, local.at[2]),
        pltpu.make_async_copy(w_out, w_out_v, local.at[3]),
    ]
    for copy in loads:
        copy.start()
    wires.greet(zs, n)
    loads[0].wait()
    gu_z = [
        DepthGather(wires, lambda i, p=p: w_gu_v.at[i, p * chunk : (p + 1) * chunk])
        for p in range(chunks)
    ]
    for part_z in gu_z:
        part_z.start()
    stores = []

    def store(src, dst):
        copy = pltpu.make_async_copy(src, dst, drain.at[len(stores)])
        copy.start()
        stores.append(copy)

    for copy in loads[1:]:
        copy.wait()

    def project(i, carry):
        x = xs_v[pl.ds(2 * i, 2)].reshape(2 * slots * rows, width).astype(f32)
        a1 = (layer_stats(x)[0] * norms[0:1] + norms[1:2]).astype(b16)
        a1_v[pl.ds(2 * i, 2)] = a1.reshape(2, slots * rows, width)
        joined = dot(a1, w_qkv_v[...].reshape(width, 3 * hc)) + bias[...]
        for j in range(2):
            table = tables[:, 2 * i + j]
            for s in range(slots):
                at = (j * slots + s) * rows
                piece = joined[at : at + rows]
                qkv_v[0, s, 2 * i + j] = turn_pair(piece[:, :hc], table, 1.0).astype(b16)
                qkv_v[1, s, 2 * i + j] = turn_pair(piece[:, hc : 2 * hc], table, 1.0).astype(b16)
                qkv_v[2, s, 2 * i + j] = piece[:, 2 * hc :].astype(b16)
        return carry

    lax.fori_loop(0, n // 2, project, 0)
    store(a1_v, a1_out)
    store(qkv_v, qkv_out)

    half = seq // 2

    def attend(s, carry):
        q, k, v = [qkv_v[i, s].reshape(seq, hc) for i in range(3)]
        length = lengths[0, s]
        for part_q in range(2):
            keys = (part_q + 1) * half
            at = part_q * half
            query = q[at : at + half]
            row = lax.broadcasted_iota(jnp.int32, (half, keys), 0) + at
            key = lax.broadcasted_iota(jnp.int32, (half, keys), 1)
            allowed = (key <= row) & (row < length)
            out = jnp.zeros((half, hc), f32)
            for h in range(heads):
                mask = head_mask(half, hc, h)
                scores = dot(jnp.where(mask, query, 0).astype(b16), k[:keys], ((1,), (1,)))
                scores = jnp.where(allowed, scores * 0.125, masked_value)
                peak = jnp.max(scores, -1, keepdims=True)
                weights = jnp.where(allowed, jnp.exp(scores - peak), 0.0)
                total = jnp.maximum(jnp.sum(weights, -1, keepdims=True), 1.0)
                probs = (weights * (1.0 / total)).astype(b16)
                probs_v[s, h, at : at + half, 0:keys] = probs
                out = jnp.where(mask, dot(probs, v[:keys]), out)
            ob_v[part_q * n // 2 : (part_q + 1) * n // 2, s] = out.astype(b16).reshape(
                n // 2, rows, hc
            )
        return carry

    lax.fori_loop(0, slots, attend, 0)
    store(probs_v, probs_out)
    store(ob_v, ob_out)

    def to_hidden(i, carry):
        part[i] = dot(
            ob_v[i].reshape(slots * rows, hc), w_out_v[...].reshape(hc, width)
        ).astype(b16)
        return carry

    lax.fori_loop(0, n, to_hidden, 0)
    sums = LayerScatter(wires, part, near, far)
    sums.start()
    for m in (6, 4, 2):
        sums.step(m)
    gu_z[0].forward()
    hidden = xs_v[c].astype(f32) + sums.total()
    hidden_v[...] = hidden
    store(hidden_v, hidden_out)
    a2_v[c] = (layer_stats(hidden)[0] * norms[2:3] + norms[3:4]).astype(b16)
    a2_g = LayerGather(wires, a2_v)
    a2_g.start()
    gu_z[1].forward()
    for m in (2, 4, 6):
        a2_g.forward(m)
    gu_z[2].forward()
    for m in (1, 3, 5, 7):
        a2_g.arrived(m)
    gu_z[3].forward()
    store(a2_v, a2_out)
    for part_z in gu_z:
        part_z.finish()
    store(w_gu_v, w_gu_out)

    def feed(i, carry):
        a2 = a2_v[pl.ds(2 * i, 2)].reshape(2 * slots * rows, width)
        gu = dot(a2, w_gu_v[...].reshape(width, 2 * ffc))
        gu_v[i] = gu
        gate = gu[:, :ffc]
        zz_v[i] = (gate * jax.nn.sigmoid(gate) * gu[:, ffc:]).astype(b16)
        return carry

    lax.fori_loop(0, n // 2, feed, 0)
    store(gu_v, gu_out)
    store(zz_v, zz_out)
    sums.sent()
    a2_g.sent()
    for copy in stores:
        copy.wait()


def forward(zs, n, slots, lengths, norms, bias, tables, xs_all, w_qkv, w_out, gu_own):
    _, local, width = xs_all.shape
    rows = local // slots
    seq = rows * n
    heads = HEADS // n
    hc = heads * HEAD_DIM
    gc = gu_own.shape[-1]
    f32, b16 = jnp.float32, jnp.bfloat16
    kept = [
        ((n, local, width), b16),
        ((3, slots, n, rows, hc), b16),
        ((slots, heads, seq, seq), b16),
        ((n, slots, rows, hc), b16),
        ((local, width), f32),
        ((n, local, width), b16),
        ((zs, *gu_own.shape), b16),
        ((n // 2, 2 * local, gc), f32),
        ((n // 2, 2 * local, gc // 2), b16),
    ]
    a1, qkv, probs, ob, hidden, a2, w_gu, gu, zz = [pltpu.VMEM(*k) for k in kept]
    return pl.pallas_call(
        functools.partial(forward_kernel, zs, n),
        out_shape=[jax.ShapeDtypeStruct(*k) for k in kept],
        in_specs=[pl.BlockSpec(memory_space=pltpu.SMEM)] + [VMEM] * 3 + [HBM] * 4,
        out_specs=[HBM] * len(kept),
        scratch_shapes=[
            pltpu.VMEM(xs_all.shape, b16),
            a1,
            pltpu.VMEM(w_qkv.shape, b16),
            pltpu.VMEM(w_out.shape, b16),
            qkv,
            probs,
            ob,
            pltpu.VMEM((n, local, width), b16),
            pltpu.VMEM((n // 2, local, width), b16),
            pltpu.VMEM((n // 2 - 1, local, width), b16),
            hidden,
            a2,
            w_gu,
            gu,
            zz,
            pltpu.SemaphoreType.DMA((40,)),
            pltpu.SemaphoreType.DMA((40,)),
            pltpu.SemaphoreType.DMA((4,)),
            pltpu.SemaphoreType.DMA((len(kept),)),
        ],
        compiler_params=pltpu.CompilerParams(
            collective_id=2, has_side_effects=True, vmem_limit_bytes=60 << 20
        ),
        name="forward",
    )(lengths, norms, bias, tables, xs_all, w_qkv, w_out, gu_own)


class DepthScatter:
    def __init__(self, wires, part, relay, boxes):
        z = wires.z
        self.wires, self.part, self.relay_box, self.boxes = wires, part, relay, boxes
        self.far = wires.put(part(flip(z, 3)), relay, 1, 0)
        self.skip = wires.put(part(flip(z, 2)), boxes[1], 2, 0)
        self.near = wires.put(part(flip(z, 1)), boxes[0], 1, 0)
        self.mid = wires.put(part(flip(z, 3)), boxes[2], 3, 0)

    def start(self):
        @pl.when(self.wires.outer)
        def _():
            self.far.start()
            self.skip.start()
            self.boxes[2][...] = jnp.zeros_like(self.boxes[2])

        pl.when(self.wires.inner)(self.mid.start)
        self.near.start()

    def relay(self):
        @pl.when(self.wires.inner)
        def _():
            self.far.wait_recv()
            to = self.part(flip(self.wires.z, 2))
            to[...] = (
                to[...].astype(jnp.float32) + self.relay_box[...].astype(jnp.float32)
            ).astype(to.dtype)
            self.skip.start()

    def total(self):
        self.near.wait_recv()
        self.skip.wait_recv()
        pl.when(self.wires.inner)(self.mid.wait_recv)
        result = self.part(self.wires.z)[...].astype(jnp.float32)
        for box in self.boxes:
            result = result + box[...].astype(jnp.float32)
        return result

    def sent(self):
        self.near.wait_send()
        self.skip.wait_send()
        pl.when(self.wires.outer)(self.far.wait_send)
        pl.when(self.wires.inner)(self.mid.wait_send)


class Moves:
    def __init__(self, sems):
        self.sems, self.number, self.stores = sems, itertools.count(), []

    def load(self, src, dst):
        copy = pltpu.make_async_copy(src, dst, self.sems.at[next(self.number)])
        copy.start()
        return copy

    def store(self, src, dst):
        self.stores.append(self.load(src, dst))

    def finish(self):
        for copy in self.stores:
            copy.wait()


def pieces_of(total, number, unit):
    units = total // unit
    cuts = [units * i // number * unit for i in range(number + 1)]
    return [(a, b - a) for a, b in zip(cuts[:-1], cuts[1:])]


def middle_kernel(
    zs,
    n,
    zz,
    gu,
    dy_all,
    w_down,
    dgu_out,
    w_down_out,
    grad_down_out,
    zz_v,
    gu_v,
    dy_v,
    w_down_v,
    dgu_v,
    gd_v,
    relay_v,
    box_v,
    total_v,
    send,
    recv,
    local,
):
    f32, b16 = jnp.float32, jnp.bfloat16
    wires = Wires(send, recv)
    moves = Moves(local)
    z = wires.z
    _, block, width = w_down_v.shape
    ffc = zs * block
    tokens = n * dy_v.shape[1]
    wait_down = moves.load(w_down, w_down_v.at[z])
    wait_zz = moves.load(zz, zz_v)
    wait_dy = moves.load(dy_all, dy_v)
    wait_gu = moves.load(gu, gu_v)
    wires.greet(zs, n)
    wait_down.wait()
    down_z = [
        DepthGather(wires, lambda i, a=a, s=s: w_down_v.at[i, a : a + s])
        for a, s in pieces_of(block, 4, 16)
    ]
    for part in down_z:
        part.start()
    wait_zz.wait()
    wait_dy.wait()
    number = 4
    tile = width // number
    sums = [
        DepthScatter(
            wires,
            lambda i, a=p * tile: gd_v.at[i, :, a : a + tile],
            relay_v.at[:, p * tile : (p + 1) * tile],
            [box_v.at[j, :, p * tile : (p + 1) * tile] for j in range(3)],
        )
        for p in range(number)
    ]
    for p in range(number):
        gd = dot(
            zz_v[...].reshape(tokens, ffc),
            dy_v[:, :, p * tile : (p + 1) * tile].reshape(tokens, tile),
            ((0,), (0,)),
        )
        gd_v[:, :, p * tile : (p + 1) * tile] = gd.astype(b16).reshape(zs, block, tile)
        sums[p].start()
    for p in range(number):
        down_z[p].forward()
        sums[p].relay()
    for part in down_z:
        part.finish()
    moves.store(w_down_v, w_down_out)
    wait_gu.wait()

    def back(i, carry):
        dz = dot(
            dy_v[pl.ds(2 * i, 2)].reshape(tokens // (n // 2), width),
            w_down_v[...].reshape(ffc, width),
            ((1,), (1,)),
        )
        gu_block = gu_v[i]
        gate, up = gu_block[:, :ffc], gu_block[:, ffc:]
        sig = jax.nn.sigmoid(gate)
        dg = dz * up * sig * (1.0 + gate * (1.0 - sig))
        du = dz * gate * sig
        dgu_v[i] = jnp.concatenate([dg, du], -1).astype(b16)
        return carry

    lax.fori_loop(0, n // 2, back, 0)
    moves.store(dgu_v, dgu_out)
    for p in range(number):
        total_v[:, p * tile : (p + 1) * tile] = sums[p].total()
    moves.store(total_v, grad_down_out)
    for part in sums:
        part.sent()
    moves.finish()


def middle(zs, n, zz, gu, dy_all, w_down):
    f32, b16 = jnp.float32, jnp.bfloat16
    block, width = w_down.shape
    return pl.pallas_call(
        functools.partial(middle_kernel, zs, n),
        out_shape=[
            jax.ShapeDtypeStruct(gu.shape, b16),
            jax.ShapeDtypeStruct((zs, block, width), b16),
            jax.ShapeDtypeStruct((block, width), f32),
        ],
        in_specs=[HBM] * 4,
        out_specs=[HBM] * 3,
        scratch_shapes=[
            pltpu.VMEM(zz.shape, b16),
            pltpu.VMEM(gu.shape, f32),
            pltpu.VMEM(dy_all.shape, b16),
            pltpu.VMEM((zs, block, width), b16),
            pltpu.VMEM(gu.shape, b16),
            pltpu.VMEM((zs, block, width), b16),
            pltpu.VMEM((block, width), b16),
            pltpu.VMEM((3, block, width), b16),
            pltpu.VMEM((block, width), f32),
            pltpu.SemaphoreType.DMA((40,)),
            pltpu.SemaphoreType.DMA((40,)),
            pltpu.SemaphoreType.DMA((8,)),
        ],
        compiler_params=pltpu.CompilerParams(
            collective_id=3, has_side_effects=True, vmem_limit_bytes=60 << 20
        ),
        name="middle",
    )(zz, gu, dy_all, w_down)


def backward_kernel(
    zs,
    n,
    norms,
    tables,
    a2_all,
    dgu,
    w_gu,
    w_out,
    qkv,
    probs,
    ob,
    hidden,
    dy_all,
    ggu_out,
    grad_out_out,
    dh_out,
    dj_out,
    gains_out,
    bias_out,
    a2_v,
    dgu_v,
    w_gu_v,
    w_out_v,
    qkv_v,
    probs_v,
    ob_v,
    hidden_v,
    dy_v,
    ggu_v,
    relay_v,
    box_v,
    part,
    near,
    far,
    dh_v,
    dh_all,
    go_v,
    go_relay,
    go_box,
    go_total,
    do_v,
    dqkv_v,
    dj_v,
    send,
    recv,
    local,
):
    f32, b16 = jnp.float32, jnp.bfloat16
    wires = Wires(send, recv)
    moves = Moves(local)
    z, c = wires.z, wires.c
    _, slots, rows, hc = ob_v.shape
    width = dh_v.shape[-1]
    tokens, seq, local_rows = n * slots * rows, n * rows, slots * rows
    heads = hc // HEAD_DIM
    depth, gc = ggu_v.shape[1:]

    wait_a2 = moves.load(a2_all, a2_v)
    wait_dgu = moves.load(dgu, dgu_v)
    wait_w = moves.load(w_gu, w_gu_v)
    waits = [
        moves.load(hidden, hidden_v),
        moves.load(dy_all.at[c], dy_v),
        moves.load(w_out, w_out_v),
        moves.load(qkv, qkv_v),
        moves.load(probs, probs_v),
        moves.load(ob, ob_v),
    ]
    wires.greet(zs, n)
    wait_a2.wait()
    wait_dgu.wait()

    number = 4
    size = depth // number
    sums = [
        DepthScatter(
            wires,
            lambda i, a=p * size: ggu_v.at[i, a : a + size],
            relay_v.at[p * size : (p + 1) * size],
            [box_v.at[j, p * size : (p + 1) * size] for j in range(3)],
        )
        for p in range(number)
    ]
    step = 2 * size
    for p in range(number // 2):

        def weigh(i, carry, p=p):
            at = pl.multiple_of(i * depth + p * step, step)
            left = a2_v[:, :, pl.ds(at, step)].reshape(tokens, step)
            ggu_v[i, p * step : (p + 1) * step] = dot(
                left, dgu_v[...].reshape(tokens, gc), ((0,), (0,))
            ).astype(b16)
            return carry

        lax.fori_loop(0, zs, weigh, 0)
        sums[2 * p].start()
        sums[2 * p + 1].start()

    wait_w.wait()

    def normed(i, carry):
        part[pl.ds(2 * i, 2)] = (
            dot(dgu_v[i], w_gu_v[...].reshape(width, gc), ((1,), (1,)))
            .astype(b16)
            .reshape(2, local_rows, width)
        )
        return carry

    lax.fori_loop(0, n // 2, normed, 0)
    sums[0].relay()
    da2_sums = LayerScatter(wires, part, near, far)
    da2_sums.start()
    for m in (6, 4, 2):
        da2_sums.step(m)
    for copy in waits:
        copy.wait()
    n2, r2 = layer_stats(hidden_v[...])
    sums[1].relay()
    da2 = da2_sums.total()
    gains_out[0:1] = jnp.sum(da2 * n2, 0, keepdims=True)
    gains_out[1:2] = jnp.sum(da2, 0, keepdims=True)
    dh = dy_v[...].astype(f32) + norm_back(da2, n2, r2, norms[2:3])
    dh_v[...] = dh
    moves.store(dh_v, dh_out)
    dh_all[c] = dh.astype(b16)
    dh_g = LayerGather(wires, dh_all)
    dh_g.start()
    for m in (2, 4, 6):
        dh_g.forward(m)
    sums[2].relay()
    for m in (1, 3, 5, 7):
        dh_g.arrived(m)

    def heads_back(i, carry):
        do_v[i] = (
            dot(dh_all[i], w_out_v[...].reshape(hc, width), ((1,), (1,)))
            .astype(b16)
            .reshape(slots, rows, hc)
        )
        return carry

    lax.fori_loop(0, n, heads_back, 0)

    half = seq // 2

    def attend(s, carry):
        q, k, v = [qkv_v[i, s].reshape(seq, hc) for i in range(3)]
        do_s = do_v[:, s].reshape(seq, hc)
        dqkv_v[...] = jnp.zeros_like(dqkv_v)
        for part_q in range(2):
            keys = (part_q + 1) * half
            at = part_q * half
            query, do_q = q[at : at + half], do_s[at : at + half]
            dq = jnp.zeros((half, hc), f32)
            for h in range(heads):
                mask, mask_k = head_mask(half, hc, h), head_mask(keys, hc, h)
                do_h = jnp.where(mask, do_q, 0).astype(b16)
                low = probs_v[s, h, at : at + half, 0:keys]
                p32 = low.astype(f32)
                t = p32 * dot(do_h, v[:keys], ((1,), (1,)))
                ds = (t - p32 * jnp.sum(t, -1, keepdims=True)).astype(b16)
                dq = jnp.where(mask, dot(ds, k[:keys]), dq)
                dk = dot(ds, query, ((0,), (0,)))
                dv = dot(low, do_h, ((0,), (0,)))
                dqkv_v[1, 0:keys] += jnp.where(mask_k, dk, 0.0)
                dqkv_v[2, 0:keys] += dv
            dqkv_v[0, at : at + half] = dq
        dq, dk = dqkv_v[0] * 0.125, dqkv_v[1] * 0.125
        table = [tables[i].reshape(seq, hc) for i in range(3)]
        dj = [turn_pair(dq, table, -1.0), turn_pair(dk, table, -1.0), dqkv_v[2]]
        for i in range(3):
            dj_v[:, s, :, i * hc : (i + 1) * hc] = dj[i].astype(b16).reshape(n, rows, hc)
        return carry

    lax.fori_loop(0, slots, attend, 0)
    moves.store(dj_v, dj_out)
    sums[3].relay()
    dj_all = dj_v[...].reshape(tokens, 3 * hc).astype(f32)
    bias_out[...] = jnp.sum(dj_all, 0, keepdims=True)

    go_sums = DepthScatter(
        wires, lambda i: go_v.at[i], go_relay, [go_box.at[j] for j in range(3)]
    )
    tile = width // 4
    for p in range(4):
        go = dot(
            ob_v[...].reshape(tokens, hc),
            dh_all[:, :, p * tile : (p + 1) * tile].reshape(tokens, tile),
            ((0,), (0,)),
        )
        go_v[:, :, p * tile : (p + 1) * tile] = go.astype(b16).reshape(zs, hc // zs, tile)
    go_sums.start()
    for p in range(number):
        a = p * size
        ggu_v[z, a : a + size] = sums[p].total().astype(b16)
        moves.store(ggu_v.at[z, a : a + size], ggu_out.at[a : a + size])
    go_sums.relay()
    go_total[...] = go_sums.total()
    moves.store(go_total, grad_out_out)
    for group in (*sums, go_sums, da2_sums, dh_g):
        group.sent()
    moves.finish()


def backward(zs, n, norms, tables, a2_all, dgu, w_gu, w_out, qkv, probs, ob, hidden, dy_all):
    f32, b16 = jnp.float32, jnp.bfloat16
    _, slots, rows, hc = ob.shape
    local, width = hidden.shape
    _, depth, gc = w_gu.shape
    seq = n * rows
    wide = (n, local, width)

    def buf(like):
        return pltpu.VMEM(like.shape, like.dtype)

    return pl.pallas_call(
        functools.partial(backward_kernel, zs, n),
        out_shape=[
            jax.ShapeDtypeStruct((depth, gc), b16),
            jax.ShapeDtypeStruct((hc // zs, width), f32),
            jax.ShapeDtypeStruct((local, width), f32),
            jax.ShapeDtypeStruct((n, slots, rows, 3 * hc), b16),
            jax.ShapeDtypeStruct((2, width), f32),
            jax.ShapeDtypeStruct((1, 3 * hc), f32),
        ],
        in_specs=[VMEM] * 2 + [HBM] * 9,
        out_specs=[HBM] * 4 + [VMEM] * 2,
        scratch_shapes=[
            *[buf(v) for v in (a2_all, dgu, w_gu, w_out, qkv, probs, ob, hidden)],
            pltpu.VMEM((local, width), b16),
            pltpu.VMEM((zs, depth, gc), b16),
            pltpu.VMEM((depth, gc), b16),
            pltpu.VMEM((3, depth, gc), b16),
            pltpu.VMEM(wide, b16),
            pltpu.VMEM((n // 2, local, width), b16),
            pltpu.VMEM((n // 2 - 1, local, width), b16),
            pltpu.VMEM((local, width), f32),
            pltpu.VMEM(wide, b16),
            pltpu.VMEM((zs, hc // zs, width), b16),
            pltpu.VMEM((hc // zs, width), b16),
            pltpu.VMEM((3, hc // zs, width), b16),
            pltpu.VMEM((hc // zs, width), f32),
            pltpu.VMEM(ob.shape, b16),
            pltpu.VMEM((3, seq, hc), f32),
            pltpu.VMEM((n, slots, rows, 3 * hc), b16),
            pltpu.SemaphoreType.DMA((48,)),
            pltpu.SemaphoreType.DMA((48,)),
            pltpu.SemaphoreType.DMA((24,)),
        ],
        compiler_params=pltpu.CompilerParams(
            collective_id=4, has_side_effects=True, vmem_limit_bytes=62 << 20
        ),
        name="backward",
    )(norms, tables, a2_all, dgu, w_gu, w_out, qkv, probs, ob, hidden, dy_all)

def unpack_columns(dst, src, at, block, n, zs):
    dst[...] = jnp.concatenate(
        [
            src[i, :, at + block * j : at + block * (j + 1)]
            for j in range(zs)
            for i in range(n)
        ],
        -1,
    )


def last_kernel(
    zs,
    n,
    norms,
    gains_two,
    bias_part,
    a1_all,
    dj,
    w_qkv,
    ggu,
    zz,
    w_down,
    hidden,
    xs,
    dh,
    result_out,
    input_grad_out,
    qkv_out,
    gate_out,
    up_out,
    small_out,
    a1_v,
    dj_v,
    w_qkv_v,
    zz_v,
    w_down_v,
    hidden_v,
    xs_v,
    dh_v,
    gq_v,
    relay_v,
    box_v,
    part,
    near,
    far,
    part_y,
    near_y,
    far_y,
    gu_box,
    gq_box,
    small_v,
    small_x,
    small_r,
    small_z,
    send,
    recv,
    local,
):
    f32, b16 = jnp.float32, jnp.bfloat16
    wires = Wires(send, recv)
    moves = Moves(local)
    z, c = wires.z, wires.c
    _, local_rows, width = a1_v.shape
    tokens = n * local_rows
    _, depth, qc = gq_v.shape
    hc = qc // 3
    wrows = depth // n
    ffc = zz_v.shape[-1]
    ff_block = ffc // zs

    wait_a1 = moves.load(a1_all, a1_v)
    wait_dj = moves.load(dj, dj_v)
    wait_gu = moves.load(ggu.at[c], gu_box.at[c])
    wait_w = moves.load(w_qkv, w_qkv_v)
    wait_y = [moves.load(zz, zz_v), moves.load(w_down, w_down_v)]
    waits = [moves.load(hidden, hidden_v), moves.load(xs, xs_v), moves.load(dh, dh_v)]
    wires.greet(zs, n)
    wait_a1.wait()
    wait_dj.wait()

    number = 4
    size = depth // number
    sums = [
        DepthScatter(
            wires,
            lambda i, a=p * size: gq_v.at[i, a : a + size],
            relay_v.at[p * size : (p + 1) * size],
            [box_v.at[j, p * size : (p + 1) * size] for j in range(3)],
        )
        for p in range(number)
    ]
    step = 2 * size
    for p in range(number // 2):

        def weigh(i, carry, p=p):
            at = pl.multiple_of(i * depth + p * step, step)
            left = a1_v[:, :, pl.ds(at, step)].reshape(tokens, step)
            gq_v[i, p * step : (p + 1) * step] = dot(
                left, dj_v[...].reshape(tokens, qc), ((0,), (0,))
            ).astype(b16)
            return carry

        lax.fori_loop(0, zs, weigh, 0)
        sums[2 * p].start()
        sums[2 * p + 1].start()

    wait_w.wait()

    def normed(i, carry):
        part[pl.ds(2 * i, 2)] = (
            dot(
                dj_v[pl.ds(2 * i, 2)].reshape(2 * local_rows, qc),
                w_qkv_v[...].reshape(width, qc),
                ((1,), (1,)),
            )
            .astype(b16)
            .reshape(2, local_rows, width)
        )
        return carry

    lax.fori_loop(0, n // 2, normed, 0)
    da1_sums = LayerScatter(wires, part, near, far)
    da1_sums.start()
    for m in (6, 4, 2):
        da1_sums.step(m)
    gu_x = [wires.put(ggu.at[flip(c, m)], gu_box.at[c], 0, m) for m in range(1, n)]
    for copy in gu_x:
        copy.start()

    for copy in wait_y:
        copy.wait()

    def down(i, carry):
        part_y[pl.ds(2 * i, 2)] = (
            dot(zz_v[i], w_down_v[...].reshape(ffc, width))
            .astype(b16)
            .reshape(2, local_rows, width)
        )
        return carry

    lax.fori_loop(0, n // 2, down, 0)
    sums[0].relay()
    y_sums = LayerScatter(wires, part_y, near_y, far_y)
    y_sums.start()
    for m in (6, 4, 2):
        y_sums.step(m)

    for copy in waits:
        copy.wait()
    n1, r1 = layer_stats(xs_v[...].astype(f32))
    da1 = da1_sums.total()
    input_grad_out[...] = dh_v[...] + norm_back(da1, n1, r1, norms[0:1])
    gains = [
        jnp.sum(da1 * n1, 0, keepdims=True),
        jnp.sum(da1, 0, keepdims=True),
        gains_two[0:1],
        gains_two[1:2],
    ]
    sums[1].relay()
    chips = n // 2
    lane_half = lax.broadcasted_iota(jnp.int32, (1, 2 * HEAD_DIM), 1) // HEAD_DIM
    lanes = 2 * HEAD_DIM
    for j in range(zs):
        for chip in range(chips):
            k = j * chips + chip
            for r in range(4):
                small_v[j, chip, r : r + 1] = gains[r][:, k * lanes : (k + 1) * lanes]
            small_v[j, chip, 7:8] = jnp.zeros((1, lanes), f32)
    for i in range(3):
        for j in range(zs):
            at = i * hc + j * HEAD_DIM
            piece = bias_part[:, at : at + HEAD_DIM]
            both = jnp.concatenate([piece, piece], -1)
            for chip in range(chips):
                tile = (i * zs + j) * chips + chip
                pair, row = tile // 3, tile % 3
                small_v[pair // chips, pair % chips, 4 + row : 5 + row] = jnp.where(
                    (lane_half == c % 2) & (c // 2 == chip), both, 0.0
                )
    small_v_x = [
        wires.put(small_v.at[:, flip(c, m) // 2], small_x.at[m], 0, m) for m in range(1, n)
    ]
    for copy in small_v_x:
        copy.start()
    for copy in gu_x:
        copy.wait_recv()
    wait_gu.wait()
    unpack_columns(gate_out, gu_box, 0, ff_block, n, zs)
    unpack_columns(up_out, gu_box, ffc, ff_block, n, zs)
    small_sum = small_v[:, c // 2]
    for m in range(1, n):
        small_v_x[m - 1].wait_recv()
        small_sum = small_sum + small_x[m]
    small_r[...] = small_sum
    small_z_x = [wires.put(small_r.at[flip(z, m)], small_z.at[m], m, 0) for m in range(1, zs)]
    for copy in small_z_x:
        copy.start()
    sums[2].relay()
    result_out[...] = (hidden_v[...] + y_sums.total()).astype(b16)
    small_sum = small_r[z]
    for m in range(1, zs):
        small_z_x[m - 1].wait_recv()
        small_sum = small_sum + small_z[m]
    small_out[...] = small_sum
    sums[3].relay()
    for p in range(number):
        a = p * size
        gq_v[z, a : a + size] = sums[p].total().astype(b16)
    gq_x = [
        wires.put(
            gq_v.at[z, pl.ds(pl.multiple_of(flip(c, m) * wrows, wrows), wrows)],
            gq_box.at[c],
            0,
            m,
        )
        for m in range(1, n)
    ]
    for copy in gq_x:
        copy.start()
    gq_box[c] = gq_v[z, pl.ds(pl.multiple_of(c * wrows, wrows), wrows)]
    for group in (*sums, da1_sums, y_sums):
        group.sent()
    for copy in (*gu_x, *small_v_x, *small_z_x):
        copy.wait_send()
    for copy in gq_x:
        copy.wait()
    for i in range(3):
        unpack_columns(
            qkv_out.at[:, i * width : (i + 1) * width], gq_box, i * hc, HEAD_DIM, n, zs
        )


def last(
    zs, n, norms, gains_two, bias_part, a1_all, dj, w_qkv, ggu, zz, w_down, hidden, xs, dh
):
    f32, b16 = jnp.float32, jnp.bfloat16
    local, width = hidden.shape
    _, wrows, gc = ggu.shape
    qc = dj.shape[-1]
    depth = n * wrows
    wide = (n, local, width)

    def buf(like):
        return pltpu.VMEM(like.shape, like.dtype)

    return pl.pallas_call(
        functools.partial(last_kernel, zs, n),
        out_shape=[
            jax.ShapeDtypeStruct((local, width), b16),
            jax.ShapeDtypeStruct((local, width), f32),
            jax.ShapeDtypeStruct((wrows, n * qc), b16),
            jax.ShapeDtypeStruct((wrows, n * gc // 2), b16),
            jax.ShapeDtypeStruct((wrows, n * gc // 2), b16),
            jax.ShapeDtypeStruct((8, 2 * HEAD_DIM), f32),
        ],
        in_specs=[VMEM] * 3 + [HBM] * 9,
        out_specs=[VMEM] * 6,
        scratch_shapes=[
            *[buf(v) for v in (a1_all, dj, w_qkv, zz, w_down, hidden, xs, dh)],
            pltpu.VMEM((zs, depth, qc), b16),
            pltpu.VMEM((depth, qc), b16),
            pltpu.VMEM((3, depth, qc), b16),
            pltpu.VMEM(wide, b16),
            pltpu.VMEM((n // 2, local, width), b16),
            pltpu.VMEM((n // 2 - 1, local, width), b16),
            pltpu.VMEM(wide, b16),
            pltpu.VMEM((n // 2, local, width), b16),
            pltpu.VMEM((n // 2 - 1, local, width), b16),
            pltpu.VMEM(ggu.shape, b16),
            pltpu.VMEM((n, wrows, qc), b16),
            pltpu.VMEM((zs, n // 2, 8, 2 * HEAD_DIM), f32),
            pltpu.VMEM((n, zs, 8, 2 * HEAD_DIM), f32),
            pltpu.VMEM((zs, 8, 2 * HEAD_DIM), f32),
            pltpu.VMEM((zs, 8, 2 * HEAD_DIM), f32),
            pltpu.SemaphoreType.DMA((64,)),
            pltpu.SemaphoreType.DMA((64,)),
            pltpu.SemaphoreType.DMA((16,)),
        ],
        compiler_params=pltpu.CompilerParams(
            collective_id=5, has_side_effects=True, vmem_limit_bytes=60 << 20
        ),
        name="last",
    )(norms, gains_two, bias_part, a1_all, dj, w_qkv, ggu, zz, w_down, hidden, xs, dh)


def tensor_shards(
    inputs,
    lengths,
    w_qkv,
    b_qkv,
    w_out,
    w_gate,
    w_up,
    w_down,
    gain_one,
    shift_one,
    gain_two,
    shift_two,
    cotangent,
):
    rows, slots, width = inputs.shape
    f32, b16 = jnp.float32, jnp.bfloat16
    zs, n = lax.axis_size("dp"), lax.axis_size("ctx")
    me = lax.axis_index("ctx")
    local = rows * slots
    tokens = local * n
    seq = rows * n
    wrows = w_qkv.shape[0]
    ff_block = w_down.shape[0]
    heads = HEADS // n
    hc = heads * HEAD_DIM
    ffc = ff_block * zs

    def dot(a, b, dims):
        return lax.dot_general(a, b, (dims, ((), ())), preferred_element_type=f32)

    def local_tokens(v):
        return jnp.transpose(v, (1, 0, 2)).reshape(local, width)

    def back_tokens(v):
        return jnp.transpose(v.reshape(slots, rows, width), (1, 0, 2))

    def exchange(v):
        return lax.all_to_all(v, "ctx", 0, 0, tiled=True)

    def gather_ctx(v):
        return lax.all_gather(v, "ctx", axis=0, tiled=True)

    def scatter_ctx(v):
        return lax.psum_scatter(v.astype(b16), "ctx", scatter_dimension=0, tiled=True).astype(f32)

    def gather_dp(v):
        return lax.all_gather(v, "dp", axis=0, tiled=True)

    def scatter_dp(v):
        return lax.psum_scatter(v.astype(b16), "dp", scatter_dimension=0, tiled=True)

    xs = local_tokens(inputs)
    dy = local_tokens(cotangent)
    small = jnp.concatenate([b_qkv, gain_one, shift_one, gain_two, shift_two]).astype(f32)
    small = jnp.pad(small, (0, 1024 - small.shape[0])).reshape(8, 128)
    w_qkv_c, w_out_c, gu_own, a_all, dy_all, small = spread(
        zs, n, w_qkv, w_gate, w_up, w_out, xs, dy, small
    )
    small = small.reshape(zs * n, 1024)
    dy_all = dy_all.reshape(tokens, width)
    nb = b_qkv.shape[0]
    bias_full = small[:, :nb].reshape(3, zs, n, HEAD_DIM)
    bias_own = lax.dynamic_index_in_dim(bias_full, me, 2, keepdims=False).reshape(1, 3 * hc)
    g1, s1, g2, s2 = [
        small[:, nb + i * wrows : nb + (i + 1) * wrows].reshape(1, width) for i in range(4)
    ]


    counter = jnp.arange(ROTARY // 2, dtype=f32)
    angles = jnp.arange(seq, dtype=f32)[:, None] * (10000.0 ** (-2.0 * counter / ROTARY))[None, :]
    cos_t, sin_t = jnp.cos(angles), jnp.sin(angles)
    zero = jnp.zeros_like(sin_t)
    rest = jnp.ones((seq, HEAD_DIM - ROTARY), f32)
    table_c = jnp.tile(jnp.concatenate([cos_t, cos_t, rest], -1), (1, heads))
    table_l = jnp.tile(jnp.concatenate([-sin_t, zero, 0 * rest], -1), (1, heads))
    table_r = jnp.tile(jnp.concatenate([zero, sin_t, 0 * rest], -1), (1, heads))

    def by_slot(v):
        return v.reshape(n, slots, rows, v.shape[-1]).transpose(1, 0, 2, 3).reshape(
            slots, seq, v.shape[-1]
        )

    def by_device(v):
        return v.reshape(slots, n, rows, v.shape[-1]).transpose(1, 0, 2, 3).reshape(
            tokens, v.shape[-1]
        )

    def turn(v, sign):
        half = ROTARY // 2
        return (
            v * table_c
            + sign * jnp.roll(v, -half, -1) * table_l
            + sign * jnp.roll(v, half, -1) * table_r
        )

    tables = jnp.stack([table_c, table_l, table_r]).reshape(3, n, rows, hc)
    norms = jnp.concatenate([g1, s1, g2, s2])
    a1_all, qkv, probs, ob, hidden, a2_all, w_gu_c, gu, z = forward(
        zs, n, slots, lengths, norms, bias_own, tables, a_all, w_qkv_c, w_out_c,
        gu_own.reshape(n * wrows, 2 * ffc),
    )
    dgu, w_down_c, grad_down = middle(zs, n, z, gu, dy_all.reshape(n, local, width), w_down)
    ggu, grad_out, dh, dj, gains_two, bias_part = backward(
        zs, n, norms, tables, a2_all, dgu, w_gu_c, w_out_c, qkv, probs, ob, hidden,
        dy_all.reshape(n, local, width),
    )
    result, input_grad, grad_qkv, grad_gate, grad_up, sums = last(
        zs, n, norms, gains_two, bias_part, a1_all, dj.reshape(n, local, 3 * hc), w_qkv_c,
        ggu.reshape(n, wrows, 2 * ffc), z, w_down_c, hidden, xs, dh,
    )
    mine = lax.dynamic_slice_in_dim(sums[:4], me % 2 * wrows, wrows, 1)
    grad_bias = lax.dynamic_slice_in_dim(sums[4:7].reshape(2 * nb), me % 2 * nb, nb)
    return (
        back_tokens(result),
        back_tokens(input_grad),
        grad_qkv.astype(f32),
        grad_bias,
        grad_out,
        grad_gate.astype(f32),
        grad_up.astype(f32),
        grad_down,
        mine[0],
        mine[1],
        mine[2],
        mine[3],
    )


def solution(mesh):
    zs, n = mesh.shape["dp"], mesh.shape["ctx"]
    shards = tensor_shards if (zs, n) == (4, 8) and HEADS == 32 else gathered_shards

    placed = (
        P("ctx", "dp", None),
        P("dp", None),
        P(("dp", "ctx"), None),
        P(("dp", "ctx")),
        P(("dp", "ctx"), None),
        P(("dp", "ctx"), None),
        P(("dp", "ctx"), None),
        P(("dp", "ctx"), None),
        P(("dp", "ctx")),
        P(("dp", "ctx")),
        P(("dp", "ctx")),
        P(("dp", "ctx")),
        P("ctx", "dp", None),
    )
    return jax.shard_map(
        shards,
        mesh=mesh,
        in_specs=placed,
        out_specs=(
            P("ctx", "dp", None),
            P("ctx", "dp", None),
            P(("dp", "ctx"), None),
            P(("dp", "ctx")),
            P(("dp", "ctx"), None),
            P(("dp", "ctx"), None),
            P(("dp", "ctx"), None),
            P(("dp", "ctx"), None),
            P(("dp", "ctx")),
            P(("dp", "ctx")),
            P(("dp", "ctx")),
            P(("dp", "ctx")),
        ),
        check_vma=False,
    )
```

```python
import functools
import itertools
import math

import jax
import jax.numpy as jnp
import numpy as np
from jax import lax
from jax.experimental import pallas as pl
from jax.experimental.pallas import tpu as pltpu
from jax.sharding import PartitionSpec as P

HEADS = 32
HEAD_DIM = 64
ROTARY = 16


epsilon = 1e-05
masked_value = -1e30


def layer_stats(values):
    row_mean = jnp.mean(values, -1, keepdims=True)
    centred = values - row_mean
    inverse = lax.rsqrt(jnp.mean(centred * centred, -1, keepdims=True) + epsilon)
    return (centred * inverse, inverse)


def norm_back(grad_normed, scaled, inverse, gain_vec):
    grad_hat = grad_normed * gain_vec
    return inverse * (
        grad_hat
        - jnp.mean(grad_hat, -1, keepdims=True)
        - scaled * jnp.mean(grad_hat * scaled, -1, keepdims=True)
    )


def rotary_tables(positions):
    counter = jnp.arange(ROTARY // 2, dtype=jnp.float32)
    frequency = 10000.0 ** (-2.0 * counter / ROTARY)
    angles = positions.astype(jnp.float32)[:, None] * frequency[None, :]
    return (jnp.cos(angles)[:, None, None, :], jnp.sin(angles)[:, None, None, :])


def rotate(values, cos_table, sin_table):
    half_dims = ROTARY // 2
    first_half = values[..., :half_dims]
    second_half = values[..., half_dims:ROTARY]
    return jnp.concatenate(
        [
            first_half * cos_table - second_half * sin_table,
            second_half * cos_table + first_half * sin_table,
            values[..., ROTARY:],
        ],
        -1,
    )


def over_blocks(step_fn, running, gathered):
    total_rows = gathered.shape[0]
    tile_rows = math.gcd(total_rows, 512)

    def visit_block(number, current):
        block_start = number * tile_rows
        block_part = lax.dynamic_slice_in_dim(gathered, block_start, tile_rows, 0)
        return step_fn(current, block_part, block_start)

    return lax.fori_loop(0, total_rows // tile_rows, visit_block, running)


def gathered_shards(
    inputs,
    lengths,
    w_qkv,
    b_qkv,
    w_out,
    w_gate,
    w_up,
    w_down,
    gain_one,
    shift_one,
    gain_two,
    shift_two,
    cotangent,
):
    local_rows, slot_count, width = inputs.shape
    positions = lax.axis_index("ctx") * local_rows + jnp.arange(local_rows, dtype=jnp.int32)
    live_rows = positions[:, None] < lengths[0][None, :]
    live_heads = jnp.transpose(live_rows)[:, None, :, None]
    cos_table, sin_table = rotary_tables(positions)

    def allowed_mask(offset, count):
        key_pos = offset + jnp.arange(count, dtype=jnp.int32)
        causal = key_pos[None, :] <= positions[:, None]
        return causal[None, None, :, :] & live_heads

    def split_heads(block_part):
        count = block_part.shape[0]
        key_part = block_part[:, :, 0].reshape(count, slot_count, HEADS, HEAD_DIM)
        value_part = block_part[:, :, 1].reshape(count, slot_count, HEADS, HEAD_DIM)
        return (key_part, value_part)

    attn_full = (
        lax.all_gather(w_qkv, ("dp", "ctx"), axis=0, tiled=True),
        lax.all_gather(b_qkv, ("dp", "ctx"), axis=0, tiled=True),
        lax.all_gather(w_out, ("dp", "ctx"), axis=0, tiled=True),
        lax.all_gather(gain_one, ("dp", "ctx"), axis=0, tiled=True),
        lax.all_gather(shift_one, ("dp", "ctx"), axis=0, tiled=True),
    )
    qkv_full, bias_full, out_full, gain_one_full, shift_one_full = attn_full
    source = inputs.astype(jnp.float32)
    scaled_one, inverse_one = layer_stats(source)
    normed_one = (
        scaled_one * gain_one_full.astype(jnp.float32) + shift_one_full.astype(jnp.float32)
    ).astype(jnp.bfloat16)
    joined = jnp.einsum(
        "rsd,de->rse", normed_one, qkv_full, preferred_element_type=jnp.float32
    ) + bias_full.astype(jnp.float32)
    query_pre = joined[..., :width].reshape(local_rows, slot_count, HEADS, HEAD_DIM)
    key_pre = joined[..., width : 2 * width].reshape(local_rows, slot_count, HEADS, HEAD_DIM)
    queries = rotate(query_pre, cos_table, sin_table).astype(jnp.bfloat16)
    keys_rot = rotate(key_pre, cos_table, sin_table).reshape(local_rows, slot_count, width)
    key_value = jnp.stack([keys_rot, joined[..., 2 * width :]], 2).astype(jnp.bfloat16)
    block_part = lax.all_gather(key_value, "ctx", axis=0, tiled=True)
    run_peak = jnp.full((slot_count, HEADS, local_rows), masked_value, jnp.float32)
    key_part, value_part = split_heads(block_part)
    scores = (
        jnp.einsum("qshd,kshd->shqk", queries, key_part, preferred_element_type=jnp.float32) * 0.125
    )
    allowed = allowed_mask(jnp.int32(0), block_part.shape[0])
    masked = jnp.where(allowed, scores, masked_value)
    new_peak = jnp.maximum(run_peak, jnp.max(masked, -1))
    weights = jnp.where(allowed, jnp.exp(masked - new_peak[..., None]), 0.0)
    new_sum = jnp.sum(weights, -1)
    new_acc = jnp.einsum(
        "shqk,kshd->shqd",
        weights.astype(jnp.bfloat16),
        value_part,
        preferred_element_type=jnp.float32,
    )
    final_sum = jnp.maximum(new_sum, 1.0)
    log_sum = new_peak + jnp.log(final_sum)
    attended = jnp.transpose(new_acc / final_sum[..., None], (2, 0, 1, 3))
    attended_low = attended.reshape(local_rows, slot_count, width).astype(jnp.bfloat16)
    hidden_in = source + jnp.einsum(
        "rsd,de->rse", attended_low, out_full, preferred_element_type=jnp.float32
    )
    mlp_full = (
        lax.all_gather(w_gate, ("dp", "ctx"), axis=0, tiled=True),
        lax.all_gather(w_up, ("dp", "ctx"), axis=0, tiled=True),
        lax.all_gather(w_down, ("dp", "ctx"), axis=0, tiled=True),
        lax.all_gather(gain_two, ("dp", "ctx"), axis=0, tiled=True),
        lax.all_gather(shift_two, ("dp", "ctx"), axis=0, tiled=True),
    )
    gate_full, up_full, down_full, gain_two_full, shift_two_full = mlp_full
    scaled_two, inverse_two = layer_stats(hidden_in)
    normed_two = (
        scaled_two * gain_two_full.astype(jnp.float32) + shift_two_full.astype(jnp.float32)
    ).astype(jnp.bfloat16)
    gate = jnp.einsum("rsd,df->rsf", normed_two, gate_full, preferred_element_type=jnp.float32)
    upward = jnp.einsum("rsd,df->rsf", normed_two, up_full, preferred_element_type=jnp.float32)
    sigmoid = jax.nn.sigmoid(gate)
    product = (gate * sigmoid * upward).astype(jnp.bfloat16)
    result = hidden_in + jnp.einsum(
        "rsf,fd->rsd", product, down_full, preferred_element_type=jnp.float32
    )
    gate_back, up_back, down_back, gain_two_back = (
        lax.all_gather(w_gate, ("dp", "ctx"), axis=0, tiled=True),
        lax.all_gather(w_up, ("dp", "ctx"), axis=0, tiled=True),
        lax.all_gather(w_down, ("dp", "ctx"), axis=0, tiled=True),
        lax.all_gather(gain_two, ("dp", "ctx"), axis=0, tiled=True),
    )
    grad_down = jnp.einsum("rsf,rsd->fd", product, cotangent, preferred_element_type=jnp.float32)
    grad_product = jnp.einsum(
        "rsd,fd->rsf", cotangent, down_back, preferred_element_type=jnp.float32
    )
    grad_gate_act = (grad_product * upward * sigmoid * (1.0 + gate * (1.0 - sigmoid))).astype(
        jnp.bfloat16
    )
    grad_up_act = (grad_product * gate * sigmoid).astype(jnp.bfloat16)
    grad_gate = jnp.einsum(
        "rsd,rsf->df", normed_two, grad_gate_act, preferred_element_type=jnp.float32
    )
    grad_up = jnp.einsum("rsd,rsf->df", normed_two, grad_up_act, preferred_element_type=jnp.float32)
    grad_normed_two = jnp.einsum(
        "rsf,df->rsd", grad_gate_act, gate_back, preferred_element_type=jnp.float32
    ) + jnp.einsum("rsf,df->rsd", grad_up_act, up_back, preferred_element_type=jnp.float32)
    grad_gain_two = jnp.sum(grad_normed_two * scaled_two, (0, 1))
    grad_shift_two = jnp.sum(grad_normed_two, (0, 1))
    grad_hidden = cotangent.astype(jnp.float32) + norm_back(
        grad_normed_two, scaled_two, inverse_two, gain_two_back.astype(jnp.float32)
    )
    mlp_sums = (
        lax.psum_scatter(grad_gate, ("dp", "ctx"), scatter_dimension=0, tiled=True),
        lax.psum_scatter(grad_up, ("dp", "ctx"), scatter_dimension=0, tiled=True),
        lax.psum_scatter(grad_down, ("dp", "ctx"), scatter_dimension=0, tiled=True),
        lax.psum_scatter(grad_gain_two, ("dp", "ctx"), scatter_dimension=0, tiled=True),
        lax.psum_scatter(grad_shift_two, ("dp", "ctx"), scatter_dimension=0, tiled=True),
    )
    qkv_back, out_back, gain_one_back = (
        lax.all_gather(w_qkv, ("dp", "ctx"), axis=0, tiled=True),
        lax.all_gather(w_out, ("dp", "ctx"), axis=0, tiled=True),
        lax.all_gather(gain_one, ("dp", "ctx"), axis=0, tiled=True),
    )
    hidden_low = grad_hidden.astype(jnp.bfloat16)
    grad_out = jnp.einsum(
        "rsd,rse->de", attended_low, hidden_low, preferred_element_type=jnp.float32
    )
    grad_attended = jnp.einsum(
        "rse,de->rsd", hidden_low, out_back, preferred_element_type=jnp.float32
    )
    grad_heads = grad_attended.reshape(local_rows, slot_count, HEADS, HEAD_DIM).astype(jnp.bfloat16)
    delta = jnp.transpose(jnp.sum(grad_heads.astype(jnp.float32) * attended, -1), (1, 2, 0))
    key_value_all = lax.all_gather(key_value, "ctx", axis=0, tiled=True)

    def grad_parts(block_part, offset):
        key_part, value_part = split_heads(block_part)
        scores = (
            jnp.einsum("qshd,kshd->shqk", queries, key_part, preferred_element_type=jnp.float32)
            * 0.125
        )
        allowed = allowed_mask(offset, block_part.shape[0])
        probs = jnp.where(allowed, jnp.exp(scores - log_sum[..., None]), 0.0)
        grad_prob = jnp.einsum(
            "qshd,kshd->shqk", grad_heads, value_part, preferred_element_type=jnp.float32
        )
        grad_score = (probs * (grad_prob - delta[..., None])).astype(jnp.bfloat16)
        return (key_part, probs, grad_score)

    def query_step(running, block_part, offset):
        key_part, probs, grad_score = grad_parts(block_part, offset)
        return running + jnp.einsum(
            "shqk,kshd->shqd", grad_score, key_part, preferred_element_type=jnp.float32
        )

    grad_query = (
        over_blocks(
            query_step,
            jnp.zeros((slot_count, HEADS, local_rows, HEAD_DIM), jnp.float32),
            key_value_all,
        )
        * 0.125
    )
    count = local_rows * lax.axis_size("ctx")
    tile_rows = math.gcd(count, 512)

    def one_block(number):
        block_start = number * tile_rows
        block_part = lax.dynamic_slice_in_dim(key_value_all, block_start, tile_rows, 0)
        key_part, probs, grad_score = grad_parts(block_part, block_start)
        grad_key = (
            jnp.einsum("shqk,qshd->kshd", grad_score, queries, preferred_element_type=jnp.float32)
            * 0.125
        )
        grad_value = jnp.einsum(
            "shqk,qshd->kshd",
            probs.astype(jnp.bfloat16),
            grad_heads,
            preferred_element_type=jnp.float32,
        )
        return jnp.stack(
            [
                grad_key.reshape(tile_rows, slot_count, width),
                grad_value.reshape(tile_rows, slot_count, width),
            ],
            2,
        )

    blocks = lax.map(one_block, jnp.arange(count // tile_rows, dtype=jnp.int32))
    grad_key_value = lax.psum_scatter(
        blocks.reshape(count, slot_count, 2, width).astype(jnp.bfloat16),
        "ctx",
        scatter_dimension=0,
        tiled=True,
    ).astype(jnp.float32)
    grad_query_pre = rotate(jnp.transpose(grad_query, (2, 0, 1, 3)), cos_table, -sin_table)
    grad_key_pre = rotate(
        grad_key_value[:, :, 0].reshape(local_rows, slot_count, HEADS, HEAD_DIM),
        cos_table,
        -sin_table,
    )
    grad_joined = jnp.concatenate(
        [
            grad_query_pre.reshape(local_rows, slot_count, width),
            grad_key_pre.reshape(local_rows, slot_count, width),
            grad_key_value[:, :, 1],
        ],
        -1,
    ).astype(jnp.bfloat16)
    grad_qkv = jnp.einsum(
        "rsd,rse->de", normed_one, grad_joined, preferred_element_type=jnp.float32
    )
    grad_bias = jnp.sum(grad_joined.astype(jnp.float32), (0, 1))
    grad_normed_one = jnp.einsum(
        "rse,de->rsd", grad_joined, qkv_back, preferred_element_type=jnp.float32
    )
    grad_gain_one = jnp.sum(grad_normed_one * scaled_one, (0, 1))
    grad_shift_one = jnp.sum(grad_normed_one, (0, 1))
    input_grad = grad_hidden + norm_back(
        grad_normed_one, scaled_one, inverse_one, gain_one_back.astype(jnp.float32)
    )
    attn_sums = (
        lax.psum_scatter(grad_qkv, ("dp", "ctx"), scatter_dimension=0, tiled=True),
        lax.psum_scatter(grad_bias, ("dp", "ctx"), scatter_dimension=0, tiled=True),
        lax.psum_scatter(grad_out, ("dp", "ctx"), scatter_dimension=0, tiled=True),
        lax.psum_scatter(grad_gain_one, ("dp", "ctx"), scatter_dimension=0, tiled=True),
        lax.psum_scatter(grad_shift_one, ("dp", "ctx"), scatter_dimension=0, tiled=True),
    )
    return (
        result.astype(jnp.bfloat16),
        input_grad,
        attn_sums[0],
        attn_sums[1],
        attn_sums[2],
        mlp_sums[0],
        mlp_sums[1],
        mlp_sums[2],
        attn_sums[3],
        attn_sums[4],
        mlp_sums[3],
        mlp_sums[4],
    )


MESH = pl.DeviceIdType.MESH
HBM = pl.BlockSpec(memory_space=pltpu.HBM)
VMEM = pl.BlockSpec(memory_space=pltpu.VMEM)
VMEM_LIMIT = 60 << 20


def flip(index, mask):
    for bit in (1, 2, 4):
        if mask & bit:
            index = index + bit - 2 * bit * ((index // bit) % 2)
    return index


class Wires:
    def __init__(self, send, recv):
        self.send, self.recv = send, recv
        self.z, self.c = lax.axis_index("dp"), lax.axis_index("ctx")
        self.inner = (self.z == 1) | (self.z == 2)
        self.outer = (self.z == 0) | (self.z == 3)
        self.number = itertools.count()

    def put(self, src, dst, z_mask, c_mask):
        return self.put_to(src, dst, flip(self.z, z_mask), flip(self.c, c_mask))

    def put_to(self, src, dst, z, c):
        i = next(self.number)
        return pltpu.make_async_remote_copy(
            src_ref=src,
            dst_ref=dst,
            send_sem=self.send.at[i],
            recv_sem=self.recv.at[i],
            device_id=(z, c),
            device_id_type=MESH,
        )

    def greet(self, zs, n):
        barrier = pltpu.get_barrier_semaphore()
        for m in range(1, zs):
            pl.semaphore_signal(
                barrier, inc=1, device_id=(flip(self.z, m), self.c), device_id_type=MESH
            )
        for m in range(1, n):
            pl.semaphore_signal(
                barrier, inc=1, device_id=(self.z, flip(self.c, m)), device_id_type=MESH
            )
        pl.semaphore_wait(barrier, zs + n - 2)


class DepthGather:
    def __init__(self, wires, part):
        z = wires.z
        self.wires = wires
        self.near = wires.put(part(z), part(z), 1, 0)
        self.skip = wires.put(part(z), part(z), 2, 0)
        self.mid = wires.put(part(z), part(z), 3, 0)
        far = flip(z, 2)
        self.on = wires.put(part(far), part(far), 1, 0)

    @staticmethod
    def start(parts):
        for part in parts:
            part.skip.start()
        for part in parts:
            pl.when(part.wires.inner)(part.mid.start)
        for part in parts:
            part.near.start()

    def forward(self):
        @pl.when(self.wires.inner)
        def _():
            self.skip.wait_recv()
            self.on.start()

    def finish(self):
        self.near.wait_recv()
        self.near.wait_send()
        self.skip.wait_send()

        @pl.when(self.wires.inner)
        def _():
            self.mid.wait_recv()
            self.mid.wait_send()
            self.on.wait_send()

        @pl.when(self.wires.outer)
        def _():
            self.skip.wait_recv()
            self.on.wait_recv()


class LayerGather:
    def __init__(self, wires, buf, source=None):
        c = wires.c
        mine = buf.at[c] if source is None else source
        self.direct = {m: wires.put(mine, buf.at[c], 0, m) for m in (2, 4, 6, 1)}
        self.on = {
            m: wires.put(buf.at[flip(c, m)], buf.at[flip(c, m)], 0, 1) for m in (2, 4, 6)
        }

    def start(self):
        for m in (2, 4, 6, 1):
            self.direct[m].start()

    def forward(self, m):
        self.direct[m].wait_recv()
        self.on[m].start()

    def arrived(self, m):
        (self.direct[1] if m == 1 else self.on[m - 1]).wait_recv()

    def sent(self):
        for copy in (*self.direct.values(), *self.on.values()):
            copy.wait_send()


def pack_columns(dst, refs, n, zs):
    for i in range(n):
        pieces = []
        for ref, block in refs:
            pieces += [ref[:, block * (j * n + i) : block * (j * n + i + 1)] for j in range(zs)]
        dst[i] = jnp.concatenate(pieces, -1)


def spread_kernel(
    zs,
    n,
    w_qkv,
    w_gate,
    w_up,
    w_out,
    xs,
    small,
    qkv_all,
    out_all,
    gu_own,
    xs_all,
    small_all,
    qkv_send,
    gu_send,
    send,
    recv,
    local,
):
    wires = Wires(send, recv)
    z, c = wires.z, wires.c
    hc = HEAD_DIM * HEADS // n
    width = HEADS * HEAD_DIM
    ff_block = w_gate.shape[1] // (zs * n)

    own = [
        pltpu.make_async_copy(w_out, out_all.at[z], local.at[0]),
        pltpu.make_async_copy(qkv_send.at[c], qkv_all.at[z, c], local.at[1]),
        pltpu.make_async_copy(gu_send.at[c], gu_own.at[c], local.at[2]),
        pltpu.make_async_copy(xs, xs_all.at[c], local.at[3]),
        pltpu.make_async_copy(small, small_all.at[z, c], local.at[4]),
    ]
    for i in (0, 3, 4):
        own[i].start()
    pack_columns(
        qkv_send, [(w_qkv.at[:, i * width : (i + 1) * width], HEAD_DIM) for i in range(3)], n, zs
    )
    own[1].start()
    wires.greet(zs, n)
    for i in (0, 4):
        own[i].wait()

    out_z = DepthGather(wires, lambda i: out_all.at[i])
    DepthGather.start([out_z])
    qkv_x = [
        wires.put(qkv_send.at[flip(c, m)], qkv_all.at[z, c], 0, m) for m in range(1, n)
    ]
    for copy in qkv_x:
        copy.start()
    small_z = [wires.put(small_all.at[z, c], small_all.at[z, c], m, 0) for m in range(1, zs)]
    for copy in small_z:
        copy.start()
    xs_g = LayerGather(wires, xs_all, xs)
    xs_g.start()
    pack_columns(gu_send, [(w_gate, ff_block), (w_up, ff_block)], n, zs)
    own[2].start()
    for copy in small_z:
        copy.wait_recv()
    small_x = [
        wires.put(small_all.at[:, c], small_all.at[:, c], 0, m) for m in range(1, n)
    ]
    for copy in small_x:
        copy.start()
    own[1].wait()
    for copy in qkv_x:
        copy.wait_recv()
    qkv_z = [
        DepthGather(wires, lambda i, a=a, s=s: qkv_all.at[i, a : a + s])
        for a, s in pieces_of(n, 4, 1)
    ]
    DepthGather.start(qkv_z)
    out_z.forward()
    gu_x = [wires.put(gu_send.at[flip(c, m)], gu_own.at[c], 0, m) for m in range(1, n)]
    for copy in gu_x:
        copy.start()
    for m in (2, 4, 6):
        xs_g.forward(m)
    for part in qkv_z:
        part.forward()

    for i in (2, 3):
        own[i].wait()
    for m in (1, 3, 5, 7):
        xs_g.arrived(m)
    xs_g.sent()
    for copy in small_z:
        copy.wait_send()
    for copy in qkv_x:
        copy.wait_send()
    for copy in (*small_x, *gu_x):
        copy.wait()
    for part in (out_z, *qkv_z):
        part.finish()


def spread(zs, n, w_qkv, w_gate, w_up, w_out, xs, small):
    wrows, width = w_out.shape
    qc, gc = w_qkv.shape[1] // n, 2 * w_gate.shape[1] // n
    b16 = jnp.bfloat16
    return pl.pallas_call(
        functools.partial(spread_kernel, zs, n),
        out_shape=[
            jax.ShapeDtypeStruct((zs, n, wrows, qc), b16),
            jax.ShapeDtypeStruct((zs, wrows, width), b16),
            jax.ShapeDtypeStruct((n, wrows, gc), b16),
            jax.ShapeDtypeStruct((n, *xs.shape), b16),
            jax.ShapeDtypeStruct((zs, n, *small.shape), small.dtype),
        ],
        in_specs=[VMEM, VMEM, VMEM, HBM, HBM, HBM],
        out_specs=[HBM] * 5,
        scratch_shapes=[
            pltpu.VMEM((n, wrows, qc), b16),
            pltpu.VMEM((n, wrows, gc), b16),
            pltpu.SemaphoreType.DMA((64,)),
            pltpu.SemaphoreType.DMA((64,)),
            pltpu.SemaphoreType.DMA((5,)),
        ],
        compiler_params=pltpu.CompilerParams(
            collective_id=1, has_side_effects=True, vmem_limit_bytes=32 << 20
        ),
        name="spread",
    )(w_qkv, w_gate, w_up, w_out, xs, small)


class LayerScatter:
    def __init__(self, wires, part, near, far):
        c = wires.c
        self.c, self.part, self.near, self.far = c, part, near, far
        self.pair = {
            m: wires.put(part.at[flip(c, m + 1)], near.at[m // 2], 0, 1) for m in (6, 4, 2, 0)
        }
        self.chips = {
            m: wires.put(part.at[flip(c, m)], far.at[m // 2 - 1], 0, m) for m in (6, 4, 2)
        }

    def start(self):
        for copy in self.pair.values():
            copy.start()

    def step(self, m):
        self.pair[m].wait_recv()
        to = flip(self.c, m)
        self.part[to] = (
            self.part[to].astype(jnp.float32) + self.near[m // 2].astype(jnp.float32)
        ).astype(self.part.dtype)
        self.chips[m].start()

    def total(self):
        self.pair[0].wait_recv()
        result = self.part[self.c].astype(jnp.float32) + self.near[0].astype(jnp.float32)
        for m in (2, 4, 6):
            self.chips[m].wait_recv()
            result = result + self.far[m // 2 - 1].astype(jnp.float32)
        return result

    def sent(self):
        for copy in (*self.pair.values(), *self.chips.values()):
            copy.wait_send()


def dot(a, b, dims=((1,), (0,))):
    return lax.dot_general(a, b, (dims, ((), ())), preferred_element_type=jnp.float32)


def turn_pair(values, table, sign):
    half = ROTARY // 2
    columns = values.shape[-1]
    table = [jnp.concatenate([t] * (columns // t.shape[-1]), -1) for t in table]
    return (
        values * table[0]
        + sign * (pltpu.roll(values, columns - half, 1) * table[1])
        + sign * (pltpu.roll(values, half, 1) * table[2])
    )


def head_mask(rows, columns, head):
    return lax.broadcasted_iota(jnp.int32, (rows, columns), 1) // HEAD_DIM == head


def forward_kernel(
    zs,
    n,
    lengths,
    norms,
    bias,
    tables,
    xs_all,
    w_qkv,
    w_out,
    gu_own,
    dy,
    a1_out,
    qkv_out,
    probs_out,
    ob_out,
    hidden_out,
    a2_out,
    w_gu_out,
    gu_out,
    zz_out,
    dy_all,
    xs_v,
    a1_v,
    w_qkv_v,
    w_out_v,
    qkv_v,
    probs_v,
    ob_v,
    part,
    near,
    far,
    hidden_v,
    a2_v,
    w_gu_v,
    gu_v,
    zz_v,
    send,
    recv,
    local,
    drain,
):
    f32, b16 = jnp.float32, jnp.bfloat16
    wires = Wires(send, recv)
    z, c = wires.z, wires.c
    _, slots, rows, hc = ob_v.shape
    tokens, width = n * slots * rows, a1_v.shape[-1]
    seq = n * rows
    heads = hc // HEAD_DIM
    ffc = zz_v.shape[-1]
    chunks = 4
    chunk = w_gu_v.shape[1] // chunks

    loads = [
        pltpu.make_async_copy(gu_own, w_gu_v.at[z], local.at[0]),
        pltpu.make_async_copy(xs_all, xs_v, local.at[1]),
        pltpu.make_async_copy(w_qkv, w_qkv_v, local.at[2]),
        pltpu.make_async_copy(w_out, w_out_v, local.at[3]),
    ]
    for copy in loads:
        copy.start()
    wires.greet(zs, n)
    loads[0].wait()
    gu_z = [
        DepthGather(wires, lambda i, p=p: w_gu_v.at[i, p * chunk : (p + 1) * chunk])
        for p in range(chunks)
    ]
    DepthGather.start(gu_z)
    dy_g = LayerGather(wires, dy_all, dy)
    dy_g.start()
    stores = []

    def store(src, dst):
        copy = pltpu.make_async_copy(src, dst, drain.at[len(stores)])
        copy.start()
        stores.append(copy)

    store(dy, dy_all.at[c])
    for copy in loads[1:]:
        copy.wait()

    def project(i, carry):
        x = xs_v[pl.ds(2 * i, 2)].reshape(2 * slots * rows, width).astype(f32)
        a1 = (layer_stats(x)[0] * norms[0:1] + norms[1:2]).astype(b16)
        a1_v[pl.ds(2 * i, 2)] = a1.reshape(2, slots * rows, width)
        joined = dot(a1, w_qkv_v[...].reshape(width, 3 * hc)) + bias[...]
        for j in range(2):
            table = [tables[k, 2 * i + j] for k in range(3)]
            for s in range(slots):
                at = (j * slots + s) * rows
                piece = joined[at : at + rows]
                qkv_v[0, s, 2 * i + j] = turn_pair(piece[:, :hc], table, 1.0).astype(b16)
                qkv_v[1, s, 2 * i + j] = turn_pair(piece[:, hc : 2 * hc], table, 1.0).astype(b16)
                qkv_v[2, s, 2 * i + j] = piece[:, 2 * hc :].astype(b16)
        return carry

    lax.fori_loop(0, n // 2, project, 0)
    store(a1_v, a1_out)
    store(qkv_v, qkv_out)

    half = seq // 2

    def attend(s, carry):
        q, k, v = [qkv_v[i, s].reshape(seq, hc) for i in range(3)]
        length = lengths[0, s]
        for part_q in range(2):
            keys = (part_q + 1) * half
            at = part_q * half
            query = q[at : at + half]
            row = lax.broadcasted_iota(jnp.int32, (half, keys), 0) + at
            key = lax.broadcasted_iota(jnp.int32, (half, keys), 1)
            allowed = (key <= row) & (row < length)
            out = jnp.zeros((half, hc), f32)
            for h in range(heads):
                mask = head_mask(half, hc, h)
                scores = dot(jnp.where(mask, query, 0).astype(b16), k[:keys], ((1,), (1,)))
                scores = jnp.where(allowed, scores * 0.125, masked_value)
                peak = jnp.max(scores, -1, keepdims=True)
                weights = jnp.where(allowed, jnp.exp(scores - peak), 0.0)
                total = jnp.maximum(jnp.sum(weights, -1, keepdims=True), 1.0)
                probs = (weights * (1.0 / total)).astype(b16)
                probs_v[s, h, at : at + half, 0:keys] = probs
                out = jnp.where(mask, dot(probs, v[:keys]), out)
            ob_v[part_q * n // 2 : (part_q + 1) * n // 2, s] = out.astype(b16).reshape(
                n // 2, rows, hc
            )
        return carry

    lax.fori_loop(0, slots, attend, 0)
    for m in (2, 4, 6):
        dy_g.forward(m)
    store(probs_v, probs_out)
    store(ob_v, ob_out)

    def to_hidden(i, carry):
        part[i] = dot(
            ob_v[i].reshape(slots * rows, hc), w_out_v[...].reshape(hc, width)
        ).astype(b16)
        return carry

    lax.fori_loop(0, n, to_hidden, 0)
    sums = LayerScatter(wires, part, near, far)
    sums.start()
    for m in (6, 4, 2):
        sums.step(m)
    gu_z[0].forward()
    hidden = xs_v[c].astype(f32) + sums.total()
    hidden_v[...] = hidden
    store(hidden_v, hidden_out)
    a2_v[c] = (layer_stats(hidden)[0] * norms[2:3] + norms[3:4]).astype(b16)
    a2_g = LayerGather(wires, a2_v)
    a2_g.start()
    gu_z[1].forward()
    for m in (2, 4, 6):
        a2_g.forward(m)
    gu_z[2].forward()
    for m in (1, 3, 5, 7):
        a2_g.arrived(m)
    gu_z[3].forward()
    store(a2_v, a2_out)
    for part_z in gu_z:
        part_z.finish()
    store(w_gu_v, w_gu_out)

    def feed(i, carry):
        a2 = a2_v[pl.ds(2 * i, 2)].reshape(2 * slots * rows, width)
        gu = dot(a2, w_gu_v[...].reshape(width, 2 * ffc))
        gu_v[i] = gu
        gate = gu[:, :ffc]
        zz_v[i] = (gate * jax.nn.sigmoid(gate) * gu[:, ffc:]).astype(b16)
        return carry

    lax.fori_loop(0, n // 2, feed, 0)
    store(gu_v, gu_out)
    store(zz_v, zz_out)
    sums.sent()
    a2_g.sent()
    for m in (1, 3, 5, 7):
        dy_g.arrived(m)
    dy_g.sent()
    for copy in stores:
        copy.wait()


def forward(zs, n, slots, lengths, norms, bias, tables, xs_all, w_qkv, w_out, gu_own, dy):
    _, local, width = xs_all.shape
    rows = local // slots
    seq = rows * n
    heads = HEADS // n
    hc = heads * HEAD_DIM
    gc = gu_own.shape[-1]
    f32, b16 = jnp.float32, jnp.bfloat16
    kept = [
        ((n, local, width), b16),
        ((3, slots, n, rows, hc), b16),
        ((slots, heads, seq, seq), b16),
        ((n, slots, rows, hc), b16),
        ((local, width), f32),
        ((n, local, width), b16),
        ((zs, *gu_own.shape), b16),
        ((n // 2, 2 * local, gc), f32),
        ((n // 2, 2 * local, gc // 2), b16),
    ]
    a1, qkv, probs, ob, hidden, a2, w_gu, gu, zz = [pltpu.VMEM(*k) for k in kept]
    return pl.pallas_call(
        functools.partial(forward_kernel, zs, n),
        out_shape=[jax.ShapeDtypeStruct(*k) for k in (*kept, ((n, local, width), b16))],
        in_specs=[pl.BlockSpec(memory_space=pltpu.SMEM)] + [VMEM] * 3 + [HBM] * 5,
        out_specs=[HBM] * (len(kept) + 1),
        scratch_shapes=[
            pltpu.VMEM(xs_all.shape, b16),
            a1,
            pltpu.VMEM(w_qkv.shape, b16),
            pltpu.VMEM(w_out.shape, b16),
            qkv,
            probs,
            ob,
            pltpu.VMEM((n, local, width), b16),
            pltpu.VMEM((n // 2, local, width), b16),
            pltpu.VMEM((n // 2 - 1, local, width), b16),
            hidden,
            a2,
            w_gu,
            gu,
            zz,
            pltpu.SemaphoreType.DMA((40,)),
            pltpu.SemaphoreType.DMA((40,)),
            pltpu.SemaphoreType.DMA((4,)),
            pltpu.SemaphoreType.DMA((len(kept) + 1,)),
        ],
        compiler_params=pltpu.CompilerParams(
            collective_id=2, has_side_effects=True, vmem_limit_bytes=60 << 20
        ),
        name="forward",
    )(lengths, norms, bias, tables, xs_all, w_qkv, w_out, gu_own, dy)


class DepthScatter:
    def __init__(self, wires, part, relay, boxes):
        z = wires.z
        self.wires, self.part, self.relay_box, self.boxes = wires, part, relay, boxes
        self.far = wires.put(part(flip(z, 3)), relay, 1, 0)
        self.skip = wires.put(part(flip(z, 2)), boxes[1], 2, 0)
        self.near = wires.put(part(flip(z, 1)), boxes[0], 1, 0)
        self.mid = wires.put(part(flip(z, 3)), boxes[2], 3, 0)

    def start(self, mask):
        outer, inner = pl.when(self.wires.outer), pl.when(self.wires.inner)
        if mask == 3:
            outer(self.far.start)
            inner(self.mid.start)
        elif mask == 2:
            outer(self.skip.start)
        elif mask == 1:
            self.near.start()
        else:

            @outer
            def _():
                self.boxes[2][...] = jnp.zeros_like(self.boxes[2])

    def relay(self):
        @pl.when(self.wires.inner)
        def _():
            self.far.wait_recv()
            to = self.part(flip(self.wires.z, 2))
            to[...] = (
                to[...].astype(jnp.float32) + self.relay_box[...].astype(jnp.float32)
            ).astype(to.dtype)
            self.skip.start()

    def total(self):
        self.near.wait_recv()
        self.skip.wait_recv()
        pl.when(self.wires.inner)(self.mid.wait_recv)
        result = self.part(self.wires.z)[...].astype(jnp.float32)
        for box in self.boxes:
            result = result + box[...].astype(jnp.float32)
        return result

    def sent(self):
        self.near.wait_send()
        self.skip.wait_send()
        pl.when(self.wires.outer)(self.far.wait_send)
        pl.when(self.wires.inner)(self.mid.wait_send)


class Moves:
    def __init__(self, sems):
        self.sems, self.number, self.stores = sems, itertools.count(), []

    def load(self, src, dst):
        copy = pltpu.make_async_copy(src, dst, self.sems.at[next(self.number)])
        copy.start()
        return copy

    def store(self, src, dst):
        self.stores.append(self.load(src, dst))

    def finish(self):
        for copy in self.stores:
            copy.wait()


def pieces_of(total, number, unit):
    units = total // unit
    cuts = [units * i // number * unit for i in range(number + 1)]
    return [(a, b - a) for a, b in zip(cuts[:-1], cuts[1:])]


class ChainGather:
    def __init__(self, wires, part):
        self.z = z = wires.z
        self.right = [
            wires.put_to(part((z - s + 4) % 4), part((z - s + 4) % 4), (z + 1) % 4, wires.c)
            for s in range(3)
        ]
        self.left = [
            wires.put_to(part((z + s) % 4), part((z + s) % 4), (z + 3) % 4, wires.c)
            for s in range(3)
        ]

    def start(self):
        pl.when(self.z <= 2)(self.right[0].start)
        pl.when(self.z >= 1)(self.left[0].start)

    def hop(self, s):
        pl.when(self.z >= s)(self.right[s - 1].wait_recv)
        pl.when((self.z >= s) & (self.z <= 2))(self.right[s].start)
        pl.when(self.z <= 3 - s)(self.left[s - 1].wait_recv)
        pl.when((self.z <= 3 - s) & (self.z >= 1))(self.left[s].start)

    def finish(self):
        pl.when(self.z >= 3)(self.right[2].wait_recv)
        pl.when(self.z <= 0)(self.left[2].wait_recv)
        for s in range(3):
            pl.when((self.z >= s) & (self.z <= 2))(self.right[s].wait_send)
            pl.when((self.z <= 3 - s) & (self.z >= 1))(self.left[s].wait_send)


class ChainScatter:
    def __init__(self, wires, part, right, left):
        self.z = z = wires.z
        self.part, self.right_box, self.left_box = part, right, left
        self.right = {
            j: wires.put_to(part(j), right(j), (z + 1) % 4, wires.c) for j in (3, 2, 1)
        }
        self.left = {j: wires.put_to(part(j), left(j), (z + 3) % 4, wires.c) for j in (0, 1, 2)}

    def clear(self):
        @pl.when(self.z == 0)
        def _():
            self.right_box(0)[...] = jnp.zeros_like(self.right_box(0))

        @pl.when(self.z == 3)
        def _():
            self.left_box(3)[...] = jnp.zeros_like(self.left_box(3))

    def start(self, distance):
        pl.when(self.z == 0)(self.right[distance].start)
        pl.when(self.z == 3)(self.left[3 - distance].start)

    def pass_on(self, copy, j, box):
        copy.wait_recv()
        to = self.part(j)
        to[...] = (to[...].astype(jnp.float32) + box(j)[...].astype(jnp.float32)).astype(to.dtype)
        copy.start()

    def hop(self, s, distance):
        @pl.when(self.z == s)
        def _():
            self.pass_on(self.right[distance], distance, self.right_box)

        @pl.when(self.z == 3 - s)
        def _():
            self.pass_on(self.left[3 - distance], 3 - distance, self.left_box)

    def total(self):
        for j in (1, 2, 3):
            pl.when(self.z == j)(self.right[j].wait_recv)
        for j in (0, 1, 2):
            pl.when(self.z == j)(self.left[j].wait_recv)
        z = self.z
        return (
            self.part(z)[...].astype(jnp.float32)
            + self.right_box(z)[...].astype(jnp.float32)
            + self.left_box(z)[...].astype(jnp.float32)
        )

    def sent(self):
        for j in (1, 2, 3):
            pl.when(self.z < j)(self.right[j].wait_send)
        for j in (0, 1, 2):
            pl.when(self.z > j)(self.left[j].wait_send)


def middle_kernel(
    zs,
    n,
    zz,
    gu,
    dy_all,
    w_down,
    hidden,
    dgu_out,
    grad_down_out,
    result_out,
    zz_v,
    gu_v,
    dy_v,
    w_down_v,
    hidden_v,
    dgu_v,
    gd_v,
    right_v,
    left_v,
    total_v,
    dz_v,
    part,
    near,
    far,
    send,
    recv,
    local,
):
    f32, b16 = jnp.float32, jnp.bfloat16
    wires = Wires(send, recv)
    moves = Moves(local)
    z = wires.z
    _, block, width = w_down_v.shape
    ffc = zs * block
    tokens = n * dy_v.shape[1]
    wait_down = moves.load(w_down, w_down_v.at[z])
    wait_zz = moves.load(zz, zz_v)
    wait_dy = moves.load(dy_all, dy_v)
    waits = [moves.load(gu, gu_v), moves.load(hidden, hidden_v)]
    wires.greet(zs, n)
    wait_down.wait()
    number = 4
    tile = width // number
    columns = [slice(p * tile, (p + 1) * tile) for p in range(number)]
    down_z = [ChainGather(wires, lambda i, k=k: w_down_v.at[i, :, k]) for k in columns]
    for chain in down_z:
        chain.start()
    wait_zz.wait()
    wait_dy.wait()
    sums = [
        ChainScatter(
            wires,
            lambda i, k=k: gd_v.at[i, :, k],
            lambda i, k=k: right_v.at[i, :, k],
            lambda i, k=k: left_v.at[i, :, k],
        )
        for k in columns
    ]
    y_sums = [
        LayerScatter(wires, part.at[:, :, k], near.at[:, :, k], far.at[:, :, k]) for k in columns
    ]
    for k, chain in zip(columns, sums):
        gd = dot(
            zz_v[...].reshape(tokens, ffc), dy_v[:, :, k].reshape(tokens, tile), ((0,), (0,))
        )
        gd_v[:, :, k] = gd.astype(b16).reshape(zs, block, tile)
        chain.start(3)
    for distance in (2, 1):
        for chain in sums:
            chain.start(distance)
    for chain in sums:
        chain.clear()
    for copy in waits:
        copy.wait()

    def products(p):
        k = columns[p]

        def rows(i, carry):
            weight = w_down_v[:, :, k].reshape(ffc, tile)
            dy_rows = dy_v[pl.ds(2 * i, 2), :, k].reshape(2 * tokens // n, tile)
            dz = dot(dy_rows, weight, ((1,), (1,)))
            dz_v[i] = dz if p == 0 else dz_v[i] + dz
            part[pl.ds(2 * i, 2), :, k] = (
                dot(zz_v[i], weight).astype(b16).reshape(2, tokens // n, tile)
            )
            return carry

        lax.fori_loop(0, n // 2, rows, 0)

    for t in range(number + 1):
        if t < number:
            down_z[t].hop(1)
        if t >= 1:
            down_z[t - 1].hop(2)
    for t in range(number):
        sums[t].hop(1, 3)
        down_z[t].finish()
        products(t)
        y_sums[t].start()
        if t >= 1:
            for m in (6, 4, 2):
                y_sums[t - 1].step(m)
    for m in (6, 4, 2):
        y_sums[number - 1].step(m)
    for chain in sums:
        chain.hop(1, 2)
        chain.hop(2, 3)

    def back(i, carry):
        dz = dz_v[i]
        gu_block = gu_v[i]
        gate, up = gu_block[:, :ffc], gu_block[:, ffc:]
        sig = jax.nn.sigmoid(gate)
        dg = dz * up * sig * (1.0 + gate * (1.0 - sig))
        du = dz * gate * sig
        dgu_v[i] = jnp.concatenate([dg, du], -1).astype(b16)
        return carry

    lax.fori_loop(0, n // 2, back, 0)
    moves.store(dgu_v, dgu_out)
    for k, chain in zip(columns, sums):
        total_v[:, k] = chain.total()
    moves.store(total_v, grad_down_out)
    for k, y_sum in zip(columns, y_sums):
        result_out[:, k] = (hidden_v[:, k] + y_sum.total()).astype(b16)
    for group in (*sums, *y_sums):
        group.sent()
    moves.finish()


def middle(zs, n, zz, gu, dy_all, w_down, hidden):
    f32, b16 = jnp.float32, jnp.bfloat16
    block, width = w_down.shape
    local = hidden.shape[0]
    return pl.pallas_call(
        functools.partial(middle_kernel, zs, n),
        out_shape=[
            jax.ShapeDtypeStruct(gu.shape, b16),
            jax.ShapeDtypeStruct((block, width), f32),
            jax.ShapeDtypeStruct((local, width), b16),
        ],
        in_specs=[HBM] * 5,
        out_specs=[HBM, HBM, VMEM],
        scratch_shapes=[
            pltpu.VMEM(zz.shape, b16),
            pltpu.VMEM(gu.shape, f32),
            pltpu.VMEM(dy_all.shape, b16),
            pltpu.VMEM((zs, block, width), b16),
            pltpu.VMEM((local, width), f32),
            pltpu.VMEM(gu.shape, b16),
            pltpu.VMEM((zs, block, width), b16),
            pltpu.VMEM((zs, block, width), b16),
            pltpu.VMEM((zs, block, width), b16),
            pltpu.VMEM((block, width), f32),
            pltpu.VMEM(zz.shape, f32),
            pltpu.VMEM((n, local, width), b16),
            pltpu.VMEM((n // 2, local, width), b16),
            pltpu.VMEM((n // 2 - 1, local, width), b16),
            pltpu.SemaphoreType.DMA((80,)),
            pltpu.SemaphoreType.DMA((80,)),
            pltpu.SemaphoreType.DMA((8,)),
        ],
        compiler_params=pltpu.CompilerParams(
            collective_id=3, has_side_effects=True, vmem_limit_bytes=60 << 20
        ),
        name="middle",
    )(zz, gu, dy_all, w_down, hidden)


def unpack_columns(dst, src, at, block, n, zs):
    dst[...] = jnp.concatenate(
        [
            src[i, :, at + block * j : at + block * (j + 1)]
            for j in range(zs)
            for i in range(n)
        ],
        -1,
    )


def backward_kernel(
    zs,
    n,
    norms,
    tables,
    a1_all,
    a2_all,
    dgu,
    w_gu,
    w_qkv,
    w_out,
    qkv,
    probs,
    ob,
    hidden,
    dy_all,
    xs,
    grad_out_out,
    input_grad_out,
    gq_out,
    gate_out,
    up_out,
    small_out,
    wide_v,
    dgu_v,
    weight_v,
    w_out_v,
    qkv_v,
    probs_v,
    ob_v,
    hidden_v,
    own_v,
    ggu_v,
    relay_v,
    box_v,
    near,
    far,
    dh_all,
    go_v,
    go_relay,
    go_box,
    dqkv_v,
    dj_v,
    bias_v,
    gq_relay,
    gq_box,
    gu_rows,
    gq_rows,
    small_v,
    small_x,
    small_r,
    small_z,
    send,
    recv,
    local,
):
    f32, b16 = jnp.float32, jnp.bfloat16
    wires = Wires(send, recv)
    moves = Moves(local)
    z, c = wires.z, wires.c
    _, slots, rows, hc = ob_v.shape
    width = dh_all.shape[-1]
    tokens, seq, local_rows = n * slots * rows, n * rows, slots * rows
    heads = hc // HEAD_DIM
    depth, gc = ggu_v.shape[1:]
    ffc, qc = gc // 2, 3 * hc
    wrows = depth // n
    part = wide_v
    gu_weight = weight_v.at[:, :, 0:gc]
    qkv_weight, gq_v = weight_v.at[:, :, 0:qc], weight_v.at[:, :, qc : 2 * qc]

    wait_a2 = moves.load(a2_all, wide_v)
    wait_dgu = moves.load(dgu, dgu_v)
    wait_w = moves.load(w_gu, gu_weight)
    waits = [
        moves.load(hidden, hidden_v),
        moves.load(dy_all.at[c], own_v),
        moves.load(w_out, w_out_v),
        moves.load(qkv, qkv_v),
        moves.load(probs.at[0], probs_v),
        moves.load(ob, ob_v),
    ]
    wires.greet(zs, n)
    wait_a2.wait()
    wait_dgu.wait()

    number = 4
    size = depth // number
    step = 2 * size

    def scatters(whole, relay, box):
        return [
            DepthScatter(
                wires,
                lambda i, a=p * size: whole.at[i, a : a + size],
                relay.at[p * size : (p + 1) * size],
                [box.at[j, p * size : (p + 1) * size] for j in range(3)],
            )
            for p in range(number)
        ]

    def weigh(sums, whole, left_v, grads):
        for mask in (3, 2, 1, 0):
            to = flip(z, mask)

            def piece(p, carry, to=to):
                at = pl.multiple_of(to * depth + p * step, step)
                left = left_v[:, :, pl.ds(at, step)].reshape(tokens, step)
                whole[to, pl.ds(pl.multiple_of(p * step, step), step)] = dot(
                    left, grads(), ((0,), (0,))
                ).astype(b16)
                return carry

            lax.fori_loop(0, number // 2, piece, 0)
            for part_sum in sums:
                part_sum.start(mask)

    gu_sums = scatters(ggu_v, relay_v, box_v)
    weigh(gu_sums, ggu_v, wide_v, lambda: dgu_v[...].reshape(tokens, gc))

    wait_w.wait()

    def normed_two(i, carry):
        part[pl.ds(2 * i, 2)] = (
            dot(dgu_v[i], gu_weight[...].reshape(width, gc), ((1,), (1,)))
            .astype(b16)
            .reshape(2, local_rows, width)
        )
        return carry

    lax.fori_loop(0, n // 2, normed_two, 0)
    wait_qkv = moves.load(w_qkv, qkv_weight)
    da2_sums = LayerScatter(wires, part, near, far)
    da2_sums.start()
    gu_sums[0].relay()
    for m in (6, 4, 2):
        da2_sums.step(m)
    for copy in waits:
        copy.wait()
    n2, r2 = layer_stats(hidden_v[...])
    for part_sum in gu_sums[1:]:
        part_sum.relay()
    da2 = da2_sums.total()
    gains = [jnp.sum(da2 * n2, 0, keepdims=True), jnp.sum(da2, 0, keepdims=True)]
    dh = own_v[...].astype(f32) + norm_back(da2, n2, r2, norms[2:3])
    input_grad_out[...] = dh
    dh_all[c] = dh.astype(b16)
    wait_xs = moves.load(xs, own_v)
    dh_g = LayerGather(wires, dh_all)
    dh_g.start()
    for m in (2, 4, 6):
        dh_g.forward(m)
    for m in (1, 3, 5, 7):
        dh_g.arrived(m)

    go_sums = DepthScatter(
        wires, lambda i: go_v.at[i], go_relay, [go_box.at[j] for j in range(3)]
    )
    tile = width // 4

    def heads_grad(p, carry):
        at = pl.ds(pl.multiple_of(p * tile, tile), tile)
        go = dot(
            ob_v[...].reshape(tokens, hc), dh_all[:, :, at].reshape(tokens, tile), ((0,), (0,))
        )
        go_v[:, :, at] = go.astype(b16).reshape(zs, hc // zs, tile)
        return carry

    lax.fori_loop(0, 4, heads_grad, 0)
    for mask in (3, 2, 1, 0):
        go_sums.start(mask)

    def heads_back(i, carry):
        ob_v[i] = (
            dot(dh_all[i], w_out_v[...].reshape(hc, width), ((1,), (1,)))
            .astype(b16)
            .reshape(slots, rows, hc)
        )
        return carry

    lax.fori_loop(0, n, heads_back, 0)
    dh_g.sent()
    wait_a1 = moves.load(a1_all, dh_all)
    half = seq // 2

    def attend(s, carry):
        q, k, v = [qkv_v[i, s].reshape(seq, hc) for i in range(3)]
        do_s = ob_v[:, s].reshape(seq, hc)
        dqkv_v[...] = jnp.zeros_like(dqkv_v)
        for part_q in range(2):
            keys = (part_q + 1) * half
            at = part_q * half
            query, do_q = q[at : at + half], do_s[at : at + half]
            dq = jnp.zeros((half, hc), f32)
            for h in range(heads):
                mask, mask_k = head_mask(half, hc, h), head_mask(keys, hc, h)
                do_h = jnp.where(mask, do_q, 0).astype(b16)
                low = probs_v[h, at : at + half, 0:keys]
                p32 = low.astype(f32)
                t = p32 * dot(do_h, v[:keys], ((1,), (1,)))
                ds = (t - p32 * jnp.sum(t, -1, keepdims=True)).astype(b16)
                dq = jnp.where(mask, dot(ds, k[:keys]), dq)
                dk = dot(ds, query, ((0,), (0,)))
                dv = dot(low, do_h, ((0,), (0,)))
                dqkv_v[1, 0:keys] += jnp.where(mask_k, dk, 0.0)
                dqkv_v[2, 0:keys] += dv
            dqkv_v[0, at : at + half] = dq

        @pl.when(s + 1 < slots)
        def _():
            copy = pltpu.make_async_copy(probs.at[s + 1], probs_v, probs_sem)
            copy.start()
            copy.wait()

        dq, dk = dqkv_v[0] * 0.125, dqkv_v[1] * 0.125
        table = [tables[i].reshape(seq, 2 * HEAD_DIM) for i in range(3)]
        dj = [turn_pair(dq, table, -1.0), turn_pair(dk, table, -1.0), dqkv_v[2]]
        for i in range(3):
            low = dj[i].astype(b16)
            dj_v[:, s, :, i * hc : (i + 1) * hc] = low.reshape(n, rows, hc)
            bias_v[:, i * hc : (i + 1) * hc] += jnp.sum(low.astype(f32), 0, keepdims=True)
        return carry

    bias_v[...] = jnp.zeros_like(bias_v)

    probs_sem = moves.sems.at[next(moves.number)]
    lax.fori_loop(0, slots, attend, 0)
    go_sums.relay()

    wait_a1.wait()
    wait_qkv.wait()
    qkv_sums = scatters(gq_v, gq_relay, gq_box)
    weigh(qkv_sums, gq_v, dh_all, lambda: dj_v[...].reshape(tokens, qc))

    def normed_one(i, carry):
        part[pl.ds(2 * i, 2)] = (
            dot(
                dj_v[pl.ds(2 * i, 2)].reshape(2 * local_rows, qc),
                qkv_weight[...].reshape(width, qc),
                ((1,), (1,)),
            )
            .astype(b16)
            .reshape(2, local_rows, width)
        )
        return carry

    da2_sums.sent()
    lax.fori_loop(0, n // 2, normed_one, 0)
    da1_sums = LayerScatter(wires, part, near, far)
    da1_sums.start()
    for m in (6, 4, 2):
        da1_sums.step(m)

    for p, part_sum in enumerate(gu_sums):
        ggu_v[z, p * size : (p + 1) * size] = part_sum.total().astype(b16)
    gu_x = [
        wires.put(
            ggu_v.at[z, pl.ds(pl.multiple_of(flip(c, m) * wrows, wrows), wrows)],
            gu_rows.at[c],
            0,
            m,
        )
        for m in range(1, n)
    ]
    for copy in gu_x:
        copy.start()
    gu_rows[c] = ggu_v[z, pl.ds(pl.multiple_of(c * wrows, wrows), wrows)]

    wait_xs.wait()
    n1, r1 = layer_stats(own_v[...].astype(f32))
    da1 = da1_sums.total()
    input_grad_out[...] += norm_back(da1, n1, r1, norms[0:1])
    gains = [jnp.sum(da1 * n1, 0, keepdims=True), jnp.sum(da1, 0, keepdims=True), *gains]
    for part_sum in qkv_sums:
        part_sum.relay()
    chips = n // 2
    lanes = 2 * HEAD_DIM
    lane_half = lax.broadcasted_iota(jnp.int32, (1, lanes), 1) // HEAD_DIM
    bias_part = bias_v[...]
    for j in range(zs):
        for chip in range(chips):
            k = j * chips + chip
            for r in range(4):
                small_v[j, chip, r : r + 1] = gains[r][:, k * lanes : (k + 1) * lanes]
            small_v[j, chip, 7:8] = jnp.zeros((1, lanes), f32)
    for i in range(3):
        for j in range(zs):
            at = i * hc + j * HEAD_DIM
            piece = bias_part[:, at : at + HEAD_DIM]
            both = jnp.concatenate([piece, piece], -1)
            for chip in range(chips):
                tile = (i * zs + j) * chips + chip
                pair, row = tile // 3, tile % 3
                small_v[pair // chips, pair % chips, 4 + row : 5 + row] = jnp.where(
                    (lane_half == c % 2) & (c // 2 == chip), both, 0.0
                )
    small_v_x = [
        wires.put(small_v.at[:, flip(c, m) // 2], small_x.at[m], 0, m) for m in range(1, n)
    ]
    for copy in small_v_x:
        copy.start()
    hidden_v[0:wrows] = go_sums.total()
    moves.store(hidden_v.at[0:wrows], grad_out_out)
    for copy in gu_x:
        copy.wait_recv()
    unpack_columns(gate_out, gu_rows, 0, ffc // zs, n, zs)
    unpack_columns(up_out, gu_rows, ffc, ffc // zs, n, zs)
    small_sum = small_v[:, c // 2]
    for m in range(1, n):
        small_v_x[m - 1].wait_recv()
        small_sum = small_sum + small_x[m]
    small_r[...] = small_sum
    small_z_x = [wires.put(small_r.at[flip(z, m)], small_z.at[m], m, 0) for m in range(1, zs)]
    for copy in small_z_x:
        copy.start()
    small_sum = small_r[z]
    for m in range(1, zs):
        small_z_x[m - 1].wait_recv()
        small_sum = small_sum + small_z[m]
    small_out[...] = small_sum

    for p, part_sum in enumerate(qkv_sums):
        gq_v[z, p * size : (p + 1) * size] = part_sum.total().astype(b16)
    gq_x = [
        wires.put(
            gq_v.at[z, pl.ds(pl.multiple_of(flip(c, m) * wrows, wrows), wrows)],
            gq_rows.at[c],
            0,
            m,
        )
        for m in range(1, n)
    ]
    for copy in gq_x:
        copy.start()
    gq_rows[c] = gq_v[z, pl.ds(pl.multiple_of(c * wrows, wrows), wrows)]
    for group in (*gu_sums, go_sums, *qkv_sums, da1_sums):
        group.sent()
    for copy in (*gu_x, *small_v_x, *small_z_x):
        copy.wait_send()
    moves.finish()
    for copy in gq_x:
        copy.wait()
    for i in range(3):
        unpack_columns(
            gq_out.at[:, i * width : (i + 1) * width], gq_rows, i * hc, HEAD_DIM, n, zs
        )


def backward(zs, n, norms, tables, *arrays):
    f32, b16 = jnp.float32, jnp.bfloat16
    a1_all, a2_all, dgu, w_gu, w_qkv, w_out, qkv, probs, ob, hidden, dy_all, xs = arrays
    _, slots, rows, hc = ob.shape
    local, width = hidden.shape
    _, depth, gc = w_gu.shape
    qc = 3 * hc
    wrows = depth // n
    seq = n * rows
    wide = (n, local, width)

    def buf(like):
        return pltpu.VMEM(like.shape, like.dtype)

    return pl.pallas_call(
        functools.partial(backward_kernel, zs, n),
        out_shape=[
            jax.ShapeDtypeStruct((hc // zs, width), f32),
            jax.ShapeDtypeStruct((local, width), f32),
            jax.ShapeDtypeStruct((wrows, n * qc), b16),
            jax.ShapeDtypeStruct((wrows, n * gc // 2), b16),
            jax.ShapeDtypeStruct((wrows, n * gc // 2), b16),
            jax.ShapeDtypeStruct((8, 2 * HEAD_DIM), f32),
        ],
        in_specs=[VMEM] * 2 + [HBM] * 12,
        out_specs=[HBM] + [VMEM] * 5,
        scratch_shapes=[
            pltpu.VMEM(wide, b16),
            buf(dgu),
            pltpu.VMEM((zs, depth, max(gc, 2 * qc)), b16),
            buf(w_out),
            buf(qkv),
            pltpu.VMEM(probs.shape[1:], b16),
            buf(ob),
            buf(hidden),
            pltpu.VMEM((local, width), b16),
            pltpu.VMEM((zs, depth, gc), b16),
            pltpu.VMEM((depth, gc), b16),
            pltpu.VMEM((3, depth, gc), b16),
            pltpu.VMEM((n // 2, local, width), b16),
            pltpu.VMEM((n // 2 - 1, local, width), b16),
            pltpu.VMEM(wide, b16),
            pltpu.VMEM((zs, hc // zs, width), b16),
            pltpu.VMEM((hc // zs, width), b16),
            pltpu.VMEM((3, hc // zs, width), b16),
            pltpu.VMEM((3, seq, hc), f32),
            pltpu.VMEM((n, slots, rows, qc), b16),
            pltpu.VMEM((1, qc), f32),
            pltpu.VMEM((depth, qc), b16),
            pltpu.VMEM((3, depth, qc), b16),
            pltpu.VMEM((n, wrows, gc), b16),
            pltpu.VMEM((n, wrows, qc), b16),
            pltpu.VMEM((zs, n // 2, 8, 2 * HEAD_DIM), f32),
            pltpu.VMEM((n, zs, 8, 2 * HEAD_DIM), f32),
            pltpu.VMEM((zs, 8, 2 * HEAD_DIM), f32),
            pltpu.VMEM((zs, 8, 2 * HEAD_DIM), f32),
            pltpu.SemaphoreType.DMA((96,)),
            pltpu.SemaphoreType.DMA((96,)),
            pltpu.SemaphoreType.DMA((24,)),
        ],
        compiler_params=pltpu.CompilerParams(
            collective_id=4, has_side_effects=True, vmem_limit_bytes=VMEM_LIMIT
        ),
        name="backward",
    )(norms, tables, *arrays)


def tensor_shards(
    inputs,
    lengths,
    w_qkv,
    b_qkv,
    w_out,
    w_gate,
    w_up,
    w_down,
    gain_one,
    shift_one,
    gain_two,
    shift_two,
    cotangent,
):
    rows, slots, width = inputs.shape
    f32, b16 = jnp.float32, jnp.bfloat16
    zs, n = lax.axis_size("dp"), lax.axis_size("ctx")
    me = lax.axis_index("ctx")
    local = rows * slots
    tokens = local * n
    seq = rows * n
    wrows = w_qkv.shape[0]
    ff_block = w_down.shape[0]
    hc = HEADS // n * HEAD_DIM
    ffc = ff_block * zs

    def local_tokens(v):
        return jnp.transpose(v, (1, 0, 2)).reshape(local, width)

    def back_tokens(v):
        return jnp.transpose(v.reshape(slots, rows, width), (1, 0, 2))

    xs = local_tokens(inputs)
    dy = local_tokens(cotangent)
    small, at = jnp.zeros(1024, f32), 0
    for vector in (b_qkv, gain_one, shift_one, gain_two, shift_two):
        size = vector.shape[0]
        small = small + jnp.pad(vector.astype(f32), (at, 1024 - at - size))
        at += size
    small = small.reshape(8, 128)
    w_qkv_c, w_out_c, gu_own, a_all, small = spread(
        zs, n, w_qkv, w_gate, w_up, w_out, xs, small
    )
    small = small.reshape(zs * n, 1024)
    nb = b_qkv.shape[0]
    bias_full = small[:, :nb].reshape(3, zs, n, HEAD_DIM)
    bias_own = lax.dynamic_index_in_dim(bias_full, me, 2, keepdims=False).reshape(1, 3 * hc)
    g1, s1, g2, s2 = [
        small[:, nb + i * wrows : nb + (i + 1) * wrows].reshape(1, width) for i in range(4)
    ]


    angles = np.arange(seq)[:, None] * 10000.0 ** (-2.0 * np.arange(ROTARY // 2) / ROTARY)[None, :]
    cos_t, sin_t = np.cos(angles), np.sin(angles)
    zero, rest = np.zeros_like(sin_t), np.zeros((seq, HEAD_DIM - ROTARY))
    tables = np.stack(
        [
            np.concatenate(two, -1)
            for two in (
                2 * [cos_t, cos_t, rest + 1.0],
                2 * [-sin_t, zero, rest],
                2 * [zero, sin_t, rest],
            )
        ]
    ).astype(np.float32)

    tables = jnp.asarray(tables.reshape(3, n, rows, 2 * HEAD_DIM))
    norms = jnp.concatenate([g1, s1, g2, s2])
    a1_all, qkv, probs, ob, hidden, a2_all, w_gu_c, gu, z, dy_all = forward(
        zs, n, slots, lengths, norms, bias_own, tables, a_all, w_qkv_c, w_out_c,
        gu_own.reshape(n * wrows, 2 * ffc), dy,
    )
    dgu, grad_down, result = middle(zs, n, z, gu, dy_all, w_down, hidden)
    grad_out, input_grad, grad_qkv, grad_gate, grad_up, sums = backward(
        zs, n, norms, tables, a1_all, a2_all, dgu, w_gu_c, w_qkv_c.reshape(zs, n * wrows, 3 * hc),
        w_out_c, qkv, probs, ob, hidden, dy_all, xs,
    )
    mine = lax.dynamic_slice_in_dim(sums[:4], me % 2 * wrows, wrows, 1)
    grad_bias = lax.dynamic_slice_in_dim(sums[4:7].reshape(2 * nb), me % 2 * nb, nb)
    return (
        back_tokens(result),
        back_tokens(input_grad),
        grad_qkv.astype(f32),
        grad_bias,
        grad_out,
        grad_gate.astype(f32),
        grad_up.astype(f32),
        grad_down,
        mine[0],
        mine[1],
        mine[2],
        mine[3],
    )


def solution(mesh):
    zs, n = mesh.shape["dp"], mesh.shape["ctx"]
    shards = tensor_shards if (zs, n) == (4, 8) and HEADS == 32 else gathered_shards

    placed = (
        P("ctx", "dp", None),
        P("dp", None),
        P(("dp", "ctx"), None),
        P(("dp", "ctx")),
        P(("dp", "ctx"), None),
        P(("dp", "ctx"), None),
        P(("dp", "ctx"), None),
        P(("dp", "ctx"), None),
        P(("dp", "ctx")),
        P(("dp", "ctx")),
        P(("dp", "ctx")),
        P(("dp", "ctx")),
        P("ctx", "dp", None),
    )
    return jax.shard_map(
        shards,
        mesh=mesh,
        in_specs=placed,
        out_specs=(
            P("ctx", "dp", None),
            P("ctx", "dp", None),
            P(("dp", "ctx"), None),
            P(("dp", "ctx")),
            P(("dp", "ctx"), None),
            P(("dp", "ctx"), None),
            P(("dp", "ctx"), None),
            P(("dp", "ctx"), None),
            P(("dp", "ctx")),
            P(("dp", "ctx")),
            P(("dp", "ctx")),
            P(("dp", "ctx")),
        ),
        check_vma=False,
    )
```

```python
import functools
import itertools
import math

import jax
import jax.numpy as jnp
import numpy as np
from jax import lax
from jax.experimental import pallas as pl
from jax.experimental.pallas import tpu as pltpu
from jax.sharding import PartitionSpec as P

HEADS = 32
HEAD_DIM = 64
ROTARY = 16


epsilon = 1e-05
masked_value = -1e30


def layer_stats(values):
    row_mean = jnp.mean(values, -1, keepdims=True)
    centred = values - row_mean
    inverse = lax.rsqrt(jnp.mean(centred * centred, -1, keepdims=True) + epsilon)
    return (centred * inverse, inverse)


def norm_back(grad_normed, scaled, inverse, gain_vec):
    grad_hat = grad_normed * gain_vec
    return inverse * (
        grad_hat
        - jnp.mean(grad_hat, -1, keepdims=True)
        - scaled * jnp.mean(grad_hat * scaled, -1, keepdims=True)
    )


def rotary_tables(positions):
    counter = jnp.arange(ROTARY // 2, dtype=jnp.float32)
    frequency = 10000.0 ** (-2.0 * counter / ROTARY)
    angles = positions.astype(jnp.float32)[:, None] * frequency[None, :]
    return (jnp.cos(angles)[:, None, None, :], jnp.sin(angles)[:, None, None, :])


def rotate(values, cos_table, sin_table):
    half_dims = ROTARY // 2
    first_half = values[..., :half_dims]
    second_half = values[..., half_dims:ROTARY]
    return jnp.concatenate(
        [
            first_half * cos_table - second_half * sin_table,
            second_half * cos_table + first_half * sin_table,
            values[..., ROTARY:],
        ],
        -1,
    )


def over_blocks(step_fn, running, gathered):
    total_rows = gathered.shape[0]
    tile_rows = math.gcd(total_rows, 512)

    def visit_block(number, current):
        block_start = number * tile_rows
        block_part = lax.dynamic_slice_in_dim(gathered, block_start, tile_rows, 0)
        return step_fn(current, block_part, block_start)

    return lax.fori_loop(0, total_rows // tile_rows, visit_block, running)


def gathered_shards(
    inputs,
    lengths,
    w_qkv,
    b_qkv,
    w_out,
    w_gate,
    w_up,
    w_down,
    gain_one,
    shift_one,
    gain_two,
    shift_two,
    cotangent,
):
    local_rows, slot_count, width = inputs.shape
    positions = lax.axis_index("ctx") * local_rows + jnp.arange(local_rows, dtype=jnp.int32)
    live_rows = positions[:, None] < lengths[0][None, :]
    live_heads = jnp.transpose(live_rows)[:, None, :, None]
    cos_table, sin_table = rotary_tables(positions)

    def allowed_mask(offset, count):
        key_pos = offset + jnp.arange(count, dtype=jnp.int32)
        causal = key_pos[None, :] <= positions[:, None]
        return causal[None, None, :, :] & live_heads

    def split_heads(block_part):
        count = block_part.shape[0]
        key_part = block_part[:, :, 0].reshape(count, slot_count, HEADS, HEAD_DIM)
        value_part = block_part[:, :, 1].reshape(count, slot_count, HEADS, HEAD_DIM)
        return (key_part, value_part)

    attn_full = (
        lax.all_gather(w_qkv, ("dp", "ctx"), axis=0, tiled=True),
        lax.all_gather(b_qkv, ("dp", "ctx"), axis=0, tiled=True),
        lax.all_gather(w_out, ("dp", "ctx"), axis=0, tiled=True),
        lax.all_gather(gain_one, ("dp", "ctx"), axis=0, tiled=True),
        lax.all_gather(shift_one, ("dp", "ctx"), axis=0, tiled=True),
    )
    qkv_full, bias_full, out_full, gain_one_full, shift_one_full = attn_full
    source = inputs.astype(jnp.float32)
    scaled_one, inverse_one = layer_stats(source)
    normed_one = (
        scaled_one * gain_one_full.astype(jnp.float32) + shift_one_full.astype(jnp.float32)
    ).astype(jnp.bfloat16)
    joined = jnp.einsum(
        "rsd,de->rse", normed_one, qkv_full, preferred_element_type=jnp.float32
    ) + bias_full.astype(jnp.float32)
    query_pre = joined[..., :width].reshape(local_rows, slot_count, HEADS, HEAD_DIM)
    key_pre = joined[..., width : 2 * width].reshape(local_rows, slot_count, HEADS, HEAD_DIM)
    queries = rotate(query_pre, cos_table, sin_table).astype(jnp.bfloat16)
    keys_rot = rotate(key_pre, cos_table, sin_table).reshape(local_rows, slot_count, width)
    key_value = jnp.stack([keys_rot, joined[..., 2 * width :]], 2).astype(jnp.bfloat16)
    block_part = lax.all_gather(key_value, "ctx", axis=0, tiled=True)
    run_peak = jnp.full((slot_count, HEADS, local_rows), masked_value, jnp.float32)
    key_part, value_part = split_heads(block_part)
    scores = (
        jnp.einsum("qshd,kshd->shqk", queries, key_part, preferred_element_type=jnp.float32) * 0.125
    )
    allowed = allowed_mask(jnp.int32(0), block_part.shape[0])
    masked = jnp.where(allowed, scores, masked_value)
    new_peak = jnp.maximum(run_peak, jnp.max(masked, -1))
    weights = jnp.where(allowed, jnp.exp(masked - new_peak[..., None]), 0.0)
    new_sum = jnp.sum(weights, -1)
    new_acc = jnp.einsum(
        "shqk,kshd->shqd",
        weights.astype(jnp.bfloat16),
        value_part,
        preferred_element_type=jnp.float32,
    )
    final_sum = jnp.maximum(new_sum, 1.0)
    log_sum = new_peak + jnp.log(final_sum)
    attended = jnp.transpose(new_acc / final_sum[..., None], (2, 0, 1, 3))
    attended_low = attended.reshape(local_rows, slot_count, width).astype(jnp.bfloat16)
    hidden_in = source + jnp.einsum(
        "rsd,de->rse", attended_low, out_full, preferred_element_type=jnp.float32
    )
    mlp_full = (
        lax.all_gather(w_gate, ("dp", "ctx"), axis=0, tiled=True),
        lax.all_gather(w_up, ("dp", "ctx"), axis=0, tiled=True),
        lax.all_gather(w_down, ("dp", "ctx"), axis=0, tiled=True),
        lax.all_gather(gain_two, ("dp", "ctx"), axis=0, tiled=True),
        lax.all_gather(shift_two, ("dp", "ctx"), axis=0, tiled=True),
    )
    gate_full, up_full, down_full, gain_two_full, shift_two_full = mlp_full
    scaled_two, inverse_two = layer_stats(hidden_in)
    normed_two = (
        scaled_two * gain_two_full.astype(jnp.float32) + shift_two_full.astype(jnp.float32)
    ).astype(jnp.bfloat16)
    gate = jnp.einsum("rsd,df->rsf", normed_two, gate_full, preferred_element_type=jnp.float32)
    upward = jnp.einsum("rsd,df->rsf", normed_two, up_full, preferred_element_type=jnp.float32)
    sigmoid = jax.nn.sigmoid(gate)
    product = (gate * sigmoid * upward).astype(jnp.bfloat16)
    result = hidden_in + jnp.einsum(
        "rsf,fd->rsd", product, down_full, preferred_element_type=jnp.float32
    )
    gate_back, up_back, down_back, gain_two_back = (
        lax.all_gather(w_gate, ("dp", "ctx"), axis=0, tiled=True),
        lax.all_gather(w_up, ("dp", "ctx"), axis=0, tiled=True),
        lax.all_gather(w_down, ("dp", "ctx"), axis=0, tiled=True),
        lax.all_gather(gain_two, ("dp", "ctx"), axis=0, tiled=True),
    )
    grad_down = jnp.einsum("rsf,rsd->fd", product, cotangent, preferred_element_type=jnp.float32)
    grad_product = jnp.einsum(
        "rsd,fd->rsf", cotangent, down_back, preferred_element_type=jnp.float32
    )
    grad_gate_act = (grad_product * upward * sigmoid * (1.0 + gate * (1.0 - sigmoid))).astype(
        jnp.bfloat16
    )
    grad_up_act = (grad_product * gate * sigmoid).astype(jnp.bfloat16)
    grad_gate = jnp.einsum(
        "rsd,rsf->df", normed_two, grad_gate_act, preferred_element_type=jnp.float32
    )
    grad_up = jnp.einsum("rsd,rsf->df", normed_two, grad_up_act, preferred_element_type=jnp.float32)
    grad_normed_two = jnp.einsum(
        "rsf,df->rsd", grad_gate_act, gate_back, preferred_element_type=jnp.float32
    ) + jnp.einsum("rsf,df->rsd", grad_up_act, up_back, preferred_element_type=jnp.float32)
    grad_gain_two = jnp.sum(grad_normed_two * scaled_two, (0, 1))
    grad_shift_two = jnp.sum(grad_normed_two, (0, 1))
    grad_hidden = cotangent.astype(jnp.float32) + norm_back(
        grad_normed_two, scaled_two, inverse_two, gain_two_back.astype(jnp.float32)
    )
    mlp_sums = (
        lax.psum_scatter(grad_gate, ("dp", "ctx"), scatter_dimension=0, tiled=True),
        lax.psum_scatter(grad_up, ("dp", "ctx"), scatter_dimension=0, tiled=True),
        lax.psum_scatter(grad_down, ("dp", "ctx"), scatter_dimension=0, tiled=True),
        lax.psum_scatter(grad_gain_two, ("dp", "ctx"), scatter_dimension=0, tiled=True),
        lax.psum_scatter(grad_shift_two, ("dp", "ctx"), scatter_dimension=0, tiled=True),
    )
    qkv_back, out_back, gain_one_back = (
        lax.all_gather(w_qkv, ("dp", "ctx"), axis=0, tiled=True),
        lax.all_gather(w_out, ("dp", "ctx"), axis=0, tiled=True),
        lax.all_gather(gain_one, ("dp", "ctx"), axis=0, tiled=True),
    )
    hidden_low = grad_hidden.astype(jnp.bfloat16)
    grad_out = jnp.einsum(
        "rsd,rse->de", attended_low, hidden_low, preferred_element_type=jnp.float32
    )
    grad_attended = jnp.einsum(
        "rse,de->rsd", hidden_low, out_back, preferred_element_type=jnp.float32
    )
    grad_heads = grad_attended.reshape(local_rows, slot_count, HEADS, HEAD_DIM).astype(jnp.bfloat16)
    delta = jnp.transpose(jnp.sum(grad_heads.astype(jnp.float32) * attended, -1), (1, 2, 0))
    key_value_all = lax.all_gather(key_value, "ctx", axis=0, tiled=True)

    def grad_parts(block_part, offset):
        key_part, value_part = split_heads(block_part)
        scores = (
            jnp.einsum("qshd,kshd->shqk", queries, key_part, preferred_element_type=jnp.float32)
            * 0.125
        )
        allowed = allowed_mask(offset, block_part.shape[0])
        probs = jnp.where(allowed, jnp.exp(scores - log_sum[..., None]), 0.0)
        grad_prob = jnp.einsum(
            "qshd,kshd->shqk", grad_heads, value_part, preferred_element_type=jnp.float32
        )
        grad_score = (probs * (grad_prob - delta[..., None])).astype(jnp.bfloat16)
        return (key_part, probs, grad_score)

    def query_step(running, block_part, offset):
        key_part, probs, grad_score = grad_parts(block_part, offset)
        return running + jnp.einsum(
            "shqk,kshd->shqd", grad_score, key_part, preferred_element_type=jnp.float32
        )

    grad_query = (
        over_blocks(
            query_step,
            jnp.zeros((slot_count, HEADS, local_rows, HEAD_DIM), jnp.float32),
            key_value_all,
        )
        * 0.125
    )
    count = local_rows * lax.axis_size("ctx")
    tile_rows = math.gcd(count, 512)

    def one_block(number):
        block_start = number * tile_rows
        block_part = lax.dynamic_slice_in_dim(key_value_all, block_start, tile_rows, 0)
        key_part, probs, grad_score = grad_parts(block_part, block_start)
        grad_key = (
            jnp.einsum("shqk,qshd->kshd", grad_score, queries, preferred_element_type=jnp.float32)
            * 0.125
        )
        grad_value = jnp.einsum(
            "shqk,qshd->kshd",
            probs.astype(jnp.bfloat16),
            grad_heads,
            preferred_element_type=jnp.float32,
        )
        return jnp.stack(
            [
                grad_key.reshape(tile_rows, slot_count, width),
                grad_value.reshape(tile_rows, slot_count, width),
            ],
            2,
        )

    blocks = lax.map(one_block, jnp.arange(count // tile_rows, dtype=jnp.int32))
    grad_key_value = lax.psum_scatter(
        blocks.reshape(count, slot_count, 2, width).astype(jnp.bfloat16),
        "ctx",
        scatter_dimension=0,
        tiled=True,
    ).astype(jnp.float32)
    grad_query_pre = rotate(jnp.transpose(grad_query, (2, 0, 1, 3)), cos_table, -sin_table)
    grad_key_pre = rotate(
        grad_key_value[:, :, 0].reshape(local_rows, slot_count, HEADS, HEAD_DIM),
        cos_table,
        -sin_table,
    )
    grad_joined = jnp.concatenate(
        [
            grad_query_pre.reshape(local_rows, slot_count, width),
            grad_key_pre.reshape(local_rows, slot_count, width),
            grad_key_value[:, :, 1],
        ],
        -1,
    ).astype(jnp.bfloat16)
    grad_qkv = jnp.einsum(
        "rsd,rse->de", normed_one, grad_joined, preferred_element_type=jnp.float32
    )
    grad_bias = jnp.sum(grad_joined.astype(jnp.float32), (0, 1))
    grad_normed_one = jnp.einsum(
        "rse,de->rsd", grad_joined, qkv_back, preferred_element_type=jnp.float32
    )
    grad_gain_one = jnp.sum(grad_normed_one * scaled_one, (0, 1))
    grad_shift_one = jnp.sum(grad_normed_one, (0, 1))
    input_grad = grad_hidden + norm_back(
        grad_normed_one, scaled_one, inverse_one, gain_one_back.astype(jnp.float32)
    )
    attn_sums = (
        lax.psum_scatter(grad_qkv, ("dp", "ctx"), scatter_dimension=0, tiled=True),
        lax.psum_scatter(grad_bias, ("dp", "ctx"), scatter_dimension=0, tiled=True),
        lax.psum_scatter(grad_out, ("dp", "ctx"), scatter_dimension=0, tiled=True),
        lax.psum_scatter(grad_gain_one, ("dp", "ctx"), scatter_dimension=0, tiled=True),
        lax.psum_scatter(grad_shift_one, ("dp", "ctx"), scatter_dimension=0, tiled=True),
    )
    return (
        result.astype(jnp.bfloat16),
        input_grad,
        attn_sums[0],
        attn_sums[1],
        attn_sums[2],
        mlp_sums[0],
        mlp_sums[1],
        mlp_sums[2],
        attn_sums[3],
        attn_sums[4],
        mlp_sums[3],
        mlp_sums[4],
    )


MESH = pl.DeviceIdType.MESH
HBM = pl.BlockSpec(memory_space=pltpu.HBM)
VMEM = pl.BlockSpec(memory_space=pltpu.VMEM)
VMEM_LIMIT = 60 << 20


def flip(index, mask):
    for bit in (1, 2, 4):
        if mask & bit:
            index = index + bit - 2 * bit * ((index // bit) % 2)
    return index


class Wires:
    def __init__(self, send, recv):
        self.send, self.recv = send, recv
        self.z, self.c = lax.axis_index("dp"), lax.axis_index("ctx")
        self.inner = (self.z == 1) | (self.z == 2)
        self.outer = (self.z == 0) | (self.z == 3)
        self.number = itertools.count()

    def put(self, src, dst, z_mask, c_mask):
        return self.put_to(src, dst, flip(self.z, z_mask), flip(self.c, c_mask))

    def put_to(self, src, dst, z, c):
        i = next(self.number)
        return pltpu.make_async_remote_copy(
            src_ref=src,
            dst_ref=dst,
            send_sem=self.send.at[i],
            recv_sem=self.recv.at[i],
            device_id=(z, c),
            device_id_type=MESH,
        )

    def greet(self, zs, n):
        barrier = pltpu.get_barrier_semaphore()
        for m in range(1, zs):
            pl.semaphore_signal(
                barrier, inc=1, device_id=(flip(self.z, m), self.c), device_id_type=MESH
            )
        for m in range(1, n):
            pl.semaphore_signal(
                barrier, inc=1, device_id=(self.z, flip(self.c, m)), device_id_type=MESH
            )
        pl.semaphore_wait(barrier, zs + n - 2)


class DepthGather:
    def __init__(self, wires, part):
        z = wires.z
        self.wires = wires
        self.near = wires.put(part(z), part(z), 1, 0)
        self.skip = wires.put(part(z), part(z), 2, 0)
        self.mid = wires.put(part(z), part(z), 3, 0)
        far = flip(z, 2)
        self.on = wires.put(part(far), part(far), 1, 0)

    @staticmethod
    def start(parts):
        for part in parts:
            part.skip.start()
        for part in parts:
            pl.when(part.wires.inner)(part.mid.start)
        for part in parts:
            part.near.start()

    def forward(self):
        @pl.when(self.wires.inner)
        def _():
            self.skip.wait_recv()
            self.on.start()

    def finish(self):
        self.near.wait_recv()
        self.near.wait_send()
        self.skip.wait_send()

        @pl.when(self.wires.inner)
        def _():
            self.mid.wait_recv()
            self.mid.wait_send()
            self.on.wait_send()

        @pl.when(self.wires.outer)
        def _():
            self.skip.wait_recv()
            self.on.wait_recv()


class LayerGather:
    def __init__(self, wires, block, source=None):
        c = wires.c
        mine = block(c) if source is None else source
        self.direct = {m: wires.put(mine, block(c), 0, m) for m in (2, 4, 6, 1)}
        self.on = {m: wires.put(block(flip(c, m)), block(flip(c, m)), 0, 1) for m in (2, 4, 6)}

    def start(self):
        for m in (2, 4, 6, 1):
            self.direct[m].start()

    def forward(self, m):
        self.direct[m].wait_recv()
        self.on[m].start()

    def arrived(self, m):
        (self.direct[1] if m == 1 else self.on[m - 1]).wait_recv()

    def sent(self):
        for copy in (*self.direct.values(), *self.on.values()):
            copy.wait_send()


def pack_columns(dst, refs, n, zs):
    for i in range(n):
        pieces = []
        for ref, block in refs:
            pieces += [ref[:, block * (j * n + i) : block * (j * n + i + 1)] for j in range(zs)]
        dst[i] = jnp.concatenate(pieces, -1)


class LayerScatter:
    def __init__(self, wires, part, near, far):
        c = wires.c
        self.c, self.part, self.near, self.far = c, part, near, far
        self.pair = {
            m: wires.put(part(flip(c, m + 1)), near(m // 2), 0, 1) for m in (6, 4, 2, 0)
        }
        self.chips = {m: wires.put(part(flip(c, m)), far(m // 2 - 1), 0, m) for m in (6, 4, 2)}

    def start(self):
        for copy in self.pair.values():
            copy.start()

    def step(self, m):
        self.pair[m].wait_recv()
        to = self.part(flip(self.c, m))
        to[...] = (
            to[...].astype(jnp.float32) + self.near(m // 2)[...].astype(jnp.float32)
        ).astype(to.dtype)
        self.chips[m].start()

    def total(self):
        self.pair[0].wait_recv()
        result = self.part(self.c)[...].astype(jnp.float32)
        result = result + self.near(0)[...].astype(jnp.float32)
        for m in (2, 4, 6):
            self.chips[m].wait_recv()
            result = result + self.far(m // 2 - 1)[...].astype(jnp.float32)
        return result

    def sent(self):
        for copy in (*self.pair.values(), *self.chips.values()):
            copy.wait_send()


def dot(a, b, dims=((1,), (0,))):
    return lax.dot_general(a, b, (dims, ((), ())), preferred_element_type=jnp.float32)


def turn_pair(values, table, sign):
    half = ROTARY // 2
    columns = values.shape[-1]
    table = [jnp.concatenate([t] * (columns // t.shape[-1]), -1) for t in table]
    return (
        values * table[0]
        + sign * (pltpu.roll(values, columns - half, 1) * table[1])
        + sign * (pltpu.roll(values, half, 1) * table[2])
    )


def head_mask(rows, columns, head):
    return lax.broadcasted_iota(jnp.int32, (rows, columns), 1) // HEAD_DIM == head


class DepthScatter:
    def __init__(self, wires, part, relay, boxes):
        z = wires.z
        self.wires, self.part, self.relay_box, self.boxes = wires, part, relay, boxes
        self.far = wires.put(part(flip(z, 3)), relay, 1, 0)
        self.skip = wires.put(part(flip(z, 2)), boxes[1], 2, 0)
        self.near = wires.put(part(flip(z, 1)), boxes[0], 1, 0)
        self.mid = wires.put(part(flip(z, 3)), boxes[2], 3, 0)

    def start(self, mask):
        outer, inner = pl.when(self.wires.outer), pl.when(self.wires.inner)
        if mask == 3:
            outer(self.far.start)
            inner(self.mid.start)
        elif mask == 2:
            outer(self.skip.start)
        elif mask == 1:
            self.near.start()
        else:

            @outer
            def _():
                self.boxes[2][...] = jnp.zeros_like(self.boxes[2])

    def relay(self):
        @pl.when(self.wires.inner)
        def _():
            self.far.wait_recv()
            to = self.part(flip(self.wires.z, 2))
            to[...] = (
                to[...].astype(jnp.float32) + self.relay_box[...].astype(jnp.float32)
            ).astype(to.dtype)
            self.skip.start()

    def total(self):
        self.near.wait_recv()
        self.skip.wait_recv()
        pl.when(self.wires.inner)(self.mid.wait_recv)
        result = self.part(self.wires.z)[...].astype(jnp.float32)
        for box in self.boxes:
            result = result + box[...].astype(jnp.float32)
        return result

    def sent(self):
        self.near.wait_send()
        self.skip.wait_send()
        pl.when(self.wires.outer)(self.far.wait_send)
        pl.when(self.wires.inner)(self.mid.wait_send)


class Moves:
    def __init__(self, sems):
        self.sems, self.number, self.stores = sems, itertools.count(), []

    def load(self, src, dst):
        copy = pltpu.make_async_copy(src, dst, self.sems.at[next(self.number)])
        copy.start()
        return copy

    def store(self, src, dst):
        self.stores.append(self.load(src, dst))

    def finish(self):
        for copy in self.stores:
            copy.wait()


def pieces_of(total, number, unit):
    units = total // unit
    cuts = [units * i // number * unit for i in range(number + 1)]
    return [(a, b - a) for a, b in zip(cuts[:-1], cuts[1:])]


class ChainGather:
    def __init__(self, wires, part):
        self.z = z = wires.z
        self.right = [
            wires.put_to(part((z - s + 4) % 4), part((z - s + 4) % 4), (z + 1) % 4, wires.c)
            for s in range(3)
        ]
        self.left = [
            wires.put_to(part((z + s) % 4), part((z + s) % 4), (z + 3) % 4, wires.c)
            for s in range(3)
        ]

    def start(self):
        pl.when(self.z <= 2)(self.right[0].start)
        pl.when(self.z >= 1)(self.left[0].start)

    def hop(self, s):
        pl.when(self.z >= s)(self.right[s - 1].wait_recv)
        pl.when((self.z >= s) & (self.z <= 2))(self.right[s].start)
        pl.when(self.z <= 3 - s)(self.left[s - 1].wait_recv)
        pl.when((self.z <= 3 - s) & (self.z >= 1))(self.left[s].start)

    def finish(self):
        pl.when(self.z >= 3)(self.right[2].wait_recv)
        pl.when(self.z <= 0)(self.left[2].wait_recv)
        for s in range(3):
            pl.when((self.z >= s) & (self.z <= 2))(self.right[s].wait_send)
            pl.when((self.z <= 3 - s) & (self.z >= 1))(self.left[s].wait_send)


class ChainScatter:
    def __init__(self, wires, part, right, left):
        self.z = z = wires.z
        self.part, self.right_box, self.left_box = part, right, left
        self.right = {
            j: wires.put_to(part(j), right(j), (z + 1) % 4, wires.c) for j in (3, 2, 1)
        }
        self.left = {j: wires.put_to(part(j), left(j), (z + 3) % 4, wires.c) for j in (0, 1, 2)}

    def clear(self):
        @pl.when(self.z == 0)
        def _():
            self.right_box(0)[...] = jnp.zeros_like(self.right_box(0))

        @pl.when(self.z == 3)
        def _():
            self.left_box(3)[...] = jnp.zeros_like(self.left_box(3))

    def start(self, distance):
        pl.when(self.z == 0)(self.right[distance].start)
        pl.when(self.z == 3)(self.left[3 - distance].start)

    def pass_on(self, copy, j, box):
        copy.wait_recv()
        to = self.part(j)
        to[...] = (to[...].astype(jnp.float32) + box(j)[...].astype(jnp.float32)).astype(to.dtype)
        copy.start()

    def hop(self, s, distance):
        @pl.when(self.z == s)
        def _():
            self.pass_on(self.right[distance], distance, self.right_box)

        @pl.when(self.z == 3 - s)
        def _():
            self.pass_on(self.left[3 - distance], 3 - distance, self.left_box)

    def total(self):
        for j in (1, 2, 3):
            pl.when(self.z == j)(self.right[j].wait_recv)
        for j in (0, 1, 2):
            pl.when(self.z == j)(self.left[j].wait_recv)
        z = self.z
        return (
            self.part(z)[...].astype(jnp.float32)
            + self.right_box(z)[...].astype(jnp.float32)
            + self.left_box(z)[...].astype(jnp.float32)
        )

    def sent(self):
        for j in (1, 2, 3):
            pl.when(self.z < j)(self.right[j].wait_send)
        for j in (0, 1, 2):
            pl.when(self.z > j)(self.left[j].wait_send)


def front_kernel(
    zs,
    n,
    slots,
    lengths,
    tables,
    small,
    w_qkv,
    w_gate,
    w_up,
    w_out,
    w_down,
    xs,
    dy,
    w_qkv_out,
    w_out_out,
    w_gu_out,
    a1_out,
    qkv_out,
    probs_out,
    ob_out,
    hidden_out,
    a2_out,
    dgu_out,
    grad_down_out,
    result_out,
    norms,
    qkv_send,
    gu_send,
    small_v,
    bias_v,
    w_qkv_v,
    w_out_v,
    w_gu_v,
    w_down_v,
    wide_x,
    wide_a,
    dy_v,
    qkv_v,
    probs_v,
    ob_v,
    near,
    far,
    hidden_v,
    gu_v,
    zz_v,
    dz_v,
    right_v,
    left_v,
    total_v,
    send,
    recv,
    local,
):
    f32, b16 = jnp.float32, jnp.bfloat16
    wires = Wires(send, recv)
    moves = Moves(local)
    z, c = wires.z, wires.c
    local_rows, width = xs.shape
    rows = local_rows // slots
    tokens, seq = n * local_rows, n * rows
    pair = 2 * local_rows
    hc = qkv_v.shape[-1]
    heads = hc // HEAD_DIM
    block = w_down_v.shape[1]
    ffc = zs * block
    lanes = 2 * HEAD_DIM
    lane_half = lax.broadcasted_iota(jnp.int32, (1, lanes), 1) // HEAD_DIM

    def block_of(ref, i):
        return ref.at[pl.ds(pl.multiple_of(i * local_rows, local_rows), local_rows)]

    def pair_at(i):
        return pl.ds(pl.multiple_of(i * pair, pair), pair)

    wait_out = moves.load(w_out, w_out_v.at[z])
    wait_small = moves.load(small, small_v.at[z, c])
    wait_xs = moves.load(xs, block_of(wide_x, c))
    wait_dy = moves.load(dy, dy_v.at[c])
    wait_down = moves.load(w_down, w_down_v.at[z])
    pack_columns(
        qkv_send, [(w_qkv.at[:, i * width : (i + 1) * width], HEAD_DIM) for i in range(3)], n, zs
    )
    wait_own_qkv = moves.load(qkv_send.at[c], w_qkv_v.at[z, c])
    wires.greet(zs, n)
    wait_out.wait()
    wait_small.wait()
    out_z = DepthGather(wires, lambda i: w_out_v.at[i])
    DepthGather.start([out_z])
    qkv_x = [wires.put(qkv_send.at[flip(c, m)], w_qkv_v.at[z, c], 0, m) for m in range(1, n)]
    for copy in qkv_x:
        copy.start()
    small_z = [wires.put(small_v.at[z, c], small_v.at[z, c], m, 0) for m in range(1, zs)]
    for copy in small_z:
        copy.start()
    xs_g = LayerGather(wires, lambda i: block_of(wide_x, i), xs)
    xs_g.start()
    pack_columns(gu_send, [(w_gate, block), (w_up, block)], n, zs)
    wait_own_gu = moves.load(gu_send.at[c], w_gu_v.at[z, c])
    for copy in small_z:
        copy.wait_recv()
    small_x = [wires.put(small_v.at[:, c], small_v.at[:, c], 0, m) for m in range(1, n)]
    for copy in small_x:
        copy.start()
    wait_own_qkv.wait()
    for copy in qkv_x:
        copy.wait_recv()
    number = 4
    qkv_z = [
        DepthGather(wires, lambda i, a=a, s=s: w_qkv_v.at[i, a : a + s])
        for a, s in pieces_of(n, number, 1)
    ]
    DepthGather.start(qkv_z)
    gu_x = [wires.put(gu_send.at[flip(c, m)], w_gu_v.at[z, c], 0, m) for m in range(1, n)]
    for copy in gu_x:
        copy.start()
    out_z.forward()
    for m in (2, 4, 6):
        xs_g.forward(m)

    for copy in small_x:
        copy.wait()
    for r in range(4):
        norms[r : r + 1] = jnp.concatenate(
            [
                jnp.where(
                    lane_half == 0,
                    small_v[d // n, d % n, r : r + 1],
                    small_v[d // n, d % n + 1, r : r + 1],
                )
                for d in range(0, zs * n, 2)
            ],
            -1,
        )
    norms[4:8] = jnp.zeros_like(norms[4:8])
    per_owner = 3 * zs * n // (zs * n)
    for i in range(3):
        for j in range(0, zs, 2):
            both = []
            for h in range(2):
                group = i * zs * n + (j + h) * n + c
                owner, k = group // per_owner, group % per_owner
                tile = small_v[owner // n, owner % n]
                row = jnp.where(k == 2, tile[5:6], tile[4:5])
                both.append(jnp.where(k % 2 == h, row, pltpu.roll(row, HEAD_DIM, 1)))
            at = (i * zs + j) * HEAD_DIM
            bias_v[:, at : at + lanes] = jnp.where(lane_half == 0, both[0], both[1])

    for m in (1, 3, 5, 7):
        xs_g.arrived(m)
    wait_xs.wait()
    hidden_v[...] = block_of(wide_x, c)[...].astype(f32)

    def norm_one(i, carry):
        x = wide_x[pair_at(i)].astype(f32)
        wide_a[pair_at(i)] = (layer_stats(x)[0] * norms[0:1] + norms[1:2]).astype(b16)
        return carry

    lax.fori_loop(0, n // 2, norm_one, 0)
    wait_a1 = moves.load(wide_a, a1_out)
    wait_own_gu.wait()
    for copy in gu_x:
        copy.wait_recv()
    gu_z = [
        DepthGather(wires, lambda i, a=a, s=s: w_gu_v.at[i, a : a + s])
        for a, s in pieces_of(n, number, 1)
    ]
    for part in qkv_z:
        part.forward()
    DepthGather.start(gu_z)
    wait_dy.wait()
    dy_g = LayerGather(wires, lambda i: dy_v.at[i])
    dy_g.start()
    for part in (out_z, *qkv_z):
        part.finish()
    moves.store(w_qkv_v, w_qkv_out)
    moves.store(w_out_v, w_out_out)

    def project(i, carry):
        joined = dot(wide_a[pair_at(i)], w_qkv_v[...].reshape(width, 3 * hc)) + bias_v[...]
        for j in range(2):
            table = [tables[k, 2 * i + j] for k in range(3)]
            for s in range(slots):
                at = (j * slots + s) * rows
                piece = joined[at : at + rows]
                qkv_v[0, s, 2 * i + j] = turn_pair(piece[:, :hc], table, 1.0).astype(b16)
                qkv_v[1, s, 2 * i + j] = turn_pair(piece[:, hc : 2 * hc], table, 1.0).astype(b16)
                qkv_v[2, s, 2 * i + j] = piece[:, 2 * hc :].astype(b16)
        return carry

    lax.fori_loop(0, n // 2, project, 0)
    moves.store(qkv_v, qkv_out)
    for m in (2, 4, 6):
        dy_g.forward(m)

    half = seq // 2
    probs_sem = moves.sems.at[next(moves.number)]

    def attend(s, carry):
        q, k, v = [qkv_v[i, s].reshape(seq, hc) for i in range(3)]
        length = lengths[0, s]
        kept = pltpu.make_async_copy(probs_v, probs_out.at[s], probs_sem)
        for part_q in range(2):
            keys = (part_q + 1) * half
            at = part_q * half
            query = q[at : at + half]
            row = lax.broadcasted_iota(jnp.int32, (half, keys), 0) + at
            key = lax.broadcasted_iota(jnp.int32, (half, keys), 1)
            allowed = (key <= row) & (row < length)
            out = jnp.zeros((half, hc), f32)
            for h in range(heads):
                mask = head_mask(half, hc, h)
                scores = dot(jnp.where(mask, query, 0).astype(b16), k[:keys], ((1,), (1,)))
                scores = jnp.where(allowed, scores * 0.125, masked_value)
                peak = jnp.max(scores, -1, keepdims=True)
                weights = jnp.where(allowed, jnp.exp(scores - peak), 0.0)
                total = jnp.maximum(jnp.sum(weights, -1, keepdims=True), 1.0)
                probs = (weights * (1.0 / total)).astype(b16)
                probs_v[h, at : at + half, 0:keys] = probs
                if keys < seq:
                    probs_v[h, at : at + half, keys:seq] = jnp.zeros((half, seq - keys), b16)
                out = jnp.where(mask, dot(probs, v[:keys]), out)
            ob_v[part_q * n // 2 : (part_q + 1) * n // 2, s] = out.astype(b16).reshape(
                n // 2, rows, hc
            )
        kept.start()
        kept.wait()
        return carry

    lax.fori_loop(0, slots, attend, 0)
    moves.store(ob_v, ob_out)
    gu_z[0].forward()

    xs_g.sent()

    def to_hidden(i, carry):
        block_of(wide_x, i)[...] = dot(
            ob_v[i].reshape(local_rows, hc), w_out_v[...].reshape(hc, width)
        ).astype(b16)
        return carry

    lax.fori_loop(0, n, to_hidden, 0)
    wait_a1.wait()
    sums = LayerScatter(
        wires, lambda i: block_of(wide_x, i), lambda j: near.at[j], lambda j: far.at[j]
    )
    sums.start()
    for m in (6, 4, 2):
        sums.step(m)
    gu_z[1].forward()
    hidden = hidden_v[...] + sums.total()
    hidden_v[...] = hidden
    moves.store(hidden_v, hidden_out)
    block_of(wide_a, c)[...] = (layer_stats(hidden)[0] * norms[2:3] + norms[3:4]).astype(b16)
    a2_g = LayerGather(wires, lambda i: block_of(wide_a, i))
    a2_g.start()
    gu_z[2].forward()
    for m in (2, 4, 6):
        a2_g.forward(m)
    gu_z[3].forward()
    wait_down.wait()
    tile = width // number
    columns = [slice(p * tile, (p + 1) * tile) for p in range(number)]
    down_z = [ChainGather(wires, lambda i, k=k: w_down_v.at[i, :, k]) for k in columns]
    for chain in down_z:
        chain.start()
    for m in (1, 3, 5, 7):
        dy_g.arrived(m)
    for m in (1, 3, 5, 7):
        a2_g.arrived(m)
    wait_a2 = moves.load(wide_a, a2_out)
    for part in gu_z:
        part.finish()
    moves.store(w_gu_v, w_gu_out)

    def feed(i, carry):
        gu = dot(wide_a[pair_at(i)], w_gu_v[...].reshape(width, 2 * ffc))
        gu_v[i] = gu.astype(b16)
        gate = gu[:, :ffc]
        zz_v[i] = (gate * jax.nn.sigmoid(gate) * gu[:, ffc:]).astype(b16)
        return carry

    lax.fori_loop(0, n // 2, feed, 0)
    a2_g.sent()
    wait_a2.wait()

    down_sums = [
        ChainScatter(
            wires,
            lambda i, k=k: wide_a.at[pl.ds(pl.multiple_of(i * block, 16), block), k],
            lambda i, k=k: right_v.at[i, :, k],
            lambda i, k=k: left_v.at[i, :, k],
        )
        for k in columns
    ]
    for k, chain in zip(columns, down_sums):
        wide_a[0:ffc, k] = dot(
            zz_v[...].reshape(tokens, ffc), dy_v[:, :, k].reshape(tokens, tile), ((0,), (0,))
        ).astype(b16)
        chain.start(3)
    for distance in (2, 1):
        for chain in down_sums:
            chain.start(distance)
    for chain in down_sums:
        chain.clear()
    sums.sent()

    y_sums = [
        LayerScatter(
            wires,
            lambda i, k=k: block_of(wide_x, i).at[:, k],
            lambda j, k=k: near.at[j, :, k],
            lambda j, k=k: far.at[j, :, k],
        )
        for k in columns
    ]

    def products(p):
        k = columns[p]

        def rows_of(i, carry):
            weight = w_down_v[:, :, k].reshape(ffc, tile)
            dy_rows = dy_v[pl.ds(2 * i, 2), :, k].reshape(pair, tile)
            dz = dot(dy_rows, weight, ((1,), (1,)))
            dz_v[i] = dz if p == 0 else dz_v[i] + dz
            wide_x[pair_at(i), k] = dot(zz_v[i], weight).astype(b16)
            return carry

        lax.fori_loop(0, n // 2, rows_of, 0)

    for t in range(number + 1):
        if t < number:
            down_z[t].hop(1)
        if t >= 1:
            down_z[t - 1].hop(2)
    for t in range(number):
        down_sums[t].hop(1, 3)
        down_z[t].finish()
        products(t)
        y_sums[t].start()
        if t >= 1:
            for m in (6, 4, 2):
                y_sums[t - 1].step(m)

    def back(i, carry):
        dz = dz_v[i]
        gu = gu_v[i].astype(f32)
        gate, up = gu[:, :ffc], gu[:, ffc:]
        sig = jax.nn.sigmoid(gate)
        dg = dz * up * sig * (1.0 + gate * (1.0 - sig))
        du = dz * gate * sig
        gu_v[i] = jnp.concatenate([dg, du], -1).astype(b16)
        return carry

    lax.fori_loop(0, n // 2, back, 0)
    moves.store(gu_v, dgu_out)
    for m in (6, 4, 2):
        y_sums[number - 1].step(m)
    for chain in down_sums:
        chain.hop(1, 2)
        chain.hop(2, 3)
    for k, y_sum in zip(columns, y_sums):
        result_out[:, k] = (hidden_v[:, k] + y_sum.total()).astype(b16)
    stored = [None, None]
    for p, (k, chain) in enumerate(zip(columns, down_sums)):
        if stored[p % 2] is not None:
            stored[p % 2].wait()
        total_v[p % 2] = chain.total()
        stored[p % 2] = moves.load(total_v.at[p % 2], grad_down_out.at[:, k])
    for copy in stored:
        copy.wait()
    for group in (*down_sums, *y_sums, dy_g):
        group.sent()
    for copy in (*small_z, *qkv_x, *gu_x):
        copy.wait_send()
    moves.finish()


def front(zs, n, slots, lengths, tables, small, w_qkv, w_gate, w_up, w_out, w_down, xs, dy):
    f32, b16 = jnp.float32, jnp.bfloat16
    local, width = xs.shape
    rows = local // slots
    seq, tokens = rows * n, local * n
    heads = HEADS // n
    hc = heads * HEAD_DIM
    wrows = w_out.shape[0]
    block = w_down.shape[0]
    gc = 2 * zs * block
    qkv_all = ((zs, n, wrows, 3 * hc), b16)
    out_all = ((zs, wrows, width), b16)
    gu_all = ((zs, n, wrows, gc), b16)
    down_all = ((zs, block, width), b16)
    wide = ((tokens, width), b16)
    qkv = ((3, slots, n, rows, hc), b16)
    probs = ((slots, heads, seq, seq), b16)
    ob = ((n, slots, rows, hc), b16)
    hidden = ((local, width), f32)
    gu = ((n // 2, 2 * local, gc), b16)
    outs = [
        qkv_all,
        out_all,
        gu_all,
        wide,
        qkv,
        probs,
        ob,
        hidden,
        wide,
        gu,
        ((block, width), f32),
        ((local, width), b16),
        ((8, width), f32),
    ]
    scratch = [
        ((n, wrows, 3 * hc), b16),
        ((n, wrows, gc), b16),
        ((zs, n, *small.shape), f32),
        ((1, 3 * hc), f32),
        qkv_all,
        out_all,
        gu_all,
        down_all,
        wide,
        wide,
        ((n, local, width), b16),
        qkv,
        (probs[0][1:], b16),
        ob,
        ((n // 2, local, width), b16),
        ((n // 2 - 1, local, width), b16),
        hidden,
        gu,
        ((n // 2, 2 * local, gc // 2), b16),
        ((n // 2, 2 * local, gc // 2), f32),
        down_all,
        down_all,
        ((2, block, width // 4), f32),
    ]
    return pl.pallas_call(
        functools.partial(front_kernel, zs, n, slots),
        out_shape=[jax.ShapeDtypeStruct(*k) for k in outs],
        in_specs=[pl.BlockSpec(memory_space=pltpu.SMEM), VMEM, HBM, *[VMEM] * 3, *[HBM] * 4],
        out_specs=[HBM] * (len(outs) - 2) + [VMEM] * 2,
        scratch_shapes=[
            *[pltpu.VMEM(*k) for k in scratch],
            pltpu.SemaphoreType.DMA((192,)),
            pltpu.SemaphoreType.DMA((192,)),
            pltpu.SemaphoreType.DMA((32,)),
        ],
        compiler_params=pltpu.CompilerParams(
            collective_id=1, has_side_effects=True, vmem_limit_bytes=VMEM_LIMIT
        ),
        name="front",
    )(lengths, tables, small, w_qkv, w_gate, w_up, w_out, w_down, xs, dy)


def unpack_columns(dst, src, at, block, n, zs):
    dst[...] = jnp.concatenate(
        [
            src[i, :, at + block * j : at + block * (j + 1)]
            for j in range(zs)
            for i in range(n)
        ],
        -1,
    )


def backward_kernel(
    zs,
    n,
    norms,
    tables,
    a1_all,
    a2_all,
    dgu,
    w_gu,
    w_qkv,
    w_out,
    qkv,
    probs,
    ob,
    hidden,
    dy,
    xs,
    grad_out_out,
    input_grad_out,
    gq_out,
    gate_out,
    up_out,
    small_out,
    wide_v,
    dgu_v,
    weight_v,
    w_out_v,
    qkv_v,
    probs_v,
    ob_v,
    hidden_v,
    own_v,
    ggu_v,
    relay_v,
    box_v,
    near,
    far,
    dh_all,
    go_v,
    go_relay,
    go_box,
    dqkv_v,
    dj_v,
    bias_v,
    gq_relay,
    gq_box,
    gu_rows,
    gq_rows,
    small_v,
    small_x,
    small_r,
    small_z,
    send,
    recv,
    local,
):
    f32, b16 = jnp.float32, jnp.bfloat16
    wires = Wires(send, recv)
    moves = Moves(local)
    z, c = wires.z, wires.c
    _, slots, rows, hc = ob_v.shape
    width = dh_all.shape[-1]
    tokens, seq, local_rows = n * slots * rows, n * rows, slots * rows
    heads = hc // HEAD_DIM
    depth, gc = ggu_v.shape[1:]
    ffc, qc = gc // 2, 3 * hc
    wrows = depth // n
    part = wide_v
    gu_weight = weight_v.at[:, :, 0:gc]
    qkv_weight, gq_v = weight_v.at[:, :, 0:qc], weight_v.at[:, :, qc : 2 * qc]

    wait_a2 = moves.load(a2_all, wide_v)
    wait_dgu = moves.load(dgu, dgu_v)
    wait_w = moves.load(w_gu, gu_weight)
    waits = [
        moves.load(hidden, hidden_v),
        moves.load(dy, own_v),
        moves.load(w_out, w_out_v),
        moves.load(qkv, qkv_v),
        moves.load(probs.at[0], probs_v),
        moves.load(ob, ob_v),
    ]
    wires.greet(zs, n)
    wait_a2.wait()
    wait_dgu.wait()

    number = 4
    size = depth // number
    step = 2 * size

    def scatters(whole, relay, box):
        return [
            DepthScatter(
                wires,
                lambda i, a=p * size: whole.at[i, a : a + size],
                relay.at[p * size : (p + 1) * size],
                [box.at[j, p * size : (p + 1) * size] for j in range(3)],
            )
            for p in range(number)
        ]

    def weigh(sums, whole, left_v, grads):
        for mask in (3, 2, 1, 0):
            to = flip(z, mask)

            def piece(p, carry, to=to):
                at = pl.multiple_of(to * depth + p * step, step)
                left = left_v[:, :, pl.ds(at, step)].reshape(tokens, step)
                whole[to, pl.ds(pl.multiple_of(p * step, step), step)] = dot(
                    left, grads(), ((0,), (0,))
                ).astype(b16)
                return carry

            lax.fori_loop(0, number // 2, piece, 0)
            for part_sum in sums:
                part_sum.start(mask)

    gu_sums = scatters(ggu_v, relay_v, box_v)
    weigh(gu_sums, ggu_v, wide_v, lambda: dgu_v[...].reshape(tokens, gc))

    wait_w.wait()

    def normed_two(i, carry):
        part[pl.ds(2 * i, 2)] = (
            dot(dgu_v[i], gu_weight[...].reshape(width, gc), ((1,), (1,)))
            .astype(b16)
            .reshape(2, local_rows, width)
        )
        return carry

    lax.fori_loop(0, n // 2, normed_two, 0)
    wait_qkv = moves.load(w_qkv, qkv_weight)
    da2_sums = LayerScatter(
        wires, lambda i: part.at[i], lambda j: near.at[j], lambda j: far.at[j]
    )
    da2_sums.start()
    gu_sums[0].relay()
    for m in (6, 4, 2):
        da2_sums.step(m)
    for copy in waits:
        copy.wait()
    n2, r2 = layer_stats(hidden_v[...])
    for part_sum in gu_sums[1:]:
        part_sum.relay()
    da2 = da2_sums.total()
    gains = [jnp.sum(da2 * n2, 0, keepdims=True), jnp.sum(da2, 0, keepdims=True)]
    dh = own_v[...].astype(f32) + norm_back(da2, n2, r2, norms[2:3])
    input_grad_out[...] = dh
    dh_all[c] = dh.astype(b16)
    wait_xs = moves.load(xs, own_v)
    dh_g = LayerGather(wires, lambda i: dh_all.at[i])
    dh_g.start()
    for m in (2, 4, 6):
        dh_g.forward(m)
    for m in (1, 3, 5, 7):
        dh_g.arrived(m)

    go_sums = DepthScatter(
        wires, lambda i: go_v.at[i], go_relay, [go_box.at[j] for j in range(3)]
    )
    tile = width // 4

    def heads_grad(p, carry):
        at = pl.ds(pl.multiple_of(p * tile, tile), tile)
        go = dot(
            ob_v[...].reshape(tokens, hc), dh_all[:, :, at].reshape(tokens, tile), ((0,), (0,))
        )
        go_v[:, :, at] = go.astype(b16).reshape(zs, hc // zs, tile)
        return carry

    lax.fori_loop(0, 4, heads_grad, 0)
    for mask in (3, 2, 1, 0):
        go_sums.start(mask)

    def heads_back(i, carry):
        ob_v[i] = (
            dot(dh_all[i], w_out_v[...].reshape(hc, width), ((1,), (1,)))
            .astype(b16)
            .reshape(slots, rows, hc)
        )
        return carry

    lax.fori_loop(0, n, heads_back, 0)
    dh_g.sent()
    wait_a1 = moves.load(a1_all, dh_all)
    half = seq // 2

    def attend(s, carry):
        q, k, v = [qkv_v[i, s].reshape(seq, hc) for i in range(3)]
        do_s = ob_v[:, s].reshape(seq, hc)
        dqkv_v[...] = jnp.zeros_like(dqkv_v)
        for part_q in range(2):
            keys = (part_q + 1) * half
            at = part_q * half
            query, do_q = q[at : at + half], do_s[at : at + half]
            dq = jnp.zeros((half, hc), f32)
            for h in range(heads):
                mask, mask_k = head_mask(half, hc, h), head_mask(keys, hc, h)
                do_h = jnp.where(mask, do_q, 0).astype(b16)
                low = probs_v[h, at : at + half, 0:keys]
                p32 = low.astype(f32)
                t = p32 * dot(do_h, v[:keys], ((1,), (1,)))
                ds = (t - p32 * jnp.sum(t, -1, keepdims=True)).astype(b16)
                dq = jnp.where(mask, dot(ds, k[:keys]), dq)
                dk = dot(ds, query, ((0,), (0,)))
                dv = dot(low, do_h, ((0,), (0,)))
                dqkv_v[1, 0:keys] += jnp.where(mask_k, dk, 0.0)
                dqkv_v[2, 0:keys] += dv
            dqkv_v[0, at : at + half] = dq

        @pl.when(s + 1 < slots)
        def _():
            copy = pltpu.make_async_copy(probs.at[s + 1], probs_v, probs_sem)
            copy.start()
            copy.wait()

        dq, dk = dqkv_v[0] * 0.125, dqkv_v[1] * 0.125
        table = [tables[i].reshape(seq, 2 * HEAD_DIM) for i in range(3)]
        dj = [turn_pair(dq, table, -1.0), turn_pair(dk, table, -1.0), dqkv_v[2]]
        for i in range(3):
            low = dj[i].astype(b16)
            dj_v[:, s, :, i * hc : (i + 1) * hc] = low.reshape(n, rows, hc)
            bias_v[:, i * hc : (i + 1) * hc] += jnp.sum(low.astype(f32), 0, keepdims=True)
        return carry

    bias_v[...] = jnp.zeros_like(bias_v)

    probs_sem = moves.sems.at[next(moves.number)]
    lax.fori_loop(0, slots, attend, 0)
    go_sums.relay()

    wait_a1.wait()
    wait_qkv.wait()
    qkv_sums = scatters(gq_v, gq_relay, gq_box)
    weigh(qkv_sums, gq_v, dh_all, lambda: dj_v[...].reshape(tokens, qc))

    def normed_one(i, carry):
        part[pl.ds(2 * i, 2)] = (
            dot(
                dj_v[pl.ds(2 * i, 2)].reshape(2 * local_rows, qc),
                qkv_weight[...].reshape(width, qc),
                ((1,), (1,)),
            )
            .astype(b16)
            .reshape(2, local_rows, width)
        )
        return carry

    da2_sums.sent()
    lax.fori_loop(0, n // 2, normed_one, 0)
    da1_sums = LayerScatter(
        wires, lambda i: part.at[i], lambda j: near.at[j], lambda j: far.at[j]
    )
    da1_sums.start()
    for m in (6, 4, 2):
        da1_sums.step(m)

    for p, part_sum in enumerate(gu_sums):
        ggu_v[z, p * size : (p + 1) * size] = part_sum.total().astype(b16)
    gu_x = [
        wires.put(
            ggu_v.at[z, pl.ds(pl.multiple_of(flip(c, m) * wrows, wrows), wrows)],
            gu_rows.at[c],
            0,
            m,
        )
        for m in range(1, n)
    ]
    for copy in gu_x:
        copy.start()
    gu_rows[c] = ggu_v[z, pl.ds(pl.multiple_of(c * wrows, wrows), wrows)]

    wait_xs.wait()
    n1, r1 = layer_stats(own_v[...].astype(f32))
    da1 = da1_sums.total()
    input_grad_out[...] += norm_back(da1, n1, r1, norms[0:1])
    gains = [jnp.sum(da1 * n1, 0, keepdims=True), jnp.sum(da1, 0, keepdims=True), *gains]
    for part_sum in qkv_sums:
        part_sum.relay()
    chips = n // 2
    lanes = 2 * HEAD_DIM
    lane_half = lax.broadcasted_iota(jnp.int32, (1, lanes), 1) // HEAD_DIM
    bias_part = bias_v[...]
    for j in range(zs):
        for chip in range(chips):
            k = j * chips + chip
            for r in range(4):
                small_v[j, chip, r : r + 1] = gains[r][:, k * lanes : (k + 1) * lanes]
            small_v[j, chip, 7:8] = jnp.zeros((1, lanes), f32)
    for i in range(3):
        for j in range(zs):
            at = i * hc + j * HEAD_DIM
            piece = bias_part[:, at : at + HEAD_DIM]
            both = jnp.concatenate([piece, piece], -1)
            for chip in range(chips):
                tile = (i * zs + j) * chips + chip
                pair, row = tile // 3, tile % 3
                small_v[pair // chips, pair % chips, 4 + row : 5 + row] = jnp.where(
                    (lane_half == c % 2) & (c // 2 == chip), both, 0.0
                )
    small_v_x = [
        wires.put(small_v.at[:, flip(c, m) // 2], small_x.at[m], 0, m) for m in range(1, n)
    ]
    for copy in small_v_x:
        copy.start()
    hidden_v[0:wrows] = go_sums.total()
    moves.store(hidden_v.at[0:wrows], grad_out_out)
    for copy in gu_x:
        copy.wait_recv()
    unpack_columns(gate_out, gu_rows, 0, ffc // zs, n, zs)
    unpack_columns(up_out, gu_rows, ffc, ffc // zs, n, zs)
    small_sum = small_v[:, c // 2]
    for m in range(1, n):
        small_v_x[m - 1].wait_recv()
        small_sum = small_sum + small_x[m]
    small_r[...] = small_sum
    small_z_x = [wires.put(small_r.at[flip(z, m)], small_z.at[m], m, 0) for m in range(1, zs)]
    for copy in small_z_x:
        copy.start()
    small_sum = small_r[z]
    for m in range(1, zs):
        small_z_x[m - 1].wait_recv()
        small_sum = small_sum + small_z[m]
    small_out[...] = small_sum

    for p, part_sum in enumerate(qkv_sums):
        gq_v[z, p * size : (p + 1) * size] = part_sum.total().astype(b16)
    gq_x = [
        wires.put(
            gq_v.at[z, pl.ds(pl.multiple_of(flip(c, m) * wrows, wrows), wrows)],
            gq_rows.at[c],
            0,
            m,
        )
        for m in range(1, n)
    ]
    for copy in gq_x:
        copy.start()
    gq_rows[c] = gq_v[z, pl.ds(pl.multiple_of(c * wrows, wrows), wrows)]
    for group in (*gu_sums, go_sums, *qkv_sums, da1_sums):
        group.sent()
    for copy in (*gu_x, *small_v_x, *small_z_x):
        copy.wait_send()
    moves.finish()
    for copy in gq_x:
        copy.wait()
    for i in range(3):
        unpack_columns(
            gq_out.at[:, i * width : (i + 1) * width], gq_rows, i * hc, HEAD_DIM, n, zs
        )


def backward(zs, n, norms, tables, *arrays):
    f32, b16 = jnp.float32, jnp.bfloat16
    a1_all, a2_all, dgu, w_gu, w_qkv, w_out, qkv, probs, ob, hidden, dy, xs = arrays
    _, slots, rows, hc = ob.shape
    local, width = hidden.shape
    _, depth, gc = w_gu.shape
    qc = 3 * hc
    wrows = depth // n
    seq = n * rows
    wide = (n, local, width)

    def buf(like):
        return pltpu.VMEM(like.shape, like.dtype)

    return pl.pallas_call(
        functools.partial(backward_kernel, zs, n),
        out_shape=[
            jax.ShapeDtypeStruct((hc // zs, width), f32),
            jax.ShapeDtypeStruct((local, width), f32),
            jax.ShapeDtypeStruct((wrows, n * qc), b16),
            jax.ShapeDtypeStruct((wrows, n * gc // 2), b16),
            jax.ShapeDtypeStruct((wrows, n * gc // 2), b16),
            jax.ShapeDtypeStruct((8, 2 * HEAD_DIM), f32),
        ],
        in_specs=[VMEM] * 2 + [HBM] * 12,
        out_specs=[HBM] + [VMEM] * 5,
        scratch_shapes=[
            pltpu.VMEM(wide, b16),
            buf(dgu),
            pltpu.VMEM((zs, depth, max(gc, 2 * qc)), b16),
            buf(w_out),
            buf(qkv),
            pltpu.VMEM(probs.shape[1:], b16),
            buf(ob),
            buf(hidden),
            pltpu.VMEM((local, width), b16),
            pltpu.VMEM((zs, depth, gc), b16),
            pltpu.VMEM((depth, gc), b16),
            pltpu.VMEM((3, depth, gc), b16),
            pltpu.VMEM((n // 2, local, width), b16),
            pltpu.VMEM((n // 2 - 1, local, width), b16),
            pltpu.VMEM(wide, b16),
            pltpu.VMEM((zs, hc // zs, width), b16),
            pltpu.VMEM((hc // zs, width), b16),
            pltpu.VMEM((3, hc // zs, width), b16),
            pltpu.VMEM((3, seq, hc), f32),
            pltpu.VMEM((n, slots, rows, qc), b16),
            pltpu.VMEM((1, qc), f32),
            pltpu.VMEM((depth, qc), b16),
            pltpu.VMEM((3, depth, qc), b16),
            pltpu.VMEM((n, wrows, gc), b16),
            pltpu.VMEM((n, wrows, qc), b16),
            pltpu.VMEM((zs, n // 2, 8, 2 * HEAD_DIM), f32),
            pltpu.VMEM((n, zs, 8, 2 * HEAD_DIM), f32),
            pltpu.VMEM((zs, 8, 2 * HEAD_DIM), f32),
            pltpu.VMEM((zs, 8, 2 * HEAD_DIM), f32),
            pltpu.SemaphoreType.DMA((96,)),
            pltpu.SemaphoreType.DMA((96,)),
            pltpu.SemaphoreType.DMA((24,)),
        ],
        compiler_params=pltpu.CompilerParams(
            collective_id=4, has_side_effects=True, vmem_limit_bytes=VMEM_LIMIT
        ),
        name="backward",
    )(norms, tables, *arrays)


def tensor_shards(
    inputs,
    lengths,
    w_qkv,
    b_qkv,
    w_out,
    w_gate,
    w_up,
    w_down,
    gain_one,
    shift_one,
    gain_two,
    shift_two,
    cotangent,
):
    rows, slots, width = inputs.shape
    f32, b16 = jnp.float32, jnp.bfloat16
    zs, n = lax.axis_size("dp"), lax.axis_size("ctx")
    me = lax.axis_index("ctx")
    local = rows * slots
    seq = rows * n
    wrows = w_qkv.shape[0]
    ff_block = w_down.shape[0]
    hc = HEADS // n * HEAD_DIM
    ffc = ff_block * zs

    def local_tokens(v):
        return jnp.transpose(v, (1, 0, 2)).reshape(local, width)

    def back_tokens(v):
        return jnp.transpose(v.reshape(slots, rows, width), (1, 0, 2))

    xs = local_tokens(inputs)
    dy = local_tokens(cotangent)
    nb = b_qkv.shape[0]
    vectors = [v for gain in (gain_one, shift_one, gain_two, shift_two) for v in (gain, gain)]
    small, at = jnp.zeros(1024, f32), 0
    for vector in (*vectors, b_qkv):
        size = vector.shape[0]
        small = small + jnp.pad(vector.astype(f32), (at, 1024 - at - size))
        at += size
    small = small.reshape(8, 128)

    angles = np.arange(seq)[:, None] * 10000.0 ** (-2.0 * np.arange(ROTARY // 2) / ROTARY)[None, :]
    cos_t, sin_t = np.cos(angles), np.sin(angles)
    zero, rest = np.zeros_like(sin_t), np.zeros((seq, HEAD_DIM - ROTARY))
    tables = np.stack(
        [
            np.concatenate(two, -1)
            for two in (
                2 * [cos_t, cos_t, rest + 1.0],
                2 * [-sin_t, zero, rest],
                2 * [zero, sin_t, rest],
            )
        ]
    ).astype(np.float32)

    tables = jnp.asarray(tables.reshape(3, n, rows, 2 * HEAD_DIM))
    w_qkv_c, w_out_c, w_gu_c, a1, qkv, probs, ob, hidden, a2, dgu, grad_down, result, norms = front(
        zs, n, slots, lengths, tables, small, w_qkv, w_gate, w_up, w_out, w_down, xs, dy
    )
    wide = (n, local, width)
    grad_out, input_grad, grad_qkv, grad_gate, grad_up, sums = backward(
        zs, n, norms, tables, a1.reshape(wide), a2.reshape(wide), dgu,
        w_gu_c.reshape(zs, n * wrows, 2 * ffc), w_qkv_c.reshape(zs, n * wrows, 3 * hc),
        w_out_c, qkv, probs, ob, hidden, dy, xs,
    )
    mine = lax.dynamic_slice_in_dim(sums[:4], me % 2 * wrows, wrows, 1)
    grad_bias = lax.dynamic_slice_in_dim(sums[4:7].reshape(2 * nb), me % 2 * nb, nb)
    return (
        back_tokens(result),
        back_tokens(input_grad),
        grad_qkv.astype(f32),
        grad_bias,
        grad_out,
        grad_gate.astype(f32),
        grad_up.astype(f32),
        grad_down,
        mine[0],
        mine[1],
        mine[2],
        mine[3],
    )


def solution(mesh):
    zs, n = mesh.shape["dp"], mesh.shape["ctx"]
    shards = tensor_shards if (zs, n) == (4, 8) and HEADS == 32 else gathered_shards

    placed = (
        P("ctx", "dp", None),
        P("dp", None),
        P(("dp", "ctx"), None),
        P(("dp", "ctx")),
        P(("dp", "ctx"), None),
        P(("dp", "ctx"), None),
        P(("dp", "ctx"), None),
        P(("dp", "ctx"), None),
        P(("dp", "ctx")),
        P(("dp", "ctx")),
        P(("dp", "ctx")),
        P(("dp", "ctx")),
        P("ctx", "dp", None),
    )
    return jax.shard_map(
        shards,
        mesh=mesh,
        in_specs=placed,
        out_specs=(
            P("ctx", "dp", None),
            P("ctx", "dp", None),
            P(("dp", "ctx"), None),
            P(("dp", "ctx")),
            P(("dp", "ctx"), None),
            P(("dp", "ctx"), None),
            P(("dp", "ctx"), None),
            P(("dp", "ctx"), None),
            P(("dp", "ctx")),
            P(("dp", "ctx")),
            P(("dp", "ctx")),
            P(("dp", "ctx")),
        ),
        check_vma=False,
    )
```

```python
import functools
import itertools
import math

import jax
import jax.numpy as jnp
import numpy as np
from jax import lax
from jax.experimental import pallas as pl
from jax.experimental.pallas import tpu as pltpu
from jax.sharding import PartitionSpec as P

HEADS = 32
HEAD_DIM = 64
ROTARY = 16


epsilon = 1e-05
masked_value = -1e30


def layer_stats(values):
    row_mean = jnp.mean(values, -1, keepdims=True)
    centred = values - row_mean
    inverse = lax.rsqrt(jnp.mean(centred * centred, -1, keepdims=True) + epsilon)
    return (centred * inverse, inverse)


def norm_back(grad_normed, scaled, inverse, gain_vec):
    grad_hat = grad_normed * gain_vec
    return inverse * (
        grad_hat
        - jnp.mean(grad_hat, -1, keepdims=True)
        - scaled * jnp.mean(grad_hat * scaled, -1, keepdims=True)
    )


def rotary_tables(positions):
    counter = jnp.arange(ROTARY // 2, dtype=jnp.float32)
    frequency = 10000.0 ** (-2.0 * counter / ROTARY)
    angles = positions.astype(jnp.float32)[:, None] * frequency[None, :]
    return (jnp.cos(angles)[:, None, None, :], jnp.sin(angles)[:, None, None, :])


def rotate(values, cos_table, sin_table):
    half_dims = ROTARY // 2
    first_half = values[..., :half_dims]
    second_half = values[..., half_dims:ROTARY]
    return jnp.concatenate(
        [
            first_half * cos_table - second_half * sin_table,
            second_half * cos_table + first_half * sin_table,
            values[..., ROTARY:],
        ],
        -1,
    )


def over_blocks(step_fn, running, gathered):
    total_rows = gathered.shape[0]
    tile_rows = math.gcd(total_rows, 512)

    def visit_block(number, current):
        block_start = number * tile_rows
        block_part = lax.dynamic_slice_in_dim(gathered, block_start, tile_rows, 0)
        return step_fn(current, block_part, block_start)

    return lax.fori_loop(0, total_rows // tile_rows, visit_block, running)


def gathered_shards(
    inputs,
    lengths,
    w_qkv,
    b_qkv,
    w_out,
    w_gate,
    w_up,
    w_down,
    gain_one,
    shift_one,
    gain_two,
    shift_two,
    cotangent,
):
    local_rows, slot_count, width = inputs.shape
    positions = lax.axis_index("ctx") * local_rows + jnp.arange(local_rows, dtype=jnp.int32)
    live_rows = positions[:, None] < lengths[0][None, :]
    live_heads = jnp.transpose(live_rows)[:, None, :, None]
    cos_table, sin_table = rotary_tables(positions)

    def allowed_mask(offset, count):
        key_pos = offset + jnp.arange(count, dtype=jnp.int32)
        causal = key_pos[None, :] <= positions[:, None]
        return causal[None, None, :, :] & live_heads

    def split_heads(block_part):
        count = block_part.shape[0]
        key_part = block_part[:, :, 0].reshape(count, slot_count, HEADS, HEAD_DIM)
        value_part = block_part[:, :, 1].reshape(count, slot_count, HEADS, HEAD_DIM)
        return (key_part, value_part)

    attn_full = (
        lax.all_gather(w_qkv, ("dp", "ctx"), axis=0, tiled=True),
        lax.all_gather(b_qkv, ("dp", "ctx"), axis=0, tiled=True),
        lax.all_gather(w_out, ("dp", "ctx"), axis=0, tiled=True),
        lax.all_gather(gain_one, ("dp", "ctx"), axis=0, tiled=True),
        lax.all_gather(shift_one, ("dp", "ctx"), axis=0, tiled=True),
    )
    qkv_full, bias_full, out_full, gain_one_full, shift_one_full = attn_full
    source = inputs.astype(jnp.float32)
    scaled_one, inverse_one = layer_stats(source)
    normed_one = (
        scaled_one * gain_one_full.astype(jnp.float32) + shift_one_full.astype(jnp.float32)
    ).astype(jnp.bfloat16)
    joined = jnp.einsum(
        "rsd,de->rse", normed_one, qkv_full, preferred_element_type=jnp.float32
    ) + bias_full.astype(jnp.float32)
    query_pre = joined[..., :width].reshape(local_rows, slot_count, HEADS, HEAD_DIM)
    key_pre = joined[..., width : 2 * width].reshape(local_rows, slot_count, HEADS, HEAD_DIM)
    queries = rotate(query_pre, cos_table, sin_table).astype(jnp.bfloat16)
    keys_rot = rotate(key_pre, cos_table, sin_table).reshape(local_rows, slot_count, width)
    key_value = jnp.stack([keys_rot, joined[..., 2 * width :]], 2).astype(jnp.bfloat16)
    block_part = lax.all_gather(key_value, "ctx", axis=0, tiled=True)
    run_peak = jnp.full((slot_count, HEADS, local_rows), masked_value, jnp.float32)
    key_part, value_part = split_heads(block_part)
    scores = (
        jnp.einsum("qshd,kshd->shqk", queries, key_part, preferred_element_type=jnp.float32) * 0.125
    )
    allowed = allowed_mask(jnp.int32(0), block_part.shape[0])
    masked = jnp.where(allowed, scores, masked_value)
    new_peak = jnp.maximum(run_peak, jnp.max(masked, -1))
    weights = jnp.where(allowed, jnp.exp(masked - new_peak[..., None]), 0.0)
    new_sum = jnp.sum(weights, -1)
    new_acc = jnp.einsum(
        "shqk,kshd->shqd",
        weights.astype(jnp.bfloat16),
        value_part,
        preferred_element_type=jnp.float32,
    )
    final_sum = jnp.maximum(new_sum, 1.0)
    log_sum = new_peak + jnp.log(final_sum)
    attended = jnp.transpose(new_acc / final_sum[..., None], (2, 0, 1, 3))
    attended_low = attended.reshape(local_rows, slot_count, width).astype(jnp.bfloat16)
    hidden_in = source + jnp.einsum(
        "rsd,de->rse", attended_low, out_full, preferred_element_type=jnp.float32
    )
    mlp_full = (
        lax.all_gather(w_gate, ("dp", "ctx"), axis=0, tiled=True),
        lax.all_gather(w_up, ("dp", "ctx"), axis=0, tiled=True),
        lax.all_gather(w_down, ("dp", "ctx"), axis=0, tiled=True),
        lax.all_gather(gain_two, ("dp", "ctx"), axis=0, tiled=True),
        lax.all_gather(shift_two, ("dp", "ctx"), axis=0, tiled=True),
    )
    gate_full, up_full, down_full, gain_two_full, shift_two_full = mlp_full
    scaled_two, inverse_two = layer_stats(hidden_in)
    normed_two = (
        scaled_two * gain_two_full.astype(jnp.float32) + shift_two_full.astype(jnp.float32)
    ).astype(jnp.bfloat16)
    gate = jnp.einsum("rsd,df->rsf", normed_two, gate_full, preferred_element_type=jnp.float32)
    upward = jnp.einsum("rsd,df->rsf", normed_two, up_full, preferred_element_type=jnp.float32)
    sigmoid = jax.nn.sigmoid(gate)
    product = (gate * sigmoid * upward).astype(jnp.bfloat16)
    result = hidden_in + jnp.einsum(
        "rsf,fd->rsd", product, down_full, preferred_element_type=jnp.float32
    )
    gate_back, up_back, down_back, gain_two_back = (
        lax.all_gather(w_gate, ("dp", "ctx"), axis=0, tiled=True),
        lax.all_gather(w_up, ("dp", "ctx"), axis=0, tiled=True),
        lax.all_gather(w_down, ("dp", "ctx"), axis=0, tiled=True),
        lax.all_gather(gain_two, ("dp", "ctx"), axis=0, tiled=True),
    )
    grad_down = jnp.einsum("rsf,rsd->fd", product, cotangent, preferred_element_type=jnp.float32)
    grad_product = jnp.einsum(
        "rsd,fd->rsf", cotangent, down_back, preferred_element_type=jnp.float32
    )
    grad_gate_act = (grad_product * upward * sigmoid * (1.0 + gate * (1.0 - sigmoid))).astype(
        jnp.bfloat16
    )
    grad_up_act = (grad_product * gate * sigmoid).astype(jnp.bfloat16)
    grad_gate = jnp.einsum(
        "rsd,rsf->df", normed_two, grad_gate_act, preferred_element_type=jnp.float32
    )
    grad_up = jnp.einsum("rsd,rsf->df", normed_two, grad_up_act, preferred_element_type=jnp.float32)
    grad_normed_two = jnp.einsum(
        "rsf,df->rsd", grad_gate_act, gate_back, preferred_element_type=jnp.float32
    ) + jnp.einsum("rsf,df->rsd", grad_up_act, up_back, preferred_element_type=jnp.float32)
    grad_gain_two = jnp.sum(grad_normed_two * scaled_two, (0, 1))
    grad_shift_two = jnp.sum(grad_normed_two, (0, 1))
    grad_hidden = cotangent.astype(jnp.float32) + norm_back(
        grad_normed_two, scaled_two, inverse_two, gain_two_back.astype(jnp.float32)
    )
    mlp_sums = (
        lax.psum_scatter(grad_gate, ("dp", "ctx"), scatter_dimension=0, tiled=True),
        lax.psum_scatter(grad_up, ("dp", "ctx"), scatter_dimension=0, tiled=True),
        lax.psum_scatter(grad_down, ("dp", "ctx"), scatter_dimension=0, tiled=True),
        lax.psum_scatter(grad_gain_two, ("dp", "ctx"), scatter_dimension=0, tiled=True),
        lax.psum_scatter(grad_shift_two, ("dp", "ctx"), scatter_dimension=0, tiled=True),
    )
    qkv_back, out_back, gain_one_back = (
        lax.all_gather(w_qkv, ("dp", "ctx"), axis=0, tiled=True),
        lax.all_gather(w_out, ("dp", "ctx"), axis=0, tiled=True),
        lax.all_gather(gain_one, ("dp", "ctx"), axis=0, tiled=True),
    )
    hidden_low = grad_hidden.astype(jnp.bfloat16)
    grad_out = jnp.einsum(
        "rsd,rse->de", attended_low, hidden_low, preferred_element_type=jnp.float32
    )
    grad_attended = jnp.einsum(
        "rse,de->rsd", hidden_low, out_back, preferred_element_type=jnp.float32
    )
    grad_heads = grad_attended.reshape(local_rows, slot_count, HEADS, HEAD_DIM).astype(jnp.bfloat16)
    delta = jnp.transpose(jnp.sum(grad_heads.astype(jnp.float32) * attended, -1), (1, 2, 0))
    key_value_all = lax.all_gather(key_value, "ctx", axis=0, tiled=True)

    def grad_parts(block_part, offset):
        key_part, value_part = split_heads(block_part)
        scores = (
            jnp.einsum("qshd,kshd->shqk", queries, key_part, preferred_element_type=jnp.float32)
            * 0.125
        )
        allowed = allowed_mask(offset, block_part.shape[0])
        probs = jnp.where(allowed, jnp.exp(scores - log_sum[..., None]), 0.0)
        grad_prob = jnp.einsum(
            "qshd,kshd->shqk", grad_heads, value_part, preferred_element_type=jnp.float32
        )
        grad_score = (probs * (grad_prob - delta[..., None])).astype(jnp.bfloat16)
        return (key_part, probs, grad_score)

    def query_step(running, block_part, offset):
        key_part, probs, grad_score = grad_parts(block_part, offset)
        return running + jnp.einsum(
            "shqk,kshd->shqd", grad_score, key_part, preferred_element_type=jnp.float32
        )

    grad_query = (
        over_blocks(
            query_step,
            jnp.zeros((slot_count, HEADS, local_rows, HEAD_DIM), jnp.float32),
            key_value_all,
        )
        * 0.125
    )
    count = local_rows * lax.axis_size("ctx")
    tile_rows = math.gcd(count, 512)

    def one_block(number):
        block_start = number * tile_rows
        block_part = lax.dynamic_slice_in_dim(key_value_all, block_start, tile_rows, 0)
        key_part, probs, grad_score = grad_parts(block_part, block_start)
        grad_key = (
            jnp.einsum("shqk,qshd->kshd", grad_score, queries, preferred_element_type=jnp.float32)
            * 0.125
        )
        grad_value = jnp.einsum(
            "shqk,qshd->kshd",
            probs.astype(jnp.bfloat16),
            grad_heads,
            preferred_element_type=jnp.float32,
        )
        return jnp.stack(
            [
                grad_key.reshape(tile_rows, slot_count, width),
                grad_value.reshape(tile_rows, slot_count, width),
            ],
            2,
        )

    blocks = lax.map(one_block, jnp.arange(count // tile_rows, dtype=jnp.int32))
    grad_key_value = lax.psum_scatter(
        blocks.reshape(count, slot_count, 2, width).astype(jnp.bfloat16),
        "ctx",
        scatter_dimension=0,
        tiled=True,
    ).astype(jnp.float32)
    grad_query_pre = rotate(jnp.transpose(grad_query, (2, 0, 1, 3)), cos_table, -sin_table)
    grad_key_pre = rotate(
        grad_key_value[:, :, 0].reshape(local_rows, slot_count, HEADS, HEAD_DIM),
        cos_table,
        -sin_table,
    )
    grad_joined = jnp.concatenate(
        [
            grad_query_pre.reshape(local_rows, slot_count, width),
            grad_key_pre.reshape(local_rows, slot_count, width),
            grad_key_value[:, :, 1],
        ],
        -1,
    ).astype(jnp.bfloat16)
    grad_qkv = jnp.einsum(
        "rsd,rse->de", normed_one, grad_joined, preferred_element_type=jnp.float32
    )
    grad_bias = jnp.sum(grad_joined.astype(jnp.float32), (0, 1))
    grad_normed_one = jnp.einsum(
        "rse,de->rsd", grad_joined, qkv_back, preferred_element_type=jnp.float32
    )
    grad_gain_one = jnp.sum(grad_normed_one * scaled_one, (0, 1))
    grad_shift_one = jnp.sum(grad_normed_one, (0, 1))
    input_grad = grad_hidden + norm_back(
        grad_normed_one, scaled_one, inverse_one, gain_one_back.astype(jnp.float32)
    )
    attn_sums = (
        lax.psum_scatter(grad_qkv, ("dp", "ctx"), scatter_dimension=0, tiled=True),
        lax.psum_scatter(grad_bias, ("dp", "ctx"), scatter_dimension=0, tiled=True),
        lax.psum_scatter(grad_out, ("dp", "ctx"), scatter_dimension=0, tiled=True),
        lax.psum_scatter(grad_gain_one, ("dp", "ctx"), scatter_dimension=0, tiled=True),
        lax.psum_scatter(grad_shift_one, ("dp", "ctx"), scatter_dimension=0, tiled=True),
    )
    return (
        result.astype(jnp.bfloat16),
        input_grad,
        attn_sums[0],
        attn_sums[1],
        attn_sums[2],
        mlp_sums[0],
        mlp_sums[1],
        mlp_sums[2],
        attn_sums[3],
        attn_sums[4],
        mlp_sums[3],
        mlp_sums[4],
    )


MESH = pl.DeviceIdType.MESH
HBM = pl.BlockSpec(memory_space=pltpu.HBM)
VMEM = pl.BlockSpec(memory_space=pltpu.VMEM)
VMEM_LIMIT = 60 << 20


def flip(index, mask):
    for bit in (1, 2, 4):
        if mask & bit:
            index = index + bit - 2 * bit * ((index // bit) % 2)
    return index


class Wires:
    def __init__(self, send, recv):
        self.send, self.recv = send, recv
        self.z, self.c = lax.axis_index("dp"), lax.axis_index("ctx")
        self.inner = (self.z == 1) | (self.z == 2)
        self.outer = (self.z == 0) | (self.z == 3)
        self.number = itertools.count()

    def put(self, src, dst, z_mask, c_mask):
        return self.put_to(src, dst, flip(self.z, z_mask), flip(self.c, c_mask))

    def put_to(self, src, dst, z, c):
        i = next(self.number)
        return pltpu.make_async_remote_copy(
            src_ref=src,
            dst_ref=dst,
            send_sem=self.send.at[i],
            recv_sem=self.recv.at[i],
            device_id=(z, c),
            device_id_type=MESH,
        )

    def greet(self, zs, n):
        barrier = pltpu.get_barrier_semaphore()
        for m in range(1, zs):
            pl.semaphore_signal(
                barrier, inc=1, device_id=(flip(self.z, m), self.c), device_id_type=MESH
            )
        for m in range(1, n):
            pl.semaphore_signal(
                barrier, inc=1, device_id=(self.z, flip(self.c, m)), device_id_type=MESH
            )
        pl.semaphore_wait(barrier, zs + n - 2)


class DepthGather:
    def __init__(self, wires, part):
        z = wires.z
        self.wires = wires
        self.near = wires.put(part(z), part(z), 1, 0)
        self.skip = wires.put(part(z), part(z), 2, 0)
        self.mid = wires.put(part(z), part(z), 3, 0)
        far = flip(z, 2)
        self.on = wires.put(part(far), part(far), 1, 0)

    @staticmethod
    def start(parts):
        for part in parts:
            part.skip.start()
        for part in parts:
            pl.when(part.wires.inner)(part.mid.start)
        for part in parts:
            part.near.start()

    def forward(self):
        @pl.when(self.wires.inner)
        def _():
            self.skip.wait_recv()
            self.on.start()

    def finish(self):
        self.near.wait_recv()
        self.near.wait_send()
        self.skip.wait_send()

        @pl.when(self.wires.inner)
        def _():
            self.mid.wait_recv()
            self.mid.wait_send()
            self.on.wait_send()

        @pl.when(self.wires.outer)
        def _():
            self.skip.wait_recv()
            self.on.wait_recv()


class LayerGather:
    def __init__(self, wires, block, source=None):
        c = wires.c
        mine = block(c) if source is None else source
        self.direct = {m: wires.put(mine, block(c), 0, m) for m in (2, 4, 6, 1)}
        self.on = {m: wires.put(block(flip(c, m)), block(flip(c, m)), 0, 1) for m in (2, 4, 6)}

    def start(self):
        for m in (2, 4, 6, 1):
            self.direct[m].start()

    def forward(self, m):
        self.direct[m].wait_recv()
        self.on[m].start()

    def arrived(self, m):
        (self.direct[1] if m == 1 else self.on[m - 1]).wait_recv()

    def sent(self):
        for copy in (*self.direct.values(), *self.on.values()):
            copy.wait_send()


def pack_columns(dst, refs, n, zs):
    for i in range(n):
        pieces = []
        for ref, block, at, size in refs:
            starts = [block * (j * n + i) + at for j in range(zs)]
            pieces += [ref[:, start : start + size] for start in starts]
        dst[i] = jnp.concatenate(pieces, -1)


class LayerScatter:
    def __init__(self, wires, part, near, far):
        c = wires.c
        self.c, self.part, self.near, self.far = c, part, near, far
        self.pair = {
            m: wires.put(part(flip(c, m + 1)), near(m // 2), 0, 1) for m in (6, 4, 2, 0)
        }
        self.chips = {m: wires.put(part(flip(c, m)), far(m // 2 - 1), 0, m) for m in (6, 4, 2)}

    def start(self):
        for copy in self.pair.values():
            copy.start()

    def step(self, m):
        self.pair[m].wait_recv()
        to = self.part(flip(self.c, m))
        to[...] = (
            to[...].astype(jnp.float32) + self.near(m // 2)[...].astype(jnp.float32)
        ).astype(to.dtype)
        self.chips[m].start()

    def total(self):
        self.pair[0].wait_recv()
        result = self.part(self.c)[...].astype(jnp.float32)
        result = result + self.near(0)[...].astype(jnp.float32)
        for m in (2, 4, 6):
            self.chips[m].wait_recv()
            result = result + self.far(m // 2 - 1)[...].astype(jnp.float32)
        return result

    def sent(self):
        for copy in (*self.pair.values(), *self.chips.values()):
            copy.wait_send()


def dot(a, b, dims=((1,), (0,))):
    return lax.dot_general(a, b, (dims, ((), ())), preferred_element_type=jnp.float32)


def turn_pair(values, table, sign):
    half = ROTARY // 2
    columns = values.shape[-1]
    table = [jnp.concatenate([t] * (columns // t.shape[-1]), -1) for t in table]
    return (
        values * table[0]
        + sign * (pltpu.roll(values, columns - half, 1) * table[1])
        + sign * (pltpu.roll(values, half, 1) * table[2])
    )


def head_mask(rows, columns, head):
    return lax.broadcasted_iota(jnp.int32, (rows, columns), 1) // HEAD_DIM == head


class DepthScatter:
    def __init__(self, wires, part, relay, boxes):
        z = wires.z
        self.wires, self.part, self.relay_box, self.boxes = wires, part, relay, boxes
        self.far = wires.put(part(flip(z, 3)), relay, 1, 0)
        self.skip = wires.put(part(flip(z, 2)), boxes[1], 2, 0)
        self.near = wires.put(part(flip(z, 1)), boxes[0], 1, 0)
        self.mid = wires.put(part(flip(z, 3)), boxes[2], 3, 0)

    def start(self, mask):
        outer, inner = pl.when(self.wires.outer), pl.when(self.wires.inner)
        if mask == 3:
            outer(self.far.start)
            inner(self.mid.start)
        elif mask == 2:
            outer(self.skip.start)
        elif mask == 1:
            self.near.start()
        else:

            @outer
            def _():
                self.boxes[2][...] = jnp.zeros_like(self.boxes[2])

    def relay(self):
        @pl.when(self.wires.inner)
        def _():
            self.far.wait_recv()
            to = self.part(flip(self.wires.z, 2))
            to[...] = (
                to[...].astype(jnp.float32) + self.relay_box[...].astype(jnp.float32)
            ).astype(to.dtype)
            self.skip.start()

    def total(self):
        self.near.wait_recv()
        self.skip.wait_recv()
        pl.when(self.wires.inner)(self.mid.wait_recv)
        result = self.part(self.wires.z)[...].astype(jnp.float32)
        for box in self.boxes:
            result = result + box[...].astype(jnp.float32)
        return result

    def sent(self):
        self.near.wait_send()
        self.skip.wait_send()
        pl.when(self.wires.outer)(self.far.wait_send)
        pl.when(self.wires.inner)(self.mid.wait_send)


class Moves:
    def __init__(self, sems):
        self.sems, self.number, self.stores = sems, itertools.count(), []

    def load(self, src, dst):
        copy = pltpu.make_async_copy(src, dst, self.sems.at[next(self.number)])
        copy.start()
        return copy

    def store(self, src, dst):
        self.stores.append(self.load(src, dst))

    def finish(self):
        for copy in self.stores:
            copy.wait()


def pieces_of(total, number, unit):
    units = total // unit
    cuts = [units * i // number * unit for i in range(number + 1)]
    return [(a, b - a) for a, b in zip(cuts[:-1], cuts[1:])]


class ChainGather:
    def __init__(self, wires, part):
        self.z = z = wires.z
        self.right = [
            wires.put_to(part((z - s + 4) % 4), part((z - s + 4) % 4), (z + 1) % 4, wires.c)
            for s in range(3)
        ]
        self.left = [
            wires.put_to(part((z + s) % 4), part((z + s) % 4), (z + 3) % 4, wires.c)
            for s in range(3)
        ]

    def start(self):
        pl.when(self.z <= 2)(self.right[0].start)
        pl.when(self.z >= 1)(self.left[0].start)

    def hop(self, s):
        pl.when(self.z >= s)(self.right[s - 1].wait_recv)
        pl.when((self.z >= s) & (self.z <= 2))(self.right[s].start)
        pl.when(self.z <= 3 - s)(self.left[s - 1].wait_recv)
        pl.when((self.z <= 3 - s) & (self.z >= 1))(self.left[s].start)

    def finish(self):
        pl.when(self.z >= 3)(self.right[2].wait_recv)
        pl.when(self.z <= 0)(self.left[2].wait_recv)
        for s in range(3):
            pl.when((self.z >= s) & (self.z <= 2))(self.right[s].wait_send)
            pl.when((self.z <= 3 - s) & (self.z >= 1))(self.left[s].wait_send)


class ChainScatter:
    def __init__(self, wires, part, right, left):
        self.z = z = wires.z
        self.part, self.right_box, self.left_box = part, right, left
        self.right = {
            j: wires.put_to(part(j), right(j), (z + 1) % 4, wires.c) for j in (3, 2, 1)
        }
        self.left = {j: wires.put_to(part(j), left(j), (z + 3) % 4, wires.c) for j in (0, 1, 2)}

    def clear(self):
        @pl.when(self.z == 0)
        def _():
            self.right_box(1)[...] = jnp.zeros_like(self.right_box(1))

        @pl.when(self.z == 3)
        def _():
            self.left_box(2)[...] = jnp.zeros_like(self.left_box(2))

    def start(self, distance):
        pl.when(self.z == 0)(self.right[distance].start)
        pl.when(self.z == 3)(self.left[3 - distance].start)

    def pass_on(self, copy, j, box):
        copy.wait_recv()
        to = self.part(j)
        to[...] = (to[...].astype(jnp.float32) + box(j)[...].astype(jnp.float32)).astype(to.dtype)
        copy.start()

    def hop(self, s, distance):
        @pl.when(self.z == s)
        def _():
            self.pass_on(self.right[distance], distance, self.right_box)

        @pl.when(self.z == 3 - s)
        def _():
            self.pass_on(self.left[3 - distance], 3 - distance, self.left_box)

    def total(self):
        for j in (1, 2, 3):
            pl.when(self.z == j)(self.right[j].wait_recv)
        for j in (0, 1, 2):
            pl.when(self.z == j)(self.left[j].wait_recv)
        z = self.z
        return (
            self.part(z)[...].astype(jnp.float32)
            + self.right_box(jnp.maximum(z, 1))[...].astype(jnp.float32)
            + self.left_box(jnp.minimum(z, 2))[...].astype(jnp.float32)
        )

    def sent(self):
        for j in (1, 2, 3):
            pl.when(self.z < j)(self.right[j].wait_send)
        for j in (0, 1, 2):
            pl.when(self.z > j)(self.left[j].wait_send)


def halves_of(block):
    first = (block // 16 + 1) // 2 * 16
    return [(0, first), (first, block - first)]


def front_kernel(
    zs,
    n,
    slots,
    lengths,
    tables,
    small,
    w_qkv,
    w_gate,
    w_up,
    w_out,
    w_down,
    xs,
    dy,
    w_qkv_out,
    w_out_out,
    w_gu_out,
    a1_out,
    qkv_out,
    probs_out,
    ob_out,
    hidden_out,
    a2_out,
    dgu_out,
    y_out,
    grad_down_out,
    norms,
    qkv_send,
    gu_send,
    small_v,
    bias_v,
    w_qkv_v,
    w_out_v,
    w_gu_v,
    w_down_v,
    wide_x,
    wide_a,
    dy_v,
    qkv_v,
    probs_v,
    ob_v,
    near,
    far,
    hidden_v,
    gu_v,
    zz_v,
    dz_v,
    gd_v,
    right_v,
    left_v,
    send,
    recv,
    local,
):
    f32, b16 = jnp.float32, jnp.bfloat16
    wires = Wires(send, recv)
    moves = Moves(local)
    z, c = wires.z, wires.c
    local_rows, width = xs.shape
    rows = local_rows // slots
    tokens, seq = n * local_rows, n * rows
    pair = 2 * local_rows
    hc = qkv_v.shape[-1]
    heads = hc // HEAD_DIM
    block = w_down_v.shape[1]
    ffc = zs * block
    halves = halves_of(block)
    spans = [(2 * zs * at, zs * size) for at, size in halves]
    lanes = 2 * HEAD_DIM
    lane_half = lax.broadcasted_iota(jnp.int32, (1, lanes), 1) // HEAD_DIM

    def block_of(ref, i):
        return ref.at[pl.ds(pl.multiple_of(i * local_rows, local_rows), local_rows)]

    def pair_at(i):
        return pl.ds(pl.multiple_of(i * pair, pair), pair)

    wait_out = moves.load(w_out, w_out_v.at[z])
    wait_small = moves.load(small, small_v.at[z, c])
    wait_xs = moves.load(xs, block_of(wide_x, c))
    wait_dy = moves.load(dy, dy_v.at[c])
    wait_down = moves.load(w_down, w_down_v.at[z])
    pack_columns(
        qkv_send,
        [(w_qkv.at[:, i * width : (i + 1) * width], HEAD_DIM, 0, HEAD_DIM) for i in range(3)],
        n,
        zs,
    )
    wait_own_qkv = moves.load(qkv_send.at[c], w_qkv_v.at[z, c])
    wires.greet(zs, n)
    wait_out.wait()
    wait_small.wait()
    out_z = DepthGather(wires, lambda i: w_out_v.at[i])
    DepthGather.start([out_z])
    qkv_x = [wires.put(qkv_send.at[flip(c, m)], w_qkv_v.at[z, c], 0, m) for m in range(1, n)]
    for copy in qkv_x:
        copy.start()
    small_z = [wires.put(small_v.at[z, c], small_v.at[z, c], m, 0) for m in range(1, zs)]
    for copy in small_z:
        copy.start()
    xs_g = LayerGather(wires, lambda i: block_of(wide_x, i), xs)
    xs_g.start()
    pack_columns(
        gu_send, [(w, block, at, size) for at, size in halves for w in (w_gate, w_up)], n, zs
    )
    wait_own_gu = moves.load(gu_send.at[c], w_gu_v.at[z, c])
    for copy in small_z:
        copy.wait_recv()
    small_x = [wires.put(small_v.at[:, c], small_v.at[:, c], 0, m) for m in range(1, n)]
    for copy in small_x:
        copy.start()
    wait_own_qkv.wait()
    for copy in qkv_x:
        copy.wait_recv()
    number = 4
    qkv_z = [
        DepthGather(wires, lambda i, a=a, s=s: w_qkv_v.at[i, a : a + s])
        for a, s in pieces_of(n, number, 1)
    ]
    DepthGather.start(qkv_z)
    gu_x = [wires.put(gu_send.at[flip(c, m)], w_gu_v.at[z, c], 0, m) for m in range(1, n)]
    for copy in gu_x:
        copy.start()
    out_z.forward()
    for m in (2, 4, 6):
        xs_g.forward(m)

    for copy in small_x:
        copy.wait()
    for r in range(4):
        norms[r : r + 1] = jnp.concatenate(
            [
                jnp.where(
                    lane_half == 0,
                    small_v[d // n, d % n, r : r + 1],
                    small_v[d // n, d % n + 1, r : r + 1],
                )
                for d in range(0, zs * n, 2)
            ],
            -1,
        )
    norms[4:8] = jnp.zeros_like(norms[4:8])
    per_owner = 3 * zs * n // (zs * n)
    for i in range(3):
        for j in range(0, zs, 2):
            both = []
            for h in range(2):
                group = i * zs * n + (j + h) * n + c
                owner, k = group // per_owner, group % per_owner
                tile = small_v[owner // n, owner % n]
                row = jnp.where(k == 2, tile[5:6], tile[4:5])
                both.append(jnp.where(k % 2 == h, row, pltpu.roll(row, HEAD_DIM, 1)))
            at = (i * zs + j) * HEAD_DIM
            bias_v[:, at : at + lanes] = jnp.where(lane_half == 0, both[0], both[1])

    for m in (1, 3, 5, 7):
        xs_g.arrived(m)
    wait_xs.wait()
    hidden_v[...] = block_of(wide_x, c)[...].astype(f32)

    def norm_one(i, carry):
        x = wide_x[pair_at(i)].astype(f32)
        wide_a[pair_at(i)] = (layer_stats(x)[0] * norms[0:1] + norms[1:2]).astype(b16)
        return carry

    lax.fori_loop(0, n // 2, norm_one, 0)
    wait_a1 = moves.load(wide_a, a1_out)
    wait_own_gu.wait()
    for copy in gu_x:
        copy.wait_recv()
    gu_z = [
        [
            DepthGather(
                wires, lambda i, a=a, s=s, k=slice(at, at + 2 * size): w_gu_v.at[i, a : a + s, :, k]
            )
            for a, s in pieces_of(n, number, 1)
        ]
        for at, size in spans
    ]
    for part in qkv_z:
        part.forward()
    for part in gu_z:
        DepthGather.start(part)
    wait_dy.wait()
    dy_g = LayerGather(wires, lambda i: dy_v.at[i])
    dy_g.start()
    for part in (out_z, *qkv_z):
        part.finish()
    moves.store(w_qkv_v, w_qkv_out)
    moves.store(w_out_v, w_out_out)

    def project(i, carry):
        joined = dot(wide_a[pair_at(i)], w_qkv_v[...].reshape(width, 3 * hc)) + bias_v[...]
        for j in range(2):
            table = [tables[k, 2 * i + j] for k in range(3)]
            for s in range(slots):
                at = (j * slots + s) * rows
                piece = joined[at : at + rows]
                qkv_v[0, s, 2 * i + j] = turn_pair(piece[:, :hc], table, 1.0).astype(b16)
                qkv_v[1, s, 2 * i + j] = turn_pair(piece[:, hc : 2 * hc], table, 1.0).astype(b16)
                qkv_v[2, s, 2 * i + j] = piece[:, 2 * hc :].astype(b16)
        return carry

    lax.fori_loop(0, n // 2, project, 0)
    moves.store(qkv_v, qkv_out)
    for m in (2, 4, 6):
        dy_g.forward(m)

    half = seq // 2
    probs_sem = moves.sems.at[next(moves.number)]

    def attend(s, carry):
        q, k, v = [qkv_v[i, s].reshape(seq, hc) for i in range(3)]
        length = lengths[0, s]
        kept = pltpu.make_async_copy(probs_v, probs_out.at[s], probs_sem)
        for part_q in range(2):
            keys = (part_q + 1) * half
            at = part_q * half
            query = q[at : at + half]
            row = lax.broadcasted_iota(jnp.int32, (half, keys), 0) + at
            key = lax.broadcasted_iota(jnp.int32, (half, keys), 1)
            allowed = (key <= row) & (row < length)
            out = jnp.zeros((half, hc), f32)
            for h in range(heads):
                mask = head_mask(half, hc, h)
                scores = dot(jnp.where(mask, query, 0).astype(b16), k[:keys], ((1,), (1,)))
                scores = jnp.where(allowed, scores * 0.125, masked_value)
                peak = jnp.max(scores, -1, keepdims=True)
                weights = jnp.where(allowed, jnp.exp(scores - peak), 0.0)
                total = jnp.maximum(jnp.sum(weights, -1, keepdims=True), 1.0)
                probs = (weights * (1.0 / total)).astype(b16)
                probs_v[h, at : at + half, 0:keys] = probs
                if keys < seq:
                    probs_v[h, at : at + half, keys:seq] = jnp.zeros((half, seq - keys), b16)
                out = jnp.where(mask, dot(probs, v[:keys]), out)
            ob_v[part_q * n // 2 : (part_q + 1) * n // 2, s] = out.astype(b16).reshape(
                n // 2, rows, hc
            )
        kept.start()
        kept.wait()
        return carry

    lax.fori_loop(0, slots, attend, 0)
    moves.store(ob_v, ob_out)
    for part in gu_z[0][:2]:
        part.forward()

    xs_g.sent()

    def to_hidden(i, carry):
        block_of(wide_x, i)[...] = dot(
            ob_v[i].reshape(local_rows, hc), w_out_v[...].reshape(hc, width)
        ).astype(b16)
        return carry

    lax.fori_loop(0, n, to_hidden, 0)
    wait_a1.wait()
    sums = LayerScatter(
        wires, lambda i: block_of(wide_x, i), lambda j: near.at[j], lambda j: far.at[j]
    )
    sums.start()
    for m in (6, 4, 2):
        sums.step(m)
    for part in gu_z[0][2:]:
        part.forward()
    hidden = hidden_v[...] + sums.total()
    hidden_v[...] = hidden
    moves.store(hidden_v, hidden_out)
    block_of(wide_a, c)[...] = (layer_stats(hidden)[0] * norms[2:3] + norms[3:4]).astype(b16)
    a2_g = LayerGather(wires, lambda i: block_of(wide_a, i))
    a2_g.start()
    gu_z[1][0].forward()
    for m in (2, 4, 6):
        a2_g.forward(m)
    for part in gu_z[1][1:]:
        part.forward()
    wait_down.wait()
    tile = width // number
    columns = [slice(p * tile, (p + 1) * tile) for p in range(number)]
    down_z = [ChainGather(wires, lambda i, k=k: w_down_v.at[i, :, k]) for k in columns]
    for chain in down_z:
        chain.start()
    for m in (1, 3, 5, 7):
        dy_g.arrived(m)
    for m in (1, 3, 5, 7):
        a2_g.arrived(m)
    wait_a2 = moves.load(wide_a, a2_out)

    down_sums = []
    for step, ((at, size), (start, count), parts) in enumerate(zip(halves, spans, gu_z)):
        units, gates = slice(at, at + size), slice(start, start + 2 * count)
        inner = slice(zs * at, zs * (at + size))
        for part in parts:
            part.finish()

        def feed(i, carry, inner=inner, gates=gates, count=count):
            gu = dot(wide_a[pair_at(i)], w_gu_v[:, :, :, gates].reshape(width, 2 * count))
            gu_v[i, :, gates] = gu.astype(b16)
            gate = gu[:, :count]
            zz_v[i, :, inner] = (gate * jax.nn.sigmoid(gate) * gu[:, count:]).astype(b16)
            return carry

        lax.fori_loop(0, n // 2, feed, 0)
        if step == 1:
            down_z[0].hop(1)
            down_z[1].hop(1)
        chains = []
        for p in range(2):
            k = slice(p * width // 2, (p + 1) * width // 2)
            for q in columns[2 * p : 2 * p + 2]:
                gd = dot(
                    zz_v[:, :, inner].reshape(tokens, count),
                    dy_v[:, :, q].reshape(tokens, tile),
                    ((0,), (0,)),
                )
                gd_v[:, units, q] = gd.astype(b16).reshape(zs, size, tile)
            chains.append(
                ChainScatter(
                    wires,
                    lambda i, u=units, k=k: gd_v.at[i, u, k],
                    lambda i, u=units, k=k: right_v.at[i - 1, u, k],
                    lambda i, u=units, k=k: left_v.at[i, u, k],
                )
            )
            chains[-1].start(3)
            down_sums.append((units, k, chains[-1]))
            if step == 1:
                down_z[2 + p].hop(1)
                down_z[p].hop(2)
        for distance in (2, 1):
            for chain in chains:
                chain.start(distance)
        for chain in chains:
            chain.clear()
    moves.store(w_gu_v, w_gu_out)
    sums.sent()
    a2_g.sent()
    wait_a2.wait()

    def products(p):
        k = columns[p]

        def rows_of(i, carry):
            dy_rows = dy_v[pl.ds(2 * i, 2), :, k].reshape(pair, tile)
            y = jnp.zeros((pair, tile), f32)
            for at, size in halves:
                weight = w_down_v[:, at : at + size, k].reshape(zs * size, tile)
                inner = slice(zs * at, zs * (at + size))
                dz = dot(dy_rows, weight, ((1,), (1,)))
                dz_v[i, :, inner] = dz if p == 0 else dz_v[i, :, inner] + dz
                y = y + dot(zz_v[i, :, inner], weight)
            wide_x[pair_at(i), k] = y.astype(b16)
            return carry

        lax.fori_loop(0, n // 2, rows_of, 0)

    down_z[2].hop(2)
    down_z[3].hop(2)
    chains = [chain for _, _, chain in down_sums]
    for t in range(number):
        chains[t].hop(1, 3)
        down_z[t].finish()
        products(t)
    moves.store(wide_x, y_out)
    for pair_of in (chains[:2], chains[2:]):
        for chain in pair_of:
            chain.hop(1, 2)
        for chain in pair_of:
            chain.hop(2, 3)

    def back(i, carry):
        for (at, size), (start, count) in zip(halves, spans):
            dz = dz_v[i, :, zs * at : zs * (at + size)]
            gate = gu_v[i, :, start : start + count].astype(f32)
            up = gu_v[i, :, start + count : start + 2 * count].astype(f32)
            sig = jax.nn.sigmoid(gate)
            dg = dz * up * sig * (1.0 + gate * (1.0 - sig))
            du = dz * gate * sig
            gu_v[i, :, start : start + 2 * count] = jnp.concatenate([dg, du], -1).astype(b16)
        return carry

    lax.fori_loop(0, n // 2, back, 0)
    moves.store(gu_v, dgu_out)
    for units, k, chain in down_sums:
        grad_down_out[units, k] = chain.total()
    for group in (*chains, dy_g):
        group.sent()
    for copy in (*small_z, *qkv_x, *gu_x):
        copy.wait_send()
    moves.finish()


def front(zs, n, slots, lengths, tables, small, w_qkv, w_gate, w_up, w_out, w_down, xs, dy):
    f32, b16 = jnp.float32, jnp.bfloat16
    local, width = xs.shape
    rows = local // slots
    seq, tokens = rows * n, local * n
    heads = HEADS // n
    hc = heads * HEAD_DIM
    wrows = w_out.shape[0]
    block = w_down.shape[0]
    gc = 2 * zs * block
    qkv_all = ((zs, n, wrows, 3 * hc), b16)
    out_all = ((zs, wrows, width), b16)
    gu_all = ((zs, n, wrows, gc), b16)
    down_all = ((zs, block, width), b16)
    wide = ((tokens, width), b16)
    qkv = ((3, slots, n, rows, hc), b16)
    probs = ((slots, heads, seq, seq), b16)
    ob = ((n, slots, rows, hc), b16)
    hidden = ((local, width), f32)
    gu = ((n // 2, 2 * local, gc), b16)
    outs = [
        qkv_all,
        out_all,
        gu_all,
        wide,
        qkv,
        probs,
        ob,
        hidden,
        wide,
        gu,
        wide,
        ((block, width), f32),
        ((8, width), f32),
    ]
    scratch = [
        ((n, wrows, 3 * hc), b16),
        ((n, wrows, gc), b16),
        ((zs, n, *small.shape), f32),
        ((1, 3 * hc), f32),
        qkv_all,
        out_all,
        gu_all,
        down_all,
        wide,
        wide,
        ((n, local, width), b16),
        qkv,
        (probs[0][1:], b16),
        ob,
        ((n // 2, local, width), b16),
        ((n // 2 - 1, local, width), b16),
        hidden,
        gu,
        ((n // 2, 2 * local, gc // 2), b16),
        ((n // 2, 2 * local, gc // 2), f32),
        down_all,
        ((zs - 1, block, width), b16),
        ((zs - 1, block, width), b16),
    ]
    return pl.pallas_call(
        functools.partial(front_kernel, zs, n, slots),
        out_shape=[jax.ShapeDtypeStruct(*k) for k in outs],
        in_specs=[pl.BlockSpec(memory_space=pltpu.SMEM), VMEM, HBM, *[VMEM] * 3, *[HBM] * 4],
        out_specs=[HBM] * (len(outs) - 2) + [VMEM] * 2,
        scratch_shapes=[
            *[pltpu.VMEM(*k) for k in scratch],
            pltpu.SemaphoreType.DMA((192,)),
            pltpu.SemaphoreType.DMA((192,)),
            pltpu.SemaphoreType.DMA((32,)),
        ],
        compiler_params=pltpu.CompilerParams(
            collective_id=1, has_side_effects=True, vmem_limit_bytes=VMEM_LIMIT
        ),
        name="front",
    )(lengths, tables, small, w_qkv, w_gate, w_up, w_out, w_down, xs, dy)


def unpack_columns(dst, src, parts, n, zs):
    dst[...] = jnp.concatenate(
        [
            src[i, :, at + size * j : at + size * (j + 1)]
            for j in range(zs)
            for i in range(n)
            for at, size in parts
        ],
        -1,
    )


def backward_kernel(
    zs,
    n,
    norms,
    tables,
    a1_all,
    a2_all,
    dgu,
    w_gu,
    w_qkv,
    w_out,
    qkv,
    probs,
    ob,
    hidden,
    dy,
    xs,
    y_part,
    grad_out_out,
    result_out,
    input_grad_out,
    gq_out,
    gate_out,
    up_out,
    small_out,
    wide_v,
    dgu_v,
    weight_v,
    w_out_v,
    qkv_v,
    probs_v,
    ob_v,
    hidden_v,
    own_v,
    ggu_v,
    relay_v,
    box_v,
    near,
    far,
    dh_all,
    go_v,
    go_relay,
    go_box,
    dqkv_v,
    dj_v,
    bias_v,
    gq_relay,
    gq_box,
    gu_rows,
    gq_rows,
    small_v,
    small_x,
    small_r,
    small_z,
    send,
    recv,
    local,
    free,
):
    f32, b16 = jnp.float32, jnp.bfloat16
    wires = Wires(send, recv)
    moves = Moves(local)
    z, c = wires.z, wires.c
    _, slots, rows, hc = ob_v.shape
    width = dh_all.shape[-1]
    tokens, seq, local_rows = n * slots * rows, n * rows, slots * rows
    heads = hc // HEAD_DIM
    depth, gc = ggu_v.shape[1:]
    ffc, qc = gc // 2, 3 * hc
    wrows = depth // n
    part = wide_v
    gu_weight = weight_v.at[:, :, 0:gc]
    qkv_weight, gq_v = weight_v.at[:, :, 0:qc], weight_v.at[:, :, qc : 2 * qc]

    wait_a2 = moves.load(a2_all, wide_v)
    wait_dgu = moves.load(dgu, dgu_v)
    wait_w = moves.load(w_gu, gu_weight)
    waits = [
        moves.load(hidden, hidden_v),
        moves.load(dy, own_v),
        moves.load(w_out, w_out_v),
        moves.load(qkv, qkv_v),
        moves.load(probs.at[0], probs_v),
        moves.load(ob, ob_v),
    ]
    wires.greet(zs, n)
    wait_a2.wait()
    wait_dgu.wait()

    number = 4
    size = depth // number
    step = 2 * size

    def scatters(whole, relay, box):
        return [
            DepthScatter(
                wires,
                lambda i, a=p * size: whole.at[i, a : a + size],
                relay.at[p * size : (p + 1) * size],
                [box.at[j, p * size : (p + 1) * size] for j in range(3)],
            )
            for p in range(number)
        ]

    def weigh(sums, whole, left_v, grads, also=None):
        for mask in (3, 2, 1, 0):
            to = flip(z, mask)

            def piece(p, carry, to=to):
                at = pl.multiple_of(to * depth + p * step, step)
                left = left_v[:, :, pl.ds(at, step)].reshape(tokens, step)
                whole[to, pl.ds(pl.multiple_of(p * step, step), step)] = dot(
                    left, grads(), ((0,), (0,))
                ).astype(b16)
                return carry

            lax.fori_loop(0, number // 2, piece, 0)
            for part_sum in sums:
                part_sum.start(mask)
            if mask == 3 and also is not None:
                also.start(3)

    gu_sums = scatters(ggu_v, relay_v, box_v)
    weigh(gu_sums, ggu_v, wide_v, lambda: dgu_v[...].reshape(tokens, gc))

    wait_w.wait()

    def normed_two(i, carry):
        part[pl.ds(2 * i, 2)] = (
            dot(dgu_v[i], gu_weight[...].reshape(width, gc), ((1,), (1,)))
            .astype(b16)
            .reshape(2, local_rows, width)
        )
        return carry

    lax.fori_loop(0, n // 2, normed_two, 0)
    wait_qkv = moves.load(w_qkv, qkv_weight)
    da2_sums = LayerScatter(
        wires, lambda i: part.at[i], lambda j: near.at[j], lambda j: far.at[j]
    )
    da2_sums.start()
    gu_sums[0].relay()
    for m in (6, 4, 2):
        da2_sums.step(m)
    for copy in waits:
        copy.wait()
    n2, r2 = layer_stats(hidden_v[...])
    for part_sum in gu_sums[1:]:
        part_sum.relay()
    da2 = da2_sums.total()
    gains = [jnp.sum(da2 * n2, 0, keepdims=True), jnp.sum(da2, 0, keepdims=True)]
    dh = own_v[...].astype(f32) + norm_back(da2, n2, r2, norms[2:3])
    input_grad_out[...] = dh
    dh_all[c] = dh.astype(b16)
    wait_xs = moves.load(xs, own_v)
    dh_g = LayerGather(wires, lambda i: dh_all.at[i])
    dh_g.start()
    for m in (2, 4, 6):
        dh_g.forward(m)
    for m in (1, 3, 5, 7):
        dh_g.arrived(m)

    go_sums = DepthScatter(
        wires, lambda i: go_v.at[i], go_relay, [go_box.at[j] for j in range(3)]
    )
    tile = width // 4

    def heads_grad(p, carry):
        at = pl.ds(pl.multiple_of(p * tile, tile), tile)
        go = dot(
            ob_v[...].reshape(tokens, hc), dh_all[:, :, at].reshape(tokens, tile), ((0,), (0,))
        )
        go_v[:, :, at] = go.astype(b16).reshape(zs, hc // zs, tile)
        return carry

    lax.fori_loop(0, 4, heads_grad, 0)

    def heads_back(i, carry):
        ob_v[i] = (
            dot(dh_all[i], w_out_v[...].reshape(hc, width), ((1,), (1,)))
            .astype(b16)
            .reshape(slots, rows, hc)
        )
        return carry

    lax.fori_loop(0, n, heads_back, 0)
    dh_g.sent()
    wait_a1 = moves.load(a1_all, dh_all)
    half = seq // 2

    def attend(s, carry):
        q, k, v = [qkv_v[i, s].reshape(seq, hc) for i in range(3)]
        do_s = ob_v[:, s].reshape(seq, hc)
        dqkv_v[...] = jnp.zeros_like(dqkv_v)
        for part_q in range(2):
            keys = (part_q + 1) * half
            at = part_q * half
            query, do_q = q[at : at + half], do_s[at : at + half]
            dq = jnp.zeros((half, hc), f32)
            for h in range(heads):
                mask, mask_k = head_mask(half, hc, h), head_mask(keys, hc, h)
                do_h = jnp.where(mask, do_q, 0).astype(b16)
                low = probs_v[h, at : at + half, 0:keys]
                p32 = low.astype(f32)
                t = p32 * dot(do_h, v[:keys], ((1,), (1,)))
                ds = (t - p32 * jnp.sum(t, -1, keepdims=True)).astype(b16)
                dq = jnp.where(mask, dot(ds, k[:keys]), dq)
                dk = dot(ds, query, ((0,), (0,)))
                dv = dot(low, do_h, ((0,), (0,)))
                dqkv_v[1, 0:keys] += jnp.where(mask_k, dk, 0.0)
                dqkv_v[2, 0:keys] += dv
            dqkv_v[0, at : at + half] = dq

        @pl.when(s + 1 < slots)
        def _():
            copy = pltpu.make_async_copy(probs.at[s + 1], probs_v, probs_sem)
            copy.start()
            copy.wait()

        dq, dk = dqkv_v[0] * 0.125, dqkv_v[1] * 0.125
        table = [tables[i].reshape(seq, 2 * HEAD_DIM) for i in range(3)]
        dj = [turn_pair(dq, table, -1.0), turn_pair(dk, table, -1.0), dqkv_v[2]]
        for i in range(3):
            low = dj[i].astype(b16)
            dj_v[:, s, :, i * hc : (i + 1) * hc] = low.reshape(n, rows, hc)
            bias_v[:, i * hc : (i + 1) * hc] += jnp.sum(low.astype(f32), 0, keepdims=True)
        return carry

    bias_v[...] = jnp.zeros_like(bias_v)

    probs_sem = moves.sems.at[next(moves.number)]
    lax.fori_loop(0, slots, attend, 0)

    wait_a1.wait()
    wait_qkv.wait()
    qkv_sums = scatters(gq_v, gq_relay, gq_box)
    weigh(qkv_sums, gq_v, dh_all, lambda: dj_v[...].reshape(tokens, qc), go_sums)
    for mask in (2, 1, 0):
        go_sums.start(mask)

    def normed_one(i, carry):
        part[pl.ds(2 * i, 2)] = (
            dot(
                dj_v[pl.ds(2 * i, 2)].reshape(2 * local_rows, qc),
                qkv_weight[...].reshape(width, qc),
                ((1,), (1,)),
            )
            .astype(b16)
            .reshape(2, local_rows, width)
        )
        return carry

    da2_sums.sent()
    lax.fori_loop(0, n // 2, normed_one, 0)
    da1_sums = LayerScatter(
        wires, lambda i: part.at[i], lambda j: near.at[j], lambda j: far.at[j]
    )
    da1_sums.start()
    for m in (6, 4, 2):
        da1_sums.step(m)

    for p, part_sum in enumerate(gu_sums):
        ggu_v[z, p * size : (p + 1) * size] = part_sum.total().astype(b16)
    gu_x = [
        wires.put(
            ggu_v.at[z, pl.ds(pl.multiple_of(flip(c, m) * wrows, wrows), wrows)],
            gu_rows.at[c],
            0,
            m,
        )
        for m in range(1, n)
    ]
    for copy in gu_x:
        copy.start()
    gu_rows[c] = ggu_v[z, pl.ds(pl.multiple_of(c * wrows, wrows), wrows)]

    for part_sum in qkv_sums:
        part_sum.relay()
    go_sums.relay()

    wait_xs.wait()
    n1, r1 = layer_stats(own_v[...].astype(f32))
    da1 = da1_sums.total()
    for m in (1, 2, 4, 6):
        pl.semaphore_signal(free, inc=1, device_id=(z, flip(c, m)), device_id_type=MESH)
    da1_sums.sent()
    wait_y = moves.load(y_part, part)
    input_grad_out[...] += norm_back(da1, n1, r1, norms[0:1])
    gains = [jnp.sum(da1 * n1, 0, keepdims=True), jnp.sum(da1, 0, keepdims=True), *gains]
    chips = n // 2
    lanes = 2 * HEAD_DIM
    lane_half = lax.broadcasted_iota(jnp.int32, (1, lanes), 1) // HEAD_DIM
    bias_part = bias_v[...]
    for j in range(zs):
        for chip in range(chips):
            k = j * chips + chip
            for r in range(4):
                small_v[j, chip, r : r + 1] = gains[r][:, k * lanes : (k + 1) * lanes]
            small_v[j, chip, 7:8] = jnp.zeros((1, lanes), f32)
    for i in range(3):
        for j in range(zs):
            at = i * hc + j * HEAD_DIM
            piece = bias_part[:, at : at + HEAD_DIM]
            both = jnp.concatenate([piece, piece], -1)
            for chip in range(chips):
                tile = (i * zs + j) * chips + chip
                pair, row = tile // 3, tile % 3
                small_v[pair // chips, pair % chips, 4 + row : 5 + row] = jnp.where(
                    (lane_half == c % 2) & (c // 2 == chip), both, 0.0
                )
    small_v_x = [
        wires.put(small_v.at[:, flip(c, m) // 2], small_x.at[m], 0, m) for m in range(1, n)
    ]
    for copy in small_v_x:
        copy.start()

    wait_y.wait()
    pl.semaphore_wait(free, 4)
    y_sums = LayerScatter(
        wires, lambda i: part.at[i], lambda j: near.at[j], lambda j: far.at[j]
    )
    y_sums.start()
    for m in (6, 4, 2):
        y_sums.step(m)
    small_sum = small_v[:, c // 2]
    for m in range(1, n):
        small_v_x[m - 1].wait_recv()
        small_sum = small_sum + small_x[m]
    small_r[...] = small_sum
    small_z_x = [wires.put(small_r.at[flip(z, m)], small_z.at[m], m, 0) for m in range(1, zs)]
    for copy in small_z_x:
        copy.start()
    for copy in gu_x:
        copy.wait_recv()
    halves = halves_of(ffc // zs)
    unpack_columns(gate_out, gu_rows, [(2 * zs * at, size) for at, size in halves], n, zs)
    unpack_columns(up_out, gu_rows, [(zs * (2 * at + size), size) for at, size in halves], n, zs)

    for p, part_sum in enumerate(qkv_sums):
        gq_v[z, p * size : (p + 1) * size] = part_sum.total().astype(b16)
    gq_x = [
        wires.put(
            gq_v.at[z, pl.ds(pl.multiple_of(flip(c, m) * wrows, wrows), wrows)],
            gq_rows.at[c],
            0,
            m,
        )
        for m in range(1, n)
    ]
    for copy in gq_x:
        copy.start()
    gq_rows[c] = gq_v[z, pl.ds(pl.multiple_of(c * wrows, wrows), wrows)]
    result_out[...] = (hidden_v[...] + y_sums.total()).astype(b16)
    small_sum = small_r[z]
    for m in range(1, zs):
        small_z_x[m - 1].wait_recv()
        small_sum = small_sum + small_z[m]
    small_out[...] = small_sum
    hidden_v[0:wrows] = go_sums.total()
    moves.store(hidden_v.at[0:wrows], grad_out_out)
    for group in (*gu_sums, go_sums, *qkv_sums, y_sums):
        group.sent()
    for copy in (*gu_x, *small_v_x, *small_z_x):
        copy.wait_send()
    moves.finish()
    for copy in gq_x:
        copy.wait()
    for i in range(3):
        unpack_columns(
            gq_out.at[:, i * width : (i + 1) * width], gq_rows, [(i * hc, HEAD_DIM)], n, zs
        )


def backward(zs, n, norms, tables, *arrays):
    f32, b16 = jnp.float32, jnp.bfloat16
    a1_all, a2_all, dgu, w_gu, w_qkv, w_out, qkv, probs, ob, hidden, dy, xs, _ = arrays
    _, slots, rows, hc = ob.shape
    local, width = hidden.shape
    _, depth, gc = w_gu.shape
    qc = 3 * hc
    wrows = depth // n
    seq = n * rows
    wide = (n, local, width)

    def buf(like):
        return pltpu.VMEM(like.shape, like.dtype)

    return pl.pallas_call(
        functools.partial(backward_kernel, zs, n),
        out_shape=[
            jax.ShapeDtypeStruct((hc // zs, width), f32),
            jax.ShapeDtypeStruct((local, width), b16),
            jax.ShapeDtypeStruct((local, width), f32),
            jax.ShapeDtypeStruct((wrows, n * qc), b16),
            jax.ShapeDtypeStruct((wrows, n * gc // 2), b16),
            jax.ShapeDtypeStruct((wrows, n * gc // 2), b16),
            jax.ShapeDtypeStruct((8, 2 * HEAD_DIM), f32),
        ],
        in_specs=[VMEM] * 2 + [HBM] * 13,
        out_specs=[HBM] + [VMEM] * 6,
        scratch_shapes=[
            pltpu.VMEM(wide, b16),
            buf(dgu),
            pltpu.VMEM((zs, depth, max(gc, 2 * qc)), b16),
            buf(w_out),
            buf(qkv),
            pltpu.VMEM(probs.shape[1:], b16),
            buf(ob),
            buf(hidden),
            pltpu.VMEM((local, width), b16),
            pltpu.VMEM((zs, depth, gc), b16),
            pltpu.VMEM((depth, gc), b16),
            pltpu.VMEM((3, depth, gc), b16),
            pltpu.VMEM((n // 2, local, width), b16),
            pltpu.VMEM((n // 2 - 1, local, width), b16),
            pltpu.VMEM(wide, b16),
            pltpu.VMEM((zs, hc // zs, width), b16),
            pltpu.VMEM((hc // zs, width), b16),
            pltpu.VMEM((3, hc // zs, width), b16),
            pltpu.VMEM((3, seq, hc), f32),
            pltpu.VMEM((n, slots, rows, qc), b16),
            pltpu.VMEM((1, qc), f32),
            pltpu.VMEM((depth, qc), b16),
            pltpu.VMEM((3, depth, qc), b16),
            pltpu.VMEM((n, wrows, gc), b16),
            pltpu.VMEM((n, wrows, qc), b16),
            pltpu.VMEM((zs, n // 2, 8, 2 * HEAD_DIM), f32),
            pltpu.VMEM((n, zs, 8, 2 * HEAD_DIM), f32),
            pltpu.VMEM((zs, 8, 2 * HEAD_DIM), f32),
            pltpu.VMEM((zs, 8, 2 * HEAD_DIM), f32),
            pltpu.SemaphoreType.DMA((96,)),
            pltpu.SemaphoreType.DMA((96,)),
            pltpu.SemaphoreType.DMA((24,)),
            pltpu.SemaphoreType.REGULAR,
        ],
        compiler_params=pltpu.CompilerParams(
            collective_id=4, has_side_effects=True, vmem_limit_bytes=VMEM_LIMIT
        ),
        name="backward",
    )(norms, tables, *arrays)


def tensor_shards(
    inputs,
    lengths,
    w_qkv,
    b_qkv,
    w_out,
    w_gate,
    w_up,
    w_down,
    gain_one,
    shift_one,
    gain_two,
    shift_two,
    cotangent,
):
    rows, slots, width = inputs.shape
    f32, b16 = jnp.float32, jnp.bfloat16
    zs, n = lax.axis_size("dp"), lax.axis_size("ctx")
    me = lax.axis_index("ctx")
    local = rows * slots
    seq = rows * n
    wrows = w_qkv.shape[0]
    ff_block = w_down.shape[0]
    hc = HEADS // n * HEAD_DIM
    ffc = ff_block * zs

    def local_tokens(v):
        return jnp.transpose(v, (1, 0, 2)).reshape(local, width)

    def back_tokens(v):
        return jnp.transpose(v.reshape(slots, rows, width), (1, 0, 2))

    xs = local_tokens(inputs)
    dy = local_tokens(cotangent)
    nb = b_qkv.shape[0]
    vectors = [v for gain in (gain_one, shift_one, gain_two, shift_two) for v in (gain, gain)]
    small, at = jnp.zeros(1024, f32), 0
    for vector in (*vectors, b_qkv):
        size = vector.shape[0]
        small = small + jnp.pad(vector.astype(f32), (at, 1024 - at - size))
        at += size
    small = small.reshape(8, 128)

    angles = np.arange(seq)[:, None] * 10000.0 ** (-2.0 * np.arange(ROTARY // 2) / ROTARY)[None, :]
    cos_t, sin_t = np.cos(angles), np.sin(angles)
    zero, rest = np.zeros_like(sin_t), np.zeros((seq, HEAD_DIM - ROTARY))
    tables = np.stack(
        [
            np.concatenate(two, -1)
            for two in (
                2 * [cos_t, cos_t, rest + 1.0],
                2 * [-sin_t, zero, rest],
                2 * [zero, sin_t, rest],
            )
        ]
    ).astype(np.float32)

    tables = jnp.asarray(tables.reshape(3, n, rows, 2 * HEAD_DIM))
    w_qkv_c, w_out_c, w_gu_c, a1, qkv, probs, ob, hidden, a2, dgu, y, grad_down, norms = front(
        zs, n, slots, lengths, tables, small, w_qkv, w_gate, w_up, w_out, w_down, xs, dy
    )
    wide = (n, local, width)
    grad_out, result, input_grad, grad_qkv, grad_gate, grad_up, sums = backward(
        zs, n, norms, tables, a1.reshape(wide), a2.reshape(wide), dgu,
        w_gu_c.reshape(zs, n * wrows, 2 * ffc), w_qkv_c.reshape(zs, n * wrows, 3 * hc),
        w_out_c, qkv, probs, ob, hidden, dy, xs, y.reshape(wide),
    )
    mine = lax.dynamic_slice_in_dim(sums[:4], me % 2 * wrows, wrows, 1)
    grad_bias = lax.dynamic_slice_in_dim(sums[4:7].reshape(2 * nb), me % 2 * nb, nb)
    return (
        back_tokens(result),
        back_tokens(input_grad),
        grad_qkv.astype(f32),
        grad_bias,
        grad_out,
        grad_gate.astype(f32),
        grad_up.astype(f32),
        grad_down,
        mine[0],
        mine[1],
        mine[2],
        mine[3],
    )


def solution(mesh):
    zs, n = mesh.shape["dp"], mesh.shape["ctx"]
    shards = tensor_shards if (zs, n) == (4, 8) and HEADS == 32 else gathered_shards

    placed = (
        P("ctx", "dp", None),
        P("dp", None),
        P(("dp", "ctx"), None),
        P(("dp", "ctx")),
        P(("dp", "ctx"), None),
        P(("dp", "ctx"), None),
        P(("dp", "ctx"), None),
        P(("dp", "ctx"), None),
        P(("dp", "ctx")),
        P(("dp", "ctx")),
        P(("dp", "ctx")),
        P(("dp", "ctx")),
        P("ctx", "dp", None),
    )
    return jax.shard_map(
        shards,
        mesh=mesh,
        in_specs=placed,
        out_specs=(
            P("ctx", "dp", None),
            P("ctx", "dp", None),
            P(("dp", "ctx"), None),
            P(("dp", "ctx")),
            P(("dp", "ctx"), None),
            P(("dp", "ctx"), None),
            P(("dp", "ctx"), None),
            P(("dp", "ctx"), None),
            P(("dp", "ctx")),
            P(("dp", "ctx")),
            P(("dp", "ctx")),
            P(("dp", "ctx")),
        ),
        check_vma=False,
    )
```

```python
import functools
import itertools
import math

import jax
import jax.numpy as jnp
import numpy as np
from jax import lax
from jax.experimental import pallas as pl
from jax.experimental.pallas import tpu as pltpu
from jax.sharding import PartitionSpec as P

HEADS = 32
HEAD_DIM = 64
ROTARY = 16


epsilon = 1e-05
masked_value = -1e30


def layer_stats(values):
    row_mean = jnp.mean(values, -1, keepdims=True)
    centred = values - row_mean
    inverse = lax.rsqrt(jnp.mean(centred * centred, -1, keepdims=True) + epsilon)
    return (centred * inverse, inverse)


def norm_back(grad_normed, scaled, inverse, gain_vec):
    grad_hat = grad_normed * gain_vec
    return inverse * (
        grad_hat
        - jnp.mean(grad_hat, -1, keepdims=True)
        - scaled * jnp.mean(grad_hat * scaled, -1, keepdims=True)
    )


def rotary_tables(positions):
    counter = jnp.arange(ROTARY // 2, dtype=jnp.float32)
    frequency = 10000.0 ** (-2.0 * counter / ROTARY)
    angles = positions.astype(jnp.float32)[:, None] * frequency[None, :]
    return (jnp.cos(angles)[:, None, None, :], jnp.sin(angles)[:, None, None, :])


def rotate(values, cos_table, sin_table):
    half_dims = ROTARY // 2
    first_half = values[..., :half_dims]
    second_half = values[..., half_dims:ROTARY]
    return jnp.concatenate(
        [
            first_half * cos_table - second_half * sin_table,
            second_half * cos_table + first_half * sin_table,
            values[..., ROTARY:],
        ],
        -1,
    )


def over_blocks(step_fn, running, gathered):
    total_rows = gathered.shape[0]
    tile_rows = math.gcd(total_rows, 512)

    def visit_block(number, current):
        block_start = number * tile_rows
        block_part = lax.dynamic_slice_in_dim(gathered, block_start, tile_rows, 0)
        return step_fn(current, block_part, block_start)

    return lax.fori_loop(0, total_rows // tile_rows, visit_block, running)


def gathered_shards(
    inputs,
    lengths,
    w_qkv,
    b_qkv,
    w_out,
    w_gate,
    w_up,
    w_down,
    gain_one,
    shift_one,
    gain_two,
    shift_two,
    cotangent,
):
    local_rows, slot_count, width = inputs.shape
    positions = lax.axis_index("ctx") * local_rows + jnp.arange(local_rows, dtype=jnp.int32)
    live_rows = positions[:, None] < lengths[0][None, :]
    live_heads = jnp.transpose(live_rows)[:, None, :, None]
    cos_table, sin_table = rotary_tables(positions)

    def allowed_mask(offset, count):
        key_pos = offset + jnp.arange(count, dtype=jnp.int32)
        causal = key_pos[None, :] <= positions[:, None]
        return causal[None, None, :, :] & live_heads

    def split_heads(block_part):
        count = block_part.shape[0]
        key_part = block_part[:, :, 0].reshape(count, slot_count, HEADS, HEAD_DIM)
        value_part = block_part[:, :, 1].reshape(count, slot_count, HEADS, HEAD_DIM)
        return (key_part, value_part)

    attn_full = (
        lax.all_gather(w_qkv, ("dp", "ctx"), axis=0, tiled=True),
        lax.all_gather(b_qkv, ("dp", "ctx"), axis=0, tiled=True),
        lax.all_gather(w_out, ("dp", "ctx"), axis=0, tiled=True),
        lax.all_gather(gain_one, ("dp", "ctx"), axis=0, tiled=True),
        lax.all_gather(shift_one, ("dp", "ctx"), axis=0, tiled=True),
    )
    qkv_full, bias_full, out_full, gain_one_full, shift_one_full = attn_full
    source = inputs.astype(jnp.float32)
    scaled_one, inverse_one = layer_stats(source)
    normed_one = (
        scaled_one * gain_one_full.astype(jnp.float32) + shift_one_full.astype(jnp.float32)
    ).astype(jnp.bfloat16)
    joined = jnp.einsum(
        "rsd,de->rse", normed_one, qkv_full, preferred_element_type=jnp.float32
    ) + bias_full.astype(jnp.float32)
    query_pre = joined[..., :width].reshape(local_rows, slot_count, HEADS, HEAD_DIM)
    key_pre = joined[..., width : 2 * width].reshape(local_rows, slot_count, HEADS, HEAD_DIM)
    queries = rotate(query_pre, cos_table, sin_table).astype(jnp.bfloat16)
    keys_rot = rotate(key_pre, cos_table, sin_table).reshape(local_rows, slot_count, width)
    key_value = jnp.stack([keys_rot, joined[..., 2 * width :]], 2).astype(jnp.bfloat16)
    block_part = lax.all_gather(key_value, "ctx", axis=0, tiled=True)
    run_peak = jnp.full((slot_count, HEADS, local_rows), masked_value, jnp.float32)
    key_part, value_part = split_heads(block_part)
    scores = (
        jnp.einsum("qshd,kshd->shqk", queries, key_part, preferred_element_type=jnp.float32) * 0.125
    )
    allowed = allowed_mask(jnp.int32(0), block_part.shape[0])
    masked = jnp.where(allowed, scores, masked_value)
    new_peak = jnp.maximum(run_peak, jnp.max(masked, -1))
    weights = jnp.where(allowed, jnp.exp(masked - new_peak[..., None]), 0.0)
    new_sum = jnp.sum(weights, -1)
    new_acc = jnp.einsum(
        "shqk,kshd->shqd",
        weights.astype(jnp.bfloat16),
        value_part,
        preferred_element_type=jnp.float32,
    )
    final_sum = jnp.maximum(new_sum, 1.0)
    log_sum = new_peak + jnp.log(final_sum)
    attended = jnp.transpose(new_acc / final_sum[..., None], (2, 0, 1, 3))
    attended_low = attended.reshape(local_rows, slot_count, width).astype(jnp.bfloat16)
    hidden_in = source + jnp.einsum(
        "rsd,de->rse", attended_low, out_full, preferred_element_type=jnp.float32
    )
    mlp_full = (
        lax.all_gather(w_gate, ("dp", "ctx"), axis=0, tiled=True),
        lax.all_gather(w_up, ("dp", "ctx"), axis=0, tiled=True),
        lax.all_gather(w_down, ("dp", "ctx"), axis=0, tiled=True),
        lax.all_gather(gain_two, ("dp", "ctx"), axis=0, tiled=True),
        lax.all_gather(shift_two, ("dp", "ctx"), axis=0, tiled=True),
    )
    gate_full, up_full, down_full, gain_two_full, shift_two_full = mlp_full
    scaled_two, inverse_two = layer_stats(hidden_in)
    normed_two = (
        scaled_two * gain_two_full.astype(jnp.float32) + shift_two_full.astype(jnp.float32)
    ).astype(jnp.bfloat16)
    gate = jnp.einsum("rsd,df->rsf", normed_two, gate_full, preferred_element_type=jnp.float32)
    upward = jnp.einsum("rsd,df->rsf", normed_two, up_full, preferred_element_type=jnp.float32)
    sigmoid = jax.nn.sigmoid(gate)
    product = (gate * sigmoid * upward).astype(jnp.bfloat16)
    result = hidden_in + jnp.einsum(
        "rsf,fd->rsd", product, down_full, preferred_element_type=jnp.float32
    )
    gate_back, up_back, down_back, gain_two_back = (
        lax.all_gather(w_gate, ("dp", "ctx"), axis=0, tiled=True),
        lax.all_gather(w_up, ("dp", "ctx"), axis=0, tiled=True),
        lax.all_gather(w_down, ("dp", "ctx"), axis=0, tiled=True),
        lax.all_gather(gain_two, ("dp", "ctx"), axis=0, tiled=True),
    )
    grad_down = jnp.einsum("rsf,rsd->fd", product, cotangent, preferred_element_type=jnp.float32)
    grad_product = jnp.einsum(
        "rsd,fd->rsf", cotangent, down_back, preferred_element_type=jnp.float32
    )
    grad_gate_act = (grad_product * upward * sigmoid * (1.0 + gate * (1.0 - sigmoid))).astype(
        jnp.bfloat16
    )
    grad_up_act = (grad_product * gate * sigmoid).astype(jnp.bfloat16)
    grad_gate = jnp.einsum(
        "rsd,rsf->df", normed_two, grad_gate_act, preferred_element_type=jnp.float32
    )
    grad_up = jnp.einsum("rsd,rsf->df", normed_two, grad_up_act, preferred_element_type=jnp.float32)
    grad_normed_two = jnp.einsum(
        "rsf,df->rsd", grad_gate_act, gate_back, preferred_element_type=jnp.float32
    ) + jnp.einsum("rsf,df->rsd", grad_up_act, up_back, preferred_element_type=jnp.float32)
    grad_gain_two = jnp.sum(grad_normed_two * scaled_two, (0, 1))
    grad_shift_two = jnp.sum(grad_normed_two, (0, 1))
    grad_hidden = cotangent.astype(jnp.float32) + norm_back(
        grad_normed_two, scaled_two, inverse_two, gain_two_back.astype(jnp.float32)
    )
    mlp_sums = (
        lax.psum_scatter(grad_gate, ("dp", "ctx"), scatter_dimension=0, tiled=True),
        lax.psum_scatter(grad_up, ("dp", "ctx"), scatter_dimension=0, tiled=True),
        lax.psum_scatter(grad_down, ("dp", "ctx"), scatter_dimension=0, tiled=True),
        lax.psum_scatter(grad_gain_two, ("dp", "ctx"), scatter_dimension=0, tiled=True),
        lax.psum_scatter(grad_shift_two, ("dp", "ctx"), scatter_dimension=0, tiled=True),
    )
    qkv_back, out_back, gain_one_back = (
        lax.all_gather(w_qkv, ("dp", "ctx"), axis=0, tiled=True),
        lax.all_gather(w_out, ("dp", "ctx"), axis=0, tiled=True),
        lax.all_gather(gain_one, ("dp", "ctx"), axis=0, tiled=True),
    )
    hidden_low = grad_hidden.astype(jnp.bfloat16)
    grad_out = jnp.einsum(
        "rsd,rse->de", attended_low, hidden_low, preferred_element_type=jnp.float32
    )
    grad_attended = jnp.einsum(
        "rse,de->rsd", hidden_low, out_back, preferred_element_type=jnp.float32
    )
    grad_heads = grad_attended.reshape(local_rows, slot_count, HEADS, HEAD_DIM).astype(jnp.bfloat16)
    delta = jnp.transpose(jnp.sum(grad_heads.astype(jnp.float32) * attended, -1), (1, 2, 0))
    key_value_all = lax.all_gather(key_value, "ctx", axis=0, tiled=True)

    def grad_parts(block_part, offset):
        key_part, value_part = split_heads(block_part)
        scores = (
            jnp.einsum("qshd,kshd->shqk", queries, key_part, preferred_element_type=jnp.float32)
            * 0.125
        )
        allowed = allowed_mask(offset, block_part.shape[0])
        probs = jnp.where(allowed, jnp.exp(scores - log_sum[..., None]), 0.0)
        grad_prob = jnp.einsum(
            "qshd,kshd->shqk", grad_heads, value_part, preferred_element_type=jnp.float32
        )
        grad_score = (probs * (grad_prob - delta[..., None])).astype(jnp.bfloat16)
        return (key_part, probs, grad_score)

    def query_step(running, block_part, offset):
        key_part, probs, grad_score = grad_parts(block_part, offset)
        return running + jnp.einsum(
            "shqk,kshd->shqd", grad_score, key_part, preferred_element_type=jnp.float32
        )

    grad_query = (
        over_blocks(
            query_step,
            jnp.zeros((slot_count, HEADS, local_rows, HEAD_DIM), jnp.float32),
            key_value_all,
        )
        * 0.125
    )
    count = local_rows * lax.axis_size("ctx")
    tile_rows = math.gcd(count, 512)

    def one_block(number):
        block_start = number * tile_rows
        block_part = lax.dynamic_slice_in_dim(key_value_all, block_start, tile_rows, 0)
        key_part, probs, grad_score = grad_parts(block_part, block_start)
        grad_key = (
            jnp.einsum("shqk,qshd->kshd", grad_score, queries, preferred_element_type=jnp.float32)
            * 0.125
        )
        grad_value = jnp.einsum(
            "shqk,qshd->kshd",
            probs.astype(jnp.bfloat16),
            grad_heads,
            preferred_element_type=jnp.float32,
        )
        return jnp.stack(
            [
                grad_key.reshape(tile_rows, slot_count, width),
                grad_value.reshape(tile_rows, slot_count, width),
            ],
            2,
        )

    blocks = lax.map(one_block, jnp.arange(count // tile_rows, dtype=jnp.int32))
    grad_key_value = lax.psum_scatter(
        blocks.reshape(count, slot_count, 2, width).astype(jnp.bfloat16),
        "ctx",
        scatter_dimension=0,
        tiled=True,
    ).astype(jnp.float32)
    grad_query_pre = rotate(jnp.transpose(grad_query, (2, 0, 1, 3)), cos_table, -sin_table)
    grad_key_pre = rotate(
        grad_key_value[:, :, 0].reshape(local_rows, slot_count, HEADS, HEAD_DIM),
        cos_table,
        -sin_table,
    )
    grad_joined = jnp.concatenate(
        [
            grad_query_pre.reshape(local_rows, slot_count, width),
            grad_key_pre.reshape(local_rows, slot_count, width),
            grad_key_value[:, :, 1],
        ],
        -1,
    ).astype(jnp.bfloat16)
    grad_qkv = jnp.einsum(
        "rsd,rse->de", normed_one, grad_joined, preferred_element_type=jnp.float32
    )
    grad_bias = jnp.sum(grad_joined.astype(jnp.float32), (0, 1))
    grad_normed_one = jnp.einsum(
        "rse,de->rsd", grad_joined, qkv_back, preferred_element_type=jnp.float32
    )
    grad_gain_one = jnp.sum(grad_normed_one * scaled_one, (0, 1))
    grad_shift_one = jnp.sum(grad_normed_one, (0, 1))
    input_grad = grad_hidden + norm_back(
        grad_normed_one, scaled_one, inverse_one, gain_one_back.astype(jnp.float32)
    )
    attn_sums = (
        lax.psum_scatter(grad_qkv, ("dp", "ctx"), scatter_dimension=0, tiled=True),
        lax.psum_scatter(grad_bias, ("dp", "ctx"), scatter_dimension=0, tiled=True),
        lax.psum_scatter(grad_out, ("dp", "ctx"), scatter_dimension=0, tiled=True),
        lax.psum_scatter(grad_gain_one, ("dp", "ctx"), scatter_dimension=0, tiled=True),
        lax.psum_scatter(grad_shift_one, ("dp", "ctx"), scatter_dimension=0, tiled=True),
    )
    return (
        result.astype(jnp.bfloat16),
        input_grad,
        attn_sums[0],
        attn_sums[1],
        attn_sums[2],
        mlp_sums[0],
        mlp_sums[1],
        mlp_sums[2],
        attn_sums[3],
        attn_sums[4],
        mlp_sums[3],
        mlp_sums[4],
    )


MESH = pl.DeviceIdType.MESH
HBM = pl.BlockSpec(memory_space=pltpu.HBM)
VMEM = pl.BlockSpec(memory_space=pltpu.VMEM)
VMEM_LIMIT = 60 << 20


def flip(index, mask):
    for bit in (1, 2, 4):
        if mask & bit:
            index = index + bit - 2 * bit * ((index // bit) % 2)
    return index


class Wires:
    def __init__(self, send, recv):
        self.send, self.recv = send, recv
        self.z, self.c = lax.axis_index("dp"), lax.axis_index("ctx")
        self.inner = (self.z == 1) | (self.z == 2)
        self.outer = (self.z == 0) | (self.z == 3)
        self.number = itertools.count()

    def put(self, src, dst, z_mask, c_mask):
        return self.put_to(src, dst, flip(self.z, z_mask), flip(self.c, c_mask))

    def put_to(self, src, dst, z, c):
        i = next(self.number)
        return pltpu.make_async_remote_copy(
            src_ref=src,
            dst_ref=dst,
            send_sem=self.send.at[i],
            recv_sem=self.recv.at[i],
            device_id=(z, c),
            device_id_type=MESH,
        )

    def greet(self, zs, n):
        barrier = pltpu.get_barrier_semaphore()
        for m in range(1, zs):
            pl.semaphore_signal(
                barrier, inc=1, device_id=(flip(self.z, m), self.c), device_id_type=MESH
            )
        for m in range(1, n):
            pl.semaphore_signal(
                barrier, inc=1, device_id=(self.z, flip(self.c, m)), device_id_type=MESH
            )
        pl.semaphore_wait(barrier, zs + n - 2)


class DepthGather:
    def __init__(self, wires, part):
        z = wires.z
        self.wires = wires
        self.near = wires.put(part(z), part(z), 1, 0)
        self.skip = wires.put(part(z), part(z), 2, 0)
        self.mid = wires.put(part(z), part(z), 3, 0)
        far = flip(z, 2)
        self.on = wires.put(part(far), part(far), 1, 0)

    @staticmethod
    def start(parts):
        for part in parts:
            part.skip.start()
        for part in parts:
            pl.when(part.wires.inner)(part.mid.start)
        for part in parts:
            part.near.start()

    def forward(self):
        @pl.when(self.wires.inner)
        def _():
            self.skip.wait_recv()
            self.on.start()

    def finish(self):
        self.near.wait_recv()
        self.near.wait_send()
        self.skip.wait_send()

        @pl.when(self.wires.inner)
        def _():
            self.mid.wait_recv()
            self.mid.wait_send()
            self.on.wait_send()

        @pl.when(self.wires.outer)
        def _():
            self.skip.wait_recv()
            self.on.wait_recv()


class LayerGather:
    def __init__(self, wires, block, source=None):
        c = wires.c
        mine = block(c) if source is None else source
        self.direct = {m: wires.put(mine, block(c), 0, m) for m in (2, 4, 6, 1)}
        self.on = {m: wires.put(block(flip(c, m)), block(flip(c, m)), 0, 1) for m in (2, 4, 6)}

    def start(self):
        for m in (2, 4, 6, 1):
            self.direct[m].start()

    def forward(self, m):
        self.direct[m].wait_recv()
        self.on[m].start()

    def arrived(self, m):
        (self.direct[1] if m == 1 else self.on[m - 1]).wait_recv()

    def sent(self):
        for copy in (*self.direct.values(), *self.on.values()):
            copy.wait_send()


def pack_columns(dst, refs, n, zs):
    for i in range(n):
        pieces = []
        for ref, block, at, size in refs:
            starts = [block * (j * n + i) + at for j in range(zs)]
            pieces += [ref[:, start : start + size] for start in starts]
        dst[i] = jnp.concatenate(pieces, -1)


class LayerScatter:
    def __init__(self, wires, part, near, far):
        c = wires.c
        self.c, self.part, self.near, self.far = c, part, near, far
        self.pair = {
            m: wires.put(part(flip(c, m + 1)), near(m // 2), 0, 1) for m in (6, 4, 2, 0)
        }
        self.chips = {m: wires.put(part(flip(c, m)), far(m // 2 - 1), 0, m) for m in (6, 4, 2)}

    def start(self):
        for copy in self.pair.values():
            copy.start()

    def step(self, m):
        self.pair[m].wait_recv()
        to = self.part(flip(self.c, m))
        to[...] = (
            to[...].astype(jnp.float32) + self.near(m // 2)[...].astype(jnp.float32)
        ).astype(to.dtype)
        self.chips[m].start()

    def total(self):
        self.pair[0].wait_recv()
        result = self.part(self.c)[...].astype(jnp.float32)
        result = result + self.near(0)[...].astype(jnp.float32)
        for m in (2, 4, 6):
            self.chips[m].wait_recv()
            result = result + self.far(m // 2 - 1)[...].astype(jnp.float32)
        return result

    def sent(self):
        for copy in (*self.pair.values(), *self.chips.values()):
            copy.wait_send()


def dot(a, b, dims=((1,), (0,))):
    return lax.dot_general(a, b, (dims, ((), ())), preferred_element_type=jnp.float32)


def turn_pair(values, table, sign):
    half = ROTARY // 2
    columns = values.shape[-1]
    table = [jnp.concatenate([t] * (columns // t.shape[-1]), -1) for t in table]
    return (
        values * table[0]
        + sign * (pltpu.roll(values, columns - half, 1) * table[1])
        + sign * (pltpu.roll(values, half, 1) * table[2])
    )


def head_mask(rows, columns, head):
    return lax.broadcasted_iota(jnp.int32, (rows, columns), 1) // HEAD_DIM == head


class DepthScatter:
    def __init__(self, wires, part, relay, boxes):
        z = wires.z
        self.wires, self.part, self.relay_box, self.boxes = wires, part, relay, boxes
        self.far = wires.put(part(flip(z, 3)), relay, 1, 0)
        self.skip = wires.put(part(flip(z, 2)), boxes[1], 2, 0)
        self.near = wires.put(part(flip(z, 1)), boxes[0], 1, 0)
        self.mid = wires.put(part(flip(z, 3)), boxes[2], 3, 0)

    def start(self, mask):
        outer, inner = pl.when(self.wires.outer), pl.when(self.wires.inner)
        if mask == 3:
            outer(self.far.start)
            inner(self.mid.start)
        elif mask == 2:
            outer(self.skip.start)
        elif mask == 1:
            self.near.start()
        else:

            @outer
            def _():
                self.boxes[2][...] = jnp.zeros_like(self.boxes[2])

    def relay(self):
        @pl.when(self.wires.inner)
        def _():
            self.far.wait_recv()
            to = self.part(flip(self.wires.z, 2))
            to[...] = (
                to[...].astype(jnp.float32) + self.relay_box[...].astype(jnp.float32)
            ).astype(to.dtype)
            self.skip.start()

    def total(self):
        self.near.wait_recv()
        self.skip.wait_recv()
        pl.when(self.wires.inner)(self.mid.wait_recv)
        result = self.part(self.wires.z)[...].astype(jnp.float32)
        for box in self.boxes:
            result = result + box[...].astype(jnp.float32)
        return result

    def sent(self):
        self.near.wait_send()
        self.skip.wait_send()
        pl.when(self.wires.outer)(self.far.wait_send)
        pl.when(self.wires.inner)(self.mid.wait_send)


class Moves:
    def __init__(self, sems):
        self.sems, self.number, self.stores = sems, itertools.count(), []

    def load(self, src, dst):
        copy = pltpu.make_async_copy(src, dst, self.sems.at[next(self.number)])
        copy.start()
        return copy

    def store(self, src, dst):
        self.stores.append(self.load(src, dst))

    def finish(self):
        for copy in self.stores:
            copy.wait()


def pieces_of(total, number, unit):
    units = total // unit
    cuts = [units * i // number * unit for i in range(number + 1)]
    return [(a, b - a) for a, b in zip(cuts[:-1], cuts[1:])]


class ChainGather:
    def __init__(self, wires, part):
        self.z = z = wires.z
        self.right = [
            wires.put_to(part((z - s + 4) % 4), part((z - s + 4) % 4), (z + 1) % 4, wires.c)
            for s in range(3)
        ]
        self.left = [
            wires.put_to(part((z + s) % 4), part((z + s) % 4), (z + 3) % 4, wires.c)
            for s in range(3)
        ]

    def start(self):
        pl.when(self.z <= 2)(self.right[0].start)
        pl.when(self.z >= 1)(self.left[0].start)

    def hop(self, s):
        pl.when(self.z >= s)(self.right[s - 1].wait_recv)
        pl.when((self.z >= s) & (self.z <= 2))(self.right[s].start)
        pl.when(self.z <= 3 - s)(self.left[s - 1].wait_recv)
        pl.when((self.z <= 3 - s) & (self.z >= 1))(self.left[s].start)

    def finish(self):
        pl.when(self.z >= 3)(self.right[2].wait_recv)
        pl.when(self.z <= 0)(self.left[2].wait_recv)
        for s in range(3):
            pl.when((self.z >= s) & (self.z <= 2))(self.right[s].wait_send)
            pl.when((self.z <= 3 - s) & (self.z >= 1))(self.left[s].wait_send)


class ChainScatter:
    def __init__(self, wires, part, right, left):
        self.z = z = wires.z
        self.part, self.right_box, self.left_box = part, right, left
        self.right = {
            j: wires.put_to(part(j), right(j), (z + 1) % 4, wires.c) for j in (3, 2, 1)
        }
        self.left = {j: wires.put_to(part(j), left(j), (z + 3) % 4, wires.c) for j in (0, 1, 2)}

    def clear(self):
        @pl.when(self.z == 0)
        def _():
            self.right_box(1)[...] = jnp.zeros_like(self.right_box(1))

        @pl.when(self.z == 3)
        def _():
            self.left_box(2)[...] = jnp.zeros_like(self.left_box(2))

    def start(self, distance):
        pl.when(self.z == 0)(self.right[distance].start)
        pl.when(self.z == 3)(self.left[3 - distance].start)

    def pass_on(self, copy, j, box):
        copy.wait_recv()
        to = self.part(j)
        to[...] = (to[...].astype(jnp.float32) + box(j)[...].astype(jnp.float32)).astype(to.dtype)
        copy.start()

    def hop(self, s, distance):
        @pl.when(self.z == s)
        def _():
            self.pass_on(self.right[distance], distance, self.right_box)

        @pl.when(self.z == 3 - s)
        def _():
            self.pass_on(self.left[3 - distance], 3 - distance, self.left_box)

    def total(self):
        for j in (1, 2, 3):
            pl.when(self.z == j)(self.right[j].wait_recv)
        for j in (0, 1, 2):
            pl.when(self.z == j)(self.left[j].wait_recv)
        z = self.z
        return (
            self.part(z)[...].astype(jnp.float32)
            + self.right_box(jnp.maximum(z, 1))[...].astype(jnp.float32)
            + self.left_box(jnp.minimum(z, 2))[...].astype(jnp.float32)
        )

    def sent(self):
        for j in (1, 2, 3):
            pl.when(self.z < j)(self.right[j].wait_send)
        for j in (0, 1, 2):
            pl.when(self.z > j)(self.left[j].wait_send)


def halves_of(block):
    first = (block // 16 + 1) // 2 * 16
    return [(0, first), (first, block - first)]


def by_slot(dst, src):
    rows, slots, _ = src.shape
    for s in range(slots):
        dst[s * rows : (s + 1) * rows] = src[:, s, :]


def by_position(dst, values):
    rows, slots, _ = dst.shape
    for s in range(slots):
        dst[:, s, :] = values[s * rows : (s + 1) * rows].astype(dst.dtype)


def front_kernel(
    zs,
    n,
    slots,
    lengths,
    tables,
    small,
    w_qkv,
    w_gate,
    w_up,
    w_out,
    w_down,
    inputs,
    cotangent,
    w_qkv_out,
    w_out_out,
    w_gu_out,
    a1_out,
    qkv_out,
    probs_out,
    ob_out,
    hidden_out,
    a2_out,
    dgu_out,
    y_out,
    grad_down_out,
    norms,
    qkv_send,
    gu_send,
    small_v,
    bias_v,
    w_qkv_v,
    w_out_v,
    w_gu_v,
    w_down_v,
    wide_x,
    wide_a,
    dy_v,
    qkv_v,
    probs_v,
    ob_v,
    near,
    far,
    hidden_v,
    gu_v,
    zz_v,
    dz_v,
    gd_v,
    right_v,
    left_v,
    raw_v,
    send,
    recv,
    local,
):
    f32, b16 = jnp.float32, jnp.bfloat16
    wires = Wires(send, recv)
    moves = Moves(local)
    z, c = wires.z, wires.c
    rows, _, width = inputs.shape
    local_rows = rows * slots
    tokens, seq = n * local_rows, n * rows
    pair = 2 * local_rows
    hc = qkv_v.shape[-1]
    heads = hc // HEAD_DIM
    block = w_down_v.shape[1]
    ffc = zs * block
    halves = halves_of(block)
    spans = [(2 * zs * at, zs * size) for at, size in halves]
    lanes = 2 * HEAD_DIM
    lane_half = lax.broadcasted_iota(jnp.int32, (1, lanes), 1) // HEAD_DIM

    def block_of(ref, i):
        return ref.at[pl.ds(pl.multiple_of(i * local_rows, local_rows), local_rows)]

    def pair_at(i):
        return pl.ds(pl.multiple_of(i * pair, pair), pair)

    wait_out = moves.load(w_out, w_out_v.at[z])
    wait_small = moves.load(small, small_v.at[z, c])
    waits = [moves.load(inputs, raw_v.at[0]), moves.load(cotangent, raw_v.at[1])]
    wait_down = moves.load(w_down, w_down_v.at[z])
    pack_columns(
        qkv_send,
        [(w_qkv.at[:, i * width : (i + 1) * width], HEAD_DIM, 0, HEAD_DIM) for i in range(3)],
        n,
        zs,
    )
    wait_own_qkv = moves.load(qkv_send.at[c], w_qkv_v.at[z, c])
    waits[0].wait()
    by_slot(block_of(wide_x, c), raw_v.at[0])
    wires.greet(zs, n)
    wait_out.wait()
    wait_small.wait()
    out_z = DepthGather(wires, lambda i: w_out_v.at[i])
    DepthGather.start([out_z])
    qkv_x = [wires.put(qkv_send.at[flip(c, m)], w_qkv_v.at[z, c], 0, m) for m in range(1, n)]
    for copy in qkv_x:
        copy.start()
    small_z = [wires.put(small_v.at[z, c], small_v.at[z, c], m, 0) for m in range(1, zs)]
    for copy in small_z:
        copy.start()
    xs_g = LayerGather(wires, lambda i: block_of(wide_x, i))
    xs_g.start()
    pack_columns(
        gu_send, [(w, block, at, size) for at, size in halves for w in (w_gate, w_up)], n, zs
    )
    wait_own_gu = moves.load(gu_send.at[c], w_gu_v.at[z, c])
    for copy in small_z:
        copy.wait_recv()
    small_x = [wires.put(small_v.at[:, c], small_v.at[:, c], 0, m) for m in range(1, n)]
    for copy in small_x:
        copy.start()
    wait_own_qkv.wait()
    for copy in qkv_x:
        copy.wait_recv()
    number = 4
    qkv_z = [
        DepthGather(wires, lambda i, a=a, s=s: w_qkv_v.at[i, a : a + s])
        for a, s in pieces_of(n, number, 1)
    ]
    DepthGather.start(qkv_z)
    gu_x = [wires.put(gu_send.at[flip(c, m)], w_gu_v.at[z, c], 0, m) for m in range(1, n)]
    for copy in gu_x:
        copy.start()
    out_z.forward()
    for m in (2, 4, 6):
        xs_g.forward(m)

    for copy in small_x:
        copy.wait()
    for r in range(4):
        norms[r : r + 1] = jnp.concatenate(
            [
                jnp.where(
                    lane_half == 0,
                    small_v[d // n, d % n, r : r + 1],
                    small_v[d // n, d % n + 1, r : r + 1],
                )
                for d in range(0, zs * n, 2)
            ],
            -1,
        )
    norms[4:8] = jnp.zeros_like(norms[4:8])
    per_owner = 3 * zs * n // (zs * n)
    for i in range(3):
        for j in range(0, zs, 2):
            both = []
            for h in range(2):
                group = i * zs * n + (j + h) * n + c
                owner, k = group // per_owner, group % per_owner
                tile = small_v[owner // n, owner % n]
                row = jnp.where(k == 2, tile[5:6], tile[4:5])
                both.append(jnp.where(k % 2 == h, row, pltpu.roll(row, HEAD_DIM, 1)))
            at = (i * zs + j) * HEAD_DIM
            bias_v[:, at : at + lanes] = jnp.where(lane_half == 0, both[0], both[1])

    for m in (1, 3, 5, 7):
        xs_g.arrived(m)
    hidden_v[...] = block_of(wide_x, c)[...].astype(f32)

    def norm_one(i, carry):
        x = wide_x[pair_at(i)].astype(f32)
        wide_a[pair_at(i)] = (layer_stats(x)[0] * norms[0:1] + norms[1:2]).astype(b16)
        return carry

    lax.fori_loop(0, n // 2, norm_one, 0)
    wait_a1 = moves.load(wide_a, a1_out)
    wait_own_gu.wait()
    for copy in gu_x:
        copy.wait_recv()
    gu_z = [
        [
            DepthGather(
                wires, lambda i, a=a, s=s, k=slice(at, at + 2 * size): w_gu_v.at[i, a : a + s, :, k]
            )
            for a, s in pieces_of(n, number, 1)
        ]
        for at, size in spans
    ]
    for part in qkv_z:
        part.forward()
    for part in gu_z:
        DepthGather.start(part)
    waits[1].wait()
    by_slot(dy_v.at[c], raw_v.at[1])
    dy_g = LayerGather(wires, lambda i: dy_v.at[i])
    dy_g.start()
    for part in (out_z, *qkv_z):
        part.finish()
    moves.store(w_qkv_v, w_qkv_out)
    moves.store(w_out_v, w_out_out)

    def project(i, carry):
        joined = dot(wide_a[pair_at(i)], w_qkv_v[...].reshape(width, 3 * hc)) + bias_v[...]
        for j in range(2):
            table = [tables[k, 2 * i + j] for k in range(3)]
            for s in range(slots):
                at = (j * slots + s) * rows
                piece = joined[at : at + rows]
                qkv_v[0, s, 2 * i + j] = turn_pair(piece[:, :hc], table, 1.0).astype(b16)
                qkv_v[1, s, 2 * i + j] = turn_pair(piece[:, hc : 2 * hc], table, 1.0).astype(b16)
                qkv_v[2, s, 2 * i + j] = piece[:, 2 * hc :].astype(b16)
        return carry

    lax.fori_loop(0, n // 2, project, 0)
    moves.store(qkv_v, qkv_out)
    for m in (2, 4, 6):
        dy_g.forward(m)

    half = seq // 2
    probs_sem = moves.sems.at[next(moves.number)]

    def attend(s, carry):
        q, k, v = [qkv_v[i, s].reshape(seq, hc) for i in range(3)]
        length = lengths[0, s]
        kept = pltpu.make_async_copy(probs_v, probs_out.at[s], probs_sem)
        for part_q in range(2):
            keys = (part_q + 1) * half
            at = part_q * half
            query = q[at : at + half]
            row = lax.broadcasted_iota(jnp.int32, (half, keys), 0) + at
            key = lax.broadcasted_iota(jnp.int32, (half, keys), 1)
            allowed = (key <= row) & (row < length)
            out = jnp.zeros((half, hc), f32)
            for h in range(heads):
                mask = head_mask(half, hc, h)
                scores = dot(jnp.where(mask, query, 0).astype(b16), k[:keys], ((1,), (1,)))
                scores = jnp.where(allowed, scores * 0.125, masked_value)
                peak = jnp.max(scores, -1, keepdims=True)
                weights = jnp.where(allowed, jnp.exp(scores - peak), 0.0)
                total = jnp.maximum(jnp.sum(weights, -1, keepdims=True), 1.0)
                probs = (weights * (1.0 / total)).astype(b16)
                probs_v[h, at : at + half, 0:keys] = probs
                if keys < seq:
                    probs_v[h, at : at + half, keys:seq] = jnp.zeros((half, seq - keys), b16)
                out = jnp.where(mask, dot(probs, v[:keys]), out)
            ob_v[part_q * n // 2 : (part_q + 1) * n // 2, s] = out.astype(b16).reshape(
                n // 2, rows, hc
            )
        kept.start()
        kept.wait()
        return carry

    lax.fori_loop(0, slots, attend, 0)
    moves.store(ob_v, ob_out)
    for part in gu_z[0][:2]:
        part.forward()

    xs_g.sent()

    def to_hidden(i, carry):
        block_of(wide_x, i)[...] = dot(
            ob_v[i].reshape(local_rows, hc), w_out_v[...].reshape(hc, width)
        ).astype(b16)
        return carry

    lax.fori_loop(0, n, to_hidden, 0)
    wait_a1.wait()
    sums = LayerScatter(
        wires, lambda i: block_of(wide_x, i), lambda j: near.at[j], lambda j: far.at[j]
    )
    sums.start()
    for m in (6, 4, 2):
        sums.step(m)
    for part in gu_z[0][2:]:
        part.forward()
    hidden = hidden_v[...] + sums.total()
    hidden_v[...] = hidden
    moves.store(hidden_v, hidden_out)
    block_of(wide_a, c)[...] = (layer_stats(hidden)[0] * norms[2:3] + norms[3:4]).astype(b16)
    a2_g = LayerGather(wires, lambda i: block_of(wide_a, i))
    a2_g.start()
    gu_z[1][0].forward()
    for m in (2, 4, 6):
        a2_g.forward(m)
    for part in gu_z[1][1:]:
        part.forward()
    wait_down.wait()
    tile = width // number
    columns = [slice(p * tile, (p + 1) * tile) for p in range(number)]
    down_z = [ChainGather(wires, lambda i, k=k: w_down_v.at[i, :, k]) for k in columns]
    for chain in down_z:
        chain.start()
    for m in (1, 3, 5, 7):
        dy_g.arrived(m)
    for m in (1, 3, 5, 7):
        a2_g.arrived(m)
    wait_a2 = moves.load(wide_a, a2_out)

    down_sums = []
    for step, ((at, size), (start, count), parts) in enumerate(zip(halves, spans, gu_z)):
        units, gates = slice(at, at + size), slice(start, start + 2 * count)
        inner = slice(zs * at, zs * (at + size))
        for part in parts:
            part.finish()

        def feed(i, carry, inner=inner, gates=gates, count=count):
            gu = dot(wide_a[pair_at(i)], w_gu_v[:, :, :, gates].reshape(width, 2 * count))
            gu_v[i, :, gates] = gu.astype(b16)
            gate = gu[:, :count]
            zz_v[i, :, inner] = (gate * jax.nn.sigmoid(gate) * gu[:, count:]).astype(b16)
            return carry

        lax.fori_loop(0, n // 2, feed, 0)
        if step == 1:
            down_z[0].hop(1)
            down_z[1].hop(1)
        chains = []
        for p in range(2):
            k = slice(p * width // 2, (p + 1) * width // 2)
            for q in columns[2 * p : 2 * p + 2]:
                gd = dot(
                    zz_v[:, :, inner].reshape(tokens, count),
                    dy_v[:, :, q].reshape(tokens, tile),
                    ((0,), (0,)),
                )
                gd_v[:, units, q] = gd.astype(b16).reshape(zs, size, tile)
            chains.append(
                ChainScatter(
                    wires,
                    lambda i, u=units, k=k: gd_v.at[i, u, k],
                    lambda i, u=units, k=k: right_v.at[i - 1, u, k],
                    lambda i, u=units, k=k: left_v.at[i, u, k],
                )
            )
            chains[-1].start(3)
            down_sums.append((units, k, chains[-1]))
            if step == 1:
                down_z[2 + p].hop(1)
                down_z[p].hop(2)
        for distance in (2, 1):
            for chain in chains:
                chain.start(distance)
        for chain in chains:
            chain.clear()
    moves.store(w_gu_v, w_gu_out)
    sums.sent()
    a2_g.sent()
    wait_a2.wait()

    def products(p):
        k = columns[p]

        def rows_of(i, carry):
            dy_rows = dy_v[pl.ds(2 * i, 2), :, k].reshape(pair, tile)
            y = jnp.zeros((pair, tile), f32)
            for at, size in halves:
                weight = w_down_v[:, at : at + size, k].reshape(zs * size, tile)
                inner = slice(zs * at, zs * (at + size))
                dz = dot(dy_rows, weight, ((1,), (1,)))
                dz_v[i, :, inner] = dz if p == 0 else dz_v[i, :, inner] + dz
                y = y + dot(zz_v[i, :, inner], weight)
            wide_x[pair_at(i), k] = y.astype(b16)
            return carry

        lax.fori_loop(0, n // 2, rows_of, 0)

    down_z[2].hop(2)
    down_z[3].hop(2)
    chains = [chain for _, _, chain in down_sums]
    for t in range(number):
        chains[t].hop(1, 3)
        down_z[t].finish()
        products(t)
    moves.store(wide_x, y_out)
    for pair_of in (chains[:2], chains[2:]):
        for chain in pair_of:
            chain.hop(1, 2)
        for chain in pair_of:
            chain.hop(2, 3)

    def back(i, carry):
        for (at, size), (start, count) in zip(halves, spans):
            dz = dz_v[i, :, zs * at : zs * (at + size)]
            gate = gu_v[i, :, start : start + count].astype(f32)
            up = gu_v[i, :, start + count : start + 2 * count].astype(f32)
            sig = jax.nn.sigmoid(gate)
            dg = dz * up * sig * (1.0 + gate * (1.0 - sig))
            du = dz * gate * sig
            gu_v[i, :, start : start + 2 * count] = jnp.concatenate([dg, du], -1).astype(b16)
        return carry

    lax.fori_loop(0, n // 2, back, 0)
    moves.store(gu_v, dgu_out)
    for units, k, chain in down_sums:
        grad_down_out[units, k] = chain.total()
    for group in (*chains, dy_g):
        group.sent()
    for copy in (*small_z, *qkv_x, *gu_x):
        copy.wait_send()
    moves.finish()


def front(zs, n, lengths, tables, small, w_qkv, w_gate, w_up, w_out, w_down, inputs, cotangent):
    f32, b16 = jnp.float32, jnp.bfloat16
    rows, slots, width = inputs.shape
    local = rows * slots
    seq, tokens = rows * n, local * n
    heads = HEADS // n
    hc = heads * HEAD_DIM
    wrows = w_out.shape[0]
    block = w_down.shape[0]
    gc = 2 * zs * block
    qkv_all = ((zs, n, wrows, 3 * hc), b16)
    out_all = ((zs, wrows, width), b16)
    gu_all = ((zs, n, wrows, gc), b16)
    down_all = ((zs, block, width), b16)
    wide = ((tokens, width), b16)
    qkv = ((3, slots, n, rows, hc), b16)
    probs = ((slots, heads, seq, seq), b16)
    ob = ((n, slots, rows, hc), b16)
    hidden = ((local, width), f32)
    gu = ((n // 2, 2 * local, gc), b16)
    outs = [
        qkv_all,
        out_all,
        gu_all,
        wide,
        qkv,
        probs,
        ob,
        hidden,
        wide,
        gu,
        wide,
        ((block, width), f32),
        ((8, width), f32),
    ]
    scratch = [
        ((n, wrows, 3 * hc), b16),
        ((n, wrows, gc), b16),
        ((zs, n, *small.shape), f32),
        ((1, 3 * hc), f32),
        qkv_all,
        out_all,
        gu_all,
        down_all,
        wide,
        wide,
        ((n, local, width), b16),
        qkv,
        (probs[0][1:], b16),
        ob,
        ((n // 2, local, width), b16),
        ((n // 2 - 1, local, width), b16),
        hidden,
        gu,
        ((n // 2, 2 * local, gc // 2), b16),
        ((n // 2, 2 * local, gc // 2), f32),
        down_all,
        ((zs - 1, block, width), b16),
        ((zs - 1, block, width), b16),
        ((2, *inputs.shape), b16),
    ]
    return pl.pallas_call(
        functools.partial(front_kernel, zs, n, slots),
        out_shape=[jax.ShapeDtypeStruct(*k) for k in outs],
        in_specs=[pl.BlockSpec(memory_space=pltpu.SMEM), VMEM, HBM, *[VMEM] * 3, *[HBM] * 4],
        out_specs=[HBM] * (len(outs) - 2) + [VMEM] * 2,
        scratch_shapes=[
            *[pltpu.VMEM(*k) for k in scratch],
            pltpu.SemaphoreType.DMA((192,)),
            pltpu.SemaphoreType.DMA((192,)),
            pltpu.SemaphoreType.DMA((32,)),
        ],
        compiler_params=pltpu.CompilerParams(
            collective_id=1, has_side_effects=True, vmem_limit_bytes=VMEM_LIMIT
        ),
        name="front",
    )(lengths, tables, small, w_qkv, w_gate, w_up, w_out, w_down, inputs, cotangent)


def unpack_columns(dst, src, parts, n, zs):
    dst[...] = jnp.concatenate(
        [
            src[i, :, at + size * j : at + size * (j + 1)]
            for j in range(zs)
            for i in range(n)
            for at, size in parts
        ],
        -1,
    ).astype(dst.dtype)


def backward_kernel(
    zs,
    n,
    norms,
    tables,
    a1_all,
    a2_all,
    dgu,
    w_gu,
    w_qkv,
    w_out,
    qkv,
    probs,
    ob,
    hidden,
    cotangent,
    inputs,
    y_part,
    grad_out_out,
    result_out,
    input_grad_out,
    gq_out,
    gu_out,
    small_out,
    wide_v,
    dgu_v,
    weight_v,
    w_out_v,
    qkv_v,
    probs_v,
    ob_v,
    hidden_v,
    own_v,
    raw_v,
    ggu_v,
    relay_v,
    box_v,
    near,
    far,
    dh_all,
    go_v,
    go_relay,
    go_box,
    dqkv_v,
    dj_v,
    bias_v,
    gq_relay,
    gq_box,
    gu_rows,
    gq_rows,
    small_v,
    small_x,
    small_r,
    small_z,
    send,
    recv,
    local,
    free,
):
    f32, b16 = jnp.float32, jnp.bfloat16
    wires = Wires(send, recv)
    moves = Moves(local)
    z, c = wires.z, wires.c
    _, slots, rows, hc = ob_v.shape
    width = dh_all.shape[-1]
    tokens, seq, local_rows = n * slots * rows, n * rows, slots * rows
    heads = hc // HEAD_DIM
    depth, gc = ggu_v.shape[1:]
    ffc, qc = gc // 2, 3 * hc
    wrows = depth // n
    part = wide_v
    gu_weight = weight_v.at[:, :, 0:gc]
    qkv_weight, gq_v = weight_v.at[:, :, 0:qc], weight_v.at[:, :, qc : 2 * qc]

    wait_a2 = moves.load(a2_all, wide_v)
    wait_dy = moves.load(cotangent, raw_v)
    wait_dgu = moves.load(dgu, dgu_v)
    wait_w = moves.load(w_gu, gu_weight)
    waits = [
        moves.load(hidden, hidden_v),
        moves.load(w_out, w_out_v),
        moves.load(qkv, qkv_v),
        moves.load(probs.at[0], probs_v),
        moves.load(ob, ob_v),
    ]
    wires.greet(zs, n)
    wait_a2.wait()
    wait_dgu.wait()

    number = 4
    size = depth // number
    step = 2 * size

    def scatters(whole, relay, box):
        return [
            DepthScatter(
                wires,
                lambda i, a=p * size: whole.at[i, a : a + size],
                relay.at[p * size : (p + 1) * size],
                [box.at[j, p * size : (p + 1) * size] for j in range(3)],
            )
            for p in range(number)
        ]

    def weigh(sums, whole, left_v, grads, also=None):
        for mask in (3, 2, 1, 0):
            to = flip(z, mask)

            def piece(p, carry, to=to):
                at = pl.multiple_of(to * depth + p * step, step)
                left = left_v[:, :, pl.ds(at, step)].reshape(tokens, step)
                whole[to, pl.ds(pl.multiple_of(p * step, step), step)] = dot(
                    left, grads(), ((0,), (0,))
                ).astype(b16)
                return carry

            lax.fori_loop(0, number // 2, piece, 0)
            for part_sum in sums:
                part_sum.start(mask)
            if mask == 3 and also is not None:
                also.start(3)

    gu_sums = scatters(ggu_v, relay_v, box_v)
    weigh(gu_sums, ggu_v, wide_v, lambda: dgu_v[...].reshape(tokens, gc))

    wait_w.wait()

    def normed_two(i, carry):
        part[pl.ds(2 * i, 2)] = (
            dot(dgu_v[i], gu_weight[...].reshape(width, gc), ((1,), (1,)))
            .astype(b16)
            .reshape(2, local_rows, width)
        )
        return carry

    lax.fori_loop(0, n // 2, normed_two, 0)
    wait_qkv = moves.load(w_qkv, qkv_weight)
    da2_sums = LayerScatter(
        wires, lambda i: part.at[i], lambda j: near.at[j], lambda j: far.at[j]
    )
    da2_sums.start()
    gu_sums[0].relay()
    for m in (6, 4, 2):
        da2_sums.step(m)
    for copy in waits:
        copy.wait()
    wait_dy.wait()
    by_slot(own_v, raw_v)
    wait_xs = moves.load(inputs, raw_v)
    n2, r2 = layer_stats(hidden_v[...])
    for part_sum in gu_sums[1:]:
        part_sum.relay()
    da2 = da2_sums.total()
    gains = [jnp.sum(da2 * n2, 0, keepdims=True), jnp.sum(da2, 0, keepdims=True)]
    dh = own_v[...].astype(f32) + norm_back(da2, n2, r2, norms[2:3])
    by_position(input_grad_out, dh)
    dh_all[c] = dh.astype(b16)
    dh_g = LayerGather(wires, lambda i: dh_all.at[i])
    dh_g.start()
    for m in (2, 4, 6):
        dh_g.forward(m)
    for m in (1, 3, 5, 7):
        dh_g.arrived(m)

    go_sums = DepthScatter(
        wires, lambda i: go_v.at[i], go_relay, [go_box.at[j] for j in range(3)]
    )
    tile = width // 4

    def heads_grad(p, carry):
        at = pl.ds(pl.multiple_of(p * tile, tile), tile)
        go = dot(
            ob_v[...].reshape(tokens, hc), dh_all[:, :, at].reshape(tokens, tile), ((0,), (0,))
        )
        go_v[:, :, at] = go.astype(b16).reshape(zs, hc // zs, tile)
        return carry

    lax.fori_loop(0, 4, heads_grad, 0)

    def heads_back(i, carry):
        ob_v[i] = (
            dot(dh_all[i], w_out_v[...].reshape(hc, width), ((1,), (1,)))
            .astype(b16)
            .reshape(slots, rows, hc)
        )
        return carry

    lax.fori_loop(0, n, heads_back, 0)
    dh_g.sent()
    wait_a1 = moves.load(a1_all, dh_all)
    half = seq // 2

    def attend(s, carry):
        q, k, v = [qkv_v[i, s].reshape(seq, hc) for i in range(3)]
        do_s = ob_v[:, s].reshape(seq, hc)
        dqkv_v[...] = jnp.zeros_like(dqkv_v)
        for part_q in range(2):
            keys = (part_q + 1) * half
            at = part_q * half
            query, do_q = q[at : at + half], do_s[at : at + half]
            dq = jnp.zeros((half, hc), f32)
            for h in range(heads):
                mask, mask_k = head_mask(half, hc, h), head_mask(keys, hc, h)
                do_h = jnp.where(mask, do_q, 0).astype(b16)
                low = probs_v[h, at : at + half, 0:keys]
                p32 = low.astype(f32)
                t = p32 * dot(do_h, v[:keys], ((1,), (1,)))
                ds = (t - p32 * jnp.sum(t, -1, keepdims=True)).astype(b16)
                dq = jnp.where(mask, dot(ds, k[:keys]), dq)
                dk = dot(ds, query, ((0,), (0,)))
                dv = dot(low, do_h, ((0,), (0,)))
                dqkv_v[1, 0:keys] += jnp.where(mask_k, dk, 0.0)
                dqkv_v[2, 0:keys] += dv
            dqkv_v[0, at : at + half] = dq

        @pl.when(s + 1 < slots)
        def _():
            copy = pltpu.make_async_copy(probs.at[s + 1], probs_v, probs_sem)
            copy.start()
            copy.wait()

        dq, dk = dqkv_v[0] * 0.125, dqkv_v[1] * 0.125
        table = [tables[i].reshape(seq, 2 * HEAD_DIM) for i in range(3)]
        dj = [turn_pair(dq, table, -1.0), turn_pair(dk, table, -1.0), dqkv_v[2]]
        for i in range(3):
            low = dj[i].astype(b16)
            dj_v[:, s, :, i * hc : (i + 1) * hc] = low.reshape(n, rows, hc)
            bias_v[:, i * hc : (i + 1) * hc] += jnp.sum(low.astype(f32), 0, keepdims=True)
        return carry

    bias_v[...] = jnp.zeros_like(bias_v)

    probs_sem = moves.sems.at[next(moves.number)]
    lax.fori_loop(0, slots, attend, 0)

    wait_a1.wait()
    wait_qkv.wait()
    qkv_sums = scatters(gq_v, gq_relay, gq_box)
    weigh(qkv_sums, gq_v, dh_all, lambda: dj_v[...].reshape(tokens, qc), go_sums)
    for mask in (2, 1, 0):
        go_sums.start(mask)

    def normed_one(i, carry):
        part[pl.ds(2 * i, 2)] = (
            dot(
                dj_v[pl.ds(2 * i, 2)].reshape(2 * local_rows, qc),
                qkv_weight[...].reshape(width, qc),
                ((1,), (1,)),
            )
            .astype(b16)
            .reshape(2, local_rows, width)
        )
        return carry

    da2_sums.sent()
    lax.fori_loop(0, n // 2, normed_one, 0)
    da1_sums = LayerScatter(
        wires, lambda i: part.at[i], lambda j: near.at[j], lambda j: far.at[j]
    )
    da1_sums.start()
    for m in (6, 4, 2):
        da1_sums.step(m)

    for p, part_sum in enumerate(gu_sums):
        ggu_v[z, p * size : (p + 1) * size] = part_sum.total().astype(b16)
    gu_x = [
        wires.put(
            ggu_v.at[z, pl.ds(pl.multiple_of(flip(c, m) * wrows, wrows), wrows)],
            gu_rows.at[c],
            0,
            m,
        )
        for m in range(1, n)
    ]
    for copy in gu_x:
        copy.start()
    gu_rows[c] = ggu_v[z, pl.ds(pl.multiple_of(c * wrows, wrows), wrows)]

    for part_sum in qkv_sums:
        part_sum.relay()
    go_sums.relay()

    wait_xs.wait()
    by_slot(own_v, raw_v)
    n1, r1 = layer_stats(own_v[...].astype(f32))
    da1 = da1_sums.total()
    for m in (1, 2, 4, 6):
        pl.semaphore_signal(free, inc=1, device_id=(z, flip(c, m)), device_id_type=MESH)
    da1_sums.sent()
    wait_y = moves.load(y_part, part)
    grad = norm_back(da1, n1, r1, norms[0:1])
    for s in range(slots):
        input_grad_out[:, s, :] += grad[s * rows : (s + 1) * rows]
    gains = [jnp.sum(da1 * n1, 0, keepdims=True), jnp.sum(da1, 0, keepdims=True), *gains]
    chips = n // 2
    lanes = 2 * HEAD_DIM
    lane_half = lax.broadcasted_iota(jnp.int32, (1, lanes), 1) // HEAD_DIM
    bias_part = bias_v[...]
    for j in range(zs):
        for chip in range(chips):
            k = j * chips + chip
            for r in range(4):
                small_v[j, chip, r : r + 1] = gains[r][:, k * lanes : (k + 1) * lanes]
            small_v[j, chip, 7:8] = jnp.zeros((1, lanes), f32)
    for i in range(3):
        for j in range(zs):
            at = i * hc + j * HEAD_DIM
            piece = bias_part[:, at : at + HEAD_DIM]
            both = jnp.concatenate([piece, piece], -1)
            for chip in range(chips):
                tile = (i * zs + j) * chips + chip
                pair, row = tile // 3, tile % 3
                small_v[pair // chips, pair % chips, 4 + row : 5 + row] = jnp.where(
                    (lane_half == c % 2) & (c // 2 == chip), both, 0.0
                )
    small_v_x = [
        wires.put(small_v.at[:, flip(c, m) // 2], small_x.at[m], 0, m) for m in range(1, n)
    ]
    for copy in small_v_x:
        copy.start()

    wait_y.wait()
    pl.semaphore_wait(free, 4)
    y_sums = LayerScatter(
        wires, lambda i: part.at[i], lambda j: near.at[j], lambda j: far.at[j]
    )
    y_sums.start()
    for m in (6, 4, 2):
        y_sums.step(m)
    small_sum = small_v[:, c // 2]
    for m in range(1, n):
        small_v_x[m - 1].wait_recv()
        small_sum = small_sum + small_x[m]
    small_r[...] = small_sum
    small_z_x = [wires.put(small_r.at[flip(z, m)], small_z.at[m], m, 0) for m in range(1, zs)]
    for copy in small_z_x:
        copy.start()
    for copy in gu_x:
        copy.wait_recv()
    moves.store(gu_rows, gu_out)
    for p, part_sum in enumerate(qkv_sums):
        gq_v[z, p * size : (p + 1) * size] = part_sum.total().astype(b16)
    gq_x = [
        wires.put(
            gq_v.at[z, pl.ds(pl.multiple_of(flip(c, m) * wrows, wrows), wrows)],
            gq_rows.at[c],
            0,
            m,
        )
        for m in range(1, n)
    ]
    for copy in gq_x:
        copy.start()
    gq_rows[c] = gq_v[z, pl.ds(pl.multiple_of(c * wrows, wrows), wrows)]
    by_position(result_out, hidden_v[...] + y_sums.total())
    small_sum = small_r[z]
    for m in range(1, zs):
        small_z_x[m - 1].wait_recv()
        small_sum = small_sum + small_z[m]
    small_out[...] = small_sum
    hidden_v[0:wrows] = go_sums.total()
    moves.store(hidden_v.at[0:wrows], grad_out_out)
    for group in (*gu_sums, go_sums, *qkv_sums, y_sums):
        group.sent()
    for copy in (*gu_x, *small_v_x, *small_z_x):
        copy.wait_send()
    for copy in gq_x:
        copy.wait()
    moves.store(gq_rows, gq_out)
    moves.finish()


def backward(zs, n, norms, tables, *arrays):
    f32, b16 = jnp.float32, jnp.bfloat16
    a1_all, a2_all, dgu, w_gu, w_qkv, w_out, qkv, probs, ob, hidden, _, inputs, _ = arrays
    _, slots, rows, hc = ob.shape
    local, width = hidden.shape
    _, depth, gc = w_gu.shape
    qc = 3 * hc
    wrows = depth // n
    seq = n * rows
    wide = (n, local, width)

    def buf(like):
        return pltpu.VMEM(like.shape, like.dtype)

    return pl.pallas_call(
        functools.partial(backward_kernel, zs, n),
        out_shape=[
            jax.ShapeDtypeStruct((hc // zs, width), f32),
            jax.ShapeDtypeStruct(inputs.shape, b16),
            jax.ShapeDtypeStruct(inputs.shape, f32),
            jax.ShapeDtypeStruct((n, wrows, qc), b16),
            jax.ShapeDtypeStruct((n, wrows, gc), b16),
            jax.ShapeDtypeStruct((8, 2 * HEAD_DIM), f32),
        ],
        in_specs=[VMEM] * 2 + [HBM] * 13,
        out_specs=[HBM, VMEM, VMEM, HBM, HBM, VMEM],
        scratch_shapes=[
            pltpu.VMEM(wide, b16),
            buf(dgu),
            pltpu.VMEM((zs, depth, max(gc, 2 * qc)), b16),
            buf(w_out),
            buf(qkv),
            pltpu.VMEM(probs.shape[1:], b16),
            buf(ob),
            buf(hidden),
            pltpu.VMEM((local, width), b16),
            pltpu.VMEM(inputs.shape, b16),
            pltpu.VMEM((zs, depth, gc), b16),
            pltpu.VMEM((depth, gc), b16),
            pltpu.VMEM((3, depth, gc), b16),
            pltpu.VMEM((n // 2, local, width), b16),
            pltpu.VMEM((n // 2 - 1, local, width), b16),
            pltpu.VMEM(wide, b16),
            pltpu.VMEM((zs, hc // zs, width), b16),
            pltpu.VMEM((hc // zs, width), b16),
            pltpu.VMEM((3, hc // zs, width), b16),
            pltpu.VMEM((3, seq, hc), f32),
            pltpu.VMEM((n, slots, rows, qc), b16),
            pltpu.VMEM((1, qc), f32),
            pltpu.VMEM((depth, qc), b16),
            pltpu.VMEM((3, depth, qc), b16),
            pltpu.VMEM((n, wrows, gc), b16),
            pltpu.VMEM((n, wrows, qc), b16),
            pltpu.VMEM((zs, n // 2, 8, 2 * HEAD_DIM), f32),
            pltpu.VMEM((n, zs, 8, 2 * HEAD_DIM), f32),
            pltpu.VMEM((zs, 8, 2 * HEAD_DIM), f32),
            pltpu.VMEM((zs, 8, 2 * HEAD_DIM), f32),
            pltpu.SemaphoreType.DMA((96,)),
            pltpu.SemaphoreType.DMA((96,)),
            pltpu.SemaphoreType.DMA((24,)),
            pltpu.SemaphoreType.REGULAR,
        ],
        compiler_params=pltpu.CompilerParams(
            collective_id=4, has_side_effects=True, vmem_limit_bytes=VMEM_LIMIT
        ),
        name="backward",
    )(norms, tables, *arrays)


def finish_kernel(
    zs,
    n,
    gq,
    gu,
    small,
    grad_out,
    grad_down,
    result,
    input_grad,
    qkv_out,
    gate_out,
    up_out,
    grad_out_out,
    grad_down_out,
    result_out,
    input_grad_out,
    bias_out,
    gain_one_out,
    shift_one_out,
    gain_two_out,
    shift_two_out,
    gq_v,
    gu_v,
    qkv_v,
    gate_v,
    up_v,
    grad_out_v,
    grad_down_v,
    result_v,
    input_grad_v,
    local,
):
    moves = Moves(local)
    width = grad_out.shape[1]
    wait_gu = moves.load(gu, gu_v)
    wait_gq = moves.load(gq, gq_v)
    passed = [
        (moves.load(src, held), held, dst)
        for src, held, dst in (
            (input_grad, input_grad_v, input_grad_out),
            (grad_down, grad_down_v, grad_down_out),
            (result, result_v, result_out),
            (grad_out, grad_out_v, grad_out_out),
        )
    ]
    odd = lax.axis_index("ctx") % 2
    for r, out in enumerate((gain_one_out, shift_one_out, gain_two_out, shift_two_out)):
        row = small[r : r + 1]
        out[...] = jnp.where(odd == 0, row[:, :HEAD_DIM], row[:, HEAD_DIM:])
    bias = jnp.concatenate([small[4 + r : 5 + r] for r in range(3)], -1)
    size = bias_out.shape[1]
    bias_out[...] = jnp.where(odd == 0, bias[:, :size], bias[:, size:])
    ffc = gu_v.shape[-1] // 2
    halves = halves_of(ffc // zs)
    for copy, held, dst in passed:
        copy.wait()
        moves.store(held, dst)
    wait_gu.wait()
    unpack_columns(gate_v, gu_v, [(2 * zs * at, size) for at, size in halves], n, zs)
    moves.store(gate_v, gate_out)
    unpack_columns(up_v, gu_v, [(zs * (2 * at + size), size) for at, size in halves], n, zs)
    moves.store(up_v, up_out)
    wait_gq.wait()
    hc = gq_v.shape[-1] // 3
    for i in range(3):
        unpack_columns(
            qkv_v.at[:, i * width : (i + 1) * width], gq_v, [(i * hc, HEAD_DIM)], n, zs
        )
    moves.store(qkv_v, qkv_out)
    moves.finish()


def finish(zs, n, gq, gu, small, grad_out, grad_down, result, input_grad):
    f32 = jnp.float32
    _, wrows, qc = gq.shape
    gc = gu.shape[-1]
    wide = [((wrows, n * qc), f32), ((wrows, n * gc // 2), f32), ((wrows, n * gc // 2), f32)]
    whole = [(v.shape, v.dtype) for v in (grad_out, grad_down, result, input_grad)]
    rows = [((1, 3 * HEAD_DIM), f32), *[((1, wrows), f32)] * 4]
    return pl.pallas_call(
        functools.partial(finish_kernel, zs, n),
        out_shape=[jax.ShapeDtypeStruct(*k) for k in (*wide, *whole, *rows)],
        in_specs=[HBM, HBM, VMEM, HBM, HBM, HBM, HBM],
        out_specs=[HBM] * 7 + [VMEM] * 5,
        scratch_shapes=[
            pltpu.VMEM(gq.shape, gq.dtype),
            pltpu.VMEM(gu.shape, gu.dtype),
            *[pltpu.VMEM(*k) for k in (*wide, *whole)],
            pltpu.SemaphoreType.DMA((16,)),
        ],
        compiler_params=pltpu.CompilerParams(vmem_limit_bytes=VMEM_LIMIT),
        name="finish",
    )(gq, gu, small, grad_out, grad_down, result, input_grad)


def tensor_shards(
    inputs,
    lengths,
    w_qkv,
    b_qkv,
    w_out,
    w_gate,
    w_up,
    w_down,
    gain_one,
    shift_one,
    gain_two,
    shift_two,
    cotangent,
):
    rows, slots, width = inputs.shape
    f32, b16 = jnp.float32, jnp.bfloat16
    zs, n = lax.axis_size("dp"), lax.axis_size("ctx")
    me = lax.axis_index("ctx")
    local = rows * slots
    seq = rows * n
    wrows = w_qkv.shape[0]
    ff_block = w_down.shape[0]
    hc = HEADS // n * HEAD_DIM
    ffc = ff_block * zs

    nb = b_qkv.shape[0]
    vectors = [v for gain in (gain_one, shift_one, gain_two, shift_two) for v in (gain, gain)]
    small, at = jnp.zeros(1024, f32), 0
    for vector in (*vectors, b_qkv):
        size = vector.shape[0]
        small = small + jnp.pad(vector.astype(f32), (at, 1024 - at - size))
        at += size
    small = small.reshape(8, 128)

    angles = np.arange(seq)[:, None] * 10000.0 ** (-2.0 * np.arange(ROTARY // 2) / ROTARY)[None, :]
    cos_t, sin_t = np.cos(angles), np.sin(angles)
    zero, rest = np.zeros_like(sin_t), np.zeros((seq, HEAD_DIM - ROTARY))
    tables = np.stack(
        [
            np.concatenate(two, -1)
            for two in (
                2 * [cos_t, cos_t, rest + 1.0],
                2 * [-sin_t, zero, rest],
                2 * [zero, sin_t, rest],
            )
        ]
    ).astype(np.float32)

    tables = jnp.asarray(tables.reshape(3, n, rows, 2 * HEAD_DIM))
    w_qkv_c, w_out_c, w_gu_c, a1, qkv, probs, ob, hidden, a2, dgu, y, grad_down, norms = front(
        zs, n, lengths, tables, small, w_qkv, w_gate, w_up, w_out, w_down, inputs, cotangent
    )
    wide = (n, local, width)
    grad_out, result, input_grad, gq, gu, sums = backward(
        zs, n, norms, tables, a1.reshape(wide), a2.reshape(wide), dgu,
        w_gu_c.reshape(zs, n * wrows, 2 * ffc), w_qkv_c.reshape(zs, n * wrows, 3 * hc),
        w_out_c, qkv, probs, ob, hidden, cotangent, inputs,
        y.reshape(wide),
    )
    grad_qkv, grad_gate, grad_up, grad_out, grad_down, result, input_grad, *rows = finish(
        zs, n, gq, gu, sums, grad_out, grad_down, result, input_grad
    )
    grad_bias, grad_gain_one, grad_shift_one, grad_gain_two, grad_shift_two = [
        row.reshape(row.shape[1]) for row in rows
    ]
    return (
        result,
        input_grad,
        grad_qkv,
        grad_bias,
        grad_out,
        grad_gate,
        grad_up,
        grad_down,
        grad_gain_one,
        grad_shift_one,
        grad_gain_two,
        grad_shift_two,
    )


def solution(mesh):
    zs, n = mesh.shape["dp"], mesh.shape["ctx"]
    shards = tensor_shards if (zs, n) == (4, 8) and HEADS == 32 else gathered_shards

    placed = (
        P("ctx", "dp", None),
        P("dp", None),
        P(("dp", "ctx"), None),
        P(("dp", "ctx")),
        P(("dp", "ctx"), None),
        P(("dp", "ctx"), None),
        P(("dp", "ctx"), None),
        P(("dp", "ctx"), None),
        P(("dp", "ctx")),
        P(("dp", "ctx")),
        P(("dp", "ctx")),
        P(("dp", "ctx")),
        P("ctx", "dp", None),
    )
    return jax.shard_map(
        shards,
        mesh=mesh,
        in_specs=placed,
        out_specs=(
            P("ctx", "dp", None),
            P("ctx", "dp", None),
            P(("dp", "ctx"), None),
            P(("dp", "ctx")),
            P(("dp", "ctx"), None),
            P(("dp", "ctx"), None),
            P(("dp", "ctx"), None),
            P(("dp", "ctx"), None),
            P(("dp", "ctx")),
            P(("dp", "ctx")),
            P(("dp", "ctx")),
            P(("dp", "ctx")),
        ),
        check_vma=False,
    )
```

```python
import functools
import itertools
import math

import jax
import jax.numpy as jnp
import numpy as np
from jax import lax
from jax.experimental import pallas as pl
from jax.experimental.pallas import tpu as pltpu
from jax.sharding import PartitionSpec as P

HEADS = 32
HEAD_DIM = 64
ROTARY = 16


epsilon = 1e-05
masked_value = -1e30


def layer_stats(values):
    row_mean = jnp.mean(values, -1, keepdims=True)
    centred = values - row_mean
    inverse = lax.rsqrt(jnp.mean(centred * centred, -1, keepdims=True) + epsilon)
    return (centred * inverse, inverse)


def norm_back(grad_normed, scaled, inverse, gain_vec):
    grad_hat = grad_normed * gain_vec
    return inverse * (
        grad_hat
        - jnp.mean(grad_hat, -1, keepdims=True)
        - scaled * jnp.mean(grad_hat * scaled, -1, keepdims=True)
    )


def rotary_tables(positions):
    counter = jnp.arange(ROTARY // 2, dtype=jnp.float32)
    frequency = 10000.0 ** (-2.0 * counter / ROTARY)
    angles = positions.astype(jnp.float32)[:, None] * frequency[None, :]
    return (jnp.cos(angles)[:, None, None, :], jnp.sin(angles)[:, None, None, :])


def rotate(values, cos_table, sin_table):
    half_dims = ROTARY // 2
    first_half = values[..., :half_dims]
    second_half = values[..., half_dims:ROTARY]
    return jnp.concatenate(
        [
            first_half * cos_table - second_half * sin_table,
            second_half * cos_table + first_half * sin_table,
            values[..., ROTARY:],
        ],
        -1,
    )


def over_blocks(step_fn, running, gathered):
    total_rows = gathered.shape[0]
    tile_rows = math.gcd(total_rows, 512)

    def visit_block(number, current):
        block_start = number * tile_rows
        block_part = lax.dynamic_slice_in_dim(gathered, block_start, tile_rows, 0)
        return step_fn(current, block_part, block_start)

    return lax.fori_loop(0, total_rows // tile_rows, visit_block, running)


def gathered_shards(
    inputs,
    lengths,
    w_qkv,
    b_qkv,
    w_out,
    w_gate,
    w_up,
    w_down,
    gain_one,
    shift_one,
    gain_two,
    shift_two,
    cotangent,
):
    local_rows, slot_count, width = inputs.shape
    positions = lax.axis_index("ctx") * local_rows + jnp.arange(local_rows, dtype=jnp.int32)
    live_rows = positions[:, None] < lengths[0][None, :]
    live_heads = jnp.transpose(live_rows)[:, None, :, None]
    cos_table, sin_table = rotary_tables(positions)

    def allowed_mask(offset, count):
        key_pos = offset + jnp.arange(count, dtype=jnp.int32)
        causal = key_pos[None, :] <= positions[:, None]
        return causal[None, None, :, :] & live_heads

    def split_heads(block_part):
        count = block_part.shape[0]
        key_part = block_part[:, :, 0].reshape(count, slot_count, HEADS, HEAD_DIM)
        value_part = block_part[:, :, 1].reshape(count, slot_count, HEADS, HEAD_DIM)
        return (key_part, value_part)

    attn_full = (
        lax.all_gather(w_qkv, ("dp", "ctx"), axis=0, tiled=True),
        lax.all_gather(b_qkv, ("dp", "ctx"), axis=0, tiled=True),
        lax.all_gather(w_out, ("dp", "ctx"), axis=0, tiled=True),
        lax.all_gather(gain_one, ("dp", "ctx"), axis=0, tiled=True),
        lax.all_gather(shift_one, ("dp", "ctx"), axis=0, tiled=True),
    )
    qkv_full, bias_full, out_full, gain_one_full, shift_one_full = attn_full
    source = inputs.astype(jnp.float32)
    scaled_one, inverse_one = layer_stats(source)
    normed_one = (
        scaled_one * gain_one_full.astype(jnp.float32) + shift_one_full.astype(jnp.float32)
    ).astype(jnp.bfloat16)
    joined = jnp.einsum(
        "rsd,de->rse", normed_one, qkv_full, preferred_element_type=jnp.float32
    ) + bias_full.astype(jnp.float32)
    query_pre = joined[..., :width].reshape(local_rows, slot_count, HEADS, HEAD_DIM)
    key_pre = joined[..., width : 2 * width].reshape(local_rows, slot_count, HEADS, HEAD_DIM)
    queries = rotate(query_pre, cos_table, sin_table).astype(jnp.bfloat16)
    keys_rot = rotate(key_pre, cos_table, sin_table).reshape(local_rows, slot_count, width)
    key_value = jnp.stack([keys_rot, joined[..., 2 * width :]], 2).astype(jnp.bfloat16)
    block_part = lax.all_gather(key_value, "ctx", axis=0, tiled=True)
    run_peak = jnp.full((slot_count, HEADS, local_rows), masked_value, jnp.float32)
    key_part, value_part = split_heads(block_part)
    scores = (
        jnp.einsum("qshd,kshd->shqk", queries, key_part, preferred_element_type=jnp.float32) * 0.125
    )
    allowed = allowed_mask(jnp.int32(0), block_part.shape[0])
    masked = jnp.where(allowed, scores, masked_value)
    new_peak = jnp.maximum(run_peak, jnp.max(masked, -1))
    weights = jnp.where(allowed, jnp.exp(masked - new_peak[..., None]), 0.0)
    new_sum = jnp.sum(weights, -1)
    new_acc = jnp.einsum(
        "shqk,kshd->shqd",
        weights.astype(jnp.bfloat16),
        value_part,
        preferred_element_type=jnp.float32,
    )
    final_sum = jnp.maximum(new_sum, 1.0)
    log_sum = new_peak + jnp.log(final_sum)
    attended = jnp.transpose(new_acc / final_sum[..., None], (2, 0, 1, 3))
    attended_low = attended.reshape(local_rows, slot_count, width).astype(jnp.bfloat16)
    hidden_in = source + jnp.einsum(
        "rsd,de->rse", attended_low, out_full, preferred_element_type=jnp.float32
    )
    mlp_full = (
        lax.all_gather(w_gate, ("dp", "ctx"), axis=0, tiled=True),
        lax.all_gather(w_up, ("dp", "ctx"), axis=0, tiled=True),
        lax.all_gather(w_down, ("dp", "ctx"), axis=0, tiled=True),
        lax.all_gather(gain_two, ("dp", "ctx"), axis=0, tiled=True),
        lax.all_gather(shift_two, ("dp", "ctx"), axis=0, tiled=True),
    )
    gate_full, up_full, down_full, gain_two_full, shift_two_full = mlp_full
    scaled_two, inverse_two = layer_stats(hidden_in)
    normed_two = (
        scaled_two * gain_two_full.astype(jnp.float32) + shift_two_full.astype(jnp.float32)
    ).astype(jnp.bfloat16)
    gate = jnp.einsum("rsd,df->rsf", normed_two, gate_full, preferred_element_type=jnp.float32)
    upward = jnp.einsum("rsd,df->rsf", normed_two, up_full, preferred_element_type=jnp.float32)
    sigmoid = jax.nn.sigmoid(gate)
    product = (gate * sigmoid * upward).astype(jnp.bfloat16)
    result = hidden_in + jnp.einsum(
        "rsf,fd->rsd", product, down_full, preferred_element_type=jnp.float32
    )
    gate_back, up_back, down_back, gain_two_back = (
        lax.all_gather(w_gate, ("dp", "ctx"), axis=0, tiled=True),
        lax.all_gather(w_up, ("dp", "ctx"), axis=0, tiled=True),
        lax.all_gather(w_down, ("dp", "ctx"), axis=0, tiled=True),
        lax.all_gather(gain_two, ("dp", "ctx"), axis=0, tiled=True),
    )
    grad_down = jnp.einsum("rsf,rsd->fd", product, cotangent, preferred_element_type=jnp.float32)
    grad_product = jnp.einsum(
        "rsd,fd->rsf", cotangent, down_back, preferred_element_type=jnp.float32
    )
    grad_gate_act = (grad_product * upward * sigmoid * (1.0 + gate * (1.0 - sigmoid))).astype(
        jnp.bfloat16
    )
    grad_up_act = (grad_product * gate * sigmoid).astype(jnp.bfloat16)
    grad_gate = jnp.einsum(
        "rsd,rsf->df", normed_two, grad_gate_act, preferred_element_type=jnp.float32
    )
    grad_up = jnp.einsum("rsd,rsf->df", normed_two, grad_up_act, preferred_element_type=jnp.float32)
    grad_normed_two = jnp.einsum(
        "rsf,df->rsd", grad_gate_act, gate_back, preferred_element_type=jnp.float32
    ) + jnp.einsum("rsf,df->rsd", grad_up_act, up_back, preferred_element_type=jnp.float32)
    grad_gain_two = jnp.sum(grad_normed_two * scaled_two, (0, 1))
    grad_shift_two = jnp.sum(grad_normed_two, (0, 1))
    grad_hidden = cotangent.astype(jnp.float32) + norm_back(
        grad_normed_two, scaled_two, inverse_two, gain_two_back.astype(jnp.float32)
    )
    mlp_sums = (
        lax.psum_scatter(grad_gate, ("dp", "ctx"), scatter_dimension=0, tiled=True),
        lax.psum_scatter(grad_up, ("dp", "ctx"), scatter_dimension=0, tiled=True),
        lax.psum_scatter(grad_down, ("dp", "ctx"), scatter_dimension=0, tiled=True),
        lax.psum_scatter(grad_gain_two, ("dp", "ctx"), scatter_dimension=0, tiled=True),
        lax.psum_scatter(grad_shift_two, ("dp", "ctx"), scatter_dimension=0, tiled=True),
    )
    qkv_back, out_back, gain_one_back = (
        lax.all_gather(w_qkv, ("dp", "ctx"), axis=0, tiled=True),
        lax.all_gather(w_out, ("dp", "ctx"), axis=0, tiled=True),
        lax.all_gather(gain_one, ("dp", "ctx"), axis=0, tiled=True),
    )
    hidden_low = grad_hidden.astype(jnp.bfloat16)
    grad_out = jnp.einsum(
        "rsd,rse->de", attended_low, hidden_low, preferred_element_type=jnp.float32
    )
    grad_attended = jnp.einsum(
        "rse,de->rsd", hidden_low, out_back, preferred_element_type=jnp.float32
    )
    grad_heads = grad_attended.reshape(local_rows, slot_count, HEADS, HEAD_DIM).astype(jnp.bfloat16)
    delta = jnp.transpose(jnp.sum(grad_heads.astype(jnp.float32) * attended, -1), (1, 2, 0))
    key_value_all = lax.all_gather(key_value, "ctx", axis=0, tiled=True)

    def grad_parts(block_part, offset):
        key_part, value_part = split_heads(block_part)
        scores = (
            jnp.einsum("qshd,kshd->shqk", queries, key_part, preferred_element_type=jnp.float32)
            * 0.125
        )
        allowed = allowed_mask(offset, block_part.shape[0])
        probs = jnp.where(allowed, jnp.exp(scores - log_sum[..., None]), 0.0)
        grad_prob = jnp.einsum(
            "qshd,kshd->shqk", grad_heads, value_part, preferred_element_type=jnp.float32
        )
        grad_score = (probs * (grad_prob - delta[..., None])).astype(jnp.bfloat16)
        return (key_part, probs, grad_score)

    def query_step(running, block_part, offset):
        key_part, probs, grad_score = grad_parts(block_part, offset)
        return running + jnp.einsum(
            "shqk,kshd->shqd", grad_score, key_part, preferred_element_type=jnp.float32
        )

    grad_query = (
        over_blocks(
            query_step,
            jnp.zeros((slot_count, HEADS, local_rows, HEAD_DIM), jnp.float32),
            key_value_all,
        )
        * 0.125
    )
    count = local_rows * lax.axis_size("ctx")
    tile_rows = math.gcd(count, 512)

    def one_block(number):
        block_start = number * tile_rows
        block_part = lax.dynamic_slice_in_dim(key_value_all, block_start, tile_rows, 0)
        key_part, probs, grad_score = grad_parts(block_part, block_start)
        grad_key = (
            jnp.einsum("shqk,qshd->kshd", grad_score, queries, preferred_element_type=jnp.float32)
            * 0.125
        )
        grad_value = jnp.einsum(
            "shqk,qshd->kshd",
            probs.astype(jnp.bfloat16),
            grad_heads,
            preferred_element_type=jnp.float32,
        )
        return jnp.stack(
            [
                grad_key.reshape(tile_rows, slot_count, width),
                grad_value.reshape(tile_rows, slot_count, width),
            ],
            2,
        )

    blocks = lax.map(one_block, jnp.arange(count // tile_rows, dtype=jnp.int32))
    grad_key_value = lax.psum_scatter(
        blocks.reshape(count, slot_count, 2, width).astype(jnp.bfloat16),
        "ctx",
        scatter_dimension=0,
        tiled=True,
    ).astype(jnp.float32)
    grad_query_pre = rotate(jnp.transpose(grad_query, (2, 0, 1, 3)), cos_table, -sin_table)
    grad_key_pre = rotate(
        grad_key_value[:, :, 0].reshape(local_rows, slot_count, HEADS, HEAD_DIM),
        cos_table,
        -sin_table,
    )
    grad_joined = jnp.concatenate(
        [
            grad_query_pre.reshape(local_rows, slot_count, width),
            grad_key_pre.reshape(local_rows, slot_count, width),
            grad_key_value[:, :, 1],
        ],
        -1,
    ).astype(jnp.bfloat16)
    grad_qkv = jnp.einsum(
        "rsd,rse->de", normed_one, grad_joined, preferred_element_type=jnp.float32
    )
    grad_bias = jnp.sum(grad_joined.astype(jnp.float32), (0, 1))
    grad_normed_one = jnp.einsum(
        "rse,de->rsd", grad_joined, qkv_back, preferred_element_type=jnp.float32
    )
    grad_gain_one = jnp.sum(grad_normed_one * scaled_one, (0, 1))
    grad_shift_one = jnp.sum(grad_normed_one, (0, 1))
    input_grad = grad_hidden + norm_back(
        grad_normed_one, scaled_one, inverse_one, gain_one_back.astype(jnp.float32)
    )
    attn_sums = (
        lax.psum_scatter(grad_qkv, ("dp", "ctx"), scatter_dimension=0, tiled=True),
        lax.psum_scatter(grad_bias, ("dp", "ctx"), scatter_dimension=0, tiled=True),
        lax.psum_scatter(grad_out, ("dp", "ctx"), scatter_dimension=0, tiled=True),
        lax.psum_scatter(grad_gain_one, ("dp", "ctx"), scatter_dimension=0, tiled=True),
        lax.psum_scatter(grad_shift_one, ("dp", "ctx"), scatter_dimension=0, tiled=True),
    )
    return (
        result.astype(jnp.bfloat16),
        input_grad,
        attn_sums[0],
        attn_sums[1],
        attn_sums[2],
        mlp_sums[0],
        mlp_sums[1],
        mlp_sums[2],
        attn_sums[3],
        attn_sums[4],
        mlp_sums[3],
        mlp_sums[4],
    )


MESH = pl.DeviceIdType.MESH
HBM = pl.BlockSpec(memory_space=pltpu.HBM)
VMEM = pl.BlockSpec(memory_space=pltpu.VMEM)
VMEM_LIMIT = 60 << 20


def flip(index, mask):
    for bit in (1, 2, 4):
        if mask & bit:
            index = index + bit - 2 * bit * ((index // bit) % 2)
    return index


class Wires:
    def __init__(self, send, recv):
        self.send, self.recv = send, recv
        self.z, self.c = lax.axis_index("dp"), lax.axis_index("ctx")
        self.inner = (self.z == 1) | (self.z == 2)
        self.outer = (self.z == 0) | (self.z == 3)
        self.number = itertools.count()

    def put(self, src, dst, z_mask, c_mask):
        return self.put_to(src, dst, flip(self.z, z_mask), flip(self.c, c_mask))

    def put_to(self, src, dst, z, c):
        i = next(self.number)
        return pltpu.make_async_remote_copy(
            src_ref=src,
            dst_ref=dst,
            send_sem=self.send.at[i],
            recv_sem=self.recv.at[i],
            device_id=(z, c),
            device_id_type=MESH,
        )

    def greet(self, zs, n):
        self.call(zs, n)
        self.met(zs, n)

    def met(self, zs, n):
        pl.semaphore_wait(pltpu.get_barrier_semaphore(), zs + n - 2)

    def call(self, zs, n):
        barrier = pltpu.get_barrier_semaphore()
        for m in range(1, zs):
            pl.semaphore_signal(
                barrier, inc=1, device_id=(flip(self.z, m), self.c), device_id_type=MESH
            )
        for m in range(1, n):
            pl.semaphore_signal(
                barrier, inc=1, device_id=(self.z, flip(self.c, m)), device_id_type=MESH
            )


class DepthGather:
    def __init__(self, wires, part):
        z = wires.z
        self.wires = wires
        self.near = wires.put(part(z), part(z), 1, 0)
        self.skip = wires.put(part(z), part(z), 2, 0)
        self.mid = wires.put(part(z), part(z), 3, 0)
        far = flip(z, 2)
        self.on = wires.put(part(far), part(far), 1, 0)

    @staticmethod
    def start(parts):
        for part in parts:
            part.skip.start()
        for part in parts:
            pl.when(part.wires.inner)(part.mid.start)
        for part in parts:
            part.near.start()

    def forward(self):
        @pl.when(self.wires.inner)
        def _():
            self.skip.wait_recv()
            self.on.start()

    def finish(self):
        self.near.wait_recv()
        self.near.wait_send()
        self.skip.wait_send()

        @pl.when(self.wires.inner)
        def _():
            self.mid.wait_recv()
            self.mid.wait_send()
            self.on.wait_send()

        @pl.when(self.wires.outer)
        def _():
            self.skip.wait_recv()
            self.on.wait_recv()


class LayerGather:
    def __init__(self, wires, block, source=None):
        c = wires.c
        mine = block(c) if source is None else source
        self.direct = {m: wires.put(mine, block(c), 0, m) for m in (2, 4, 6, 1)}
        self.on = {m: wires.put(block(flip(c, m)), block(flip(c, m)), 0, 1) for m in (2, 4, 6)}

    def start(self):
        for m in (2, 4, 6, 1):
            self.direct[m].start()

    def forward(self, m):
        self.direct[m].wait_recv()
        self.on[m].start()

    def arrived(self, m):
        (self.direct[1] if m == 1 else self.on[m - 1]).wait_recv()

    def sent(self):
        for copy in (*self.direct.values(), *self.on.values()):
            copy.wait_send()


def pack_columns(dst, refs, n, zs):
    for i in range(n):
        pieces = []
        for ref, block, at, size in refs:
            starts = [block * (j * n + i) + at for j in range(zs)]
            pieces += [ref[:, start : start + size] for start in starts]
        dst[i] = jnp.concatenate(pieces, -1)


class LayerScatter:
    def __init__(self, wires, part, near, far):
        c = wires.c
        self.c, self.part, self.near, self.far = c, part, near, far
        self.pair = {
            m: wires.put(part(flip(c, m + 1)), near(m // 2), 0, 1) for m in (6, 4, 2, 0)
        }
        self.chips = {m: wires.put(part(flip(c, m)), far(m // 2 - 1), 0, m) for m in (6, 4, 2)}

    def start(self):
        for copy in self.pair.values():
            copy.start()

    def step(self, m):
        self.pair[m].wait_recv()
        to = self.part(flip(self.c, m))
        to[...] = (
            to[...].astype(jnp.float32) + self.near(m // 2)[...].astype(jnp.float32)
        ).astype(to.dtype)
        self.chips[m].start()

    def total(self):
        self.pair[0].wait_recv()
        result = self.part(self.c)[...].astype(jnp.float32)
        result = result + self.near(0)[...].astype(jnp.float32)
        for m in (2, 4, 6):
            self.chips[m].wait_recv()
            result = result + self.far(m // 2 - 1)[...].astype(jnp.float32)
        return result

    def sent(self):
        for copy in (*self.pair.values(), *self.chips.values()):
            copy.wait_send()


def dot(a, b, dims=((1,), (0,))):
    return lax.dot_general(a, b, (dims, ((), ())), preferred_element_type=jnp.float32)


def turn_pair(values, table, sign):
    half = ROTARY // 2
    columns = values.shape[-1]
    table = [jnp.concatenate([t] * (columns // t.shape[-1]), -1) for t in table]
    return (
        values * table[0]
        + sign * (pltpu.roll(values, columns - half, 1) * table[1])
        + sign * (pltpu.roll(values, half, 1) * table[2])
    )


def head_mask(rows, columns, head):
    return lax.broadcasted_iota(jnp.int32, (rows, columns), 1) // HEAD_DIM == head


class DepthScatter:
    def __init__(self, wires, part, relay, boxes):
        z = wires.z
        self.wires, self.part, self.relay_box, self.boxes = wires, part, relay, boxes
        self.far = wires.put(part(flip(z, 3)), relay, 1, 0)
        self.skip = wires.put(part(flip(z, 2)), boxes[1], 2, 0)
        self.near = wires.put(part(flip(z, 1)), boxes[0], 1, 0)
        self.mid = wires.put(part(flip(z, 3)), boxes[2], 3, 0)

    def start(self, mask):
        outer, inner = pl.when(self.wires.outer), pl.when(self.wires.inner)
        if mask == 3:
            outer(self.far.start)
            inner(self.mid.start)
        elif mask == 2:
            outer(self.skip.start)
        elif mask == 1:
            self.near.start()
        else:

            @outer
            def _():
                self.boxes[2][...] = jnp.zeros_like(self.boxes[2])

    def relay(self):
        @pl.when(self.wires.inner)
        def _():
            self.far.wait_recv()
            to = self.part(flip(self.wires.z, 2))
            to[...] = (
                to[...].astype(jnp.float32) + self.relay_box[...].astype(jnp.float32)
            ).astype(to.dtype)
            self.skip.start()

    def total(self):
        self.near.wait_recv()
        self.skip.wait_recv()
        pl.when(self.wires.inner)(self.mid.wait_recv)
        result = self.part(self.wires.z)[...].astype(jnp.float32)
        for box in self.boxes:
            result = result + box[...].astype(jnp.float32)
        return result

    def sent(self):
        self.near.wait_send()
        self.skip.wait_send()
        pl.when(self.wires.outer)(self.far.wait_send)
        pl.when(self.wires.inner)(self.mid.wait_send)


class Moves:
    def __init__(self, sems):
        self.sems, self.number, self.stores = sems, itertools.count(), []

    def load(self, src, dst):
        copy = pltpu.make_async_copy(src, dst, self.sems.at[next(self.number)])
        copy.start()
        return copy

    def store(self, src, dst):
        self.stores.append(self.load(src, dst))

    def finish(self):
        for copy in self.stores:
            copy.wait()


def pieces_of(total, number, unit):
    units = total // unit
    cuts = [units * i // number * unit for i in range(number + 1)]
    return [(a, b - a) for a, b in zip(cuts[:-1], cuts[1:])]


class ChainGather:
    def __init__(self, wires, part):
        self.z = z = wires.z
        self.right = [
            wires.put_to(part((z - s + 4) % 4), part((z - s + 4) % 4), (z + 1) % 4, wires.c)
            for s in range(3)
        ]
        self.left = [
            wires.put_to(part((z + s) % 4), part((z + s) % 4), (z + 3) % 4, wires.c)
            for s in range(3)
        ]

    def start(self):
        pl.when(self.z <= 2)(self.right[0].start)
        pl.when(self.z >= 1)(self.left[0].start)

    def hop(self, s):
        pl.when(self.z >= s)(self.right[s - 1].wait_recv)
        pl.when((self.z >= s) & (self.z <= 2))(self.right[s].start)
        pl.when(self.z <= 3 - s)(self.left[s - 1].wait_recv)
        pl.when((self.z <= 3 - s) & (self.z >= 1))(self.left[s].start)

    def finish(self):
        pl.when(self.z >= 3)(self.right[2].wait_recv)
        pl.when(self.z <= 0)(self.left[2].wait_recv)
        for s in range(3):
            pl.when((self.z >= s) & (self.z <= 2))(self.right[s].wait_send)
            pl.when((self.z <= 3 - s) & (self.z >= 1))(self.left[s].wait_send)


class ChainScatter:
    def __init__(self, wires, part, right, left):
        self.z = z = wires.z
        self.part, self.right_box, self.left_box = part, right, left
        self.right = {
            j: wires.put_to(part(j), right(j), (z + 1) % 4, wires.c) for j in (3, 2, 1)
        }
        self.left = {j: wires.put_to(part(j), left(j), (z + 3) % 4, wires.c) for j in (0, 1, 2)}

    def clear(self):
        @pl.when(self.z == 0)
        def _():
            self.right_box(1)[...] = jnp.zeros_like(self.right_box(1))

        @pl.when(self.z == 3)
        def _():
            self.left_box(2)[...] = jnp.zeros_like(self.left_box(2))

    def start(self, distance):
        pl.when(self.z == 0)(self.right[distance].start)
        pl.when(self.z == 3)(self.left[3 - distance].start)

    def pass_on(self, copy, j, box):
        copy.wait_recv()
        to = self.part(j)
        to[...] = (to[...].astype(jnp.float32) + box(j)[...].astype(jnp.float32)).astype(to.dtype)
        copy.start()

    def hop(self, s, distance):
        @pl.when(self.z == s)
        def _():
            self.pass_on(self.right[distance], distance, self.right_box)

        @pl.when(self.z == 3 - s)
        def _():
            self.pass_on(self.left[3 - distance], 3 - distance, self.left_box)

    def total(self):
        for j in (1, 2, 3):
            pl.when(self.z == j)(self.right[j].wait_recv)
        for j in (0, 1, 2):
            pl.when(self.z == j)(self.left[j].wait_recv)
        z = self.z
        return (
            self.part(z)[...].astype(jnp.float32)
            + self.right_box(jnp.maximum(z, 1))[...].astype(jnp.float32)
            + self.left_box(jnp.minimum(z, 2))[...].astype(jnp.float32)
        )

    def sent(self):
        for j in (1, 2, 3):
            pl.when(self.z < j)(self.right[j].wait_send)
        for j in (0, 1, 2):
            pl.when(self.z > j)(self.left[j].wait_send)


def halves_of(block):
    first = (block // 16 + 1) // 2 * 16
    return [(0, first), (first, block - first)]


def by_slot(dst, src):
    rows, slots, _ = src.shape
    for s in range(slots):
        dst[s * rows : (s + 1) * rows] = src[:, s, :]


def by_position(dst, values):
    rows, slots, _ = dst.shape
    for s in range(slots):
        dst[:, s, :] = values[s * rows : (s + 1) * rows].astype(dst.dtype)


def front_kernel(
    zs,
    n,
    slots,
    lengths,
    tables,
    small,
    w_qkv,
    w_gate,
    w_up,
    w_out,
    w_down,
    inputs,
    cotangent,
    w_qkv_out,
    w_out_out,
    w_gu_out,
    a1_out,
    qkv_out,
    probs_out,
    ob_out,
    hidden_out,
    a2_out,
    dgu_out,
    y_out,
    grad_down_out,
    norms,
    qkv_send,
    gu_send,
    small_v,
    bias_v,
    w_qkv_v,
    w_out_v,
    w_gu_v,
    w_down_v,
    wide_x,
    wide_a,
    dy_v,
    qkv_v,
    probs_v,
    ob_v,
    near,
    far,
    hidden_v,
    gu_v,
    zz_v,
    dz_v,
    gd_v,
    right_v,
    left_v,
    raw_v,
    send,
    recv,
    local,
):
    f32, b16 = jnp.float32, jnp.bfloat16
    wires = Wires(send, recv)
    moves = Moves(local)
    z, c = wires.z, wires.c
    rows, _, width = inputs.shape
    local_rows = rows * slots
    tokens, seq = n * local_rows, n * rows
    pair = 2 * local_rows
    hc = qkv_v.shape[-1]
    heads = hc // HEAD_DIM
    block = w_down_v.shape[1]
    ffc = zs * block
    halves = halves_of(block)
    spans = [(2 * zs * at, zs * size) for at, size in halves]
    lanes = 2 * HEAD_DIM
    lane_half = lax.broadcasted_iota(jnp.int32, (1, lanes), 1) // HEAD_DIM

    def block_of(ref, i):
        return ref.at[pl.ds(pl.multiple_of(i * local_rows, local_rows), local_rows)]

    def pair_at(i):
        return pl.ds(pl.multiple_of(i * pair, pair), pair)

    wires.call(zs, n)
    wait_out = moves.load(w_out, w_out_v.at[z])
    wait_small = moves.load(small, small_v.at[z, c])
    waits = [moves.load(inputs, raw_v.at[0]), moves.load(cotangent, raw_v.at[1])]
    wait_down = moves.load(w_down, w_down_v.at[z])
    wait_out.wait()
    wires.met(zs, n)
    out_z = DepthGather(wires, lambda i: w_out_v.at[i])
    DepthGather.start([out_z])
    pack_columns(
        qkv_send,
        [(w_qkv.at[:, i * width : (i + 1) * width], HEAD_DIM, 0, HEAD_DIM) for i in range(3)],
        n,
        zs,
    )
    wait_own_qkv = moves.load(qkv_send.at[c], w_qkv_v.at[z, c])
    qkv_x = [wires.put(qkv_send.at[flip(c, m)], w_qkv_v.at[z, c], 0, m) for m in range(1, n)]
    for copy in qkv_x:
        copy.start()
    wait_small.wait()
    small_z = [wires.put(small_v.at[z, c], small_v.at[z, c], m, 0) for m in range(1, zs)]
    for copy in small_z:
        copy.start()
    waits[0].wait()
    by_slot(block_of(wide_x, c), raw_v.at[0])
    xs_g = LayerGather(wires, lambda i: block_of(wide_x, i))
    xs_g.start()
    pack_columns(
        gu_send, [(w, block, at, size) for at, size in halves for w in (w_gate, w_up)], n, zs
    )
    wait_own_gu = moves.load(gu_send.at[c], w_gu_v.at[z, c])
    for copy in small_z:
        copy.wait_recv()
    small_x = [wires.put(small_v.at[:, c], small_v.at[:, c], 0, m) for m in range(1, n)]
    for copy in small_x:
        copy.start()
    wait_own_qkv.wait()
    for copy in qkv_x:
        copy.wait_recv()
    number = 4
    qkv_z = [
        DepthGather(wires, lambda i, a=a, s=s: w_qkv_v.at[i, a : a + s])
        for a, s in pieces_of(n, number, 1)
    ]
    DepthGather.start(qkv_z)
    gu_x = [wires.put(gu_send.at[flip(c, m)], w_gu_v.at[z, c], 0, m) for m in range(1, n)]
    for copy in gu_x:
        copy.start()
    out_z.forward()
    for m in (2, 4, 6):
        xs_g.forward(m)

    for copy in small_x:
        copy.wait()
    for r in range(4):
        norms[r : r + 1] = jnp.concatenate(
            [
                jnp.where(
                    lane_half == 0,
                    small_v[d // n, d % n, r : r + 1],
                    small_v[d // n, d % n + 1, r : r + 1],
                )
                for d in range(0, zs * n, 2)
            ],
            -1,
        )
    norms[4:8] = jnp.zeros_like(norms[4:8])
    per_owner = 3 * zs * n // (zs * n)
    for i in range(3):
        for j in range(0, zs, 2):
            both = []
            for h in range(2):
                group = i * zs * n + (j + h) * n + c
                owner, k = group // per_owner, group % per_owner
                tile = small_v[owner // n, owner % n]
                row = jnp.where(k == 2, tile[5:6], tile[4:5])
                both.append(jnp.where(k % 2 == h, row, pltpu.roll(row, HEAD_DIM, 1)))
            at = (i * zs + j) * HEAD_DIM
            bias_v[:, at : at + lanes] = jnp.where(lane_half == 0, both[0], both[1])

    for m in (1, 3, 5, 7):
        xs_g.arrived(m)
    hidden_v[...] = block_of(wide_x, c)[...].astype(f32)

    def norm_one(i, carry):
        x = wide_x[pair_at(i)].astype(f32)
        wide_a[pair_at(i)] = (layer_stats(x)[0] * norms[0:1] + norms[1:2]).astype(b16)
        return carry

    lax.fori_loop(0, n // 2, norm_one, 0)
    wait_a1 = moves.load(wide_a, a1_out)
    wait_own_gu.wait()
    for copy in gu_x:
        copy.wait_recv()
    gu_z = [
        [
            DepthGather(
                wires, lambda i, a=a, s=s, k=slice(at, at + 2 * size): w_gu_v.at[i, a : a + s, :, k]
            )
            for a, s in pieces_of(n, number, 1)
        ]
        for at, size in spans
    ]
    for part in qkv_z:
        part.forward()
    for part in gu_z:
        DepthGather.start(part)
    waits[1].wait()
    by_slot(dy_v.at[c], raw_v.at[1])
    dy_g = LayerGather(wires, lambda i: dy_v.at[i])
    dy_g.start()
    for part in (out_z, *qkv_z):
        part.finish()
    moves.store(w_qkv_v, w_qkv_out)
    moves.store(w_out_v, w_out_out)

    def project(i, carry):
        joined = dot(wide_a[pair_at(i)], w_qkv_v[...].reshape(width, 3 * hc)) + bias_v[...]
        for j in range(2):
            table = [tables[k, 2 * i + j] for k in range(3)]
            for s in range(slots):
                at = (j * slots + s) * rows
                piece = joined[at : at + rows]
                qkv_v[0, s, 2 * i + j] = turn_pair(piece[:, :hc], table, 1.0).astype(b16)
                qkv_v[1, s, 2 * i + j] = turn_pair(piece[:, hc : 2 * hc], table, 1.0).astype(b16)
                qkv_v[2, s, 2 * i + j] = piece[:, 2 * hc :].astype(b16)
        return carry

    lax.fori_loop(0, n // 2, project, 0)
    moves.store(qkv_v, qkv_out)
    for m in (2, 4, 6):
        dy_g.forward(m)

    half = seq // 2
    probs_sem = moves.sems.at[next(moves.number)]

    def attend(s, carry):
        q, k, v = [qkv_v[i, s].reshape(seq, hc) for i in range(3)]
        length = lengths[0, s]
        kept = pltpu.make_async_copy(probs_v, probs_out.at[s], probs_sem)
        for part_q in range(2):
            keys = (part_q + 1) * half
            at = part_q * half
            query = q[at : at + half]
            row = lax.broadcasted_iota(jnp.int32, (half, keys), 0) + at
            key = lax.broadcasted_iota(jnp.int32, (half, keys), 1)
            allowed = (key <= row) & (row < length)
            out = jnp.zeros((half, hc), f32)
            for h in range(heads):
                mask = head_mask(half, hc, h)
                scores = dot(jnp.where(mask, query, 0).astype(b16), k[:keys], ((1,), (1,)))
                scores = jnp.where(allowed, scores * 0.125, masked_value)
                peak = jnp.max(scores, -1, keepdims=True)
                weights = jnp.where(allowed, jnp.exp(scores - peak), 0.0)
                total = jnp.maximum(jnp.sum(weights, -1, keepdims=True), 1.0)
                probs = (weights * (1.0 / total)).astype(b16)
                probs_v[h, at : at + half, 0:keys] = probs
                if keys < seq:
                    probs_v[h, at : at + half, keys:seq] = jnp.zeros((half, seq - keys), b16)
                out = jnp.where(mask, dot(probs, v[:keys]), out)
            ob_v[part_q * n // 2 : (part_q + 1) * n // 2, s] = out.astype(b16).reshape(
                n // 2, rows, hc
            )
        kept.start()
        kept.wait()
        return carry

    lax.fori_loop(0, slots, attend, 0)
    moves.store(ob_v, ob_out)
    for part in gu_z[0][:2]:
        part.forward()

    xs_g.sent()

    def to_hidden(i, carry):
        block_of(wide_x, i)[...] = dot(
            ob_v[i].reshape(local_rows, hc), w_out_v[...].reshape(hc, width)
        ).astype(b16)
        return carry

    lax.fori_loop(0, n, to_hidden, 0)
    wait_a1.wait()
    sums = LayerScatter(
        wires, lambda i: block_of(wide_x, i), lambda j: near.at[j], lambda j: far.at[j]
    )
    sums.start()
    for m in (6, 4, 2):
        sums.step(m)
    for part in gu_z[0][2:]:
        part.forward()
    hidden = hidden_v[...] + sums.total()
    hidden_v[...] = hidden
    moves.store(hidden_v, hidden_out)
    block_of(wide_a, c)[...] = (layer_stats(hidden)[0] * norms[2:3] + norms[3:4]).astype(b16)
    a2_g = LayerGather(wires, lambda i: block_of(wide_a, i))
    a2_g.start()
    gu_z[1][0].forward()
    for m in (2, 4, 6):
        a2_g.forward(m)
    for part in gu_z[1][1:]:
        part.forward()
    wait_down.wait()
    tile = width // number
    columns = [slice(p * tile, (p + 1) * tile) for p in range(number)]
    down_z = [ChainGather(wires, lambda i, k=k: w_down_v.at[i, :, k]) for k in columns]
    for chain in down_z:
        chain.start()
    for m in (1, 3, 5, 7):
        dy_g.arrived(m)
    for m in (1, 3, 5, 7):
        a2_g.arrived(m)
    wait_a2 = moves.load(wide_a, a2_out)

    down_sums = []
    for step, ((at, size), (start, count), parts) in enumerate(zip(halves, spans, gu_z)):
        units, gates = slice(at, at + size), slice(start, start + 2 * count)
        inner = slice(zs * at, zs * (at + size))
        for _, _, chain in down_sums:
            chain.hop(1, 3)
        for part in parts:
            part.finish()

        def feed(i, carry, inner=inner, gates=gates, count=count):
            gu = dot(wide_a[pair_at(i)], w_gu_v[:, :, :, gates].reshape(width, 2 * count))
            gu_v[i, :, gates] = gu.astype(b16)
            gate = gu[:, :count]
            zz_v[i, :, inner] = (gate * jax.nn.sigmoid(gate) * gu[:, count:]).astype(b16)
            return carry

        lax.fori_loop(0, n // 2, feed, 0)
        if step == 1:
            down_z[0].hop(1)
            down_z[1].hop(1)
        chains = []
        for p in range(2):
            k = slice(p * width // 2, (p + 1) * width // 2)
            for q in columns[2 * p : 2 * p + 2]:
                gd = dot(
                    zz_v[:, :, inner].reshape(tokens, count),
                    dy_v[:, :, q].reshape(tokens, tile),
                    ((0,), (0,)),
                )
                gd_v[:, units, q] = gd.astype(b16).reshape(zs, size, tile)
            chains.append(
                ChainScatter(
                    wires,
                    lambda i, u=units, k=k: gd_v.at[i, u, k],
                    lambda i, u=units, k=k: right_v.at[i - 1, u, k],
                    lambda i, u=units, k=k: left_v.at[i, u, k],
                )
            )
            chains[-1].start(3)
            down_sums.append((units, k, chains[-1]))
            if step == 1:
                down_z[2 + p].hop(1)
                down_z[p].hop(2)
                down_sums[p][2].hop(1, 2)
        for distance in (2, 1):
            for chain in chains:
                chain.start(distance)
        for chain in chains:
            chain.clear()
    moves.store(w_gu_v, w_gu_out)
    sums.sent()
    a2_g.sent()
    wait_a2.wait()

    def products(p):
        k = columns[p]

        def rows_of(i, carry):
            dy_rows = dy_v[pl.ds(2 * i, 2), :, k].reshape(pair, tile)
            y = jnp.zeros((pair, tile), f32)
            for at, size in halves:
                weight = w_down_v[:, at : at + size, k].reshape(zs * size, tile)
                inner = slice(zs * at, zs * (at + size))
                dz = dot(dy_rows, weight, ((1,), (1,)))
                dz_v[i, :, inner] = dz if p == 0 else dz_v[i, :, inner] + dz
                y = y + dot(zz_v[i, :, inner], weight)
            wide_x[pair_at(i), k] = y.astype(b16)
            return carry

        lax.fori_loop(0, n // 2, rows_of, 0)

    chains = [chain for _, _, chain in down_sums]
    for t in (0, 1):
        chains[t].hop(2, 3)
        down_z[2 + t].hop(2)
    for t in (2, 3):
        chains[t].hop(1, 3)
    for t in (2, 3):
        chains[t].hop(1, 2)
    for t in (2, 3):
        chains[t].hop(2, 3)
    for t in range(number):
        down_z[t].finish()
        products(t)
    moves.store(wide_x, y_out)

    def back(i, carry):
        for (at, size), (start, count) in zip(halves, spans):
            dz = dz_v[i, :, zs * at : zs * (at + size)]
            gate = gu_v[i, :, start : start + count].astype(f32)
            up = gu_v[i, :, start + count : start + 2 * count].astype(f32)
            sig = jax.nn.sigmoid(gate)
            dg = dz * up * sig * (1.0 + gate * (1.0 - sig))
            du = dz * gate * sig
            gu_v[i, :, start : start + 2 * count] = jnp.concatenate([dg, du], -1).astype(b16)
        return carry

    lax.fori_loop(0, n // 2, back, 0)
    moves.store(gu_v, dgu_out)
    for units, k, chain in down_sums:
        grad_down_out[units, k] = chain.total()
    for group in (*chains, dy_g):
        group.sent()
    for copy in (*small_z, *qkv_x, *gu_x):
        copy.wait_send()
    moves.finish()


def front(zs, n, lengths, tables, small, w_qkv, w_gate, w_up, w_out, w_down, inputs, cotangent):
    f32, b16 = jnp.float32, jnp.bfloat16
    rows, slots, width = inputs.shape
    local = rows * slots
    seq, tokens = rows * n, local * n
    heads = HEADS // n
    hc = heads * HEAD_DIM
    wrows = w_out.shape[0]
    block = w_down.shape[0]
    gc = 2 * zs * block
    qkv_all = ((zs, n, wrows, 3 * hc), b16)
    out_all = ((zs, wrows, width), b16)
    gu_all = ((zs, n, wrows, gc), b16)
    down_all = ((zs, block, width), b16)
    wide = ((tokens, width), b16)
    qkv = ((3, slots, n, rows, hc), b16)
    probs = ((slots, heads, seq, seq), b16)
    ob = ((n, slots, rows, hc), b16)
    hidden = ((local, width), f32)
    gu = ((n // 2, 2 * local, gc), b16)
    outs = [
        qkv_all,
        out_all,
        gu_all,
        wide,
        qkv,
        probs,
        ob,
        hidden,
        wide,
        gu,
        wide,
        ((block, width), f32),
        ((8, width), f32),
    ]
    scratch = [
        ((n, wrows, 3 * hc), b16),
        ((n, wrows, gc), b16),
        ((zs, n, *small.shape), f32),
        ((1, 3 * hc), f32),
        qkv_all,
        out_all,
        gu_all,
        down_all,
        wide,
        wide,
        ((n, local, width), b16),
        qkv,
        (probs[0][1:], b16),
        ob,
        ((n // 2, local, width), b16),
        ((n // 2 - 1, local, width), b16),
        hidden,
        gu,
        ((n // 2, 2 * local, gc // 2), b16),
        ((n // 2, 2 * local, gc // 2), f32),
        down_all,
        ((zs - 1, block, width), b16),
        ((zs - 1, block, width), b16),
        ((2, *inputs.shape), b16),
    ]
    return pl.pallas_call(
        functools.partial(front_kernel, zs, n, slots),
        out_shape=[jax.ShapeDtypeStruct(*k) for k in outs],
        in_specs=[pl.BlockSpec(memory_space=pltpu.SMEM), VMEM, HBM, *[VMEM] * 3, *[HBM] * 4],
        out_specs=[HBM] * (len(outs) - 2) + [VMEM] * 2,
        scratch_shapes=[
            *[pltpu.VMEM(*k) for k in scratch],
            pltpu.SemaphoreType.DMA((192,)),
            pltpu.SemaphoreType.DMA((192,)),
            pltpu.SemaphoreType.DMA((32,)),
        ],
        compiler_params=pltpu.CompilerParams(
            collective_id=1, has_side_effects=True, vmem_limit_bytes=VMEM_LIMIT
        ),
        name="front",
    )(lengths, tables, small, w_qkv, w_gate, w_up, w_out, w_down, inputs, cotangent)


def unpack_columns(dst, src, parts, n, zs):
    dst[...] = jnp.concatenate(
        [
            src[i, :, at + size * j : at + size * (j + 1)]
            for j in range(zs)
            for i in range(n)
            for at, size in parts
        ],
        -1,
    ).astype(dst.dtype)


def backward_kernel(
    zs,
    n,
    norms,
    tables,
    a1_all,
    a2_all,
    dgu,
    w_gu,
    w_qkv,
    w_out,
    qkv,
    probs,
    ob,
    hidden,
    cotangent,
    inputs,
    y_part,
    grad_out_out,
    result_out,
    input_grad_out,
    gq_out,
    gu_out,
    small_out,
    wide_v,
    dgu_v,
    weight_v,
    w_out_v,
    qkv_v,
    probs_v,
    ob_v,
    hidden_v,
    own_v,
    raw_v,
    ggu_v,
    relay_v,
    box_v,
    near,
    far,
    dh_all,
    go_v,
    go_relay,
    go_box,
    dqkv_v,
    dj_v,
    bias_v,
    gq_relay,
    gq_box,
    gu_rows,
    gq_rows,
    small_v,
    small_x,
    small_r,
    small_z,
    send,
    recv,
    local,
    free,
):
    f32, b16 = jnp.float32, jnp.bfloat16
    wires = Wires(send, recv)
    moves = Moves(local)
    z, c = wires.z, wires.c
    _, slots, rows, hc = ob_v.shape
    width = dh_all.shape[-1]
    tokens, seq, local_rows = n * slots * rows, n * rows, slots * rows
    heads = hc // HEAD_DIM
    wrows, gc = ggu_v.shape[2:]
    depth = n * wrows
    ffc, qc = gc // 2, 3 * hc
    part = wide_v
    gu_weight = weight_v.at[:, :, :, 0:gc]
    qkv_weight, gq_v = weight_v.at[:, :, :, 0:qc], weight_v.at[:, :, :, qc : 2 * qc]

    wait_a2 = moves.load(a2_all, wide_v)
    wait_dy = moves.load(cotangent, raw_v)
    wait_dgu = moves.load(dgu, dgu_v)
    wait_w = moves.load(w_gu, gu_weight)
    waits = [
        moves.load(hidden, hidden_v),
        moves.load(w_out, w_out_v),
        moves.load(qkv, qkv_v),
        moves.load(probs.at[0], probs_v),
        moves.load(ob, ob_v),
    ]
    wires.greet(zs, n)
    wait_a2.wait()
    wait_dgu.wait()

    number = 4
    step = depth // 2

    quarter = wrows // number

    def scatters(whole, relay, box):
        rows_of = [slice(p * quarter, (p + 1) * quarter) for p in range(number)]
        return [
            DepthScatter(
                wires,
                lambda i, k=k: whole.at[i, :, k],
                relay.at[:, k],
                [box.at[j, :, k] for j in range(3)],
            )
            for k in rows_of
        ]

    def weigh(sums, whole, left_v, grads, also=None):
        for mask in (3, 2, 1, 0):
            to = flip(z, mask)

            def piece(p, carry, to=to):
                at = pl.multiple_of(to * depth + p * step, step)
                left = left_v[:, :, pl.ds(at, step)].reshape(tokens, step)
                gradient = dot(left, grads(), ((0,), (0,))).astype(b16)
                whole[to, pl.ds(p * (n // 2), n // 2)] = gradient.reshape(n // 2, wrows, -1)
                return carry

            lax.fori_loop(0, 2, piece, 0)
            for part_sum in sums:
                part_sum.start(mask)
            if mask == 3 and also is not None:
                also.start(3)

    gu_sums = scatters(ggu_v, relay_v, box_v)
    weigh(gu_sums, ggu_v, wide_v, lambda: dgu_v[...].reshape(tokens, gc))

    wait_w.wait()

    def normed_two(i, carry):
        part[pl.ds(2 * i, 2)] = (
            dot(dgu_v[i], gu_weight[...].reshape(width, gc), ((1,), (1,)))
            .astype(b16)
            .reshape(2, local_rows, width)
        )
        return carry

    lax.fori_loop(0, n // 2, normed_two, 0)
    wait_qkv = moves.load(w_qkv, qkv_weight)
    da2_sums = LayerScatter(
        wires, lambda i: part.at[i], lambda j: near.at[j], lambda j: far.at[j]
    )
    da2_sums.start()
    gu_sums[0].relay()
    for m in (6, 4, 2):
        da2_sums.step(m)
    for copy in waits:
        copy.wait()
    wait_dy.wait()
    by_slot(own_v, raw_v)
    wait_xs = moves.load(inputs, raw_v)
    n2, r2 = layer_stats(hidden_v[...])
    for part_sum in gu_sums[1:]:
        part_sum.relay()
    da2 = da2_sums.total()
    gains = [jnp.sum(da2 * n2, 0, keepdims=True), jnp.sum(da2, 0, keepdims=True)]
    dh = own_v[...].astype(f32) + norm_back(da2, n2, r2, norms[2:3])
    by_position(input_grad_out, dh)
    dh_all[c] = dh.astype(b16)
    dh_g = LayerGather(wires, lambda i: dh_all.at[i])
    dh_g.start()
    da2_sums.sent()
    wait_y = moves.load(y_part, part)
    for m in (2, 4, 6):
        dh_g.forward(m)
    for m in (1, 3, 5, 7):
        dh_g.arrived(m)
    wait_y.wait()
    y_sums = LayerScatter(
        wires, lambda i: part.at[i], lambda j: near.at[j], lambda j: far.at[j]
    )
    y_sums.start()

    go_sums = DepthScatter(
        wires, lambda i: go_v.at[i], go_relay, [go_box.at[j] for j in range(3)]
    )
    tile = width // 4

    def heads_grad(p, carry):
        at = pl.ds(pl.multiple_of(p * tile, tile), tile)
        go = dot(
            ob_v[...].reshape(tokens, hc), dh_all[:, :, at].reshape(tokens, tile), ((0,), (0,))
        )
        go_v[:, :, at] = go.astype(b16).reshape(zs, hc // zs, tile)
        return carry

    lax.fori_loop(0, 4, heads_grad, 0)

    def heads_back(i, carry):
        ob_v[i] = (
            dot(dh_all[i], w_out_v[...].reshape(hc, width), ((1,), (1,)))
            .astype(b16)
            .reshape(slots, rows, hc)
        )
        return carry

    for m in (6, 4, 2):
        y_sums.step(m)
    lax.fori_loop(0, n, heads_back, 0)
    dh_g.sent()
    wait_a1 = moves.load(a1_all, dh_all)
    half = seq // 2

    def attend(s, carry):
        q, k, v = [qkv_v[i, s].reshape(seq, hc) for i in range(3)]
        do_s = ob_v[:, s].reshape(seq, hc)
        dqkv_v[...] = jnp.zeros_like(dqkv_v)
        for part_q in range(2):
            keys = (part_q + 1) * half
            at = part_q * half
            query, do_q = q[at : at + half], do_s[at : at + half]
            dq = jnp.zeros((half, hc), f32)
            for h in range(heads):
                mask, mask_k = head_mask(half, hc, h), head_mask(keys, hc, h)
                do_h = jnp.where(mask, do_q, 0).astype(b16)
                low = probs_v[h, at : at + half, 0:keys]
                p32 = low.astype(f32)
                t = p32 * dot(do_h, v[:keys], ((1,), (1,)))
                ds = (t - p32 * jnp.sum(t, -1, keepdims=True)).astype(b16)
                dq = jnp.where(mask, dot(ds, k[:keys]), dq)
                dk = dot(ds, query, ((0,), (0,)))
                dv = dot(low, do_h, ((0,), (0,)))
                dqkv_v[1, 0:keys] += jnp.where(mask_k, dk, 0.0)
                dqkv_v[2, 0:keys] += dv
            dqkv_v[0, at : at + half] = dq

        @pl.when(s + 1 < slots)
        def _():
            copy = pltpu.make_async_copy(probs.at[s + 1], probs_v, probs_sem)
            copy.start()
            copy.wait()

        dq, dk = dqkv_v[0] * 0.125, dqkv_v[1] * 0.125
        table = [tables[i].reshape(seq, 2 * HEAD_DIM) for i in range(3)]
        dj = [turn_pair(dq, table, -1.0), turn_pair(dk, table, -1.0), dqkv_v[2]]
        for i in range(3):
            low = dj[i].astype(b16)
            dj_v[:, s, :, i * hc : (i + 1) * hc] = low.reshape(n, rows, hc)
            bias_v[:, i * hc : (i + 1) * hc] += jnp.sum(low.astype(f32), 0, keepdims=True)
        return carry

    bias_v[...] = jnp.zeros_like(bias_v)

    probs_sem = moves.sems.at[next(moves.number)]
    lax.fori_loop(0, slots, attend, 0)

    wait_a1.wait()
    wait_qkv.wait()
    qkv_sums = scatters(gq_v, gq_relay, gq_box)
    weigh(qkv_sums, gq_v, dh_all, lambda: dj_v[...].reshape(tokens, qc), go_sums)
    for mask in (2, 1, 0):
        go_sums.start(mask)

    def normed_one(i, carry):
        part[pl.ds(2 * i, 2)] = (
            dot(
                dj_v[pl.ds(2 * i, 2)].reshape(2 * local_rows, qc),
                qkv_weight[...].reshape(width, qc),
                ((1,), (1,)),
            )
            .astype(b16)
            .reshape(2, local_rows, width)
        )
        return carry

    by_position(result_out, hidden_v[...] + y_sums.total())
    for m in (1, 2, 4, 6):
        pl.semaphore_signal(free, inc=1, device_id=(z, flip(c, m)), device_id_type=MESH)
    y_sums.sent()
    lax.fori_loop(0, n // 2, normed_one, 0)
    pl.semaphore_wait(free, 4)
    da1_sums = LayerScatter(
        wires, lambda i: part.at[i], lambda j: near.at[j], lambda j: far.at[j]
    )
    da1_sums.start()
    for m in (6, 4, 2):
        da1_sums.step(m)

    for p, part_sum in enumerate(gu_sums):
        ggu_v[z, :, p * quarter : (p + 1) * quarter] = part_sum.total().astype(b16)
    gu_x = [wires.put(ggu_v.at[z, flip(c, m)], gu_rows.at[c], 0, m) for m in range(1, n)]
    for copy in gu_x:
        copy.start()
    gu_rows[c] = ggu_v[z, c]

    for part_sum in qkv_sums:
        part_sum.relay()
    go_sums.relay()

    wait_xs.wait()
    by_slot(own_v, raw_v)
    n1, r1 = layer_stats(own_v[...].astype(f32))
    da1 = da1_sums.total()
    grad = norm_back(da1, n1, r1, norms[0:1])
    for s in range(slots):
        input_grad_out[:, s, :] += grad[s * rows : (s + 1) * rows]
    gains = [jnp.sum(da1 * n1, 0, keepdims=True), jnp.sum(da1, 0, keepdims=True), *gains]
    chips = n // 2
    lanes = 2 * HEAD_DIM
    lane_half = lax.broadcasted_iota(jnp.int32, (1, lanes), 1) // HEAD_DIM
    bias_part = bias_v[...]
    for j in range(zs):
        for chip in range(chips):
            k = j * chips + chip
            for r in range(4):
                small_v[j, chip, r : r + 1] = gains[r][:, k * lanes : (k + 1) * lanes]
            small_v[j, chip, 7:8] = jnp.zeros((1, lanes), f32)
    for i in range(3):
        for j in range(zs):
            at = i * hc + j * HEAD_DIM
            piece = bias_part[:, at : at + HEAD_DIM]
            both = jnp.concatenate([piece, piece], -1)
            for chip in range(chips):
                tile = (i * zs + j) * chips + chip
                pair, row = tile // 3, tile % 3
                small_v[pair // chips, pair % chips, 4 + row : 5 + row] = jnp.where(
                    (lane_half == c % 2) & (c // 2 == chip), both, 0.0
                )
    small_v_x = [
        wires.put(small_v.at[:, flip(c, m) // 2], small_x.at[m], 0, m) for m in range(1, n)
    ]
    for copy in small_v_x:
        copy.start()

    small_sum = small_v[:, c // 2]
    for m in range(1, n):
        small_v_x[m - 1].wait_recv()
        small_sum = small_sum + small_x[m]
    small_r[...] = small_sum
    small_z_x = [wires.put(small_r.at[flip(z, m)], small_z.at[m], m, 0) for m in range(1, zs)]
    for copy in small_z_x:
        copy.start()
    for copy in gu_x:
        copy.wait_recv()
    moves.store(gu_rows, gu_out)
    gq_x = []
    for p, part_sum in enumerate(qkv_sums):
        k = slice(p * quarter, (p + 1) * quarter)
        gq_v[z, :, k] = part_sum.total().astype(b16)
        copies = [
            wires.put(gq_v.at[z, flip(c, m), k], gq_rows.at[c, k], 0, m) for m in range(1, n)
        ]
        for copy in copies:
            copy.start()
        gq_x += copies
    gq_rows[c] = gq_v[z, c]
    small_sum = small_r[z]
    for m in range(1, zs):
        small_z_x[m - 1].wait_recv()
        small_sum = small_sum + small_z[m]
    small_out[...] = small_sum
    hidden_v[0:wrows] = go_sums.total()
    moves.store(hidden_v.at[0:wrows], grad_out_out)
    for group in (*gu_sums, go_sums, *qkv_sums, da1_sums):
        group.sent()
    for copy in (*gu_x, *small_v_x, *small_z_x):
        copy.wait_send()
    for copy in gq_x:
        copy.wait()
    moves.store(gq_rows, gq_out)
    moves.finish()


def backward(zs, n, norms, tables, *arrays):
    f32, b16 = jnp.float32, jnp.bfloat16
    a1_all, a2_all, dgu, w_gu, w_qkv, w_out, qkv, probs, ob, hidden, _, inputs, _ = arrays
    _, slots, rows, hc = ob.shape
    local, width = hidden.shape
    _, _, wrows, gc = w_gu.shape
    qc = 3 * hc
    seq = n * rows
    wide = (n, local, width)

    def buf(like):
        return pltpu.VMEM(like.shape, like.dtype)

    return pl.pallas_call(
        functools.partial(backward_kernel, zs, n),
        out_shape=[
            jax.ShapeDtypeStruct((hc // zs, width), f32),
            jax.ShapeDtypeStruct(inputs.shape, b16),
            jax.ShapeDtypeStruct(inputs.shape, f32),
            jax.ShapeDtypeStruct((n, wrows, qc), b16),
            jax.ShapeDtypeStruct((n, wrows, gc), b16),
            jax.ShapeDtypeStruct((8, 2 * HEAD_DIM), f32),
        ],
        in_specs=[VMEM] * 2 + [HBM] * 13,
        out_specs=[HBM, VMEM, VMEM, HBM, HBM, VMEM],
        scratch_shapes=[
            pltpu.VMEM(wide, b16),
            buf(dgu),
            pltpu.VMEM((zs, n, wrows, max(gc, 2 * qc)), b16),
            buf(w_out),
            buf(qkv),
            pltpu.VMEM(probs.shape[1:], b16),
            buf(ob),
            buf(hidden),
            pltpu.VMEM((local, width), b16),
            pltpu.VMEM(inputs.shape, b16),
            pltpu.VMEM((zs, n, wrows, gc), b16),
            pltpu.VMEM((n, wrows, gc), b16),
            pltpu.VMEM((3, n, wrows, gc), b16),
            pltpu.VMEM((n // 2, local, width), b16),
            pltpu.VMEM((n // 2 - 1, local, width), b16),
            pltpu.VMEM(wide, b16),
            pltpu.VMEM((zs, hc // zs, width), b16),
            pltpu.VMEM((hc // zs, width), b16),
            pltpu.VMEM((3, hc // zs, width), b16),
            pltpu.VMEM((3, seq, hc), f32),
            pltpu.VMEM((n, slots, rows, qc), b16),
            pltpu.VMEM((1, qc), f32),
            pltpu.VMEM((n, wrows, qc), b16),
            pltpu.VMEM((3, n, wrows, qc), b16),
            pltpu.VMEM((n, wrows, gc), b16),
            pltpu.VMEM((n, wrows, qc), b16),
            pltpu.VMEM((zs, n // 2, 8, 2 * HEAD_DIM), f32),
            pltpu.VMEM((n, zs, 8, 2 * HEAD_DIM), f32),
            pltpu.VMEM((zs, 8, 2 * HEAD_DIM), f32),
            pltpu.VMEM((zs, 8, 2 * HEAD_DIM), f32),
            pltpu.SemaphoreType.DMA((128,)),
            pltpu.SemaphoreType.DMA((128,)),
            pltpu.SemaphoreType.DMA((24,)),
            pltpu.SemaphoreType.REGULAR,
        ],
        compiler_params=pltpu.CompilerParams(
            collective_id=4, has_side_effects=True, vmem_limit_bytes=VMEM_LIMIT
        ),
        name="backward",
    )(norms, tables, *arrays)


def finish_kernel(
    zs,
    n,
    gq,
    gu,
    small,
    grad_out,
    grad_down,
    result,
    input_grad,
    qkv_out,
    gate_out,
    up_out,
    grad_out_out,
    grad_down_out,
    result_out,
    input_grad_out,
    bias_out,
    gain_one_out,
    shift_one_out,
    gain_two_out,
    shift_two_out,
    gq_v,
    gu_v,
    qkv_v,
    gate_v,
    up_v,
    grad_out_v,
    grad_down_v,
    result_v,
    input_grad_v,
    local,
):
    moves = Moves(local)
    width = grad_out.shape[1]
    wait_gu = moves.load(gu, gu_v)
    wait_gq = moves.load(gq, gq_v)
    passed = [
        (moves.load(src, held), held, dst)
        for src, held, dst in (
            (input_grad, input_grad_v, input_grad_out),
            (grad_down, grad_down_v, grad_down_out),
            (result, result_v, result_out),
            (grad_out, grad_out_v, grad_out_out),
        )
    ]
    odd = lax.axis_index("ctx") % 2
    for r, out in enumerate((gain_one_out, shift_one_out, gain_two_out, shift_two_out)):
        row = small[r : r + 1]
        out[...] = jnp.where(odd == 0, row[:, :HEAD_DIM], row[:, HEAD_DIM:])
    bias = jnp.concatenate([small[4 + r : 5 + r] for r in range(3)], -1)
    size = bias_out.shape[1]
    bias_out[...] = jnp.where(odd == 0, bias[:, :size], bias[:, size:])
    ffc = gu_v.shape[-1] // 2
    halves = halves_of(ffc // zs)
    for copy, held, dst in passed:
        copy.wait()
        moves.store(held, dst)
    wait_gu.wait()
    unpack_columns(gate_v, gu_v, [(2 * zs * at, size) for at, size in halves], n, zs)
    moves.store(gate_v, gate_out)
    unpack_columns(up_v, gu_v, [(zs * (2 * at + size), size) for at, size in halves], n, zs)
    moves.store(up_v, up_out)
    wait_gq.wait()
    hc = gq_v.shape[-1] // 3
    for i in range(3):
        unpack_columns(
            qkv_v.at[:, i * width : (i + 1) * width], gq_v, [(i * hc, HEAD_DIM)], n, zs
        )
    moves.store(qkv_v, qkv_out)
    moves.finish()


def finish(zs, n, gq, gu, small, grad_out, grad_down, result, input_grad):
    f32 = jnp.float32
    _, wrows, qc = gq.shape
    gc = gu.shape[-1]
    wide = [((wrows, n * qc), f32), ((wrows, n * gc // 2), f32), ((wrows, n * gc // 2), f32)]
    whole = [(v.shape, v.dtype) for v in (grad_out, grad_down, result, input_grad)]
    rows = [((1, 3 * HEAD_DIM), f32), *[((1, wrows), f32)] * 4]
    return pl.pallas_call(
        functools.partial(finish_kernel, zs, n),
        out_shape=[jax.ShapeDtypeStruct(*k) for k in (*wide, *whole, *rows)],
        in_specs=[HBM, HBM, VMEM, HBM, HBM, HBM, HBM],
        out_specs=[HBM] * 7 + [VMEM] * 5,
        scratch_shapes=[
            pltpu.VMEM(gq.shape, gq.dtype),
            pltpu.VMEM(gu.shape, gu.dtype),
            *[pltpu.VMEM(*k) for k in (*wide, *whole)],
            pltpu.SemaphoreType.DMA((16,)),
        ],
        compiler_params=pltpu.CompilerParams(vmem_limit_bytes=VMEM_LIMIT),
        name="finish",
    )(gq, gu, small, grad_out, grad_down, result, input_grad)


def tensor_shards(
    inputs,
    lengths,
    w_qkv,
    b_qkv,
    w_out,
    w_gate,
    w_up,
    w_down,
    gain_one,
    shift_one,
    gain_two,
    shift_two,
    cotangent,
):
    rows, slots, width = inputs.shape
    f32, b16 = jnp.float32, jnp.bfloat16
    zs, n = lax.axis_size("dp"), lax.axis_size("ctx")
    me = lax.axis_index("ctx")
    local = rows * slots
    seq = rows * n
    wrows = w_qkv.shape[0]
    ff_block = w_down.shape[0]
    hc = HEADS // n * HEAD_DIM
    ffc = ff_block * zs

    nb = b_qkv.shape[0]
    vectors = [v for gain in (gain_one, shift_one, gain_two, shift_two) for v in (gain, gain)]
    small, at = jnp.zeros(1024, f32), 0
    for vector in (*vectors, b_qkv):
        size = vector.shape[0]
        small = small + jnp.pad(vector.astype(f32), (at, 1024 - at - size))
        at += size
    small = small.reshape(8, 128)

    angles = np.arange(seq)[:, None] * 10000.0 ** (-2.0 * np.arange(ROTARY // 2) / ROTARY)[None, :]
    cos_t, sin_t = np.cos(angles), np.sin(angles)
    zero, rest = np.zeros_like(sin_t), np.zeros((seq, HEAD_DIM - ROTARY))
    tables = np.stack(
        [
            np.concatenate(two, -1)
            for two in (
                2 * [cos_t, cos_t, rest + 1.0],
                2 * [-sin_t, zero, rest],
                2 * [zero, sin_t, rest],
            )
        ]
    ).astype(np.float32)

    tables = jnp.asarray(tables.reshape(3, n, rows, 2 * HEAD_DIM))
    w_qkv_c, w_out_c, w_gu_c, a1, qkv, probs, ob, hidden, a2, dgu, y, grad_down, norms = front(
        zs, n, lengths, tables, small, w_qkv, w_gate, w_up, w_out, w_down, inputs, cotangent
    )
    wide = (n, local, width)
    grad_out, result, input_grad, gq, gu, sums = backward(
        zs, n, norms, tables, a1.reshape(wide), a2.reshape(wide), dgu,
        w_gu_c, w_qkv_c, w_out_c, qkv, probs, ob, hidden, cotangent, inputs,
        y.reshape(wide),
    )
    grad_qkv, grad_gate, grad_up, grad_out, grad_down, result, input_grad, *rows = finish(
        zs, n, gq, gu, sums, grad_out, grad_down, result, input_grad
    )
    grad_bias, grad_gain_one, grad_shift_one, grad_gain_two, grad_shift_two = [
        row.reshape(row.shape[1]) for row in rows
    ]
    return (
        result,
        input_grad,
        grad_qkv,
        grad_bias,
        grad_out,
        grad_gate,
        grad_up,
        grad_down,
        grad_gain_one,
        grad_shift_one,
        grad_gain_two,
        grad_shift_two,
    )


def solution(mesh):
    zs, n = mesh.shape["dp"], mesh.shape["ctx"]
    shards = tensor_shards if (zs, n) == (4, 8) and HEADS == 32 else gathered_shards

    placed = (
        P("ctx", "dp", None),
        P("dp", None),
        P(("dp", "ctx"), None),
        P(("dp", "ctx")),
        P(("dp", "ctx"), None),
        P(("dp", "ctx"), None),
        P(("dp", "ctx"), None),
        P(("dp", "ctx"), None),
        P(("dp", "ctx")),
        P(("dp", "ctx")),
        P(("dp", "ctx")),
        P(("dp", "ctx")),
        P("ctx", "dp", None),
    )
    return jax.shard_map(
        shards,
        mesh=mesh,
        in_specs=placed,
        out_specs=(
            P("ctx", "dp", None),
            P("ctx", "dp", None),
            P(("dp", "ctx"), None),
            P(("dp", "ctx")),
            P(("dp", "ctx"), None),
            P(("dp", "ctx"), None),
            P(("dp", "ctx"), None),
            P(("dp", "ctx"), None),
            P(("dp", "ctx")),
            P(("dp", "ctx")),
            P(("dp", "ctx")),
            P(("dp", "ctx")),
        ),
        check_vma=False,
    )
```

```python
import functools
import itertools
import math

import jax
import jax.numpy as jnp
import numpy as np
from jax import lax
from jax.experimental import pallas as pl
from jax.experimental.pallas import tpu as pltpu
from jax.sharding import PartitionSpec as P

HEADS = 32
HEAD_DIM = 64
ROTARY = 16


epsilon = 1e-05
masked_value = -1e30


def layer_stats(values):
    row_mean = jnp.mean(values, -1, keepdims=True)
    centred = values - row_mean
    inverse = lax.rsqrt(jnp.mean(centred * centred, -1, keepdims=True) + epsilon)
    return (centred * inverse, inverse)


def norm_back(grad_normed, scaled, inverse, gain_vec):
    grad_hat = grad_normed * gain_vec
    return inverse * (
        grad_hat
        - jnp.mean(grad_hat, -1, keepdims=True)
        - scaled * jnp.mean(grad_hat * scaled, -1, keepdims=True)
    )


def rotary_tables(positions):
    counter = jnp.arange(ROTARY // 2, dtype=jnp.float32)
    frequency = 10000.0 ** (-2.0 * counter / ROTARY)
    angles = positions.astype(jnp.float32)[:, None] * frequency[None, :]
    return (jnp.cos(angles)[:, None, None, :], jnp.sin(angles)[:, None, None, :])


def rotate(values, cos_table, sin_table):
    half_dims = ROTARY // 2
    first_half = values[..., :half_dims]
    second_half = values[..., half_dims:ROTARY]
    return jnp.concatenate(
        [
            first_half * cos_table - second_half * sin_table,
            second_half * cos_table + first_half * sin_table,
            values[..., ROTARY:],
        ],
        -1,
    )


def over_blocks(step_fn, running, gathered):
    total_rows = gathered.shape[0]
    tile_rows = math.gcd(total_rows, 512)

    def visit_block(number, current):
        block_start = number * tile_rows
        block_part = lax.dynamic_slice_in_dim(gathered, block_start, tile_rows, 0)
        return step_fn(current, block_part, block_start)

    return lax.fori_loop(0, total_rows // tile_rows, visit_block, running)


def gathered_shards(
    inputs,
    lengths,
    w_qkv,
    b_qkv,
    w_out,
    w_gate,
    w_up,
    w_down,
    gain_one,
    shift_one,
    gain_two,
    shift_two,
    cotangent,
):
    local_rows, slot_count, width = inputs.shape
    positions = lax.axis_index("ctx") * local_rows + jnp.arange(local_rows, dtype=jnp.int32)
    live_rows = positions[:, None] < lengths[0][None, :]
    live_heads = jnp.transpose(live_rows)[:, None, :, None]
    cos_table, sin_table = rotary_tables(positions)

    def allowed_mask(offset, count):
        key_pos = offset + jnp.arange(count, dtype=jnp.int32)
        causal = key_pos[None, :] <= positions[:, None]
        return causal[None, None, :, :] & live_heads

    def split_heads(block_part):
        count = block_part.shape[0]
        key_part = block_part[:, :, 0].reshape(count, slot_count, HEADS, HEAD_DIM)
        value_part = block_part[:, :, 1].reshape(count, slot_count, HEADS, HEAD_DIM)
        return (key_part, value_part)

    attn_full = (
        lax.all_gather(w_qkv, ("dp", "ctx"), axis=0, tiled=True),
        lax.all_gather(b_qkv, ("dp", "ctx"), axis=0, tiled=True),
        lax.all_gather(w_out, ("dp", "ctx"), axis=0, tiled=True),
        lax.all_gather(gain_one, ("dp", "ctx"), axis=0, tiled=True),
        lax.all_gather(shift_one, ("dp", "ctx"), axis=0, tiled=True),
    )
    qkv_full, bias_full, out_full, gain_one_full, shift_one_full = attn_full
    source = inputs.astype(jnp.float32)
    scaled_one, inverse_one = layer_stats(source)
    normed_one = (
        scaled_one * gain_one_full.astype(jnp.float32) + shift_one_full.astype(jnp.float32)
    ).astype(jnp.bfloat16)
    joined = jnp.einsum(
        "rsd,de->rse", normed_one, qkv_full, preferred_element_type=jnp.float32
    ) + bias_full.astype(jnp.float32)
    query_pre = joined[..., :width].reshape(local_rows, slot_count, HEADS, HEAD_DIM)
    key_pre = joined[..., width : 2 * width].reshape(local_rows, slot_count, HEADS, HEAD_DIM)
    queries = rotate(query_pre, cos_table, sin_table).astype(jnp.bfloat16)
    keys_rot = rotate(key_pre, cos_table, sin_table).reshape(local_rows, slot_count, width)
    key_value = jnp.stack([keys_rot, joined[..., 2 * width :]], 2).astype(jnp.bfloat16)
    block_part = lax.all_gather(key_value, "ctx", axis=0, tiled=True)
    run_peak = jnp.full((slot_count, HEADS, local_rows), masked_value, jnp.float32)
    key_part, value_part = split_heads(block_part)
    scores = (
        jnp.einsum("qshd,kshd->shqk", queries, key_part, preferred_element_type=jnp.float32) * 0.125
    )
    allowed = allowed_mask(jnp.int32(0), block_part.shape[0])
    masked = jnp.where(allowed, scores, masked_value)
    new_peak = jnp.maximum(run_peak, jnp.max(masked, -1))
    weights = jnp.where(allowed, jnp.exp(masked - new_peak[..., None]), 0.0)
    new_sum = jnp.sum(weights, -1)
    new_acc = jnp.einsum(
        "shqk,kshd->shqd",
        weights.astype(jnp.bfloat16),
        value_part,
        preferred_element_type=jnp.float32,
    )
    final_sum = jnp.maximum(new_sum, 1.0)
    log_sum = new_peak + jnp.log(final_sum)
    attended = jnp.transpose(new_acc / final_sum[..., None], (2, 0, 1, 3))
    attended_low = attended.reshape(local_rows, slot_count, width).astype(jnp.bfloat16)
    hidden_in = source + jnp.einsum(
        "rsd,de->rse", attended_low, out_full, preferred_element_type=jnp.float32
    )
    mlp_full = (
        lax.all_gather(w_gate, ("dp", "ctx"), axis=0, tiled=True),
        lax.all_gather(w_up, ("dp", "ctx"), axis=0, tiled=True),
        lax.all_gather(w_down, ("dp", "ctx"), axis=0, tiled=True),
        lax.all_gather(gain_two, ("dp", "ctx"), axis=0, tiled=True),
        lax.all_gather(shift_two, ("dp", "ctx"), axis=0, tiled=True),
    )
    gate_full, up_full, down_full, gain_two_full, shift_two_full = mlp_full
    scaled_two, inverse_two = layer_stats(hidden_in)
    normed_two = (
        scaled_two * gain_two_full.astype(jnp.float32) + shift_two_full.astype(jnp.float32)
    ).astype(jnp.bfloat16)
    gate = jnp.einsum("rsd,df->rsf", normed_two, gate_full, preferred_element_type=jnp.float32)
    upward = jnp.einsum("rsd,df->rsf", normed_two, up_full, preferred_element_type=jnp.float32)
    sigmoid = jax.nn.sigmoid(gate)
    product = (gate * sigmoid * upward).astype(jnp.bfloat16)
    result = hidden_in + jnp.einsum(
        "rsf,fd->rsd", product, down_full, preferred_element_type=jnp.float32
    )
    gate_back, up_back, down_back, gain_two_back = (
        lax.all_gather(w_gate, ("dp", "ctx"), axis=0, tiled=True),
        lax.all_gather(w_up, ("dp", "ctx"), axis=0, tiled=True),
        lax.all_gather(w_down, ("dp", "ctx"), axis=0, tiled=True),
        lax.all_gather(gain_two, ("dp", "ctx"), axis=0, tiled=True),
    )
    grad_down = jnp.einsum("rsf,rsd->fd", product, cotangent, preferred_element_type=jnp.float32)
    grad_product = jnp.einsum(
        "rsd,fd->rsf", cotangent, down_back, preferred_element_type=jnp.float32
    )
    grad_gate_act = (grad_product * upward * sigmoid * (1.0 + gate * (1.0 - sigmoid))).astype(
        jnp.bfloat16
    )
    grad_up_act = (grad_product * gate * sigmoid).astype(jnp.bfloat16)
    grad_gate = jnp.einsum(
        "rsd,rsf->df", normed_two, grad_gate_act, preferred_element_type=jnp.float32
    )
    grad_up = jnp.einsum("rsd,rsf->df", normed_two, grad_up_act, preferred_element_type=jnp.float32)
    grad_normed_two = jnp.einsum(
        "rsf,df->rsd", grad_gate_act, gate_back, preferred_element_type=jnp.float32
    ) + jnp.einsum("rsf,df->rsd", grad_up_act, up_back, preferred_element_type=jnp.float32)
    grad_gain_two = jnp.sum(grad_normed_two * scaled_two, (0, 1))
    grad_shift_two = jnp.sum(grad_normed_two, (0, 1))
    grad_hidden = cotangent.astype(jnp.float32) + norm_back(
        grad_normed_two, scaled_two, inverse_two, gain_two_back.astype(jnp.float32)
    )
    mlp_sums = (
        lax.psum_scatter(grad_gate, ("dp", "ctx"), scatter_dimension=0, tiled=True),
        lax.psum_scatter(grad_up, ("dp", "ctx"), scatter_dimension=0, tiled=True),
        lax.psum_scatter(grad_down, ("dp", "ctx"), scatter_dimension=0, tiled=True),
        lax.psum_scatter(grad_gain_two, ("dp", "ctx"), scatter_dimension=0, tiled=True),
        lax.psum_scatter(grad_shift_two, ("dp", "ctx"), scatter_dimension=0, tiled=True),
    )
    qkv_back, out_back, gain_one_back = (
        lax.all_gather(w_qkv, ("dp", "ctx"), axis=0, tiled=True),
        lax.all_gather(w_out, ("dp", "ctx"), axis=0, tiled=True),
        lax.all_gather(gain_one, ("dp", "ctx"), axis=0, tiled=True),
    )
    hidden_low = grad_hidden.astype(jnp.bfloat16)
    grad_out = jnp.einsum(
        "rsd,rse->de", attended_low, hidden_low, preferred_element_type=jnp.float32
    )
    grad_attended = jnp.einsum(
        "rse,de->rsd", hidden_low, out_back, preferred_element_type=jnp.float32
    )
    grad_heads = grad_attended.reshape(local_rows, slot_count, HEADS, HEAD_DIM).astype(jnp.bfloat16)
    delta = jnp.transpose(jnp.sum(grad_heads.astype(jnp.float32) * attended, -1), (1, 2, 0))
    key_value_all = lax.all_gather(key_value, "ctx", axis=0, tiled=True)

    def grad_parts(block_part, offset):
        key_part, value_part = split_heads(block_part)
        scores = (
            jnp.einsum("qshd,kshd->shqk", queries, key_part, preferred_element_type=jnp.float32)
            * 0.125
        )
        allowed = allowed_mask(offset, block_part.shape[0])
        probs = jnp.where(allowed, jnp.exp(scores - log_sum[..., None]), 0.0)
        grad_prob = jnp.einsum(
            "qshd,kshd->shqk", grad_heads, value_part, preferred_element_type=jnp.float32
        )
        grad_score = (probs * (grad_prob - delta[..., None])).astype(jnp.bfloat16)
        return (key_part, probs, grad_score)

    def query_step(running, block_part, offset):
        key_part, probs, grad_score = grad_parts(block_part, offset)
        return running + jnp.einsum(
            "shqk,kshd->shqd", grad_score, key_part, preferred_element_type=jnp.float32
        )

    grad_query = (
        over_blocks(
            query_step,
            jnp.zeros((slot_count, HEADS, local_rows, HEAD_DIM), jnp.float32),
            key_value_all,
        )
        * 0.125
    )
    count = local_rows * lax.axis_size("ctx")
    tile_rows = math.gcd(count, 512)

    def one_block(number):
        block_start = number * tile_rows
        block_part = lax.dynamic_slice_in_dim(key_value_all, block_start, tile_rows, 0)
        key_part, probs, grad_score = grad_parts(block_part, block_start)
        grad_key = (
            jnp.einsum("shqk,qshd->kshd", grad_score, queries, preferred_element_type=jnp.float32)
            * 0.125
        )
        grad_value = jnp.einsum(
            "shqk,qshd->kshd",
            probs.astype(jnp.bfloat16),
            grad_heads,
            preferred_element_type=jnp.float32,
        )
        return jnp.stack(
            [
                grad_key.reshape(tile_rows, slot_count, width),
                grad_value.reshape(tile_rows, slot_count, width),
            ],
            2,
        )

    blocks = lax.map(one_block, jnp.arange(count // tile_rows, dtype=jnp.int32))
    grad_key_value = lax.psum_scatter(
        blocks.reshape(count, slot_count, 2, width).astype(jnp.bfloat16),
        "ctx",
        scatter_dimension=0,
        tiled=True,
    ).astype(jnp.float32)
    grad_query_pre = rotate(jnp.transpose(grad_query, (2, 0, 1, 3)), cos_table, -sin_table)
    grad_key_pre = rotate(
        grad_key_value[:, :, 0].reshape(local_rows, slot_count, HEADS, HEAD_DIM),
        cos_table,
        -sin_table,
    )
    grad_joined = jnp.concatenate(
        [
            grad_query_pre.reshape(local_rows, slot_count, width),
            grad_key_pre.reshape(local_rows, slot_count, width),
            grad_key_value[:, :, 1],
        ],
        -1,
    ).astype(jnp.bfloat16)
    grad_qkv = jnp.einsum(
        "rsd,rse->de", normed_one, grad_joined, preferred_element_type=jnp.float32
    )
    grad_bias = jnp.sum(grad_joined.astype(jnp.float32), (0, 1))
    grad_normed_one = jnp.einsum(
        "rse,de->rsd", grad_joined, qkv_back, preferred_element_type=jnp.float32
    )
    grad_gain_one = jnp.sum(grad_normed_one * scaled_one, (0, 1))
    grad_shift_one = jnp.sum(grad_normed_one, (0, 1))
    input_grad = grad_hidden + norm_back(
        grad_normed_one, scaled_one, inverse_one, gain_one_back.astype(jnp.float32)
    )
    attn_sums = (
        lax.psum_scatter(grad_qkv, ("dp", "ctx"), scatter_dimension=0, tiled=True),
        lax.psum_scatter(grad_bias, ("dp", "ctx"), scatter_dimension=0, tiled=True),
        lax.psum_scatter(grad_out, ("dp", "ctx"), scatter_dimension=0, tiled=True),
        lax.psum_scatter(grad_gain_one, ("dp", "ctx"), scatter_dimension=0, tiled=True),
        lax.psum_scatter(grad_shift_one, ("dp", "ctx"), scatter_dimension=0, tiled=True),
    )
    return (
        result.astype(jnp.bfloat16),
        input_grad,
        attn_sums[0],
        attn_sums[1],
        attn_sums[2],
        mlp_sums[0],
        mlp_sums[1],
        mlp_sums[2],
        attn_sums[3],
        attn_sums[4],
        mlp_sums[3],
        mlp_sums[4],
    )


MESH = pl.DeviceIdType.MESH
HBM = pl.BlockSpec(memory_space=pltpu.HBM)
VMEM = pl.BlockSpec(memory_space=pltpu.VMEM)
VMEM_LIMIT = 60 << 20


def flip(index, mask):
    for bit in (1, 2, 4):
        if mask & bit:
            index = index + bit - 2 * bit * ((index // bit) % 2)
    return index


class Wires:
    def __init__(self, send, recv):
        self.send, self.recv = send, recv
        self.z, self.c = lax.axis_index("dp"), lax.axis_index("ctx")
        self.inner = (self.z == 1) | (self.z == 2)
        self.outer = (self.z == 0) | (self.z == 3)
        self.number = itertools.count()

    def put(self, src, dst, z_mask, c_mask):
        return self.put_to(src, dst, flip(self.z, z_mask), flip(self.c, c_mask))

    def put_to(self, src, dst, z, c):
        i = next(self.number)
        return pltpu.make_async_remote_copy(
            src_ref=src,
            dst_ref=dst,
            send_sem=self.send.at[i],
            recv_sem=self.recv.at[i],
            device_id=(z, c),
            device_id_type=MESH,
        )

    def greet(self, zs, n):
        self.call(zs, n)
        self.met(zs, n)

    def met(self, zs, n):
        pl.semaphore_wait(pltpu.get_barrier_semaphore(), zs + n - 2)

    def call(self, zs, n):
        barrier = pltpu.get_barrier_semaphore()
        for m in range(1, zs):
            pl.semaphore_signal(
                barrier, inc=1, device_id=(flip(self.z, m), self.c), device_id_type=MESH
            )
        for m in range(1, n):
            pl.semaphore_signal(
                barrier, inc=1, device_id=(self.z, flip(self.c, m)), device_id_type=MESH
            )


class DepthGather:
    def __init__(self, wires, part):
        z = wires.z
        self.wires = wires
        self.near = wires.put(part(z), part(z), 1, 0)
        self.skip = wires.put(part(z), part(z), 2, 0)
        self.mid = wires.put(part(z), part(z), 3, 0)
        far = flip(z, 2)
        self.on = wires.put(part(far), part(far), 1, 0)

    @staticmethod
    def start(parts):
        for part in parts:
            part.skip.start()
        for part in parts:
            pl.when(part.wires.inner)(part.mid.start)
        for part in parts:
            part.near.start()

    def forward(self):
        @pl.when(self.wires.inner)
        def _():
            self.skip.wait_recv()
            self.on.start()

    def finish(self):
        self.near.wait_recv()
        self.near.wait_send()
        self.skip.wait_send()

        @pl.when(self.wires.inner)
        def _():
            self.mid.wait_recv()
            self.mid.wait_send()
            self.on.wait_send()

        @pl.when(self.wires.outer)
        def _():
            self.skip.wait_recv()
            self.on.wait_recv()


class LayerGather:
    def __init__(self, wires, block, source=None):
        c = wires.c
        mine = block(c) if source is None else source
        self.direct = {m: wires.put(mine, block(c), 0, m) for m in (2, 4, 6, 1)}
        self.on = {m: wires.put(block(flip(c, m)), block(flip(c, m)), 0, 1) for m in (2, 4, 6)}

    def start(self):
        for m in (2, 4, 6, 1):
            self.direct[m].start()

    def forward(self, m):
        self.direct[m].wait_recv()
        self.on[m].start()

    def arrived(self, m):
        (self.direct[1] if m == 1 else self.on[m - 1]).wait_recv()

    def sent(self):
        for copy in (*self.direct.values(), *self.on.values()):
            copy.wait_send()


def pack_columns(dst, refs, n, zs):
    for i in range(n):
        pieces = []
        for ref, block, at, size in refs:
            starts = [block * (j * n + i) + at for j in range(zs)]
            pieces += [ref[:, start : start + size] for start in starts]
        dst[i] = jnp.concatenate(pieces, -1)


class LayerScatter:
    def __init__(self, wires, part, near, far):
        c = wires.c
        self.c, self.part, self.near, self.far = c, part, near, far
        self.pair = {
            m: wires.put(part(flip(c, m + 1)), near(m // 2), 0, 1) for m in (6, 4, 2, 0)
        }
        self.chips = {m: wires.put(part(flip(c, m)), far(m // 2 - 1), 0, m) for m in (6, 4, 2)}

    def start(self):
        for copy in self.pair.values():
            copy.start()

    def step(self, m):
        self.pair[m].wait_recv()
        to = self.part(flip(self.c, m))
        to[...] = (
            to[...].astype(jnp.float32) + self.near(m // 2)[...].astype(jnp.float32)
        ).astype(to.dtype)
        self.chips[m].start()

    def total(self):
        self.pair[0].wait_recv()
        result = self.part(self.c)[...].astype(jnp.float32)
        result = result + self.near(0)[...].astype(jnp.float32)
        for m in (2, 4, 6):
            self.chips[m].wait_recv()
            result = result + self.far(m // 2 - 1)[...].astype(jnp.float32)
        return result

    def sent(self):
        for copy in (*self.pair.values(), *self.chips.values()):
            copy.wait_send()


def dot(a, b, dims=((1,), (0,))):
    return lax.dot_general(a, b, (dims, ((), ())), preferred_element_type=jnp.float32)


def turn_pair(values, table, sign):
    half = ROTARY // 2
    columns = values.shape[-1]
    table = [jnp.concatenate([t] * (columns // t.shape[-1]), -1) for t in table]
    return (
        values * table[0]
        + sign * (pltpu.roll(values, columns - half, 1) * table[1])
        + sign * (pltpu.roll(values, half, 1) * table[2])
    )


def head_mask(rows, columns, head):
    return lax.broadcasted_iota(jnp.int32, (rows, columns), 1) // HEAD_DIM == head


class DepthScatter:
    def __init__(self, wires, part, relay, boxes):
        z = wires.z
        self.wires, self.part, self.relay_box, self.boxes = wires, part, relay, boxes
        self.far = wires.put(part(flip(z, 3)), relay, 1, 0)
        self.skip = wires.put(part(flip(z, 2)), boxes[1], 2, 0)
        self.near = wires.put(part(flip(z, 1)), boxes[0], 1, 0)
        self.mid = wires.put(part(flip(z, 3)), boxes[2], 3, 0)

    def start(self, mask):
        outer, inner = pl.when(self.wires.outer), pl.when(self.wires.inner)
        if mask == 3:
            outer(self.far.start)
            inner(self.mid.start)
        elif mask == 2:
            outer(self.skip.start)
        elif mask == 1:
            self.near.start()
        else:

            @outer
            def _():
                self.boxes[2][...] = jnp.zeros_like(self.boxes[2])

    def relay(self):
        @pl.when(self.wires.inner)
        def _():
            self.far.wait_recv()
            to = self.part(flip(self.wires.z, 2))
            to[...] = (
                to[...].astype(jnp.float32) + self.relay_box[...].astype(jnp.float32)
            ).astype(to.dtype)
            self.skip.start()

    def total(self):
        self.near.wait_recv()
        self.skip.wait_recv()
        pl.when(self.wires.inner)(self.mid.wait_recv)
        result = self.part(self.wires.z)[...].astype(jnp.float32)
        for box in self.boxes:
            result = result + box[...].astype(jnp.float32)
        return result

    def sent(self):
        self.near.wait_send()
        self.skip.wait_send()
        pl.when(self.wires.outer)(self.far.wait_send)
        pl.when(self.wires.inner)(self.mid.wait_send)


class Moves:
    def __init__(self, sems):
        self.sems, self.number, self.stores = sems, itertools.count(), []

    def load(self, src, dst):
        copy = pltpu.make_async_copy(src, dst, self.sems.at[next(self.number)])
        copy.start()
        return copy

    def store(self, src, dst):
        self.stores.append(self.load(src, dst))

    def finish(self):
        for copy in self.stores:
            copy.wait()


def pieces_of(total, number, unit):
    units = total // unit
    cuts = [units * i // number * unit for i in range(number + 1)]
    return [(a, b - a) for a, b in zip(cuts[:-1], cuts[1:])]


class ChainGather:
    def __init__(self, wires, part):
        self.z = z = wires.z
        self.right = [
            wires.put_to(part((z - s + 4) % 4), part((z - s + 4) % 4), (z + 1) % 4, wires.c)
            for s in range(3)
        ]
        self.left = [
            wires.put_to(part((z + s) % 4), part((z + s) % 4), (z + 3) % 4, wires.c)
            for s in range(3)
        ]

    def start(self):
        pl.when(self.z <= 2)(self.right[0].start)
        pl.when(self.z >= 1)(self.left[0].start)

    def hop(self, s):
        pl.when(self.z >= s)(self.right[s - 1].wait_recv)
        pl.when((self.z >= s) & (self.z <= 2))(self.right[s].start)
        pl.when(self.z <= 3 - s)(self.left[s - 1].wait_recv)
        pl.when((self.z <= 3 - s) & (self.z >= 1))(self.left[s].start)

    def finish(self):
        pl.when(self.z >= 3)(self.right[2].wait_recv)
        pl.when(self.z <= 0)(self.left[2].wait_recv)
        for s in range(3):
            pl.when((self.z >= s) & (self.z <= 2))(self.right[s].wait_send)
            pl.when((self.z <= 3 - s) & (self.z >= 1))(self.left[s].wait_send)


class ChainScatter:
    def __init__(self, wires, part, right, left):
        self.z = z = wires.z
        self.part, self.right_box, self.left_box = part, right, left
        self.right = {
            j: wires.put_to(part(j), right(j), (z + 1) % 4, wires.c) for j in (3, 2, 1)
        }
        self.left = {j: wires.put_to(part(j), left(j), (z + 3) % 4, wires.c) for j in (0, 1, 2)}

    def clear(self):
        @pl.when(self.z == 0)
        def _():
            self.right_box(1)[...] = jnp.zeros_like(self.right_box(1))

        @pl.when(self.z == 3)
        def _():
            self.left_box(2)[...] = jnp.zeros_like(self.left_box(2))

    def start(self, distance):
        pl.when(self.z == 0)(self.right[distance].start)
        pl.when(self.z == 3)(self.left[3 - distance].start)

    def pass_on(self, copy, j, box):
        copy.wait_recv()
        to = self.part(j)
        to[...] = (to[...].astype(jnp.float32) + box(j)[...].astype(jnp.float32)).astype(to.dtype)
        copy.start()

    def hop(self, s, distance):
        @pl.when(self.z == s)
        def _():
            self.pass_on(self.right[distance], distance, self.right_box)

        @pl.when(self.z == 3 - s)
        def _():
            self.pass_on(self.left[3 - distance], 3 - distance, self.left_box)

    def total(self):
        for j in (1, 2, 3):
            pl.when(self.z == j)(self.right[j].wait_recv)
        for j in (0, 1, 2):
            pl.when(self.z == j)(self.left[j].wait_recv)
        z = self.z
        return (
            self.part(z)[...].astype(jnp.float32)
            + self.right_box(jnp.maximum(z, 1))[...].astype(jnp.float32)
            + self.left_box(jnp.minimum(z, 2))[...].astype(jnp.float32)
        )

    def sent(self):
        for j in (1, 2, 3):
            pl.when(self.z < j)(self.right[j].wait_send)
        for j in (0, 1, 2):
            pl.when(self.z > j)(self.left[j].wait_send)


def halves_of(block):
    first = (block // 16 + 1) // 2 * 16
    return [(0, first), (first, block - first)]


def by_slot(dst, src):
    rows, slots, _ = src.shape
    for s in range(slots):
        dst[s * rows : (s + 1) * rows] = src[:, s, :]


def by_position(dst, values):
    rows, slots, _ = dst.shape
    for s in range(slots):
        dst[:, s, :] = values[s * rows : (s + 1) * rows].astype(dst.dtype)


def front_kernel(
    zs,
    n,
    slots,
    lengths,
    tables,
    small,
    w_qkv,
    w_gate,
    w_up,
    w_out,
    w_down,
    inputs,
    cotangent,
    w_qkv_out,
    w_out_out,
    w_gu_out,
    a1_out,
    qkv_out,
    probs_out,
    ob_out,
    hidden_out,
    a2_out,
    dgu_out,
    y_out,
    grad_down_out,
    norms,
    qkv_send,
    gu_send,
    small_v,
    bias_v,
    w_qkv_v,
    w_out_v,
    w_gu_v,
    w_down_v,
    wide_x,
    wide_a,
    dy_v,
    qkv_v,
    probs_v,
    ob_v,
    near,
    far,
    hidden_v,
    gu_v,
    zz_v,
    dz_v,
    gd_v,
    right_v,
    left_v,
    raw_v,
    send,
    recv,
    local,
):
    f32, b16 = jnp.float32, jnp.bfloat16
    wires = Wires(send, recv)
    moves = Moves(local)
    z, c = wires.z, wires.c
    rows, _, width = inputs.shape
    local_rows = rows * slots
    tokens, seq = n * local_rows, n * rows
    pair = 2 * local_rows
    hc = qkv_v.shape[-1]
    heads = hc // HEAD_DIM
    block = w_down_v.shape[1]
    ffc = zs * block
    halves = halves_of(block)
    spans = [(2 * zs * at, zs * size) for at, size in halves]
    lanes = 2 * HEAD_DIM
    lane_half = lax.broadcasted_iota(jnp.int32, (1, lanes), 1) // HEAD_DIM

    def block_of(ref, i):
        return ref.at[pl.ds(pl.multiple_of(i * local_rows, local_rows), local_rows)]

    def pair_at(i):
        return pl.ds(pl.multiple_of(i * pair, pair), pair)

    wires.call(zs, n)
    wait_out = moves.load(w_out, w_out_v.at[z])
    wait_small = moves.load(small, small_v.at[z, c])
    waits = [moves.load(inputs, raw_v.at[0]), moves.load(cotangent, raw_v.at[1])]
    wait_down = moves.load(w_down, w_down_v.at[z])
    wait_out.wait()
    wires.met(zs, n)
    out_z = DepthGather(wires, lambda i: w_out_v.at[i])
    DepthGather.start([out_z])
    pack_columns(
        qkv_send,
        [(w_qkv.at[:, i * width : (i + 1) * width], HEAD_DIM, 0, HEAD_DIM) for i in range(3)],
        n,
        zs,
    )
    wait_own_qkv = moves.load(qkv_send.at[c], w_qkv_v.at[z, c])
    qkv_x = [wires.put(qkv_send.at[flip(c, m)], w_qkv_v.at[z, c], 0, m) for m in range(1, n)]
    for copy in qkv_x:
        copy.start()
    wait_small.wait()
    small_z = [wires.put(small_v.at[z, c], small_v.at[z, c], m, 0) for m in range(1, zs)]
    for copy in small_z:
        copy.start()
    waits[0].wait()
    by_slot(block_of(wide_x, c), raw_v.at[0])
    xs_g = LayerGather(wires, lambda i: block_of(wide_x, i))
    xs_g.start()
    pack_columns(
        gu_send, [(w, block, at, size) for at, size in halves for w in (w_gate, w_up)], n, zs
    )
    wait_own_gu = moves.load(gu_send.at[c], w_gu_v.at[z, c])
    for copy in small_z:
        copy.wait_recv()
    small_x = [wires.put(small_v.at[:, c], small_v.at[:, c], 0, m) for m in range(1, n)]
    for copy in small_x:
        copy.start()
    wait_own_qkv.wait()
    for copy in qkv_x:
        copy.wait_recv()
    number = 4
    qkv_z = [
        DepthGather(wires, lambda i, a=a, s=s: w_qkv_v.at[i, a : a + s])
        for a, s in pieces_of(n, number, 1)
    ]
    DepthGather.start(qkv_z)
    gu_x = [wires.put(gu_send.at[flip(c, m)], w_gu_v.at[z, c], 0, m) for m in range(1, n)]
    for copy in gu_x:
        copy.start()
    out_z.forward()
    for m in (2, 4, 6):
        xs_g.forward(m)

    for copy in small_x:
        copy.wait()
    for r in range(4):
        norms[r : r + 1] = jnp.concatenate(
            [
                jnp.where(
                    lane_half == 0,
                    small_v[d // n, d % n, r : r + 1],
                    small_v[d // n, d % n + 1, r : r + 1],
                )
                for d in range(0, zs * n, 2)
            ],
            -1,
        )
    norms[4:8] = jnp.zeros_like(norms[4:8])
    per_owner = 3 * zs * n // (zs * n)
    for i in range(3):
        for j in range(0, zs, 2):
            both = []
            for h in range(2):
                group = i * zs * n + (j + h) * n + c
                owner, k = group // per_owner, group % per_owner
                tile = small_v[owner // n, owner % n]
                row = jnp.where(k == 2, tile[5:6], tile[4:5])
                both.append(jnp.where(k % 2 == h, row, pltpu.roll(row, HEAD_DIM, 1)))
            at = (i * zs + j) * HEAD_DIM
            bias_v[:, at : at + lanes] = jnp.where(lane_half == 0, both[0], both[1])

    for m in (1, 3, 5, 7):
        xs_g.arrived(m)
    hidden_v[...] = block_of(wide_x, c)[...].astype(f32)

    def norm_one(i, carry):
        x = wide_x[pair_at(i)].astype(f32)
        wide_a[pair_at(i)] = (layer_stats(x)[0] * norms[0:1] + norms[1:2]).astype(b16)
        return carry

    lax.fori_loop(0, n // 2, norm_one, 0)
    wait_a1 = moves.load(wide_a, a1_out)
    wait_own_gu.wait()
    for copy in gu_x:
        copy.wait_recv()
    gu_z = [
        [
            DepthGather(
                wires, lambda i, a=a, s=s, k=slice(at, at + 2 * size): w_gu_v.at[i, a : a + s, :, k]
            )
            for a, s in pieces_of(n, number, 1)
        ]
        for at, size in spans
    ]
    for part in qkv_z:
        part.forward()
    for part in gu_z:
        DepthGather.start(part)
    waits[1].wait()
    by_slot(dy_v.at[c], raw_v.at[1])
    dy_g = LayerGather(wires, lambda i: dy_v.at[i])
    dy_g.start()
    for part in (out_z, *qkv_z):
        part.finish()
    moves.store(w_qkv_v, w_qkv_out)
    moves.store(w_out_v, w_out_out)

    def project(i, carry):
        joined = dot(wide_a[pair_at(i)], w_qkv_v[...].reshape(width, 3 * hc)) + bias_v[...]
        for j in range(2):
            table = [tables[k, 2 * i + j] for k in range(3)]
            for s in range(slots):
                at = (j * slots + s) * rows
                piece = joined[at : at + rows]
                qkv_v[0, s, 2 * i + j] = turn_pair(piece[:, :hc], table, 1.0).astype(b16)
                qkv_v[1, s, 2 * i + j] = turn_pair(piece[:, hc : 2 * hc], table, 1.0).astype(b16)
                qkv_v[2, s, 2 * i + j] = piece[:, 2 * hc :].astype(b16)
        return carry

    lax.fori_loop(0, n // 2, project, 0)
    moves.store(qkv_v, qkv_out)
    for m in (2, 4, 6):
        dy_g.forward(m)

    half = seq // 2
    probs_sem = moves.sems.at[next(moves.number)]

    def attend(s, carry):
        q, k, v = [qkv_v[i, s].reshape(seq, hc) for i in range(3)]
        length = lengths[0, s]
        kept = pltpu.make_async_copy(probs_v, probs_out.at[s], probs_sem)
        for part_q in range(2):
            keys = (part_q + 1) * half
            at = part_q * half
            query = q[at : at + half]
            row = lax.broadcasted_iota(jnp.int32, (half, keys), 0) + at
            key = lax.broadcasted_iota(jnp.int32, (half, keys), 1)
            allowed = (key <= row) & (row < length)
            out = jnp.zeros((half, hc), f32)
            for h in range(heads):
                mask = head_mask(half, hc, h)
                scores = dot(jnp.where(mask, query, 0).astype(b16), k[:keys], ((1,), (1,)))
                scores = jnp.where(allowed, scores * 0.125, masked_value)
                peak = jnp.max(scores, -1, keepdims=True)
                weights = jnp.where(allowed, jnp.exp(scores - peak), 0.0)
                total = jnp.maximum(jnp.sum(weights, -1, keepdims=True), 1.0)
                probs = (weights * (1.0 / total)).astype(b16)
                probs_v[h, at : at + half, 0:keys] = probs
                if keys < seq:
                    probs_v[h, at : at + half, keys:seq] = jnp.zeros((half, seq - keys), b16)
                out = jnp.where(mask, dot(probs, v[:keys]), out)
            ob_v[part_q * n // 2 : (part_q + 1) * n // 2, s] = out.astype(b16).reshape(
                n // 2, rows, hc
            )
        kept.start()
        kept.wait()
        return carry

    lax.fori_loop(0, slots, attend, 0)
    moves.store(ob_v, ob_out)
    for part in gu_z[0][:2]:
        part.forward()

    xs_g.sent()

    def to_hidden(i, carry):
        block_of(wide_x, i)[...] = dot(
            ob_v[i].reshape(local_rows, hc), w_out_v[...].reshape(hc, width)
        ).astype(b16)
        return carry

    lax.fori_loop(0, n, to_hidden, 0)
    wait_a1.wait()
    sums = LayerScatter(
        wires, lambda i: block_of(wide_x, i), lambda j: near.at[j], lambda j: far.at[j]
    )
    sums.start()
    for m in (6, 4, 2):
        sums.step(m)
    for part in gu_z[0][2:]:
        part.forward()
    hidden = hidden_v[...] + sums.total()
    hidden_v[...] = hidden
    moves.store(hidden_v, hidden_out)
    block_of(wide_a, c)[...] = (layer_stats(hidden)[0] * norms[2:3] + norms[3:4]).astype(b16)
    a2_g = LayerGather(wires, lambda i: block_of(wide_a, i))
    a2_g.start()
    gu_z[1][0].forward()
    for m in (2, 4, 6):
        a2_g.forward(m)
    for part in gu_z[1][1:]:
        part.forward()
    wait_down.wait()
    tile = width // number
    columns = [slice(p * tile, (p + 1) * tile) for p in range(number)]
    down_z = [ChainGather(wires, lambda i, k=k: w_down_v.at[i, :, k]) for k in columns]
    for chain in down_z:
        chain.start()
    for m in (1, 3, 5, 7):
        dy_g.arrived(m)
    for m in (1, 3, 5, 7):
        a2_g.arrived(m)
    wait_a2 = moves.load(wide_a, a2_out)

    down_sums = []
    for step, ((at, size), (start, count), parts) in enumerate(zip(halves, spans, gu_z)):
        units, gates = slice(at, at + size), slice(start, start + 2 * count)
        inner = slice(zs * at, zs * (at + size))
        for _, _, chain in down_sums:
            chain.hop(1, 3)
        for part in parts:
            part.finish()

        def feed(i, carry, inner=inner, gates=gates, count=count):
            gu = dot(wide_a[pair_at(i)], w_gu_v[:, :, :, gates].reshape(width, 2 * count))
            gu_v[i, :, gates] = gu.astype(b16)
            gate = gu[:, :count]
            zz_v[i, :, inner] = (gate * jax.nn.sigmoid(gate) * gu[:, count:]).astype(b16)
            return carry

        lax.fori_loop(0, n // 2, feed, 0)
        if step == 1:
            down_z[0].hop(1)
            down_z[1].hop(1)
        chains = []
        for p in range(2):
            k = slice(p * width // 2, (p + 1) * width // 2)
            for q in columns[2 * p : 2 * p + 2]:
                gd = dot(
                    zz_v[:, :, inner].reshape(tokens, count),
                    dy_v[:, :, q].reshape(tokens, tile),
                    ((0,), (0,)),
                )
                gd_v[:, units, q] = gd.astype(b16).reshape(zs, size, tile)
            chains.append(
                ChainScatter(
                    wires,
                    lambda i, u=units, k=k: gd_v.at[i, u, k],
                    lambda i, u=units, k=k: right_v.at[i - 1, u, k],
                    lambda i, u=units, k=k: left_v.at[i, u, k],
                )
            )
            chains[-1].start(3)
            down_sums.append((units, k, chains[-1]))
            if step == 1:
                down_z[2 + p].hop(1)
                down_z[p].hop(2)
                down_sums[p][2].hop(1, 2)
        for distance in (2, 1):
            for chain in chains:
                chain.start(distance)
        for chain in chains:
            chain.clear()
    moves.store(w_gu_v, w_gu_out)
    sums.sent()
    a2_g.sent()
    wait_a2.wait()

    def products(p):
        k = columns[p]

        def rows_of(i, carry):
            dy_rows = dy_v[pl.ds(2 * i, 2), :, k].reshape(pair, tile)
            y = jnp.zeros((pair, tile), f32)
            for at, size in halves:
                weight = w_down_v[:, at : at + size, k].reshape(zs * size, tile)
                inner = slice(zs * at, zs * (at + size))
                dz = dot(dy_rows, weight, ((1,), (1,)))
                dz_v[i, :, inner] = dz if p == 0 else dz_v[i, :, inner] + dz
                y = y + dot(zz_v[i, :, inner], weight)
            wide_x[pair_at(i), k] = y.astype(b16)
            return carry

        lax.fori_loop(0, n // 2, rows_of, 0)

    chains = [chain for _, _, chain in down_sums]
    for t in (0, 1):
        chains[t].hop(2, 3)
        down_z[2 + t].hop(2)
    for t in (2, 3):
        chains[t].hop(1, 3)
    for t in (2, 3):
        chains[t].hop(1, 2)
    for t in (2, 3):
        chains[t].hop(2, 3)
    for t in range(number):
        down_z[t].finish()
        products(t)
    moves.store(wide_x, y_out)

    def back(i, carry):
        for (at, size), (start, count) in zip(halves, spans):
            dz = dz_v[i, :, zs * at : zs * (at + size)]
            gate = gu_v[i, :, start : start + count].astype(f32)
            up = gu_v[i, :, start + count : start + 2 * count].astype(f32)
            sig = jax.nn.sigmoid(gate)
            dg = dz * up * sig * (1.0 + gate * (1.0 - sig))
            du = dz * gate * sig
            gu_v[i, :, start : start + 2 * count] = jnp.concatenate([dg, du], -1).astype(b16)
        return carry

    lax.fori_loop(0, n // 2, back, 0)
    moves.store(gu_v, dgu_out)
    for units, k, chain in down_sums:
        grad_down_out[units, k] = chain.total()
    for group in (*chains, dy_g):
        group.sent()
    for copy in (*small_z, *qkv_x, *gu_x):
        copy.wait_send()
    moves.finish()


def front(zs, n, lengths, tables, small, w_qkv, w_gate, w_up, w_out, w_down, inputs, cotangent):
    f32, b16 = jnp.float32, jnp.bfloat16
    rows, slots, width = inputs.shape
    local = rows * slots
    seq, tokens = rows * n, local * n
    heads = HEADS // n
    hc = heads * HEAD_DIM
    wrows = w_out.shape[0]
    block = w_down.shape[0]
    gc = 2 * zs * block
    qkv_all = ((zs, n, wrows, 3 * hc), b16)
    out_all = ((zs, wrows, width), b16)
    gu_all = ((zs, n, wrows, gc), b16)
    down_all = ((zs, block, width), b16)
    wide = ((tokens, width), b16)
    qkv = ((3, slots, n, rows, hc), b16)
    probs = ((slots, heads, seq, seq), b16)
    ob = ((n, slots, rows, hc), b16)
    hidden = ((local, width), f32)
    gu = ((n // 2, 2 * local, gc), b16)
    outs = [
        qkv_all,
        out_all,
        gu_all,
        wide,
        qkv,
        probs,
        ob,
        hidden,
        wide,
        gu,
        wide,
        ((block, width), f32),
        ((8, width), f32),
    ]
    scratch = [
        ((n, wrows, 3 * hc), b16),
        ((n, wrows, gc), b16),
        ((zs, n, *small.shape), f32),
        ((1, 3 * hc), f32),
        qkv_all,
        out_all,
        gu_all,
        down_all,
        wide,
        wide,
        ((n, local, width), b16),
        qkv,
        (probs[0][1:], b16),
        ob,
        ((n // 2, local, width), b16),
        ((n // 2 - 1, local, width), b16),
        hidden,
        gu,
        ((n // 2, 2 * local, gc // 2), b16),
        ((n // 2, 2 * local, gc // 2), f32),
        down_all,
        ((zs - 1, block, width), b16),
        ((zs - 1, block, width), b16),
        ((2, *inputs.shape), b16),
    ]
    return pl.pallas_call(
        functools.partial(front_kernel, zs, n, slots),
        out_shape=[jax.ShapeDtypeStruct(*k) for k in outs],
        in_specs=[pl.BlockSpec(memory_space=pltpu.SMEM), VMEM, HBM, *[VMEM] * 3, *[HBM] * 4],
        out_specs=[HBM] * (len(outs) - 2) + [VMEM] * 2,
        scratch_shapes=[
            *[pltpu.VMEM(*k) for k in scratch],
            pltpu.SemaphoreType.DMA((192,)),
            pltpu.SemaphoreType.DMA((192,)),
            pltpu.SemaphoreType.DMA((32,)),
        ],
        compiler_params=pltpu.CompilerParams(
            collective_id=1, has_side_effects=True, vmem_limit_bytes=VMEM_LIMIT
        ),
        name="front",
    )(lengths, tables, small, w_qkv, w_gate, w_up, w_out, w_down, inputs, cotangent)


def unpack_columns(dst, src, parts, n, zs):
    dst[...] = jnp.concatenate(
        [
            src[i, :, at + size * j : at + size * (j + 1)]
            for j in range(zs)
            for i in range(n)
            for at, size in parts
        ],
        -1,
    ).astype(dst.dtype)


def backward_kernel(
    zs,
    n,
    norms,
    tables,
    a1_all,
    a2_all,
    dgu,
    w_gu,
    w_qkv,
    w_out,
    qkv,
    probs,
    ob,
    hidden,
    cotangent,
    inputs,
    y_part,
    grad_out_out,
    result_out,
    input_grad_out,
    gq_out,
    gu_out,
    small_out,
    wide_v,
    dgu_v,
    weight_v,
    w_out_v,
    qkv_v,
    probs_v,
    ob_v,
    hidden_v,
    own_v,
    raw_v,
    ggu_v,
    relay_v,
    box_v,
    near,
    far,
    dh_all,
    go_v,
    go_relay,
    go_box,
    dqkv_v,
    dj_v,
    bias_v,
    gq_relay,
    gq_box,
    gu_rows,
    gq_rows,
    small_v,
    small_x,
    small_r,
    small_z,
    send,
    recv,
    local,
    free,
):
    f32, b16 = jnp.float32, jnp.bfloat16
    wires = Wires(send, recv)
    moves = Moves(local)
    z, c = wires.z, wires.c
    _, slots, rows, hc = ob_v.shape
    width = dh_all.shape[-1]
    tokens, seq, local_rows = n * slots * rows, n * rows, slots * rows
    heads = hc // HEAD_DIM
    wrows, gc = ggu_v.shape[2:]
    depth = n * wrows
    ffc, qc = gc // 2, 3 * hc
    part = wide_v
    gu_weight = weight_v.at[:, :, :, 0:gc]
    qkv_weight, gq_v = weight_v.at[:, :, :, 0:qc], weight_v.at[:, :, :, qc : 2 * qc]

    wait_a2 = moves.load(a2_all, wide_v)
    wait_dy = moves.load(cotangent, raw_v)
    wait_dgu = moves.load(dgu, dgu_v)
    wait_w = moves.load(w_gu, gu_weight)
    waits = [
        moves.load(hidden, hidden_v),
        moves.load(w_out, w_out_v),
        moves.load(qkv, qkv_v),
        moves.load(probs.at[0], probs_v),
        moves.load(ob, ob_v),
    ]
    wires.greet(zs, n)
    wait_a2.wait()
    wait_dgu.wait()

    number = 4
    step = depth // 2

    quarter = wrows // number

    def scatters(whole, relay, box):
        rows_of = [slice(p * quarter, (p + 1) * quarter) for p in range(number)]
        return [
            DepthScatter(
                wires,
                lambda i, k=k: whole.at[i, :, k],
                relay.at[:, k],
                [box.at[j, :, k] for j in range(3)],
            )
            for k in rows_of
        ]

    def weigh(sums, whole, left_v, grads, also=None):
        for mask in (3, 2, 1, 0):
            to = flip(z, mask)

            def piece(p, carry, to=to):
                at = pl.multiple_of(to * depth + p * step, step)
                left = left_v[:, :, pl.ds(at, step)].reshape(tokens, step)
                gradient = dot(left, grads(), ((0,), (0,))).astype(b16)
                whole[to, pl.ds(p * (n // 2), n // 2)] = gradient.reshape(n // 2, wrows, -1)
                return carry

            lax.fori_loop(0, 2, piece, 0)
            for part_sum in sums:
                part_sum.start(mask)
            if mask == 3 and also is not None:
                also.start(3)

    gu_sums = scatters(ggu_v, relay_v, box_v)
    weigh(gu_sums, ggu_v, wide_v, lambda: dgu_v[...].reshape(tokens, gc))

    wait_w.wait()

    def normed_two(i, carry):
        part[pl.ds(2 * i, 2)] = (
            dot(dgu_v[i], gu_weight[...].reshape(width, gc), ((1,), (1,)))
            .astype(b16)
            .reshape(2, local_rows, width)
        )
        return carry

    lax.fori_loop(0, n // 2, normed_two, 0)
    wait_qkv = moves.load(w_qkv, qkv_weight)
    da2_sums = LayerScatter(
        wires, lambda i: part.at[i], lambda j: near.at[j], lambda j: far.at[j]
    )
    da2_sums.start()
    gu_sums[0].relay()
    for m in (6, 4, 2):
        da2_sums.step(m)
    for copy in waits:
        copy.wait()
    wait_dy.wait()
    by_slot(own_v, raw_v)
    wait_xs = moves.load(inputs, raw_v)
    n2, r2 = layer_stats(hidden_v[...])
    for part_sum in gu_sums[1:]:
        part_sum.relay()
    da2 = da2_sums.total()
    gains = [jnp.sum(da2 * n2, 0, keepdims=True), jnp.sum(da2, 0, keepdims=True)]
    dh = own_v[...].astype(f32) + norm_back(da2, n2, r2, norms[2:3])
    by_position(input_grad_out, dh)
    dh_all[c] = dh.astype(b16)
    dh_g = LayerGather(wires, lambda i: dh_all.at[i])
    dh_g.start()
    da2_sums.sent()
    wait_y = moves.load(y_part, part)
    for m in (2, 4, 6):
        dh_g.forward(m)
    for m in (1, 3, 5, 7):
        dh_g.arrived(m)
    wait_y.wait()
    y_sums = LayerScatter(
        wires, lambda i: part.at[i], lambda j: near.at[j], lambda j: far.at[j]
    )
    y_sums.start()

    go_sums = DepthScatter(
        wires, lambda i: go_v.at[i], go_relay, [go_box.at[j] for j in range(3)]
    )
    tile = width // 4

    def heads_grad(p, carry):
        at = pl.ds(pl.multiple_of(p * tile, tile), tile)
        go = dot(
            ob_v[...].reshape(tokens, hc), dh_all[:, :, at].reshape(tokens, tile), ((0,), (0,))
        )
        go_v[:, :, at] = go.astype(b16).reshape(zs, hc // zs, tile)
        return carry

    lax.fori_loop(0, 4, heads_grad, 0)

    def heads_back(i, carry):
        ob_v[i] = (
            dot(dh_all[i], w_out_v[...].reshape(hc, width), ((1,), (1,)))
            .astype(b16)
            .reshape(slots, rows, hc)
        )
        return carry

    for m in (6, 4, 2):
        y_sums.step(m)
    lax.fori_loop(0, n, heads_back, 0)
    dh_g.sent()
    wait_a1 = moves.load(a1_all, dh_all)
    half = seq // 2

    def attend(s, carry):
        q, k, v = [qkv_v[i, s].reshape(seq, hc) for i in range(3)]
        do_s = ob_v[:, s].reshape(seq, hc)
        dqkv_v[...] = jnp.zeros_like(dqkv_v)
        for part_q in range(2):
            keys = (part_q + 1) * half
            at = part_q * half
            query, do_q = q[at : at + half], do_s[at : at + half]
            dq = jnp.zeros((half, hc), f32)
            for h in range(heads):
                mask, mask_k = head_mask(half, hc, h), head_mask(keys, hc, h)
                do_h = jnp.where(mask, do_q, 0).astype(b16)
                low = probs_v[h, at : at + half, 0:keys]
                p32 = low.astype(f32)
                t = p32 * dot(do_h, v[:keys], ((1,), (1,)))
                ds = (t - p32 * jnp.sum(t, -1, keepdims=True)).astype(b16)
                dq = jnp.where(mask, dot(ds, k[:keys]), dq)
                dk = dot(ds, query, ((0,), (0,)))
                dv = dot(low, do_h, ((0,), (0,)))
                dqkv_v[1, 0:keys] += jnp.where(mask_k, dk, 0.0)
                dqkv_v[2, 0:keys] += dv
            dqkv_v[0, at : at + half] = dq

        @pl.when(s + 1 < slots)
        def _():
            copy = pltpu.make_async_copy(probs.at[s + 1], probs_v, probs_sem)
            copy.start()
            copy.wait()

        dq, dk = dqkv_v[0] * 0.125, dqkv_v[1] * 0.125
        table = [tables[i].reshape(seq, 2 * HEAD_DIM) for i in range(3)]
        dj = [turn_pair(dq, table, -1.0), turn_pair(dk, table, -1.0), dqkv_v[2]]
        for i in range(3):
            low = dj[i].astype(b16)
            dj_v[:, s, :, i * hc : (i + 1) * hc] = low.reshape(n, rows, hc)
            bias_v[:, i * hc : (i + 1) * hc] += jnp.sum(low.astype(f32), 0, keepdims=True)
        return carry

    bias_v[...] = jnp.zeros_like(bias_v)

    probs_sem = moves.sems.at[next(moves.number)]
    lax.fori_loop(0, slots, attend, 0)

    wait_a1.wait()
    wait_qkv.wait()
    qkv_sums = scatters(gq_v, gq_relay, gq_box)
    weigh(qkv_sums, gq_v, dh_all, lambda: dj_v[...].reshape(tokens, qc), go_sums)
    for mask in (2, 1, 0):
        go_sums.start(mask)

    def normed_one(i, carry):
        part[pl.ds(2 * i, 2)] = (
            dot(
                dj_v[pl.ds(2 * i, 2)].reshape(2 * local_rows, qc),
                qkv_weight[...].reshape(width, qc),
                ((1,), (1,)),
            )
            .astype(b16)
            .reshape(2, local_rows, width)
        )
        return carry

    by_position(result_out, hidden_v[...] + y_sums.total())
    for m in (1, 2, 4, 6):
        pl.semaphore_signal(free, inc=1, device_id=(z, flip(c, m)), device_id_type=MESH)
    y_sums.sent()
    lax.fori_loop(0, n // 2, normed_one, 0)
    pl.semaphore_wait(free, 4)
    da1_sums = LayerScatter(
        wires, lambda i: part.at[i], lambda j: near.at[j], lambda j: far.at[j]
    )
    da1_sums.start()
    for m in (6, 4, 2):
        da1_sums.step(m)

    for p, part_sum in enumerate(gu_sums):
        ggu_v[z, :, p * quarter : (p + 1) * quarter] = part_sum.total().astype(b16)
    gu_x = [wires.put(ggu_v.at[z, flip(c, m)], gu_rows.at[c], 0, m) for m in range(1, n)]
    for copy in gu_x:
        copy.start()
    gu_rows[c] = ggu_v[z, c]

    for part_sum in qkv_sums:
        part_sum.relay()
    go_sums.relay()

    wait_xs.wait()
    by_slot(own_v, raw_v)
    n1, r1 = layer_stats(own_v[...].astype(f32))
    da1 = da1_sums.total()
    grad = norm_back(da1, n1, r1, norms[0:1])
    for s in range(slots):
        input_grad_out[:, s, :] += grad[s * rows : (s + 1) * rows]
    gains = [jnp.sum(da1 * n1, 0, keepdims=True), jnp.sum(da1, 0, keepdims=True), *gains]
    chips = n // 2
    lanes = 2 * HEAD_DIM
    lane_half = lax.broadcasted_iota(jnp.int32, (1, lanes), 1) // HEAD_DIM
    bias_part = bias_v[...]
    for j in range(zs):
        for chip in range(chips):
            k = j * chips + chip
            for r in range(4):
                small_v[j, chip, r : r + 1] = gains[r][:, k * lanes : (k + 1) * lanes]
            small_v[j, chip, 7:8] = jnp.zeros((1, lanes), f32)
    for i in range(3):
        for j in range(zs):
            at = i * hc + j * HEAD_DIM
            piece = bias_part[:, at : at + HEAD_DIM]
            both = jnp.concatenate([piece, piece], -1)
            for chip in range(chips):
                tile = (i * zs + j) * chips + chip
                pair, row = tile // 3, tile % 3
                small_v[pair // chips, pair % chips, 4 + row : 5 + row] = jnp.where(
                    (lane_half == c % 2) & (c // 2 == chip), both, 0.0
                )
    small_v_x = [
        wires.put(small_v.at[:, flip(c, m) // 2], small_x.at[m], 0, m) for m in range(1, n)
    ]
    for copy in small_v_x:
        copy.start()

    small_sum = small_v[:, c // 2]
    for m in range(1, n):
        small_v_x[m - 1].wait_recv()
        small_sum = small_sum + small_x[m]
    small_r[...] = small_sum
    small_z_x = [wires.put(small_r.at[flip(z, m)], small_z.at[m], m, 0) for m in range(1, zs)]
    for copy in small_z_x:
        copy.start()
    for copy in gu_x:
        copy.wait_recv()
    moves.store(gu_rows, gu_out)
    gq_x = []
    for p, part_sum in enumerate(qkv_sums):
        k = slice(p * quarter, (p + 1) * quarter)
        gq_v[z, :, k] = part_sum.total().astype(b16)
        copies = [
            wires.put(gq_v.at[z, flip(c, m), k], gq_rows.at[c, k], 0, m) for m in range(1, n)
        ]
        for copy in copies:
            copy.start()
        gq_x += copies
    gq_rows[c] = gq_v[z, c]
    small_sum = small_r[z]
    for m in range(1, zs):
        small_z_x[m - 1].wait_recv()
        small_sum = small_sum + small_z[m]
    small_out[...] = small_sum
    hidden_v[0:wrows] = go_sums.total()
    moves.store(hidden_v.at[0:wrows], grad_out_out)
    for group in (*gu_sums, go_sums, *qkv_sums, da1_sums):
        group.sent()
    for copy in (*gu_x, *small_v_x, *small_z_x):
        copy.wait_send()
    for copy in gq_x:
        copy.wait()
    moves.store(gq_rows, gq_out)
    moves.finish()


def backward(zs, n, norms, tables, *arrays):
    f32, b16 = jnp.float32, jnp.bfloat16
    a1_all, a2_all, dgu, w_gu, w_qkv, w_out, qkv, probs, ob, hidden, _, inputs, _ = arrays
    _, slots, rows, hc = ob.shape
    local, width = hidden.shape
    _, _, wrows, gc = w_gu.shape
    qc = 3 * hc
    seq = n * rows
    wide = (n, local, width)

    def buf(like):
        return pltpu.VMEM(like.shape, like.dtype)

    return pl.pallas_call(
        functools.partial(backward_kernel, zs, n),
        out_shape=[
            jax.ShapeDtypeStruct((hc // zs, width), f32),
            jax.ShapeDtypeStruct(inputs.shape, b16),
            jax.ShapeDtypeStruct(inputs.shape, f32),
            jax.ShapeDtypeStruct((n, wrows, qc), b16),
            jax.ShapeDtypeStruct((n, wrows, gc), b16),
            jax.ShapeDtypeStruct((8, 2 * HEAD_DIM), f32),
        ],
        in_specs=[VMEM] * 2 + [HBM] * 13,
        out_specs=[HBM, VMEM, VMEM, HBM, HBM, VMEM],
        scratch_shapes=[
            pltpu.VMEM(wide, b16),
            buf(dgu),
            pltpu.VMEM((zs, n, wrows, max(gc, 2 * qc)), b16),
            buf(w_out),
            buf(qkv),
            pltpu.VMEM(probs.shape[1:], b16),
            buf(ob),
            buf(hidden),
            pltpu.VMEM((local, width), b16),
            pltpu.VMEM(inputs.shape, b16),
            pltpu.VMEM((zs, n, wrows, gc), b16),
            pltpu.VMEM((n, wrows, gc), b16),
            pltpu.VMEM((3, n, wrows, gc), b16),
            pltpu.VMEM((n // 2, local, width), b16),
            pltpu.VMEM((n // 2 - 1, local, width), b16),
            pltpu.VMEM(wide, b16),
            pltpu.VMEM((zs, hc // zs, width), b16),
            pltpu.VMEM((hc // zs, width), b16),
            pltpu.VMEM((3, hc // zs, width), b16),
            pltpu.VMEM((3, seq, hc), f32),
            pltpu.VMEM((n, slots, rows, qc), b16),
            pltpu.VMEM((1, qc), f32),
            pltpu.VMEM((n, wrows, qc), b16),
            pltpu.VMEM((3, n, wrows, qc), b16),
            pltpu.VMEM((n, wrows, gc), b16),
            pltpu.VMEM((n, wrows, qc), b16),
            pltpu.VMEM((zs, n // 2, 8, 2 * HEAD_DIM), f32),
            pltpu.VMEM((n, zs, 8, 2 * HEAD_DIM), f32),
            pltpu.VMEM((zs, 8, 2 * HEAD_DIM), f32),
            pltpu.VMEM((zs, 8, 2 * HEAD_DIM), f32),
            pltpu.SemaphoreType.DMA((128,)),
            pltpu.SemaphoreType.DMA((128,)),
            pltpu.SemaphoreType.DMA((24,)),
            pltpu.SemaphoreType.REGULAR,
        ],
        compiler_params=pltpu.CompilerParams(
            collective_id=4, has_side_effects=True, vmem_limit_bytes=VMEM_LIMIT
        ),
        name="backward",
    )(norms, tables, *arrays)


def finish_kernel(
    zs,
    n,
    gq,
    gu,
    small,
    grad_out,
    grad_down,
    result,
    input_grad,
    qkv_out,
    gate_out,
    up_out,
    grad_out_out,
    grad_down_out,
    result_out,
    input_grad_out,
    bias_out,
    gain_one_out,
    shift_one_out,
    gain_two_out,
    shift_two_out,
    gq_v,
    gu_v,
    qkv_v,
    gate_v,
    up_v,
    grad_out_v,
    grad_down_v,
    result_v,
    input_grad_v,
    local,
):
    moves = Moves(local)
    width = grad_out.shape[1]
    wait_gu = moves.load(gu, gu_v)
    wait_gq = moves.load(gq, gq_v)
    passed = [
        (moves.load(src, held), held, dst)
        for src, held, dst in (
            (input_grad, input_grad_v, input_grad_out),
            (grad_down, grad_down_v, grad_down_out),
            (result, result_v, result_out),
            (grad_out, grad_out_v, grad_out_out),
        )
    ]
    odd = lax.axis_index("ctx") % 2
    for r, out in enumerate((gain_one_out, shift_one_out, gain_two_out, shift_two_out)):
        row = small[r : r + 1]
        out[...] = jnp.where(odd == 0, row[:, :HEAD_DIM], row[:, HEAD_DIM:])
    bias = jnp.concatenate([small[4 + r : 5 + r] for r in range(3)], -1)
    size = bias_out.shape[1]
    bias_out[...] = jnp.where(odd == 0, bias[:, :size], bias[:, size:])
    ffc = gu_v.shape[-1] // 2
    halves = halves_of(ffc // zs)
    for copy, held, dst in passed:
        copy.wait()
        moves.store(held, dst)
    wait_gu.wait()
    unpack_columns(gate_v, gu_v, [(2 * zs * at, size) for at, size in halves], n, zs)
    moves.store(gate_v, gate_out)
    unpack_columns(up_v, gu_v, [(zs * (2 * at + size), size) for at, size in halves], n, zs)
    moves.store(up_v, up_out)
    wait_gq.wait()
    hc = gq_v.shape[-1] // 3
    for i in range(3):
        unpack_columns(
            qkv_v.at[:, i * width : (i + 1) * width], gq_v, [(i * hc, HEAD_DIM)], n, zs
        )
    moves.store(qkv_v, qkv_out)
    moves.finish()


def finish(zs, n, gq, gu, small, grad_out, grad_down, result, input_grad):
    f32 = jnp.float32
    _, wrows, qc = gq.shape
    gc = gu.shape[-1]
    wide = [((wrows, n * qc), f32), ((wrows, n * gc // 2), f32), ((wrows, n * gc // 2), f32)]
    whole = [(v.shape, v.dtype) for v in (grad_out, grad_down, result, input_grad)]
    rows = [((1, 3 * HEAD_DIM), f32), *[((1, wrows), f32)] * 4]
    return pl.pallas_call(
        functools.partial(finish_kernel, zs, n),
        out_shape=[jax.ShapeDtypeStruct(*k) for k in (*wide, *whole, *rows)],
        in_specs=[HBM, HBM, VMEM, HBM, HBM, HBM, HBM],
        out_specs=[HBM] * 7 + [VMEM] * 5,
        scratch_shapes=[
            pltpu.VMEM(gq.shape, gq.dtype),
            pltpu.VMEM(gu.shape, gu.dtype),
            *[pltpu.VMEM(*k) for k in (*wide, *whole)],
            pltpu.SemaphoreType.DMA((16,)),
        ],
        compiler_params=pltpu.CompilerParams(vmem_limit_bytes=VMEM_LIMIT),
        name="finish",
    )(gq, gu, small, grad_out, grad_down, result, input_grad)


def tensor_shards(
    inputs,
    lengths,
    w_qkv,
    b_qkv,
    w_out,
    w_gate,
    w_up,
    w_down,
    gain_one,
    shift_one,
    gain_two,
    shift_two,
    cotangent,
):
    rows, slots, width = inputs.shape
    f32, b16 = jnp.float32, jnp.bfloat16
    zs, n = lax.axis_size("dp"), lax.axis_size("ctx")
    me = lax.axis_index("ctx")
    local = rows * slots
    seq = rows * n
    wrows = w_qkv.shape[0]
    ff_block = w_down.shape[0]
    hc = HEADS // n * HEAD_DIM
    ffc = ff_block * zs

    nb = b_qkv.shape[0]
    vectors = [v for gain in (gain_one, shift_one, gain_two, shift_two) for v in (gain, gain)]
    small, at = jnp.zeros(1024, jnp.bfloat16), 0
    for vector in (*vectors, b_qkv):
        size = vector.shape[0]
        small = small + jnp.pad(vector, (at, 1024 - at - size))
        at += size
    small = small.reshape(8, 128).astype(f32)

    angles = np.arange(seq)[:, None] * 10000.0 ** (-2.0 * np.arange(ROTARY // 2) / ROTARY)[None, :]
    cos_t, sin_t = np.cos(angles), np.sin(angles)
    zero, rest = np.zeros_like(sin_t), np.zeros((seq, HEAD_DIM - ROTARY))
    tables = np.stack(
        [
            np.concatenate(two, -1)
            for two in (
                2 * [cos_t, cos_t, rest + 1.0],
                2 * [-sin_t, zero, rest],
                2 * [zero, sin_t, rest],
            )
        ]
    ).astype(np.float32)

    tables = jnp.asarray(tables.reshape(3, n, rows, 2 * HEAD_DIM))
    w_qkv_c, w_out_c, w_gu_c, a1, qkv, probs, ob, hidden, a2, dgu, y, grad_down, norms = front(
        zs, n, lengths, tables, small, w_qkv, w_gate, w_up, w_out, w_down, inputs, cotangent
    )
    wide = (n, local, width)
    grad_out, result, input_grad, gq, gu, sums = backward(
        zs, n, norms, tables, a1.reshape(wide), a2.reshape(wide), dgu,
        w_gu_c, w_qkv_c, w_out_c, qkv, probs, ob, hidden, cotangent, inputs,
        y.reshape(wide),
    )
    grad_qkv, grad_gate, grad_up, grad_out, grad_down, result, input_grad, *rows = finish(
        zs, n, gq, gu, sums, grad_out, grad_down, result, input_grad
    )
    grad_bias, grad_gain_one, grad_shift_one, grad_gain_two, grad_shift_two = [
        row.reshape(row.shape[1]) for row in rows
    ]
    return (
        result,
        input_grad,
        grad_qkv,
        grad_bias,
        grad_out,
        grad_gate,
        grad_up,
        grad_down,
        grad_gain_one,
        grad_shift_one,
        grad_gain_two,
        grad_shift_two,
    )


def solution(mesh):
    zs, n = mesh.shape["dp"], mesh.shape["ctx"]
    shards = tensor_shards if (zs, n) == (4, 8) and HEADS == 32 else gathered_shards

    placed = (
        P("ctx", "dp", None),
        P("dp", None),
        P(("dp", "ctx"), None),
        P(("dp", "ctx")),
        P(("dp", "ctx"), None),
        P(("dp", "ctx"), None),
        P(("dp", "ctx"), None),
        P(("dp", "ctx"), None),
        P(("dp", "ctx")),
        P(("dp", "ctx")),
        P(("dp", "ctx")),
        P(("dp", "ctx")),
        P("ctx", "dp", None),
    )
    return jax.shard_map(
        shards,
        mesh=mesh,
        in_specs=placed,
        out_specs=(
            P("ctx", "dp", None),
            P("ctx", "dp", None),
            P(("dp", "ctx"), None),
            P(("dp", "ctx")),
            P(("dp", "ctx"), None),
            P(("dp", "ctx"), None),
            P(("dp", "ctx"), None),
            P(("dp", "ctx"), None),
            P(("dp", "ctx")),
            P(("dp", "ctx")),
            P(("dp", "ctx")),
            P(("dp", "ctx")),
        ),
        check_vma=False,
    )
```

```python
import functools
import itertools
import math

import jax
import jax.numpy as jnp
import numpy as np
from jax import lax
from jax.experimental import pallas as pl
from jax.experimental.pallas import tpu as pltpu
from jax.sharding import PartitionSpec as P

HEADS = 32
HEAD_DIM = 64
ROTARY = 16


epsilon = 1e-05
masked_value = -1e30


def layer_stats(values):
    row_mean = jnp.mean(values, -1, keepdims=True)
    centred = values - row_mean
    inverse = lax.rsqrt(jnp.mean(centred * centred, -1, keepdims=True) + epsilon)
    return (centred * inverse, inverse)


def norm_back(grad_normed, scaled, inverse, gain_vec):
    grad_hat = grad_normed * gain_vec
    return inverse * (
        grad_hat
        - jnp.mean(grad_hat, -1, keepdims=True)
        - scaled * jnp.mean(grad_hat * scaled, -1, keepdims=True)
    )


def rotary_tables(positions):
    counter = jnp.arange(ROTARY // 2, dtype=jnp.float32)
    frequency = 10000.0 ** (-2.0 * counter / ROTARY)
    angles = positions.astype(jnp.float32)[:, None] * frequency[None, :]
    return (jnp.cos(angles)[:, None, None, :], jnp.sin(angles)[:, None, None, :])


def rotate(values, cos_table, sin_table):
    half_dims = ROTARY // 2
    first_half = values[..., :half_dims]
    second_half = values[..., half_dims:ROTARY]
    return jnp.concatenate(
        [
            first_half * cos_table - second_half * sin_table,
            second_half * cos_table + first_half * sin_table,
            values[..., ROTARY:],
        ],
        -1,
    )


def over_blocks(step_fn, running, gathered):
    total_rows = gathered.shape[0]
    tile_rows = math.gcd(total_rows, 512)

    def visit_block(number, current):
        block_start = number * tile_rows
        block_part = lax.dynamic_slice_in_dim(gathered, block_start, tile_rows, 0)
        return step_fn(current, block_part, block_start)

    return lax.fori_loop(0, total_rows // tile_rows, visit_block, running)


def gathered_shards(
    inputs,
    lengths,
    w_qkv,
    b_qkv,
    w_out,
    w_gate,
    w_up,
    w_down,
    gain_one,
    shift_one,
    gain_two,
    shift_two,
    cotangent,
):
    local_rows, slot_count, width = inputs.shape
    positions = lax.axis_index("ctx") * local_rows + jnp.arange(local_rows, dtype=jnp.int32)
    live_rows = positions[:, None] < lengths[0][None, :]
    live_heads = jnp.transpose(live_rows)[:, None, :, None]
    cos_table, sin_table = rotary_tables(positions)

    def allowed_mask(offset, count):
        key_pos = offset + jnp.arange(count, dtype=jnp.int32)
        causal = key_pos[None, :] <= positions[:, None]
        return causal[None, None, :, :] & live_heads

    def split_heads(block_part):
        count = block_part.shape[0]
        key_part = block_part[:, :, 0].reshape(count, slot_count, HEADS, HEAD_DIM)
        value_part = block_part[:, :, 1].reshape(count, slot_count, HEADS, HEAD_DIM)
        return (key_part, value_part)

    attn_full = (
        lax.all_gather(w_qkv, ("dp", "ctx"), axis=0, tiled=True),
        lax.all_gather(b_qkv, ("dp", "ctx"), axis=0, tiled=True),
        lax.all_gather(w_out, ("dp", "ctx"), axis=0, tiled=True),
        lax.all_gather(gain_one, ("dp", "ctx"), axis=0, tiled=True),
        lax.all_gather(shift_one, ("dp", "ctx"), axis=0, tiled=True),
    )
    qkv_full, bias_full, out_full, gain_one_full, shift_one_full = attn_full
    source = inputs.astype(jnp.float32)
    scaled_one, inverse_one = layer_stats(source)
    normed_one = (
        scaled_one * gain_one_full.astype(jnp.float32) + shift_one_full.astype(jnp.float32)
    ).astype(jnp.bfloat16)
    joined = jnp.einsum(
        "rsd,de->rse", normed_one, qkv_full, preferred_element_type=jnp.float32
    ) + bias_full.astype(jnp.float32)
    query_pre = joined[..., :width].reshape(local_rows, slot_count, HEADS, HEAD_DIM)
    key_pre = joined[..., width : 2 * width].reshape(local_rows, slot_count, HEADS, HEAD_DIM)
    queries = rotate(query_pre, cos_table, sin_table).astype(jnp.bfloat16)
    keys_rot = rotate(key_pre, cos_table, sin_table).reshape(local_rows, slot_count, width)
    key_value = jnp.stack([keys_rot, joined[..., 2 * width :]], 2).astype(jnp.bfloat16)
    block_part = lax.all_gather(key_value, "ctx", axis=0, tiled=True)
    run_peak = jnp.full((slot_count, HEADS, local_rows), masked_value, jnp.float32)
    key_part, value_part = split_heads(block_part)
    scores = (
        jnp.einsum("qshd,kshd->shqk", queries, key_part, preferred_element_type=jnp.float32) * 0.125
    )
    allowed = allowed_mask(jnp.int32(0), block_part.shape[0])
    masked = jnp.where(allowed, scores, masked_value)
    new_peak = jnp.maximum(run_peak, jnp.max(masked, -1))
    weights = jnp.where(allowed, jnp.exp(masked - new_peak[..., None]), 0.0)
    new_sum = jnp.sum(weights, -1)
    new_acc = jnp.einsum(
        "shqk,kshd->shqd",
        weights.astype(jnp.bfloat16),
        value_part,
        preferred_element_type=jnp.float32,
    )
    final_sum = jnp.maximum(new_sum, 1.0)
    log_sum = new_peak + jnp.log(final_sum)
    attended = jnp.transpose(new_acc / final_sum[..., None], (2, 0, 1, 3))
    attended_low = attended.reshape(local_rows, slot_count, width).astype(jnp.bfloat16)
    hidden_in = source + jnp.einsum(
        "rsd,de->rse", attended_low, out_full, preferred_element_type=jnp.float32
    )
    mlp_full = (
        lax.all_gather(w_gate, ("dp", "ctx"), axis=0, tiled=True),
        lax.all_gather(w_up, ("dp", "ctx"), axis=0, tiled=True),
        lax.all_gather(w_down, ("dp", "ctx"), axis=0, tiled=True),
        lax.all_gather(gain_two, ("dp", "ctx"), axis=0, tiled=True),
        lax.all_gather(shift_two, ("dp", "ctx"), axis=0, tiled=True),
    )
    gate_full, up_full, down_full, gain_two_full, shift_two_full = mlp_full
    scaled_two, inverse_two = layer_stats(hidden_in)
    normed_two = (
        scaled_two * gain_two_full.astype(jnp.float32) + shift_two_full.astype(jnp.float32)
    ).astype(jnp.bfloat16)
    gate = jnp.einsum("rsd,df->rsf", normed_two, gate_full, preferred_element_type=jnp.float32)
    upward = jnp.einsum("rsd,df->rsf", normed_two, up_full, preferred_element_type=jnp.float32)
    sigmoid = jax.nn.sigmoid(gate)
    product = (gate * sigmoid * upward).astype(jnp.bfloat16)
    result = hidden_in + jnp.einsum(
        "rsf,fd->rsd", product, down_full, preferred_element_type=jnp.float32
    )
    gate_back, up_back, down_back, gain_two_back = (
        lax.all_gather(w_gate, ("dp", "ctx"), axis=0, tiled=True),
        lax.all_gather(w_up, ("dp", "ctx"), axis=0, tiled=True),
        lax.all_gather(w_down, ("dp", "ctx"), axis=0, tiled=True),
        lax.all_gather(gain_two, ("dp", "ctx"), axis=0, tiled=True),
    )
    grad_down = jnp.einsum("rsf,rsd->fd", product, cotangent, preferred_element_type=jnp.float32)
    grad_product = jnp.einsum(
        "rsd,fd->rsf", cotangent, down_back, preferred_element_type=jnp.float32
    )
    grad_gate_act = (grad_product * upward * sigmoid * (1.0 + gate * (1.0 - sigmoid))).astype(
        jnp.bfloat16
    )
    grad_up_act = (grad_product * gate * sigmoid).astype(jnp.bfloat16)
    grad_gate = jnp.einsum(
        "rsd,rsf->df", normed_two, grad_gate_act, preferred_element_type=jnp.float32
    )
    grad_up = jnp.einsum("rsd,rsf->df", normed_two, grad_up_act, preferred_element_type=jnp.float32)
    grad_normed_two = jnp.einsum(
        "rsf,df->rsd", grad_gate_act, gate_back, preferred_element_type=jnp.float32
    ) + jnp.einsum("rsf,df->rsd", grad_up_act, up_back, preferred_element_type=jnp.float32)
    grad_gain_two = jnp.sum(grad_normed_two * scaled_two, (0, 1))
    grad_shift_two = jnp.sum(grad_normed_two, (0, 1))
    grad_hidden = cotangent.astype(jnp.float32) + norm_back(
        grad_normed_two, scaled_two, inverse_two, gain_two_back.astype(jnp.float32)
    )
    mlp_sums = (
        lax.psum_scatter(grad_gate, ("dp", "ctx"), scatter_dimension=0, tiled=True),
        lax.psum_scatter(grad_up, ("dp", "ctx"), scatter_dimension=0, tiled=True),
        lax.psum_scatter(grad_down, ("dp", "ctx"), scatter_dimension=0, tiled=True),
        lax.psum_scatter(grad_gain_two, ("dp", "ctx"), scatter_dimension=0, tiled=True),
        lax.psum_scatter(grad_shift_two, ("dp", "ctx"), scatter_dimension=0, tiled=True),
    )
    qkv_back, out_back, gain_one_back = (
        lax.all_gather(w_qkv, ("dp", "ctx"), axis=0, tiled=True),
        lax.all_gather(w_out, ("dp", "ctx"), axis=0, tiled=True),
        lax.all_gather(gain_one, ("dp", "ctx"), axis=0, tiled=True),
    )
    hidden_low = grad_hidden.astype(jnp.bfloat16)
    grad_out = jnp.einsum(
        "rsd,rse->de", attended_low, hidden_low, preferred_element_type=jnp.float32
    )
    grad_attended = jnp.einsum(
        "rse,de->rsd", hidden_low, out_back, preferred_element_type=jnp.float32
    )
    grad_heads = grad_attended.reshape(local_rows, slot_count, HEADS, HEAD_DIM).astype(jnp.bfloat16)
    delta = jnp.transpose(jnp.sum(grad_heads.astype(jnp.float32) * attended, -1), (1, 2, 0))
    key_value_all = lax.all_gather(key_value, "ctx", axis=0, tiled=True)

    def grad_parts(block_part, offset):
        key_part, value_part = split_heads(block_part)
        scores = (
            jnp.einsum("qshd,kshd->shqk", queries, key_part, preferred_element_type=jnp.float32)
            * 0.125
        )
        allowed = allowed_mask(offset, block_part.shape[0])
        probs = jnp.where(allowed, jnp.exp(scores - log_sum[..., None]), 0.0)
        grad_prob = jnp.einsum(
            "qshd,kshd->shqk", grad_heads, value_part, preferred_element_type=jnp.float32
        )
        grad_score = (probs * (grad_prob - delta[..., None])).astype(jnp.bfloat16)
        return (key_part, probs, grad_score)

    def query_step(running, block_part, offset):
        key_part, probs, grad_score = grad_parts(block_part, offset)
        return running + jnp.einsum(
            "shqk,kshd->shqd", grad_score, key_part, preferred_element_type=jnp.float32
        )

    grad_query = (
        over_blocks(
            query_step,
            jnp.zeros((slot_count, HEADS, local_rows, HEAD_DIM), jnp.float32),
            key_value_all,
        )
        * 0.125
    )
    count = local_rows * lax.axis_size("ctx")
    tile_rows = math.gcd(count, 512)

    def one_block(number):
        block_start = number * tile_rows
        block_part = lax.dynamic_slice_in_dim(key_value_all, block_start, tile_rows, 0)
        key_part, probs, grad_score = grad_parts(block_part, block_start)
        grad_key = (
            jnp.einsum("shqk,qshd->kshd", grad_score, queries, preferred_element_type=jnp.float32)
            * 0.125
        )
        grad_value = jnp.einsum(
            "shqk,qshd->kshd",
            probs.astype(jnp.bfloat16),
            grad_heads,
            preferred_element_type=jnp.float32,
        )
        return jnp.stack(
            [
                grad_key.reshape(tile_rows, slot_count, width),
                grad_value.reshape(tile_rows, slot_count, width),
            ],
            2,
        )

    blocks = lax.map(one_block, jnp.arange(count // tile_rows, dtype=jnp.int32))
    grad_key_value = lax.psum_scatter(
        blocks.reshape(count, slot_count, 2, width).astype(jnp.bfloat16),
        "ctx",
        scatter_dimension=0,
        tiled=True,
    ).astype(jnp.float32)
    grad_query_pre = rotate(jnp.transpose(grad_query, (2, 0, 1, 3)), cos_table, -sin_table)
    grad_key_pre = rotate(
        grad_key_value[:, :, 0].reshape(local_rows, slot_count, HEADS, HEAD_DIM),
        cos_table,
        -sin_table,
    )
    grad_joined = jnp.concatenate(
        [
            grad_query_pre.reshape(local_rows, slot_count, width),
            grad_key_pre.reshape(local_rows, slot_count, width),
            grad_key_value[:, :, 1],
        ],
        -1,
    ).astype(jnp.bfloat16)
    grad_qkv = jnp.einsum(
        "rsd,rse->de", normed_one, grad_joined, preferred_element_type=jnp.float32
    )
    grad_bias = jnp.sum(grad_joined.astype(jnp.float32), (0, 1))
    grad_normed_one = jnp.einsum(
        "rse,de->rsd", grad_joined, qkv_back, preferred_element_type=jnp.float32
    )
    grad_gain_one = jnp.sum(grad_normed_one * scaled_one, (0, 1))
    grad_shift_one = jnp.sum(grad_normed_one, (0, 1))
    input_grad = grad_hidden + norm_back(
        grad_normed_one, scaled_one, inverse_one, gain_one_back.astype(jnp.float32)
    )
    attn_sums = (
        lax.psum_scatter(grad_qkv, ("dp", "ctx"), scatter_dimension=0, tiled=True),
        lax.psum_scatter(grad_bias, ("dp", "ctx"), scatter_dimension=0, tiled=True),
        lax.psum_scatter(grad_out, ("dp", "ctx"), scatter_dimension=0, tiled=True),
        lax.psum_scatter(grad_gain_one, ("dp", "ctx"), scatter_dimension=0, tiled=True),
        lax.psum_scatter(grad_shift_one, ("dp", "ctx"), scatter_dimension=0, tiled=True),
    )
    return (
        result.astype(jnp.bfloat16),
        input_grad,
        attn_sums[0],
        attn_sums[1],
        attn_sums[2],
        mlp_sums[0],
        mlp_sums[1],
        mlp_sums[2],
        attn_sums[3],
        attn_sums[4],
        mlp_sums[3],
        mlp_sums[4],
    )


MESH = pl.DeviceIdType.MESH
HBM = pl.BlockSpec(memory_space=pltpu.HBM)
VMEM = pl.BlockSpec(memory_space=pltpu.VMEM)
VMEM_LIMIT = 60 << 20


def flip(index, mask):
    for bit in (1, 2, 4):
        if mask & bit:
            index = index + bit - 2 * bit * ((index // bit) % 2)
    return index


class Wires:
    def __init__(self, send, recv):
        self.send, self.recv = send, recv
        self.z, self.c = lax.axis_index("dp"), lax.axis_index("ctx")
        self.inner = (self.z == 1) | (self.z == 2)
        self.outer = (self.z == 0) | (self.z == 3)
        self.number = itertools.count()

    def put(self, src, dst, z_mask, c_mask):
        return self.put_to(src, dst, flip(self.z, z_mask), flip(self.c, c_mask))

    def put_to(self, src, dst, z, c):
        i = next(self.number)
        return pltpu.make_async_remote_copy(
            src_ref=src,
            dst_ref=dst,
            send_sem=self.send.at[i],
            recv_sem=self.recv.at[i],
            device_id=(z, c),
            device_id_type=MESH,
        )

    def greet(self, zs, n):
        self.call(zs, n)
        self.met(zs, n)

    def met(self, zs, n):
        pl.semaphore_wait(pltpu.get_barrier_semaphore(), zs + n - 2)

    def call(self, zs, n):
        barrier = pltpu.get_barrier_semaphore()
        for m in range(1, zs):
            pl.semaphore_signal(
                barrier, inc=1, device_id=(flip(self.z, m), self.c), device_id_type=MESH
            )
        for m in range(1, n):
            pl.semaphore_signal(
                barrier, inc=1, device_id=(self.z, flip(self.c, m)), device_id_type=MESH
            )


class DepthGather:
    def __init__(self, wires, part):
        z = wires.z
        self.wires = wires
        self.near = wires.put(part(z), part(z), 1, 0)
        self.skip = wires.put(part(z), part(z), 2, 0)
        self.mid = wires.put(part(z), part(z), 3, 0)
        far = flip(z, 2)
        self.on = wires.put(part(far), part(far), 1, 0)

    @staticmethod
    def start(parts):
        for part in parts:
            part.skip.start()
        for part in parts:
            pl.when(part.wires.inner)(part.mid.start)
        for part in parts:
            part.near.start()

    def forward(self):
        @pl.when(self.wires.inner)
        def _():
            self.skip.wait_recv()
            self.on.start()

    def finish(self):
        self.near.wait_recv()
        self.near.wait_send()
        self.skip.wait_send()

        @pl.when(self.wires.inner)
        def _():
            self.mid.wait_recv()
            self.mid.wait_send()
            self.on.wait_send()

        @pl.when(self.wires.outer)
        def _():
            self.skip.wait_recv()
            self.on.wait_recv()


class LayerGather:
    def __init__(self, wires, block, source=None):
        c = wires.c
        mine = block(c) if source is None else source
        self.direct = {m: wires.put(mine, block(c), 0, m) for m in (2, 4, 6, 1)}
        self.on = {m: wires.put(block(flip(c, m)), block(flip(c, m)), 0, 1) for m in (2, 4, 6)}

    def start(self):
        for m in (2, 4, 6, 1):
            self.direct[m].start()

    def forward(self, m):
        self.direct[m].wait_recv()
        self.on[m].start()

    def arrived(self, m):
        (self.direct[1] if m == 1 else self.on[m - 1]).wait_recv()

    def sent(self):
        for copy in (*self.direct.values(), *self.on.values()):
            copy.wait_send()


def pack_columns(dst, refs, n, zs):
    for i in range(n):
        pieces = []
        for ref, block, at, size in refs:
            starts = [block * (j * n + i) + at for j in range(zs)]
            pieces += [ref[:, start : start + size] for start in starts]
        dst[i] = jnp.concatenate(pieces, -1)


class LayerScatter:
    def __init__(self, wires, part, near, far):
        c = wires.c
        self.c, self.part, self.near, self.far = c, part, near, far
        self.pair = {
            m: wires.put(part(flip(c, m + 1)), near(m // 2), 0, 1) for m in (6, 4, 2, 0)
        }
        self.chips = {m: wires.put(part(flip(c, m)), far(m // 2 - 1), 0, m) for m in (6, 4, 2)}

    def start(self):
        for copy in self.pair.values():
            copy.start()

    def step(self, m):
        self.pair[m].wait_recv()
        to = self.part(flip(self.c, m))
        to[...] = (
            to[...].astype(jnp.float32) + self.near(m // 2)[...].astype(jnp.float32)
        ).astype(to.dtype)
        self.chips[m].start()

    def total(self):
        self.pair[0].wait_recv()
        result = self.part(self.c)[...].astype(jnp.float32)
        result = result + self.near(0)[...].astype(jnp.float32)
        for m in (2, 4, 6):
            self.chips[m].wait_recv()
            result = result + self.far(m // 2 - 1)[...].astype(jnp.float32)
        return result

    def sent(self):
        for copy in (*self.pair.values(), *self.chips.values()):
            copy.wait_send()


def dot(a, b, dims=((1,), (0,))):
    return lax.dot_general(a, b, (dims, ((), ())), preferred_element_type=jnp.float32)


def turn_pair(values, table, sign):
    half = ROTARY // 2
    columns = values.shape[-1]
    table = [jnp.concatenate([t] * (columns // t.shape[-1]), -1) for t in table]
    return (
        values * table[0]
        + sign * (pltpu.roll(values, columns - half, 1) * table[1])
        + sign * (pltpu.roll(values, half, 1) * table[2])
    )


def head_mask(rows, columns, head):
    return lax.broadcasted_iota(jnp.int32, (rows, columns), 1) // HEAD_DIM == head


class DepthScatter:
    def __init__(self, wires, part, relay, boxes):
        z = wires.z
        self.wires, self.part, self.relay_box, self.boxes = wires, part, relay, boxes
        self.far = wires.put(part(flip(z, 3)), relay, 1, 0)
        self.skip = wires.put(part(flip(z, 2)), boxes[1], 2, 0)
        self.near = wires.put(part(flip(z, 1)), boxes[0], 1, 0)
        self.mid = wires.put(part(flip(z, 3)), boxes[2], 3, 0)

    def start(self, mask):
        outer, inner = pl.when(self.wires.outer), pl.when(self.wires.inner)
        if mask == 3:
            outer(self.far.start)
            inner(self.mid.start)
        elif mask == 2:
            outer(self.skip.start)
        elif mask == 1:
            self.near.start()
        else:

            @outer
            def _():
                self.boxes[2][...] = jnp.zeros_like(self.boxes[2])

    def relay(self):
        @pl.when(self.wires.inner)
        def _():
            self.far.wait_recv()
            to = self.part(flip(self.wires.z, 2))
            to[...] = (
                to[...].astype(jnp.float32) + self.relay_box[...].astype(jnp.float32)
            ).astype(to.dtype)
            self.skip.start()

    def total(self):
        self.near.wait_recv()
        self.skip.wait_recv()
        pl.when(self.wires.inner)(self.mid.wait_recv)
        result = self.part(self.wires.z)[...].astype(jnp.float32)
        for box in self.boxes:
            result = result + box[...].astype(jnp.float32)
        return result

    def sent(self):
        self.near.wait_send()
        self.skip.wait_send()
        pl.when(self.wires.outer)(self.far.wait_send)
        pl.when(self.wires.inner)(self.mid.wait_send)


class Moves:
    def __init__(self, sems):
        self.sems, self.number, self.stores = sems, itertools.count(), []

    def load(self, src, dst):
        copy = pltpu.make_async_copy(src, dst, self.sems.at[next(self.number)])
        copy.start()
        return copy

    def store(self, src, dst):
        self.stores.append(self.load(src, dst))

    def finish(self):
        for copy in self.stores:
            copy.wait()


def pieces_of(total, number, unit):
    units = total // unit
    cuts = [units * i // number * unit for i in range(number + 1)]
    return [(a, b - a) for a, b in zip(cuts[:-1], cuts[1:])]


class ChainGather:
    def __init__(self, wires, part):
        self.z = z = wires.z
        self.right = [
            wires.put_to(part((z - s + 4) % 4), part((z - s + 4) % 4), (z + 1) % 4, wires.c)
            for s in range(3)
        ]
        self.left = [
            wires.put_to(part((z + s) % 4), part((z + s) % 4), (z + 3) % 4, wires.c)
            for s in range(3)
        ]

    def start(self):
        pl.when(self.z <= 2)(self.right[0].start)
        pl.when(self.z >= 1)(self.left[0].start)

    def hop(self, s):
        pl.when(self.z >= s)(self.right[s - 1].wait_recv)
        pl.when((self.z >= s) & (self.z <= 2))(self.right[s].start)
        pl.when(self.z <= 3 - s)(self.left[s - 1].wait_recv)
        pl.when((self.z <= 3 - s) & (self.z >= 1))(self.left[s].start)

    def finish(self):
        pl.when(self.z >= 3)(self.right[2].wait_recv)
        pl.when(self.z <= 0)(self.left[2].wait_recv)
        for s in range(3):
            pl.when((self.z >= s) & (self.z <= 2))(self.right[s].wait_send)
            pl.when((self.z <= 3 - s) & (self.z >= 1))(self.left[s].wait_send)


class ChainScatter:
    def __init__(self, wires, part, right, left):
        self.z = z = wires.z
        self.part, self.right_box, self.left_box = part, right, left
        self.right = {
            j: wires.put_to(part(j), right(j), (z + 1) % 4, wires.c) for j in (3, 2, 1)
        }
        self.left = {j: wires.put_to(part(j), left(j), (z + 3) % 4, wires.c) for j in (0, 1, 2)}

    def clear(self):
        @pl.when(self.z == 0)
        def _():
            self.right_box(1)[...] = jnp.zeros_like(self.right_box(1))

        @pl.when(self.z == 3)
        def _():
            self.left_box(2)[...] = jnp.zeros_like(self.left_box(2))

    def start(self, distance):
        pl.when(self.z == 0)(self.right[distance].start)
        pl.when(self.z == 3)(self.left[3 - distance].start)

    def pass_on(self, copy, j, box):
        copy.wait_recv()
        to = self.part(j)
        to[...] = (to[...].astype(jnp.float32) + box(j)[...].astype(jnp.float32)).astype(to.dtype)
        copy.start()

    def hop(self, s, distance):
        @pl.when(self.z == s)
        def _():
            self.pass_on(self.right[distance], distance, self.right_box)

        @pl.when(self.z == 3 - s)
        def _():
            self.pass_on(self.left[3 - distance], 3 - distance, self.left_box)

    def total(self):
        for j in (1, 2, 3):
            pl.when(self.z == j)(self.right[j].wait_recv)
        for j in (0, 1, 2):
            pl.when(self.z == j)(self.left[j].wait_recv)
        z = self.z
        return (
            self.part(z)[...].astype(jnp.float32)
            + self.right_box(jnp.maximum(z, 1))[...].astype(jnp.float32)
            + self.left_box(jnp.minimum(z, 2))[...].astype(jnp.float32)
        )

    def sent(self):
        for j in (1, 2, 3):
            pl.when(self.z < j)(self.right[j].wait_send)
        for j in (0, 1, 2):
            pl.when(self.z > j)(self.left[j].wait_send)


def halves_of(block):
    first = (block // 16 + 1) // 2 * 16
    return [(0, first), (first, block - first)]


def by_slot(dst, src):
    rows, slots, _ = src.shape
    for s in range(slots):
        dst[s * rows : (s + 1) * rows] = src[:, s, :]


def by_position(dst, values):
    rows, slots, _ = dst.shape
    for s in range(slots):
        dst[:, s, :] = values[s * rows : (s + 1) * rows].astype(dst.dtype)


def front_kernel(
    zs,
    n,
    slots,
    lengths,
    tables,
    small,
    w_qkv,
    w_gate,
    w_up,
    w_out,
    w_down,
    inputs,
    cotangent,
    w_qkv_out,
    w_out_out,
    w_gu_out,
    a1_out,
    qkv_out,
    probs_out,
    ob_out,
    hidden_out,
    a2_out,
    dgu_out,
    y_out,
    grad_down_out,
    norms,
    qkv_send,
    gu_send,
    small_v,
    bias_v,
    w_qkv_v,
    w_out_v,
    w_gu_v,
    w_down_v,
    wide_x,
    wide_a,
    dy_v,
    qkv_v,
    probs_v,
    ob_v,
    near,
    far,
    hidden_v,
    gu_v,
    zz_v,
    dz_v,
    gd_v,
    right_v,
    left_v,
    raw_v,
    send,
    recv,
    local,
):
    f32, b16 = jnp.float32, jnp.bfloat16
    wires = Wires(send, recv)
    moves = Moves(local)
    z, c = wires.z, wires.c
    rows, _, width = inputs.shape
    local_rows = rows * slots
    tokens, seq = n * local_rows, n * rows
    pair = 2 * local_rows
    hc = qkv_v.shape[-1]
    heads = hc // HEAD_DIM
    block = w_down_v.shape[1]
    ffc = zs * block
    halves = halves_of(block)
    spans = [(2 * zs * at, zs * size) for at, size in halves]
    lanes = 2 * HEAD_DIM
    lane_half = lax.broadcasted_iota(jnp.int32, (1, lanes), 1) // HEAD_DIM

    def block_of(ref, i):
        return ref.at[pl.ds(pl.multiple_of(i * local_rows, local_rows), local_rows)]

    def pair_at(i):
        return pl.ds(pl.multiple_of(i * pair, pair), pair)

    wires.call(zs, n)
    wait_out = moves.load(w_out, w_out_v.at[z])
    wait_small = moves.load(small, small_v.at[z, c])
    waits = [moves.load(inputs, raw_v.at[0]), moves.load(cotangent, raw_v.at[1])]
    wait_down = moves.load(w_down, w_down_v.at[z])
    wait_out.wait()
    wires.met(zs, n)
    out_z = DepthGather(wires, lambda i: w_out_v.at[i])
    DepthGather.start([out_z])
    pack_columns(
        qkv_send,
        [(w_qkv.at[:, i * width : (i + 1) * width], HEAD_DIM, 0, HEAD_DIM) for i in range(3)],
        n,
        zs,
    )
    wait_own_qkv = moves.load(qkv_send.at[c], w_qkv_v.at[z, c])
    qkv_x = [wires.put(qkv_send.at[flip(c, m)], w_qkv_v.at[z, c], 0, m) for m in range(1, n)]
    for copy in qkv_x:
        copy.start()
    wait_small.wait()
    small_z = [wires.put(small_v.at[z, c], small_v.at[z, c], m, 0) for m in range(1, zs)]
    for copy in small_z:
        copy.start()
    waits[0].wait()
    by_slot(block_of(wide_x, c), raw_v.at[0])
    xs_g = LayerGather(wires, lambda i: block_of(wide_x, i))
    xs_g.start()
    pack_columns(
        gu_send, [(w, block, at, size) for at, size in halves for w in (w_gate, w_up)], n, zs
    )
    wait_own_gu = moves.load(gu_send.at[c], w_gu_v.at[z, c])
    for copy in small_z:
        copy.wait_recv()
    small_x = [wires.put(small_v.at[:, c], small_v.at[:, c], 0, m) for m in range(1, n)]
    for copy in small_x:
        copy.start()
    wait_own_qkv.wait()
    for copy in qkv_x:
        copy.wait_recv()
    number = 4
    qkv_z = [
        DepthGather(wires, lambda i, a=a, s=s: w_qkv_v.at[i, a : a + s])
        for a, s in pieces_of(n, number, 1)
    ]
    DepthGather.start(qkv_z)
    gu_x = [wires.put(gu_send.at[flip(c, m)], w_gu_v.at[z, c], 0, m) for m in range(1, n)]
    for copy in gu_x:
        copy.start()
    out_z.forward()
    for m in (2, 4, 6):
        xs_g.forward(m)

    for copy in small_x:
        copy.wait()
    for r in range(4):
        norms[r : r + 1] = jnp.concatenate(
            [
                jnp.where(
                    lane_half == 0,
                    small_v[d // n, d % n, r : r + 1],
                    small_v[d // n, d % n + 1, r : r + 1],
                )
                for d in range(0, zs * n, 2)
            ],
            -1,
        )
    norms[4:8] = jnp.zeros_like(norms[4:8])
    per_owner = 3 * zs * n // (zs * n)
    for i in range(3):
        for j in range(0, zs, 2):
            both = []
            for h in range(2):
                group = i * zs * n + (j + h) * n + c
                owner, k = group // per_owner, group % per_owner
                tile = small_v[owner // n, owner % n]
                row = jnp.where(k == 2, tile[5:6], tile[4:5])
                both.append(jnp.where(k % 2 == h, row, pltpu.roll(row, HEAD_DIM, 1)))
            at = (i * zs + j) * HEAD_DIM
            bias_v[:, at : at + lanes] = jnp.where(lane_half == 0, both[0], both[1])

    for m in (1, 3, 5, 7):
        xs_g.arrived(m)
    hidden_v[...] = block_of(wide_x, c)[...].astype(f32)

    def norm_one(i, carry):
        x = wide_x[pair_at(i)].astype(f32)
        wide_a[pair_at(i)] = (layer_stats(x)[0] * norms[0:1] + norms[1:2]).astype(b16)
        return carry

    lax.fori_loop(0, n // 2, norm_one, 0)
    wait_a1 = moves.load(wide_a, a1_out)
    wait_own_gu.wait()
    for copy in gu_x:
        copy.wait_recv()
    gu_z = [
        [
            DepthGather(
                wires, lambda i, a=a, s=s, k=slice(at, at + 2 * size): w_gu_v.at[i, a : a + s, :, k]
            )
            for a, s in pieces_of(n, number, 1)
        ]
        for at, size in spans
    ]
    for part in qkv_z:
        part.forward()
    for part in gu_z:
        DepthGather.start(part)
    tile = width // number
    columns = [slice(p * tile, (p + 1) * tile) for p in range(number)]
    down_z = [ChainGather(wires, lambda i, k=k: w_down_v.at[i, :, k]) for k in columns]
    wait_down.wait()
    for chain in down_z:
        chain.start()
    waits[1].wait()
    by_slot(dy_v.at[c], raw_v.at[1])
    dy_g = LayerGather(wires, lambda i: dy_v.at[i])
    dy_g.start()
    for part in (out_z, *qkv_z):
        part.finish()
    moves.store(w_qkv_v, w_qkv_out)
    moves.store(w_out_v, w_out_out)

    def project(i, carry):
        joined = dot(wide_a[pair_at(i)], w_qkv_v[...].reshape(width, 3 * hc)) + bias_v[...]
        for j in range(2):
            table = [tables[k, 2 * i + j] for k in range(3)]
            for s in range(slots):
                at = (j * slots + s) * rows
                piece = joined[at : at + rows]
                qkv_v[0, s, 2 * i + j] = turn_pair(piece[:, :hc], table, 1.0).astype(b16)
                qkv_v[1, s, 2 * i + j] = turn_pair(piece[:, hc : 2 * hc], table, 1.0).astype(b16)
                qkv_v[2, s, 2 * i + j] = piece[:, 2 * hc :].astype(b16)
        return carry

    lax.fori_loop(0, n // 2, project, 0)
    moves.store(qkv_v, qkv_out)
    for m in (2, 4, 6):
        dy_g.forward(m)

    half = seq // 2
    probs_sem = moves.sems.at[next(moves.number)]

    def attend(s, carry):
        q, k, v = [qkv_v[i, s].reshape(seq, hc) for i in range(3)]
        length = lengths[0, s]
        kept = pltpu.make_async_copy(probs_v, probs_out.at[s], probs_sem)
        for part_q in range(2):
            keys = (part_q + 1) * half
            at = part_q * half
            query = q[at : at + half]
            row = lax.broadcasted_iota(jnp.int32, (half, keys), 0) + at
            key = lax.broadcasted_iota(jnp.int32, (half, keys), 1)
            allowed = (key <= row) & (row < length)
            out = jnp.zeros((half, hc), f32)
            for h in range(heads):
                mask = head_mask(half, hc, h)
                scores = dot(jnp.where(mask, query, 0).astype(b16), k[:keys], ((1,), (1,)))
                scores = jnp.where(allowed, scores * 0.125, masked_value)
                peak = jnp.max(scores, -1, keepdims=True)
                weights = jnp.where(allowed, jnp.exp(scores - peak), 0.0)
                total = jnp.maximum(jnp.sum(weights, -1, keepdims=True), 1.0)
                probs = (weights * (1.0 / total)).astype(b16)
                probs_v[h, at : at + half, 0:keys] = probs
                if keys < seq:
                    probs_v[h, at : at + half, keys:seq] = jnp.zeros((half, seq - keys), b16)
                out = jnp.where(mask, dot(probs, v[:keys]), out)
            ob_v[part_q * n // 2 : (part_q + 1) * n // 2, s] = out.astype(b16).reshape(
                n // 2, rows, hc
            )
        kept.start()
        kept.wait()
        return carry

    lax.fori_loop(0, slots, attend, 0)
    moves.store(ob_v, ob_out)
    for part in gu_z[0][:2]:
        part.forward()

    xs_g.sent()

    def to_hidden(i, carry):
        block_of(wide_x, i)[...] = dot(
            ob_v[i].reshape(local_rows, hc), w_out_v[...].reshape(hc, width)
        ).astype(b16)
        return carry

    lax.fori_loop(0, n, to_hidden, 0)
    wait_a1.wait()
    sums = LayerScatter(
        wires, lambda i: block_of(wide_x, i), lambda j: near.at[j], lambda j: far.at[j]
    )
    sums.start()
    for m in (6, 4, 2):
        sums.step(m)
    for part in gu_z[0][2:]:
        part.forward()
    hidden = hidden_v[...] + sums.total()
    hidden_v[...] = hidden
    moves.store(hidden_v, hidden_out)
    block_of(wide_a, c)[...] = (layer_stats(hidden)[0] * norms[2:3] + norms[3:4]).astype(b16)
    a2_g = LayerGather(wires, lambda i: block_of(wide_a, i))
    a2_g.start()
    gu_z[1][0].forward()
    for m in (2, 4, 6):
        a2_g.forward(m)
    for part in gu_z[1][1:]:
        part.forward()
    for m in (1, 3, 5, 7):
        dy_g.arrived(m)
    for m in (1, 3, 5, 7):
        a2_g.arrived(m)
    wait_a2 = moves.load(wide_a, a2_out)

    down_sums = []
    for step, ((at, size), (start, count), parts) in enumerate(zip(halves, spans, gu_z)):
        units, gates = slice(at, at + size), slice(start, start + 2 * count)
        inner = slice(zs * at, zs * (at + size))
        for _, _, chain in down_sums:
            chain.hop(1, 3)
        for part in parts:
            part.finish()

        def feed(i, carry, inner=inner, gates=gates, count=count):
            gu = dot(wide_a[pair_at(i)], w_gu_v[:, :, :, gates].reshape(width, 2 * count))
            gu_v[i, :, gates] = gu.astype(b16)
            gate = gu[:, :count]
            zz_v[i, :, inner] = (gate * jax.nn.sigmoid(gate) * gu[:, count:]).astype(b16)
            return carry

        lax.fori_loop(0, n // 2, feed, 0)
        if step == 1:
            down_z[0].hop(1)
            down_z[1].hop(1)
        chains = []
        for p in range(2):
            k = slice(p * width // 2, (p + 1) * width // 2)
            for q in columns[2 * p : 2 * p + 2]:
                gd = dot(
                    zz_v[:, :, inner].reshape(tokens, count),
                    dy_v[:, :, q].reshape(tokens, tile),
                    ((0,), (0,)),
                )
                gd_v[:, units, q] = gd.astype(b16).reshape(zs, size, tile)
            chains.append(
                ChainScatter(
                    wires,
                    lambda i, u=units, k=k: gd_v.at[i, u, k],
                    lambda i, u=units, k=k: right_v.at[i - 1, u, k],
                    lambda i, u=units, k=k: left_v.at[i, u, k],
                )
            )
            chains[-1].start(3)
            down_sums.append((units, k, chains[-1]))
            if step == 1:
                down_z[2 + p].hop(1)
                down_z[p].hop(2)
                down_sums[p][2].hop(1, 2)
        for distance in (2, 1):
            for chain in chains:
                chain.start(distance)
        for chain in chains:
            chain.clear()
    moves.store(w_gu_v, w_gu_out)
    sums.sent()
    a2_g.sent()
    wait_a2.wait()

    def products(p):
        k = columns[p]

        def rows_of(i, carry):
            dy_rows = dy_v[pl.ds(2 * i, 2), :, k].reshape(pair, tile)
            y = jnp.zeros((pair, tile), f32)
            for at, size in halves:
                weight = w_down_v[:, at : at + size, k].reshape(zs * size, tile)
                inner = slice(zs * at, zs * (at + size))
                dz = dot(dy_rows, weight, ((1,), (1,)))
                dz_v[i, :, inner] = dz if p == 0 else dz_v[i, :, inner] + dz
                y = y + dot(zz_v[i, :, inner], weight)
            wide_x[pair_at(i), k] = y.astype(b16)
            return carry

        lax.fori_loop(0, n // 2, rows_of, 0)

    chains = [chain for _, _, chain in down_sums]
    for t in (0, 1):
        chains[t].hop(2, 3)
        down_z[2 + t].hop(2)
    for t in (2, 3):
        chains[t].hop(1, 3)
    for t in (2, 3):
        chains[t].hop(1, 2)
    for t in (2, 3):
        chains[t].hop(2, 3)
    for t in range(number):
        down_z[t].finish()
        products(t)
    moves.store(wide_x, y_out)

    def back(i, carry):
        for (at, size), (start, count) in zip(halves, spans):
            dz = dz_v[i, :, zs * at : zs * (at + size)]
            gate = gu_v[i, :, start : start + count].astype(f32)
            up = gu_v[i, :, start + count : start + 2 * count].astype(f32)
            sig = jax.nn.sigmoid(gate)
            dg = dz * up * sig * (1.0 + gate * (1.0 - sig))
            du = dz * gate * sig
            gu_v[i, :, start : start + 2 * count] = jnp.concatenate([dg, du], -1).astype(b16)
        return carry

    lax.fori_loop(0, n // 2, back, 0)
    moves.store(gu_v, dgu_out)
    for units, k, chain in down_sums:
        grad_down_out[units, k] = chain.total()
    for group in (*chains, dy_g):
        group.sent()
    for copy in (*small_z, *qkv_x, *gu_x):
        copy.wait_send()
    moves.finish()


def front(zs, n, lengths, tables, small, w_qkv, w_gate, w_up, w_out, w_down, inputs, cotangent):
    f32, b16 = jnp.float32, jnp.bfloat16
    rows, slots, width = inputs.shape
    local = rows * slots
    seq, tokens = rows * n, local * n
    heads = HEADS // n
    hc = heads * HEAD_DIM
    wrows = w_out.shape[0]
    block = w_down.shape[0]
    gc = 2 * zs * block
    qkv_all = ((zs, n, wrows, 3 * hc), b16)
    out_all = ((zs, wrows, width), b16)
    gu_all = ((zs, n, wrows, gc), b16)
    down_all = ((zs, block, width), b16)
    wide = ((tokens, width), b16)
    qkv = ((3, slots, n, rows, hc), b16)
    probs = ((slots, heads, seq, seq), b16)
    ob = ((n, slots, rows, hc), b16)
    hidden = ((local, width), f32)
    gu = ((n // 2, 2 * local, gc), b16)
    outs = [
        qkv_all,
        out_all,
        gu_all,
        wide,
        qkv,
        probs,
        ob,
        hidden,
        wide,
        gu,
        wide,
        ((block, width), f32),
        ((8, width), f32),
    ]
    scratch = [
        ((n, wrows, 3 * hc), b16),
        ((n, wrows, gc), b16),
        ((zs, n, *small.shape), f32),
        ((1, 3 * hc), f32),
        qkv_all,
        out_all,
        gu_all,
        down_all,
        wide,
        wide,
        ((n, local, width), b16),
        qkv,
        (probs[0][1:], b16),
        ob,
        ((n // 2, local, width), b16),
        ((n // 2 - 1, local, width), b16),
        hidden,
        gu,
        ((n // 2, 2 * local, gc // 2), b16),
        ((n // 2, 2 * local, gc // 2), f32),
        down_all,
        ((zs - 1, block, width), b16),
        ((zs - 1, block, width), b16),
        ((2, *inputs.shape), b16),
    ]
    return pl.pallas_call(
        functools.partial(front_kernel, zs, n, slots),
        out_shape=[jax.ShapeDtypeStruct(*k) for k in outs],
        in_specs=[pl.BlockSpec(memory_space=pltpu.SMEM), VMEM, HBM, *[VMEM] * 3, *[HBM] * 4],
        out_specs=[HBM] * (len(outs) - 2) + [VMEM] * 2,
        scratch_shapes=[
            *[pltpu.VMEM(*k) for k in scratch],
            pltpu.SemaphoreType.DMA((192,)),
            pltpu.SemaphoreType.DMA((192,)),
            pltpu.SemaphoreType.DMA((32,)),
        ],
        compiler_params=pltpu.CompilerParams(
            collective_id=1, has_side_effects=True, vmem_limit_bytes=VMEM_LIMIT
        ),
        name="front",
    )(lengths, tables, small, w_qkv, w_gate, w_up, w_out, w_down, inputs, cotangent)


def unpack_columns(dst, src, parts, n, zs):
    dst[...] = jnp.concatenate(
        [
            src[i, :, at + size * j : at + size * (j + 1)]
            for j in range(zs)
            for i in range(n)
            for at, size in parts
        ],
        -1,
    ).astype(dst.dtype)


def backward_kernel(
    zs,
    n,
    norms,
    tables,
    a1_all,
    a2_all,
    dgu,
    w_gu,
    w_qkv,
    w_out,
    qkv,
    probs,
    ob,
    hidden,
    cotangent,
    inputs,
    y_part,
    grad_out_out,
    result_out,
    input_grad_out,
    gq_out,
    gu_out,
    small_out,
    wide_v,
    dgu_v,
    weight_v,
    w_out_v,
    qkv_v,
    probs_v,
    ob_v,
    hidden_v,
    own_v,
    raw_v,
    ggu_v,
    relay_v,
    box_v,
    near,
    far,
    dh_all,
    go_v,
    go_relay,
    go_box,
    dqkv_v,
    dj_v,
    bias_v,
    gq_relay,
    gq_box,
    gu_rows,
    gq_rows,
    small_v,
    small_x,
    small_r,
    small_z,
    send,
    recv,
    local,
    free,
):
    f32, b16 = jnp.float32, jnp.bfloat16
    wires = Wires(send, recv)
    moves = Moves(local)
    z, c = wires.z, wires.c
    _, slots, rows, hc = ob_v.shape
    width = dh_all.shape[-1]
    tokens, seq, local_rows = n * slots * rows, n * rows, slots * rows
    heads = hc // HEAD_DIM
    wrows, gc = ggu_v.shape[2:]
    depth = n * wrows
    ffc, qc = gc // 2, 3 * hc
    part = wide_v
    gu_weight = weight_v.at[:, :, :, 0:gc]
    qkv_weight, gq_v = weight_v.at[:, :, :, 0:qc], weight_v.at[:, :, :, qc : 2 * qc]

    wait_a2 = moves.load(a2_all, wide_v)
    wait_dy = moves.load(cotangent, raw_v)
    wait_dgu = moves.load(dgu, dgu_v)
    wait_w = moves.load(w_gu, gu_weight)
    waits = [
        moves.load(hidden, hidden_v),
        moves.load(w_out, w_out_v),
        moves.load(qkv, qkv_v),
        moves.load(probs.at[0], probs_v),
        moves.load(ob, ob_v),
    ]
    wires.greet(zs, n)
    wait_a2.wait()
    wait_dgu.wait()

    number = 4
    step = depth // 2

    quarter = wrows // number

    def scatters(whole, relay, box):
        rows_of = [slice(p * quarter, (p + 1) * quarter) for p in range(number)]
        return [
            DepthScatter(
                wires,
                lambda i, k=k: whole.at[i, :, k],
                relay.at[:, k],
                [box.at[j, :, k] for j in range(3)],
            )
            for k in rows_of
        ]

    def weigh(sums, whole, left_v, grads, also=None):
        for mask in (3, 2, 1, 0):
            to = flip(z, mask)

            def piece(p, carry, to=to):
                at = pl.multiple_of(to * depth + p * step, step)
                left = left_v[:, :, pl.ds(at, step)].reshape(tokens, step)
                gradient = dot(left, grads(), ((0,), (0,))).astype(b16)
                whole[to, pl.ds(p * (n // 2), n // 2)] = gradient.reshape(n // 2, wrows, -1)
                return carry

            lax.fori_loop(0, 2, piece, 0)
            for part_sum in sums:
                part_sum.start(mask)
            if mask == 3 and also is not None:
                also.start(3)

    gu_sums = scatters(ggu_v, relay_v, box_v)
    weigh(gu_sums, ggu_v, wide_v, lambda: dgu_v[...].reshape(tokens, gc))

    wait_w.wait()

    def normed_two(i, carry):
        part[pl.ds(2 * i, 2)] = (
            dot(dgu_v[i], gu_weight[...].reshape(width, gc), ((1,), (1,)))
            .astype(b16)
            .reshape(2, local_rows, width)
        )
        return carry

    lax.fori_loop(0, n // 2, normed_two, 0)
    wait_qkv = moves.load(w_qkv, qkv_weight)
    da2_sums = LayerScatter(
        wires, lambda i: part.at[i], lambda j: near.at[j], lambda j: far.at[j]
    )
    da2_sums.start()
    gu_sums[0].relay()
    for m in (6, 4, 2):
        da2_sums.step(m)
    for copy in waits:
        copy.wait()
    wait_dy.wait()
    by_slot(own_v, raw_v)
    wait_xs = moves.load(inputs, raw_v)
    n2, r2 = layer_stats(hidden_v[...])
    for part_sum in gu_sums[1:]:
        part_sum.relay()
    da2 = da2_sums.total()
    gains = [jnp.sum(da2 * n2, 0, keepdims=True), jnp.sum(da2, 0, keepdims=True)]
    dh = own_v[...].astype(f32) + norm_back(da2, n2, r2, norms[2:3])
    by_position(input_grad_out, dh)
    dh_all[c] = dh.astype(b16)
    dh_g = LayerGather(wires, lambda i: dh_all.at[i])
    dh_g.start()
    da2_sums.sent()
    wait_y = moves.load(y_part, part)
    for m in (2, 4, 6):
        dh_g.forward(m)
    for m in (1, 3, 5, 7):
        dh_g.arrived(m)
    wait_y.wait()
    y_sums = LayerScatter(
        wires, lambda i: part.at[i], lambda j: near.at[j], lambda j: far.at[j]
    )
    y_sums.start()

    go_sums = DepthScatter(
        wires, lambda i: go_v.at[i], go_relay, [go_box.at[j] for j in range(3)]
    )
    tile = width // 4

    def heads_grad(p, carry):
        at = pl.ds(pl.multiple_of(p * tile, tile), tile)
        go = dot(
            ob_v[...].reshape(tokens, hc), dh_all[:, :, at].reshape(tokens, tile), ((0,), (0,))
        )
        go_v[:, :, at] = go.astype(b16).reshape(zs, hc // zs, tile)
        return carry

    lax.fori_loop(0, 4, heads_grad, 0)

    def heads_back(i, carry):
        ob_v[i] = (
            dot(dh_all[i], w_out_v[...].reshape(hc, width), ((1,), (1,)))
            .astype(b16)
            .reshape(slots, rows, hc)
        )
        return carry

    for m in (6, 4, 2):
        y_sums.step(m)
    lax.fori_loop(0, n, heads_back, 0)
    dh_g.sent()
    wait_a1 = moves.load(a1_all, dh_all)
    half = seq // 2

    def attend(s, carry):
        q, k, v = [qkv_v[i, s].reshape(seq, hc) for i in range(3)]
        do_s = ob_v[:, s].reshape(seq, hc)
        dqkv_v[...] = jnp.zeros_like(dqkv_v)
        for part_q in range(2):
            keys = (part_q + 1) * half
            at = part_q * half
            query, do_q = q[at : at + half], do_s[at : at + half]
            dq = jnp.zeros((half, hc), f32)
            for h in range(heads):
                mask, mask_k = head_mask(half, hc, h), head_mask(keys, hc, h)
                do_h = jnp.where(mask, do_q, 0).astype(b16)
                low = probs_v[h, at : at + half, 0:keys]
                p32 = low.astype(f32)
                t = p32 * dot(do_h, v[:keys], ((1,), (1,)))
                ds = (t - p32 * jnp.sum(t, -1, keepdims=True)).astype(b16)
                dq = jnp.where(mask, dot(ds, k[:keys]), dq)
                dk = dot(ds, query, ((0,), (0,)))
                dv = dot(low, do_h, ((0,), (0,)))
                dqkv_v[1, 0:keys] += jnp.where(mask_k, dk, 0.0)
                dqkv_v[2, 0:keys] += dv
            dqkv_v[0, at : at + half] = dq

        @pl.when(s + 1 < slots)
        def _():
            copy = pltpu.make_async_copy(probs.at[s + 1], probs_v, probs_sem)
            copy.start()
            copy.wait()

        dq, dk = dqkv_v[0] * 0.125, dqkv_v[1] * 0.125
        table = [tables[i].reshape(seq, 2 * HEAD_DIM) for i in range(3)]
        dj = [turn_pair(dq, table, -1.0), turn_pair(dk, table, -1.0), dqkv_v[2]]
        for i in range(3):
            low = dj[i].astype(b16)
            dj_v[:, s, :, i * hc : (i + 1) * hc] = low.reshape(n, rows, hc)
            bias_v[:, i * hc : (i + 1) * hc] += jnp.sum(low.astype(f32), 0, keepdims=True)
        return carry

    bias_v[...] = jnp.zeros_like(bias_v)

    probs_sem = moves.sems.at[next(moves.number)]
    lax.fori_loop(0, slots, attend, 0)

    wait_a1.wait()
    wait_qkv.wait()
    qkv_sums = scatters(gq_v, gq_relay, gq_box)
    weigh(qkv_sums, gq_v, dh_all, lambda: dj_v[...].reshape(tokens, qc), go_sums)
    for mask in (2, 1, 0):
        go_sums.start(mask)

    def normed_one(i, carry):
        part[pl.ds(2 * i, 2)] = (
            dot(
                dj_v[pl.ds(2 * i, 2)].reshape(2 * local_rows, qc),
                qkv_weight[...].reshape(width, qc),
                ((1,), (1,)),
            )
            .astype(b16)
            .reshape(2, local_rows, width)
        )
        return carry

    by_position(result_out, hidden_v[...] + y_sums.total())
    for m in (1, 2, 4, 6):
        pl.semaphore_signal(free, inc=1, device_id=(z, flip(c, m)), device_id_type=MESH)
    y_sums.sent()
    lax.fori_loop(0, n // 2, normed_one, 0)
    pl.semaphore_wait(free, 4)
    da1_sums = LayerScatter(
        wires, lambda i: part.at[i], lambda j: near.at[j], lambda j: far.at[j]
    )
    da1_sums.start()
    for m in (6, 4, 2):
        da1_sums.step(m)

    for p, part_sum in enumerate(gu_sums):
        ggu_v[z, :, p * quarter : (p + 1) * quarter] = part_sum.total().astype(b16)
    gu_x = [wires.put(ggu_v.at[z, flip(c, m)], gu_rows.at[c], 0, m) for m in range(1, n)]
    for copy in gu_x:
        copy.start()
    gu_rows[c] = ggu_v[z, c]

    for part_sum in qkv_sums:
        part_sum.relay()
    go_sums.relay()

    wait_xs.wait()
    by_slot(own_v, raw_v)
    n1, r1 = layer_stats(own_v[...].astype(f32))
    da1 = da1_sums.total()
    grad = norm_back(da1, n1, r1, norms[0:1])
    for s in range(slots):
        input_grad_out[:, s, :] += grad[s * rows : (s + 1) * rows]
    gains = [jnp.sum(da1 * n1, 0, keepdims=True), jnp.sum(da1, 0, keepdims=True), *gains]
    chips = n // 2
    lanes = 2 * HEAD_DIM
    lane_half = lax.broadcasted_iota(jnp.int32, (1, lanes), 1) // HEAD_DIM
    bias_part = bias_v[...]
    for j in range(zs):
        for chip in range(chips):
            k = j * chips + chip
            for r in range(4):
                small_v[j, chip, r : r + 1] = gains[r][:, k * lanes : (k + 1) * lanes]
            small_v[j, chip, 7:8] = jnp.zeros((1, lanes), f32)
    for i in range(3):
        for j in range(zs):
            at = i * hc + j * HEAD_DIM
            piece = bias_part[:, at : at + HEAD_DIM]
            both = jnp.concatenate([piece, piece], -1)
            for chip in range(chips):
                tile = (i * zs + j) * chips + chip
                pair, row = tile // 3, tile % 3
                small_v[pair // chips, pair % chips, 4 + row : 5 + row] = jnp.where(
                    (lane_half == c % 2) & (c // 2 == chip), both, 0.0
                )
    small_v_x = [
        wires.put(small_v.at[:, flip(c, m) // 2], small_x.at[m], 0, m) for m in range(1, n)
    ]
    for copy in small_v_x:
        copy.start()

    small_sum = small_v[:, c // 2]
    for m in range(1, n):
        small_v_x[m - 1].wait_recv()
        small_sum = small_sum + small_x[m]
    small_r[...] = small_sum
    small_z_x = [wires.put(small_r.at[flip(z, m)], small_z.at[m], m, 0) for m in range(1, zs)]
    for copy in small_z_x:
        copy.start()
    for copy in gu_x:
        copy.wait_recv()
    moves.store(gu_rows, gu_out)
    gq_x = []
    for p, part_sum in enumerate(qkv_sums):
        k = slice(p * quarter, (p + 1) * quarter)
        gq_v[z, :, k] = part_sum.total().astype(b16)
        copies = [
            wires.put(gq_v.at[z, flip(c, m), k], gq_rows.at[c, k], 0, m) for m in range(1, n)
        ]
        for copy in copies:
            copy.start()
        gq_x += copies
    gq_rows[c] = gq_v[z, c]
    small_sum = small_r[z]
    for m in range(1, zs):
        small_z_x[m - 1].wait_recv()
        small_sum = small_sum + small_z[m]
    small_out[...] = small_sum
    hidden_v[0:wrows] = go_sums.total()
    moves.store(hidden_v.at[0:wrows], grad_out_out)
    for group in (*gu_sums, go_sums, *qkv_sums, da1_sums):
        group.sent()
    for copy in (*gu_x, *small_v_x, *small_z_x):
        copy.wait_send()
    for copy in gq_x:
        copy.wait()
    moves.store(gq_rows, gq_out)
    moves.finish()


def backward(zs, n, norms, tables, *arrays):
    f32, b16 = jnp.float32, jnp.bfloat16
    a1_all, a2_all, dgu, w_gu, w_qkv, w_out, qkv, probs, ob, hidden, _, inputs, _ = arrays
    _, slots, rows, hc = ob.shape
    local, width = hidden.shape
    _, _, wrows, gc = w_gu.shape
    qc = 3 * hc
    seq = n * rows
    wide = (n, local, width)

    def buf(like):
        return pltpu.VMEM(like.shape, like.dtype)

    return pl.pallas_call(
        functools.partial(backward_kernel, zs, n),
        out_shape=[
            jax.ShapeDtypeStruct((hc // zs, width), f32),
            jax.ShapeDtypeStruct(inputs.shape, b16),
            jax.ShapeDtypeStruct(inputs.shape, f32),
            jax.ShapeDtypeStruct((n, wrows, qc), b16),
            jax.ShapeDtypeStruct((n, wrows, gc), b16),
            jax.ShapeDtypeStruct((8, 2 * HEAD_DIM), f32),
        ],
        in_specs=[VMEM] * 2 + [HBM] * 13,
        out_specs=[HBM, VMEM, VMEM, HBM, HBM, VMEM],
        scratch_shapes=[
            pltpu.VMEM(wide, b16),
            buf(dgu),
            pltpu.VMEM((zs, n, wrows, max(gc, 2 * qc)), b16),
            buf(w_out),
            buf(qkv),
            pltpu.VMEM(probs.shape[1:], b16),
            buf(ob),
            buf(hidden),
            pltpu.VMEM((local, width), b16),
            pltpu.VMEM(inputs.shape, b16),
            pltpu.VMEM((zs, n, wrows, gc), b16),
            pltpu.VMEM((n, wrows, gc), b16),
            pltpu.VMEM((3, n, wrows, gc), b16),
            pltpu.VMEM((n // 2, local, width), b16),
            pltpu.VMEM((n // 2 - 1, local, width), b16),
            pltpu.VMEM(wide, b16),
            pltpu.VMEM((zs, hc // zs, width), b16),
            pltpu.VMEM((hc // zs, width), b16),
            pltpu.VMEM((3, hc // zs, width), b16),
            pltpu.VMEM((3, seq, hc), f32),
            pltpu.VMEM((n, slots, rows, qc), b16),
            pltpu.VMEM((1, qc), f32),
            pltpu.VMEM((n, wrows, qc), b16),
            pltpu.VMEM((3, n, wrows, qc), b16),
            pltpu.VMEM((n, wrows, gc), b16),
            pltpu.VMEM((n, wrows, qc), b16),
            pltpu.VMEM((zs, n // 2, 8, 2 * HEAD_DIM), f32),
            pltpu.VMEM((n, zs, 8, 2 * HEAD_DIM), f32),
            pltpu.VMEM((zs, 8, 2 * HEAD_DIM), f32),
            pltpu.VMEM((zs, 8, 2 * HEAD_DIM), f32),
            pltpu.SemaphoreType.DMA((128,)),
            pltpu.SemaphoreType.DMA((128,)),
            pltpu.SemaphoreType.DMA((24,)),
            pltpu.SemaphoreType.REGULAR,
        ],
        compiler_params=pltpu.CompilerParams(
            collective_id=4, has_side_effects=True, vmem_limit_bytes=VMEM_LIMIT
        ),
        name="backward",
    )(norms, tables, *arrays)


def finish_kernel(
    zs,
    n,
    gq,
    gu,
    small,
    grad_out,
    grad_down,
    result,
    input_grad,
    qkv_out,
    gate_out,
    up_out,
    grad_out_out,
    grad_down_out,
    result_out,
    input_grad_out,
    bias_out,
    gain_one_out,
    shift_one_out,
    gain_two_out,
    shift_two_out,
    gq_v,
    gu_v,
    qkv_v,
    gate_v,
    up_v,
    grad_out_v,
    grad_down_v,
    result_v,
    input_grad_v,
    local,
):
    moves = Moves(local)
    width = grad_out.shape[1]
    wait_gu = moves.load(gu, gu_v)
    wait_gq = moves.load(gq, gq_v)
    passed = [
        (moves.load(src, held), held, dst)
        for src, held, dst in (
            (input_grad, input_grad_v, input_grad_out),
            (grad_down, grad_down_v, grad_down_out),
            (result, result_v, result_out),
            (grad_out, grad_out_v, grad_out_out),
        )
    ]
    odd = lax.axis_index("ctx") % 2
    for r, out in enumerate((gain_one_out, shift_one_out, gain_two_out, shift_two_out)):
        row = small[r : r + 1]
        out[...] = jnp.where(odd == 0, row[:, :HEAD_DIM], row[:, HEAD_DIM:])
    bias = jnp.concatenate([small[4 + r : 5 + r] for r in range(3)], -1)
    size = bias_out.shape[1]
    bias_out[...] = jnp.where(odd == 0, bias[:, :size], bias[:, size:])
    ffc = gu_v.shape[-1] // 2
    halves = halves_of(ffc // zs)
    for copy, held, dst in passed:
        copy.wait()
        moves.store(held, dst)
    wait_gu.wait()
    unpack_columns(gate_v, gu_v, [(2 * zs * at, size) for at, size in halves], n, zs)
    moves.store(gate_v, gate_out)
    unpack_columns(up_v, gu_v, [(zs * (2 * at + size), size) for at, size in halves], n, zs)
    moves.store(up_v, up_out)
    wait_gq.wait()
    hc = gq_v.shape[-1] // 3
    for i in range(3):
        unpack_columns(
            qkv_v.at[:, i * width : (i + 1) * width], gq_v, [(i * hc, HEAD_DIM)], n, zs
        )
    moves.store(qkv_v, qkv_out)
    moves.finish()


def finish(zs, n, gq, gu, small, grad_out, grad_down, result, input_grad):
    f32 = jnp.float32
    _, wrows, qc = gq.shape
    gc = gu.shape[-1]
    wide = [((wrows, n * qc), f32), ((wrows, n * gc // 2), f32), ((wrows, n * gc // 2), f32)]
    whole = [(v.shape, v.dtype) for v in (grad_out, grad_down, result, input_grad)]
    rows = [((1, 3 * HEAD_DIM), f32), *[((1, wrows), f32)] * 4]
    return pl.pallas_call(
        functools.partial(finish_kernel, zs, n),
        out_shape=[jax.ShapeDtypeStruct(*k) for k in (*wide, *whole, *rows)],
        in_specs=[HBM, HBM, VMEM, HBM, HBM, HBM, HBM],
        out_specs=[HBM] * 7 + [VMEM] * 5,
        scratch_shapes=[
            pltpu.VMEM(gq.shape, gq.dtype),
            pltpu.VMEM(gu.shape, gu.dtype),
            *[pltpu.VMEM(*k) for k in (*wide, *whole)],
            pltpu.SemaphoreType.DMA((16,)),
        ],
        compiler_params=pltpu.CompilerParams(vmem_limit_bytes=VMEM_LIMIT),
        name="finish",
    )(gq, gu, small, grad_out, grad_down, result, input_grad)


def tensor_shards(
    inputs,
    lengths,
    w_qkv,
    b_qkv,
    w_out,
    w_gate,
    w_up,
    w_down,
    gain_one,
    shift_one,
    gain_two,
    shift_two,
    cotangent,
):
    rows, slots, width = inputs.shape
    f32, b16 = jnp.float32, jnp.bfloat16
    zs, n = lax.axis_size("dp"), lax.axis_size("ctx")
    me = lax.axis_index("ctx")
    local = rows * slots
    seq = rows * n
    wrows = w_qkv.shape[0]
    ff_block = w_down.shape[0]
    hc = HEADS // n * HEAD_DIM
    ffc = ff_block * zs

    nb = b_qkv.shape[0]
    vectors = [v for gain in (gain_one, shift_one, gain_two, shift_two) for v in (gain, gain)]
    small, at = jnp.zeros(1024, jnp.bfloat16), 0
    for vector in (*vectors, b_qkv):
        size = vector.shape[0]
        small = small + jnp.pad(vector, (at, 1024 - at - size))
        at += size
    small = small.reshape(8, 128).astype(f32)

    angles = np.arange(seq)[:, None] * 10000.0 ** (-2.0 * np.arange(ROTARY // 2) / ROTARY)[None, :]
    cos_t, sin_t = np.cos(angles), np.sin(angles)
    zero, rest = np.zeros_like(sin_t), np.zeros((seq, HEAD_DIM - ROTARY))
    tables = np.stack(
        [
            np.concatenate(two, -1)
            for two in (
                2 * [cos_t, cos_t, rest + 1.0],
                2 * [-sin_t, zero, rest],
                2 * [zero, sin_t, rest],
            )
        ]
    ).astype(np.float32)

    tables = jnp.asarray(tables.reshape(3, n, rows, 2 * HEAD_DIM))
    w_qkv_c, w_out_c, w_gu_c, a1, qkv, probs, ob, hidden, a2, dgu, y, grad_down, norms = front(
        zs, n, lengths, tables, small, w_qkv, w_gate, w_up, w_out, w_down, inputs, cotangent
    )
    wide = (n, local, width)
    grad_out, result, input_grad, gq, gu, sums = backward(
        zs, n, norms, tables, a1.reshape(wide), a2.reshape(wide), dgu,
        w_gu_c, w_qkv_c, w_out_c, qkv, probs, ob, hidden, cotangent, inputs,
        y.reshape(wide),
    )
    grad_qkv, grad_gate, grad_up, grad_out, grad_down, result, input_grad, *rows = finish(
        zs, n, gq, gu, sums, grad_out, grad_down, result, input_grad
    )
    grad_bias, grad_gain_one, grad_shift_one, grad_gain_two, grad_shift_two = [
        row.reshape(row.shape[1]) for row in rows
    ]
    return (
        result,
        input_grad,
        grad_qkv,
        grad_bias,
        grad_out,
        grad_gate,
        grad_up,
        grad_down,
        grad_gain_one,
        grad_shift_one,
        grad_gain_two,
        grad_shift_two,
    )


def solution(mesh):
    zs, n = mesh.shape["dp"], mesh.shape["ctx"]
    shards = tensor_shards if (zs, n) == (4, 8) and HEADS == 32 else gathered_shards

    placed = (
        P("ctx", "dp", None),
        P("dp", None),
        P(("dp", "ctx"), None),
        P(("dp", "ctx")),
        P(("dp", "ctx"), None),
        P(("dp", "ctx"), None),
        P(("dp", "ctx"), None),
        P(("dp", "ctx"), None),
        P(("dp", "ctx")),
        P(("dp", "ctx")),
        P(("dp", "ctx")),
        P(("dp", "ctx")),
        P("ctx", "dp", None),
    )
    return jax.shard_map(
        shards,
        mesh=mesh,
        in_specs=placed,
        out_specs=(
            P("ctx", "dp", None),
            P("ctx", "dp", None),
            P(("dp", "ctx"), None),
            P(("dp", "ctx")),
            P(("dp", "ctx"), None),
            P(("dp", "ctx"), None),
            P(("dp", "ctx"), None),
            P(("dp", "ctx"), None),
            P(("dp", "ctx")),
            P(("dp", "ctx")),
            P(("dp", "ctx")),
            P(("dp", "ctx")),
        ),
        check_vma=False,
    )
```
